32 devices in a mesh: dp: 4 (over z), fsdp: 8 (over y, x, core).
Axes of the slice: x: 2, y: 2, z: 4, core: 2. Of those that a mesh axis runs over, the one named last changes fastest.
Arguments:
- tokens: bfloat16 [11040, 768], P(('dp', 'fsdp')), may hold values from -6 to 6
- cotangent: bfloat16 [11040, 768], P(('dp', 'fsdp')), may hold values from -6 to 6
- norm1_gain: bfloat16 [2, 768], P(None, 'fsdp'), may hold values from 0.099609375 to 1.8984375
- norm1_bias: bfloat16 [2, 768], P(None, 'fsdp'), may hold values from -3 to 3
- qkv_weight: bfloat16 [2, 768, 2304], P(None, 'fsdp'), may hold values from -0.21875 to 0.21875
- query_bias: bfloat16 [2, 768], P(None, 'fsdp'), may hold values from -3 to 3
- value_bias: bfloat16 [2, 768], P(None, 'fsdp'), may hold values from -3 to 3
- out_weight: bfloat16 [2, 768, 768], P(None, 'fsdp'), may hold values from -1.75 to 1.75
- out_bias: bfloat16 [2, 768], P(None, 'fsdp'), may hold values from -3 to 3
- norm2_gain: bfloat16 [2, 768], P(None, 'fsdp'), may hold values from 0.099609375 to 1.8984375
- norm2_bias: bfloat16 [2, 768], P(None, 'fsdp'), may hold values from -3 to 3
- up_weight: bfloat16 [2, 768, 3072], P(None, 'fsdp'), may hold values from -0.21875 to 0.21875
- up_bias: bfloat16 [2, 3072], P(None, 'fsdp'), may hold values from -4 to 4
- down_weight: bfloat16 [2, 3072, 768], P(None, 'fsdp'), may hold values from -0.109375 to 0.109375
- down_bias: bfloat16 [2, 768], P(None, 'fsdp'), may hold values from -3 to 3
Outputs:
- encoded: bfloat16 [11040, 768], P(('dp', 'fsdp'))
- tokens_grad: float32 [11040, 768], P(('dp', 'fsdp'))
- grad_norm1_gain: float32 [2, 768], P(None, 'fsdp')
- grad_norm1_bias: float32 [2, 768], P(None, 'fsdp')
- grad_qkv_weight: float32 [2, 768, 2304], P(None, 'fsdp')
- grad_query_bias: float32 [2, 768], P(None, 'fsdp')
- grad_value_bias: float32 [2, 768], P(None, 'fsdp')
- grad_out_weight: float32 [2, 768, 768], P(None, 'fsdp')
- grad_out_bias: float32 [2, 768], P(None, 'fsdp')
- grad_norm2_gain: float32 [2, 768], P(None, 'fsdp')
- grad_norm2_bias: float32 [2, 768], P(None, 'fsdp')
- grad_up_weight: float32 [2, 768, 3072], P(None, 'fsdp')
- grad_up_bias: float32 [2, 3072], P(None, 'fsdp')
- grad_down_weight: float32 [2, 3072, 768], P(None, 'fsdp')
- grad_down_bias: float32 [2, 768], P(None, 'fsdp')
The draws below stay inside these ranges and needn't reach their ends.
All inputs are finite; a program needn't handle non-finite values.
Results may differ from the reference program's by a relative error of at most 0.015.
Values may be sent and summed in bfloat16 or wider, within the bound.
A program may use at most 192 MiB of HBM per device.

```python
import jax
import jax.numpy as jnp
from jax import lax

D = 768
HEADS = 12
HEAD_DIM = 64
FF = 3072
GLEN = 197
LLEN = 37
LAYERS = 2
G_DEV = 1
L_DEV = 4
ROWS_DEV = 345
TOKENS = 11040
N_DP = 4
N_FSDP = 8


def steps_of(rng, extent, pieces, low, largest):
    level = 1.0
    for axis_at, blocks in pieces:
        heights = jax.random.uniform(jax.random.fold_in(jax.random.fold_in(rng, 6), axis_at), (blocks,), jnp.float32, low / len(pieces), largest / len(pieces))
        level = level * jnp.repeat(jnp.exp(heights), extent[axis_at] // blocks).reshape((-1,) + (1,) * (len(extent) - 1 - axis_at))
    return level


def noise(key, shape, scale, reach, split=(), kind=jnp.bfloat16):
    values = scale * jax.random.normal(key, shape, jnp.float32)
    if split:
        values = values * steps_of(key, shape, split, -0.22, 0.18)
    return jnp.clip(values, -reach, reach).astype(kind)


def setup_inputs(seed: int = 0) -> dict:
    arg_keys = jax.random.split(jax.random.key(seed), 16)
    tokens = noise(arg_keys[0], (TOKENS, D), 1.0, 6.0, ((0, 32),))
    cotangent = noise(arg_keys[1], (TOKENS, D), 1.0, 6.0, ((0, 32),))
    norm1_gain = jnp.clip(1.0 + 0.18 * jax.random.normal(arg_keys[2], (LAYERS, D), jnp.float32), 0.099609375, 1.8984375).astype(jnp.bfloat16)
    norm1_bias = noise(arg_keys[3], (LAYERS, D), 0.5, 3.0, ((1, 8),))
    qkv_weight = noise(arg_keys[4], (LAYERS, D, 3 * D), D ** -0.5, 0.21875, ((1, 8),))
    query_bias = noise(arg_keys[5], (LAYERS, D), 0.5, 3.0, ((1, 8),))
    value_bias = noise(arg_keys[6], (LAYERS, D), 0.5, 3.0, ((1, 8),))
    out_weight = noise(arg_keys[7], (LAYERS, D, D), (D // 64) ** -0.5, 1.75, ((1, 8),))
    out_bias = noise(arg_keys[8], (LAYERS, D), 0.5, 3.0, ((1, 8),))
    norm2_gain = jnp.clip(1.0 + 0.18 * jax.random.normal(arg_keys[9], (LAYERS, D), jnp.float32), 0.099609375, 1.8984375).astype(jnp.bfloat16)
    norm2_bias = noise(arg_keys[10], (LAYERS, D), 0.5, 3.0, ((1, 8),))
    up_weight = noise(arg_keys[11], (LAYERS, D, FF), D ** -0.5, 0.21875, ((1, 8),))
    up_bias = noise(arg_keys[12], (LAYERS, FF), 1.0, 4.0, ((1, 8),))
    down_weight = noise(arg_keys[13], (LAYERS, FF, D), FF ** -0.5, 0.109375, ((1, 8),))
    down_bias = noise(arg_keys[14], (LAYERS, D), 0.5, 3.0, ((1, 8),))
    return {"tokens": tokens, "cotangent": cotangent, "norm1_gain": norm1_gain, "norm1_bias": norm1_bias, "qkv_weight": qkv_weight, "query_bias": query_bias, "value_bias": value_bias, "out_weight": out_weight, "out_bias": out_bias, "norm2_gain": norm2_gain, "norm2_bias": norm2_bias, "up_weight": up_weight, "up_bias": up_bias, "down_weight": down_weight, "down_bias": down_bias}


@jax.custom_vjp
def low(v):
    return lax.optimization_barrier(v.astype(jnp.bfloat16)).astype(jnp.float32)

@jax.custom_vjp
def low_back(v):
    return v

def low_keep(v):
    return (low(v), None)

def low_pass(kept, grad):
    return (grad,)

def back_keep(v):
    return (v, None)

def back_low(kept, grad):
    return (low(grad),)
low.defvjp(low_keep, low_pass)
low_back.defvjp(back_keep, back_low)
highest = lax.Precision.HIGHEST
epsilon = 1e-06

def norm_rows(values_in, gain, shift):
    row_mean = lax.optimization_barrier(jnp.mean(values_in, axis=-1, keepdims=True))
    centred = values_in - row_mean
    spread = lax.optimization_barrier(jnp.mean(centred * centred, axis=-1, keepdims=True))
    return centred * lax.rsqrt(spread + epsilon) * gain + shift

def attend_crops(queries, keys_in, values_in, crop_count, crop_length):
    shape_four = (crop_count, crop_length, HEADS, HEAD_DIM)
    query_four = queries.reshape(shape_four)
    key_four = keys_in.reshape(shape_four)
    value_four = values_in.reshape(shape_four)
    scores = jnp.einsum('clhe,cmhe->chlm', query_four, key_four, precision=highest) * HEAD_DIM ** (-0.5)
    scores = low_back(scores)
    attn_probs = low(jax.nn.softmax(scores, axis=-1))
    result = jnp.einsum('chlm,cmhe->clhe', attn_probs, value_four, precision=highest)
    return result.reshape(crop_count * crop_length, D)

def encoder_layer(stream, layer_weights):
    gain_one, shift_one, w_qkv, bias_query, bias_value, w_out, bias_out, gain_two, shift_two, w_up, bias_up, w_down, bias_down = layer_weights
    normed = low(norm_rows(stream, gain_one, shift_one))
    bias_all = jnp.concatenate([bias_query, jnp.zeros_like(bias_query), bias_value])
    projected = jnp.dot(normed, w_qkv, precision=highest) + bias_all
    projected = low(low_back(projected))
    queries = projected[:, :D]
    keys_in = projected[:, D:2 * D]
    values_in = projected[:, 2 * D:]
    global_rows = G_DEV * GLEN
    global_part = attend_crops(queries[:global_rows], keys_in[:global_rows], values_in[:global_rows], G_DEV, GLEN)
    local_part = attend_crops(queries[global_rows:], keys_in[global_rows:], values_in[global_rows:], L_DEV, LLEN)
    mixed = low(low_back(jnp.concatenate([global_part, local_part], axis=0)))
    stream_one = stream + low_back(jnp.dot(mixed, w_out, precision=highest) + bias_out)
    normed_two = low(norm_rows(stream_one, gain_two, shift_two))
    pre_act = low_back(jnp.dot(normed_two, w_up, precision=highest) + bias_up)
    hidden = low(jax.nn.gelu(pre_act, approximate=False))
    return stream_one + low_back(jnp.dot(hidden, w_down, precision=highest) + bias_down)

def reference(tokens, cotangent, norm1_gain, norm1_bias, qkv_weight, query_bias, value_bias, out_weight, out_bias, norm2_gain, norm2_bias, up_weight, up_bias, down_weight, down_bias):
    params = tuple((w.astype(jnp.float32) for w in (norm1_gain, norm1_bias, qkv_weight, query_bias, value_bias, out_weight, out_bias, norm2_gain, norm2_bias, up_weight, up_bias, down_weight, down_bias)))

    def run_block(block, weights_all):
        for layer_index in range(LAYERS):
            block = encoder_layer(block, tuple((w[layer_index] for w in weights_all)))
        return block
    saved_block = jax.checkpoint(run_block)

    def forward(tokens_float, weights_all):
        blocks = tokens_float.reshape(N_DP * N_FSDP, ROWS_DEV, D)

        def advance(carry, block):
            return (carry, saved_block(block, weights_all))
        unused, outputs = lax.scan(advance, jnp.zeros((), jnp.float32), blocks)
        return outputs.reshape(TOKENS, D)
    result, pullback = jax.vjp(forward, tokens.astype(jnp.float32), params)
    tokens_grad, grads = pullback(cotangent.astype(jnp.float32))
    return (result.astype(jnp.bfloat16), tokens_grad, grads[0], grads[1], grads[2], grads[3], grads[4], grads[5], grads[6], grads[7], grads[8], grads[9], grads[10], grads[11], grads[12])
```

```python
import jax
import jax.numpy as jnp
from jax import lax
from jax.sharding import PartitionSpec as P

D = 768
HEADS = 12
HEAD_DIM = 64
GLEN = 197
LLEN = 37
G_DEV = 1
L_DEV = 4


epsilon = 1e-06


def norm_rows(values_in, gain, shift):
    row_mean = jnp.mean(values_in, axis=-1, keepdims=True)
    centred = values_in - row_mean
    spread = jnp.mean(centred * centred, axis=-1, keepdims=True)
    return centred * lax.rsqrt(spread + epsilon) * gain + shift


def contract_rows(left, right):
    return lax.dot_general(
        left, right, (((0,), (0,)), ((), ())), preferred_element_type=jnp.float32
    )


def contract_cols(left, right):
    return lax.dot_general(
        left, right, (((1,), (1,)), ((), ())), preferred_element_type=jnp.float32
    )


def gather_forward(pieces):
    return (
        lax.all_gather(pieces[0], "fsdp", axis=0, tiled=True),
        lax.all_gather(pieces[1], "fsdp", axis=0, tiled=True),
        lax.all_gather(pieces[2], "fsdp", axis=0, tiled=True),
        lax.all_gather(pieces[3], "fsdp", axis=0, tiled=True),
        lax.all_gather(pieces[4], "fsdp", axis=0, tiled=True),
        lax.all_gather(pieces[5], "fsdp", axis=0, tiled=True),
        lax.all_gather(pieces[6], "fsdp", axis=0, tiled=True),
        lax.all_gather(pieces[7], "fsdp", axis=0, tiled=True),
        lax.all_gather(pieces[8], "fsdp", axis=0, tiled=True),
        lax.all_gather(pieces[9], "fsdp", axis=0, tiled=True),
        lax.all_gather(pieces[10], "fsdp", axis=0, tiled=True),
        lax.all_gather(pieces[11], "fsdp", axis=0, tiled=True),
        lax.all_gather(pieces[12], "fsdp", axis=0, tiled=True),
    )


def reduce_grads(grads):
    shares = (
        lax.psum_scatter(grads[0], "fsdp", scatter_dimension=0, tiled=True),
        lax.psum_scatter(grads[1], "fsdp", scatter_dimension=0, tiled=True),
        lax.psum_scatter(grads[2].astype(jnp.bfloat16), "fsdp", scatter_dimension=0, tiled=True),
        lax.psum_scatter(grads[3], "fsdp", scatter_dimension=0, tiled=True),
        lax.psum_scatter(grads[4], "fsdp", scatter_dimension=0, tiled=True),
        lax.psum_scatter(grads[5].astype(jnp.bfloat16), "fsdp", scatter_dimension=0, tiled=True),
        lax.psum_scatter(grads[6], "fsdp", scatter_dimension=0, tiled=True),
        lax.psum_scatter(grads[7], "fsdp", scatter_dimension=0, tiled=True),
        lax.psum_scatter(grads[8], "fsdp", scatter_dimension=0, tiled=True),
        lax.psum_scatter(grads[9].astype(jnp.bfloat16), "fsdp", scatter_dimension=0, tiled=True),
        lax.psum_scatter(grads[10], "fsdp", scatter_dimension=0, tiled=True),
        lax.psum_scatter(grads[11].astype(jnp.bfloat16), "fsdp", scatter_dimension=0, tiled=True),
        lax.psum_scatter(grads[12], "fsdp", scatter_dimension=0, tiled=True),
    )
    column_parts = (
        lax.psum_scatter(
            shares[2], "dp", scatter_dimension=1, tiled=True
        ).astype(jnp.float32),
        lax.psum_scatter(
            shares[5], "dp", scatter_dimension=1, tiled=True
        ).astype(jnp.float32),
        lax.psum_scatter(
            shares[9], "dp", scatter_dimension=1, tiled=True
        ).astype(jnp.float32),
        lax.psum_scatter(
            shares[11], "dp", scatter_dimension=1, tiled=True
        ).astype(jnp.float32),
    )
    matrices = (
        lax.all_gather(column_parts[0].astype(jnp.bfloat16), "dp", axis=1, tiled=True).astype(
            jnp.float32
        ),
        lax.all_gather(column_parts[1].astype(jnp.bfloat16), "dp", axis=1, tiled=True).astype(
            jnp.float32
        ),
        lax.all_gather(column_parts[2].astype(jnp.bfloat16), "dp", axis=1, tiled=True).astype(
            jnp.float32
        ),
        lax.all_gather(column_parts[3].astype(jnp.bfloat16), "dp", axis=1, tiled=True).astype(
            jnp.float32
        ),
    )
    vectors = lax.psum(
        (
            shares[0],
            shares[1],
            shares[3],
            shares[4],
            shares[6],
            shares[7],
            shares[8],
            shares[10],
            shares[12],
        ),
        "dp",
    )
    return (
        vectors[0],
        vectors[1],
        matrices[0],
        vectors[2],
        vectors[3],
        matrices[1],
        vectors[4],
        vectors[5],
        vectors[6],
        matrices[2],
        vectors[7],
        matrices[3],
        vectors[8],
    )


def attend_crops(queries, keys_in, values_in, crop_count, crop_length):
    shape_four = (crop_count, crop_length, HEADS, HEAD_DIM)
    scores = jnp.einsum(
        "clhe,cmhe->chlm",
        queries.reshape(shape_four),
        keys_in.reshape(shape_four),
        preferred_element_type=jnp.float32,
    ) * HEAD_DIM ** (-0.5)
    peak_score = jnp.max(scores, axis=-1, keepdims=True)
    raised = jnp.exp(scores - peak_score)
    exp_total = jnp.sum(raised, axis=-1, keepdims=True)
    attn_probs = (raised / exp_total).astype(jnp.bfloat16)
    log_total = peak_score + jnp.log(exp_total)
    result = jnp.einsum(
        "chlm,cmhe->clhe",
        attn_probs,
        values_in.reshape(shape_four),
        preferred_element_type=jnp.float32,
    )
    return (result.reshape(crop_count * crop_length, D), log_total)


def attend_back(queries, keys_in, values_in, log_total, grad_mixed, crop_count, crop_length):
    shape_four = (crop_count, crop_length, HEADS, HEAD_DIM)
    score_scale = HEAD_DIM ** (-0.5)
    query_four = queries.reshape(shape_four)
    key_four = keys_in.reshape(shape_four)
    value_four = values_in.reshape(shape_four)
    grad_four = grad_mixed.reshape(shape_four)
    scores = (
        jnp.einsum("clhe,cmhe->chlm", query_four, key_four, preferred_element_type=jnp.float32)
        * score_scale
    )
    attn_probs = jnp.exp(scores - log_total)
    grad_probs = jnp.einsum(
        "clhe,cmhe->chlm", grad_four, value_four, preferred_element_type=jnp.float32
    )
    grad_values = jnp.einsum(
        "chlm,clhe->cmhe",
        attn_probs.astype(jnp.bfloat16),
        grad_four,
        preferred_element_type=jnp.float32,
    )
    row_inner = jnp.sum(grad_probs * attn_probs, axis=-1, keepdims=True)
    grad_scores = (attn_probs * (grad_probs - row_inner)).astype(jnp.bfloat16)
    grad_queries = (
        jnp.einsum("chlm,cmhe->clhe", grad_scores, key_four, preferred_element_type=jnp.float32)
        * score_scale
    )
    grad_keys = (
        jnp.einsum("chlm,clhe->cmhe", grad_scores, query_four, preferred_element_type=jnp.float32)
        * score_scale
    )
    rows_here = crop_count * crop_length
    return jnp.concatenate(
        [
            grad_queries.reshape(rows_here, D),
            grad_keys.reshape(rows_here, D),
            grad_values.reshape(rows_here, D),
        ],
        axis=1,
    )


def forward_layer(stream, weights):
    (
        gain_one,
        shift_one,
        w_qkv,
        bias_query,
        bias_value,
        w_out,
        bias_out,
        gain_two,
        shift_two,
        w_up,
        bias_up,
        w_down,
        bias_down,
    ) = weights
    normed = norm_rows(stream, gain_one.astype(jnp.float32), shift_one.astype(jnp.float32)).astype(
        jnp.bfloat16
    )
    bias_all = jnp.concatenate([bias_query, jnp.zeros_like(bias_query), bias_value]).astype(
        jnp.float32
    )
    projected = (jnp.dot(normed, w_qkv, preferred_element_type=jnp.float32) + bias_all).astype(
        jnp.bfloat16
    )
    global_rows = G_DEV * GLEN
    global_part, global_total = attend_crops(
        projected[:global_rows, :D],
        projected[:global_rows, D : 2 * D],
        projected[:global_rows, 2 * D :],
        G_DEV,
        GLEN,
    )
    local_part, local_total = attend_crops(
        projected[global_rows:, :D],
        projected[global_rows:, D : 2 * D],
        projected[global_rows:, 2 * D :],
        L_DEV,
        LLEN,
    )
    mixed = jnp.concatenate([global_part, local_part], axis=0).astype(jnp.bfloat16)
    stream_one = (
        stream
        + jnp.dot(mixed, w_out, preferred_element_type=jnp.float32)
        + bias_out.astype(jnp.float32)
    )
    normed_two = norm_rows(
        stream_one, gain_two.astype(jnp.float32), shift_two.astype(jnp.float32)
    ).astype(jnp.bfloat16)
    pre_act = jnp.dot(normed_two, w_up, preferred_element_type=jnp.float32) + bias_up.astype(
        jnp.float32
    )
    hidden = jax.nn.gelu(pre_act, approximate=False).astype(jnp.bfloat16)
    result = (
        stream_one
        + jnp.dot(hidden, w_down, preferred_element_type=jnp.float32)
        + bias_down.astype(jnp.float32)
    )
    saved_state = (
        stream,
        normed,
        projected,
        global_total,
        local_total,
        mixed,
        stream_one,
        normed_two,
        pre_act,
        hidden,
    )
    return (result, saved_state)


def backward_layer(upstream, weights, saved_state):
    (
        gain_one,
        shift_one,
        w_qkv,
        bias_query,
        bias_value,
        w_out,
        bias_out,
        gain_two,
        shift_two,
        w_up,
        bias_up,
        w_down,
        bias_down,
    ) = weights
    (
        stream,
        normed,
        projected,
        global_total,
        local_total,
        mixed,
        stream_one,
        normed_two,
        pre_act,
        hidden,
    ) = saved_state
    branch_two = upstream.astype(jnp.bfloat16)
    grad_bias_down = jnp.sum(branch_two.astype(jnp.float32), axis=0)
    grad_w_down = contract_rows(hidden, branch_two)
    grad_hidden = contract_cols(branch_two, w_down)
    unused, gelu_pull = jax.vjp(lambda value: jax.nn.gelu(value, approximate=False), pre_act)
    grad_pre = gelu_pull(grad_hidden)[0].astype(jnp.bfloat16)
    grad_bias_up = jnp.sum(grad_pre.astype(jnp.float32), axis=0)
    grad_w_up = contract_rows(normed_two, grad_pre)
    grad_normed_two = contract_cols(grad_pre, w_up)
    unused_two, norm_pull_two = jax.vjp(
        norm_rows, stream_one, gain_two.astype(jnp.float32), shift_two.astype(jnp.float32)
    )
    grad_stream_part, grad_gain_two, grad_shift_two = norm_pull_two(grad_normed_two)
    grad_stream_one = upstream + grad_stream_part
    branch_one = grad_stream_one.astype(jnp.bfloat16)
    grad_bias_out = jnp.sum(branch_one.astype(jnp.float32), axis=0)
    grad_w_out = contract_rows(mixed, branch_one)
    grad_mixed = contract_cols(branch_one, w_out).astype(jnp.bfloat16)
    global_rows = G_DEV * GLEN
    grad_global = attend_back(
        projected[:global_rows, :D],
        projected[:global_rows, D : 2 * D],
        projected[:global_rows, 2 * D :],
        global_total,
        grad_mixed[:global_rows],
        G_DEV,
        GLEN,
    )
    grad_local = attend_back(
        projected[global_rows:, :D],
        projected[global_rows:, D : 2 * D],
        projected[global_rows:, 2 * D :],
        local_total,
        grad_mixed[global_rows:],
        L_DEV,
        LLEN,
    )
    grad_projected = jnp.concatenate([grad_global, grad_local], axis=0).astype(jnp.bfloat16)
    column_sums = jnp.sum(grad_projected.astype(jnp.float32), axis=0)
    grad_bias_query = column_sums[:D]
    grad_bias_value = column_sums[2 * D :]
    grad_w_qkv = contract_rows(normed, grad_projected)
    grad_normed = contract_cols(grad_projected, w_qkv)
    unused_one, norm_pull_one = jax.vjp(
        norm_rows, stream, gain_one.astype(jnp.float32), shift_one.astype(jnp.float32)
    )
    grad_input_part, grad_gain_one, grad_shift_one = norm_pull_one(grad_normed)
    grad_stream = grad_stream_one + grad_input_part
    grads = (
        grad_gain_one,
        grad_shift_one,
        grad_w_qkv,
        grad_bias_query,
        grad_bias_value,
        grad_w_out,
        grad_bias_out,
        grad_gain_two,
        grad_shift_two,
        grad_w_up,
        grad_bias_up,
        grad_w_down,
        grad_bias_down,
    )
    return (grad_stream, grads)


def local(
    tokens,
    cotangent,
    norm1_gain,
    norm1_bias,
    qkv_weight,
    query_bias,
    value_bias,
    out_weight,
    out_bias,
    norm2_gain,
    norm2_bias,
    up_weight,
    up_bias,
    down_weight,
    down_bias,
):
    shards = (
        norm1_gain,
        norm1_bias,
        qkv_weight,
        query_bias,
        value_bias,
        out_weight,
        out_bias,
        norm2_gain,
        norm2_bias,
        up_weight,
        up_bias,
        down_weight,
        down_bias,
    )
    layer_total = qkv_weight.shape[0]
    stream = tokens.astype(jnp.float32)
    saved_layers = []
    kept_weights = []
    for layer_index in range(layer_total):
        weights = gather_forward(tuple((w[layer_index] for w in shards)))
        stream, saved_state = forward_layer(stream, weights)
        saved_layers.append(saved_state)
        kept_weights.append(weights)
    encoded = stream.astype(jnp.bfloat16)
    upstream = cotangent.astype(jnp.float32)
    reduced_layers = [None] * layer_total
    for layer_index in reversed(range(layer_total)):
        upstream, grads = backward_layer(
            upstream, kept_weights[layer_index], saved_layers[layer_index]
        )
        reduced_layers[layer_index] = reduce_grads(grads)
    stacked = tuple(
        (
            jnp.stack(
                [reduced_layers[layer_index][member] for layer_index in range(layer_total)], axis=0
            )
            for member in range(13)
        )
    )
    return (
        encoded,
        upstream,
        stacked[0],
        stacked[1],
        stacked[2],
        stacked[3],
        stacked[4],
        stacked[5],
        stacked[6],
        stacked[7],
        stacked[8],
        stacked[9],
        stacked[10],
        stacked[11],
        stacked[12],
    )


def solution(mesh):
    in_specs = (
        P(("dp", "fsdp"), None),
        P(("dp", "fsdp"), None),
        P(None, "fsdp"),
        P(None, "fsdp"),
        P(None, "fsdp", None),
        P(None, "fsdp"),
        P(None, "fsdp"),
        P(None, "fsdp", None),
        P(None, "fsdp"),
        P(None, "fsdp"),
        P(None, "fsdp"),
        P(None, "fsdp", None),
        P(None, "fsdp"),
        P(None, "fsdp", None),
        P(None, "fsdp"),
    )
    out_specs = (
        P(("dp", "fsdp"), None),
        P(("dp", "fsdp"), None),
        P(None, "fsdp"),
        P(None, "fsdp"),
        P(None, "fsdp", None),
        P(None, "fsdp"),
        P(None, "fsdp"),
        P(None, "fsdp", None),
        P(None, "fsdp"),
        P(None, "fsdp"),
        P(None, "fsdp"),
        P(None, "fsdp", None),
        P(None, "fsdp"),
        P(None, "fsdp", None),
        P(None, "fsdp"),
    )
    return jax.shard_map(local, mesh=mesh, in_specs=in_specs, out_specs=out_specs, check_vma=False)
```

```python
import functools

import jax
import jax.numpy as jnp
from jax import lax
from jax.experimental import pallas as pl
from jax.experimental.pallas import tpu as pltpu
from jax.sharding import PartitionSpec as P

D = 768
HEADS = 12
HEAD_DIM = 64
GLEN = 197
LLEN = 37
G_DEV = 1
L_DEV = 4


epsilon = 1e-06


def norm_rows(values_in, gain, shift):
    row_mean = jnp.mean(values_in, axis=-1, keepdims=True)
    centred = values_in - row_mean
    spread = jnp.mean(centred * centred, axis=-1, keepdims=True)
    return centred * lax.rsqrt(spread + epsilon) * gain + shift


def contract_rows(left, right):
    return lax.dot_general(
        left, right, (((0,), (0,)), ((), ())), preferred_element_type=jnp.float32
    )


def contract_cols(left, right):
    return lax.dot_general(
        left, right, (((1,), (1,)), ((), ())), preferred_element_type=jnp.float32
    )


def gather_forward(pieces):
    return (
        lax.all_gather(pieces[0], "fsdp", axis=0, tiled=True),
        lax.all_gather(pieces[1], "fsdp", axis=0, tiled=True),
        lax.all_gather(pieces[2], "fsdp", axis=0, tiled=True),
        lax.all_gather(pieces[3], "fsdp", axis=0, tiled=True),
        lax.all_gather(pieces[4], "fsdp", axis=0, tiled=True),
        lax.all_gather(pieces[5], "fsdp", axis=0, tiled=True),
        lax.all_gather(pieces[6], "fsdp", axis=0, tiled=True),
        lax.all_gather(pieces[7], "fsdp", axis=0, tiled=True),
        lax.all_gather(pieces[8], "fsdp", axis=0, tiled=True),
        lax.all_gather(pieces[9], "fsdp", axis=0, tiled=True),
        lax.all_gather(pieces[10], "fsdp", axis=0, tiled=True),
        lax.all_gather(pieces[11], "fsdp", axis=0, tiled=True),
        lax.all_gather(pieces[12], "fsdp", axis=0, tiled=True),
    )


def reduce_grads(grads):
    shares = (
        lax.psum_scatter(grads[0], "fsdp", scatter_dimension=0, tiled=True),
        lax.psum_scatter(grads[1], "fsdp", scatter_dimension=0, tiled=True),
        lax.psum_scatter(grads[2].astype(jnp.bfloat16), "fsdp", scatter_dimension=0, tiled=True),
        lax.psum_scatter(grads[3], "fsdp", scatter_dimension=0, tiled=True),
        lax.psum_scatter(grads[4], "fsdp", scatter_dimension=0, tiled=True),
        lax.psum_scatter(grads[5].astype(jnp.bfloat16), "fsdp", scatter_dimension=0, tiled=True),
        lax.psum_scatter(grads[6], "fsdp", scatter_dimension=0, tiled=True),
        lax.psum_scatter(grads[7], "fsdp", scatter_dimension=0, tiled=True),
        lax.psum_scatter(grads[8], "fsdp", scatter_dimension=0, tiled=True),
        lax.psum_scatter(grads[9].astype(jnp.bfloat16), "fsdp", scatter_dimension=0, tiled=True),
        lax.psum_scatter(grads[10], "fsdp", scatter_dimension=0, tiled=True),
        lax.psum_scatter(grads[11].astype(jnp.bfloat16), "fsdp", scatter_dimension=0, tiled=True),
        lax.psum_scatter(grads[12], "fsdp", scatter_dimension=0, tiled=True),
    )
    column_parts = (
        lax.psum_scatter(
            shares[2], "dp", scatter_dimension=1, tiled=True
        ).astype(jnp.float32),
        lax.psum_scatter(
            shares[5], "dp", scatter_dimension=1, tiled=True
        ).astype(jnp.float32),
        lax.psum_scatter(
            shares[9], "dp", scatter_dimension=1, tiled=True
        ).astype(jnp.float32),
        lax.psum_scatter(
            shares[11], "dp", scatter_dimension=1, tiled=True
        ).astype(jnp.float32),
    )
    matrices = (
        lax.all_gather(column_parts[0].astype(jnp.bfloat16), "dp", axis=1, tiled=True).astype(
            jnp.float32
        ),
        lax.all_gather(column_parts[1].astype(jnp.bfloat16), "dp", axis=1, tiled=True).astype(
            jnp.float32
        ),
        lax.all_gather(column_parts[2].astype(jnp.bfloat16), "dp", axis=1, tiled=True).astype(
            jnp.float32
        ),
        lax.all_gather(column_parts[3].astype(jnp.bfloat16), "dp", axis=1, tiled=True).astype(
            jnp.float32
        ),
    )
    vectors = lax.psum(
        (
            shares[0],
            shares[1],
            shares[3],
            shares[4],
            shares[6],
            shares[7],
            shares[8],
            shares[10],
            shares[12],
        ),
        "dp",
    )
    return (
        vectors[0],
        vectors[1],
        matrices[0],
        vectors[2],
        vectors[3],
        matrices[1],
        vectors[4],
        vectors[5],
        vectors[6],
        matrices[2],
        vectors[7],
        matrices[3],
        vectors[8],
    )


def attend_crops(queries, keys_in, values_in, crop_count, crop_length):
    shape_four = (crop_count, crop_length, HEADS, HEAD_DIM)
    scores = jnp.einsum(
        "clhe,cmhe->chlm",
        queries.reshape(shape_four),
        keys_in.reshape(shape_four),
        preferred_element_type=jnp.float32,
    ) * HEAD_DIM ** (-0.5)
    peak_score = jnp.max(scores, axis=-1, keepdims=True)
    raised = jnp.exp(scores - peak_score)
    exp_total = jnp.sum(raised, axis=-1, keepdims=True)
    attn_probs = (raised / exp_total).astype(jnp.bfloat16)
    log_total = peak_score + jnp.log(exp_total)
    result = jnp.einsum(
        "chlm,cmhe->clhe",
        attn_probs,
        values_in.reshape(shape_four),
        preferred_element_type=jnp.float32,
    )
    return (result.reshape(crop_count * crop_length, D), log_total)


def attend_back(queries, keys_in, values_in, log_total, grad_mixed, crop_count, crop_length):
    shape_four = (crop_count, crop_length, HEADS, HEAD_DIM)
    score_scale = HEAD_DIM ** (-0.5)
    query_four = queries.reshape(shape_four)
    key_four = keys_in.reshape(shape_four)
    value_four = values_in.reshape(shape_four)
    grad_four = grad_mixed.reshape(shape_four)
    scores = (
        jnp.einsum("clhe,cmhe->chlm", query_four, key_four, preferred_element_type=jnp.float32)
        * score_scale
    )
    attn_probs = jnp.exp(scores - log_total)
    grad_probs = jnp.einsum(
        "clhe,cmhe->chlm", grad_four, value_four, preferred_element_type=jnp.float32
    )
    grad_values = jnp.einsum(
        "chlm,clhe->cmhe",
        attn_probs.astype(jnp.bfloat16),
        grad_four,
        preferred_element_type=jnp.float32,
    )
    row_inner = jnp.sum(grad_probs * attn_probs, axis=-1, keepdims=True)
    grad_scores = (attn_probs * (grad_probs - row_inner)).astype(jnp.bfloat16)
    grad_queries = (
        jnp.einsum("chlm,cmhe->clhe", grad_scores, key_four, preferred_element_type=jnp.float32)
        * score_scale
    )
    grad_keys = (
        jnp.einsum("chlm,clhe->cmhe", grad_scores, query_four, preferred_element_type=jnp.float32)
        * score_scale
    )
    rows_here = crop_count * crop_length
    return jnp.concatenate(
        [
            grad_queries.reshape(rows_here, D),
            grad_keys.reshape(rows_here, D),
            grad_values.reshape(rows_here, D),
        ],
        axis=1,
    )


def forward_layer(stream, weights):
    (
        gain_one,
        shift_one,
        w_qkv,
        bias_query,
        bias_value,
        w_out,
        bias_out,
        gain_two,
        shift_two,
        w_up,
        bias_up,
        w_down,
        bias_down,
    ) = weights
    normed = norm_rows(stream, gain_one.astype(jnp.float32), shift_one.astype(jnp.float32)).astype(
        jnp.bfloat16
    )
    bias_all = jnp.concatenate([bias_query, jnp.zeros_like(bias_query), bias_value]).astype(
        jnp.float32
    )
    projected = (jnp.dot(normed, w_qkv, preferred_element_type=jnp.float32) + bias_all).astype(
        jnp.bfloat16
    )
    global_rows = G_DEV * GLEN
    global_part, global_total = attend_crops(
        projected[:global_rows, :D],
        projected[:global_rows, D : 2 * D],
        projected[:global_rows, 2 * D :],
        G_DEV,
        GLEN,
    )
    local_part, local_total = attend_crops(
        projected[global_rows:, :D],
        projected[global_rows:, D : 2 * D],
        projected[global_rows:, 2 * D :],
        L_DEV,
        LLEN,
    )
    mixed = jnp.concatenate([global_part, local_part], axis=0).astype(jnp.bfloat16)
    stream_one = (
        stream
        + jnp.dot(mixed, w_out, preferred_element_type=jnp.float32)
        + bias_out.astype(jnp.float32)
    )
    normed_two = norm_rows(
        stream_one, gain_two.astype(jnp.float32), shift_two.astype(jnp.float32)
    ).astype(jnp.bfloat16)
    pre_act = jnp.dot(normed_two, w_up, preferred_element_type=jnp.float32) + bias_up.astype(
        jnp.float32
    )
    hidden = jax.nn.gelu(pre_act, approximate=False).astype(jnp.bfloat16)
    result = (
        stream_one
        + jnp.dot(hidden, w_down, preferred_element_type=jnp.float32)
        + bias_down.astype(jnp.float32)
    )
    saved_state = (
        stream,
        normed,
        projected,
        global_total,
        local_total,
        mixed,
        stream_one,
        normed_two,
        pre_act,
        hidden,
    )
    return (result, saved_state)


def backward_layer(upstream, weights, saved_state):
    (
        gain_one,
        shift_one,
        w_qkv,
        bias_query,
        bias_value,
        w_out,
        bias_out,
        gain_two,
        shift_two,
        w_up,
        bias_up,
        w_down,
        bias_down,
    ) = weights
    (
        stream,
        normed,
        projected,
        global_total,
        local_total,
        mixed,
        stream_one,
        normed_two,
        pre_act,
        hidden,
    ) = saved_state
    branch_two = upstream.astype(jnp.bfloat16)
    grad_bias_down = jnp.sum(branch_two.astype(jnp.float32), axis=0)
    grad_w_down = contract_rows(hidden, branch_two)
    grad_hidden = contract_cols(branch_two, w_down)
    unused, gelu_pull = jax.vjp(lambda value: jax.nn.gelu(value, approximate=False), pre_act)
    grad_pre = gelu_pull(grad_hidden)[0].astype(jnp.bfloat16)
    grad_bias_up = jnp.sum(grad_pre.astype(jnp.float32), axis=0)
    grad_w_up = contract_rows(normed_two, grad_pre)
    grad_normed_two = contract_cols(grad_pre, w_up)
    unused_two, norm_pull_two = jax.vjp(
        norm_rows, stream_one, gain_two.astype(jnp.float32), shift_two.astype(jnp.float32)
    )
    grad_stream_part, grad_gain_two, grad_shift_two = norm_pull_two(grad_normed_two)
    grad_stream_one = upstream + grad_stream_part
    branch_one = grad_stream_one.astype(jnp.bfloat16)
    grad_bias_out = jnp.sum(branch_one.astype(jnp.float32), axis=0)
    grad_w_out = contract_rows(mixed, branch_one)
    grad_mixed = contract_cols(branch_one, w_out).astype(jnp.bfloat16)
    global_rows = G_DEV * GLEN
    grad_global = attend_back(
        projected[:global_rows, :D],
        projected[:global_rows, D : 2 * D],
        projected[:global_rows, 2 * D :],
        global_total,
        grad_mixed[:global_rows],
        G_DEV,
        GLEN,
    )
    grad_local = attend_back(
        projected[global_rows:, :D],
        projected[global_rows:, D : 2 * D],
        projected[global_rows:, 2 * D :],
        local_total,
        grad_mixed[global_rows:],
        L_DEV,
        LLEN,
    )
    grad_projected = jnp.concatenate([grad_global, grad_local], axis=0).astype(jnp.bfloat16)
    column_sums = jnp.sum(grad_projected.astype(jnp.float32), axis=0)
    grad_bias_query = column_sums[:D]
    grad_bias_value = column_sums[2 * D :]
    grad_w_qkv = contract_rows(normed, grad_projected)
    grad_normed = contract_cols(grad_projected, w_qkv)
    unused_one, norm_pull_one = jax.vjp(
        norm_rows, stream, gain_one.astype(jnp.float32), shift_one.astype(jnp.float32)
    )
    grad_input_part, grad_gain_one, grad_shift_one = norm_pull_one(grad_normed)
    grad_stream = grad_stream_one + grad_input_part
    grads = (
        grad_gain_one,
        grad_shift_one,
        grad_w_qkv,
        grad_bias_query,
        grad_bias_value,
        grad_w_out,
        grad_bias_out,
        grad_gain_two,
        grad_shift_two,
        grad_w_up,
        grad_bias_up,
        grad_w_down,
        grad_bias_down,
    )
    return (grad_stream, grads)


def local(
    tokens,
    cotangent,
    norm1_gain,
    norm1_bias,
    qkv_weight,
    query_bias,
    value_bias,
    out_weight,
    out_bias,
    norm2_gain,
    norm2_bias,
    up_weight,
    up_bias,
    down_weight,
    down_bias,
):
    shards = (
        norm1_gain,
        norm1_bias,
        qkv_weight,
        query_bias,
        value_bias,
        out_weight,
        out_bias,
        norm2_gain,
        norm2_bias,
        up_weight,
        up_bias,
        down_weight,
        down_bias,
    )
    layer_total = qkv_weight.shape[0]
    stream = tokens.astype(jnp.float32)
    saved_layers = []
    kept_weights = []
    for layer_index in range(layer_total):
        weights = gather_forward(tuple((w[layer_index] for w in shards)))
        stream, saved_state = forward_layer(stream, weights)
        saved_layers.append(saved_state)
        kept_weights.append(weights)
    encoded = stream.astype(jnp.bfloat16)
    upstream = cotangent.astype(jnp.float32)
    reduced_layers = [None] * layer_total
    for layer_index in reversed(range(layer_total)):
        upstream, grads = backward_layer(
            upstream, kept_weights[layer_index], saved_layers[layer_index]
        )
        reduced_layers[layer_index] = reduce_grads(grads)
    stacked = tuple(
        (
            jnp.stack(
                [reduced_layers[layer_index][member] for layer_index in range(layer_total)], axis=0
            )
            for member in range(13)
        )
    )
    return (
        encoded,
        upstream,
        stacked[0],
        stacked[1],
        stacked[2],
        stacked[3],
        stacked[4],
        stacked[5],
        stacked[6],
        stacked[7],
        stacked[8],
        stacked[9],
        stacked[10],
        stacked[11],
        stacked[12],
    )


VMEM_BYTES = 63 * 1024 * 1024

MESH = pl.DeviceIdType.MESH
F32 = jnp.float32
BF16 = jnp.bfloat16

FF = 3072
ROWS = 345
PAD = 352
STEP = 32
SHARD = 96
HALF = 48
UNITS = 12
LAYER_ROWS = UNITS * D
DOWN_AT = 8 * D
SLOTS = 3
TOP_ROWS = 208
KEYS = 256
LOW_KEY = PAD - KEYS
LOW_ROWS = PAD - TOP_ROWS
V_G1, V_B1, V_QB, V_VB, V_OB, V_G2, V_B2, V_DB, V_UB = range(9)


def nt(left, right):
    return lax.dot_general(left, right, (((1,), (1,)), ((), ())), preferred_element_type=F32)


def tn(left, right):
    return lax.dot_general(left, right, (((0,), (0,)), ((), ())), preferred_element_type=F32)


def nn(left, right):
    return lax.dot_general(left, right, (((1,), (0,)), ((), ())), preferred_element_type=F32)


def aligned(value, by):
    return value if isinstance(value, int) else pl.multiple_of(value, by)


def unit_row(layer, unit, owner):
    is_down = unit // 8 if isinstance(unit, int) else lax.div(unit, 8)
    plain = unit * D + owner * SHARD
    down = DOWN_AT + owner * (4 * SHARD) + (unit - 8) * SHARD
    return aligned(layer * LAYER_ROWS + (1 - is_down) * plain + is_down * down, 16)


def forward_unit(index):
    return lax.div(index, UNITS), lax.rem(index, UNITS)


def backward_unit(layers, index):
    turn, place = lax.div(index, UNITS), lax.rem(index, UNITS)
    part = lax.div(place, 4)
    is_down, is_late = lax.div(2 - part, 2), lax.div(part, 2)
    unit = (
        is_down * (8 + place)
        + (1 - is_down - is_late) * place
        + is_late * lax.rem(place + 3, 4)
    )
    return layers - 1 - turn, unit


def stats(x):
    mean = jnp.mean(x, axis=-1, keepdims=True)
    centred = x - mean
    scale = lax.rsqrt(jnp.mean(centred * centred, axis=-1, keepdims=True) + epsilon)
    return centred * scale, scale


def fold(x):
    return jnp.sum(x.reshape(x.shape[0] // 8, 8, x.shape[1]), axis=0)


def total(x):
    return jnp.sum(x, axis=0, keepdims=True)


def step_rows(step):
    return pl.ds(aligned(step * STEP, STEP), STEP)


def encoder_kernel(
    layers,
    tokens,
    cotangent,
    vec_shard,
    w_qkv,
    w_out,
    w_up,
    w_down,
    encoded,
    tokens_grad,
    g_vec,
    g_qkv,
    g_out,
    g_up,
    g_down,
    wb,
    xs,
    x1,
    nr,
    pj,
    mx,
    n2,
    hd,
    gp,
    lse,
    gb,
    gm,
    br,
    acc,
    kacc,
    vacc,
    mask_top,
    mask_low,
    vsg,
    vec,
    ubs,
    vr,
    rc,
    r2,
    rz,
    ag_sem,
    ag_send,
    own_sem,
    core_sem,
    xy_sem,
    last_sem,
    z_sem,
    s0_send,
    rs_send,
    out_sem,
    vec_send,
    vec_recv,
    gv_send,
    gv_recv,
    credit,
):
    count = layers * UNITS
    d = lax.axis_index("dp")
    f = lax.axis_index("fsdp")
    c = lax.rem(f, 2)
    x = lax.rem(lax.div(f, 2), 2)
    y = lax.div(f, 4)
    fc = f + 1 - 2 * c
    fx = f + 2 - 4 * x
    fy = f + 4 - 8 * y
    outer = d * (3 - d) == 0
    inner = d * (3 - d) != 0
    z_in = 1 + lax.div(d, 3)
    z_out = 3 * lax.div(d, 2)
    z_pair = 3 - d
    in_plane = lambda who: {"fsdp": who}
    along = lambda who: {"dp": who}
    both = lambda a, b: jnp.logical_and(a, b)

    def block(yy, xx, cc):
        return yy * 4 + xx * 2 + cc

    def send(source, target, sent, landed, who):
        pltpu.make_async_remote_copy(
            src_ref=source,
            dst_ref=target,
            send_sem=sent,
            recv_sem=landed,
            device_id=who,
            device_id_type=MESH,
        ).start()

    def wait_rows(sem, rows):
        span = wb.at[pl.ds(0, rows)]
        pltpu.make_async_copy(span, span, sem).wait()

    barrier = pltpu.get_barrier_semaphore()
    peers = [lax.rem(f + hop, 8) for hop in range(1, 8)]
    for peer in peers:
        pl.semaphore_signal(barrier, inc=1, device_id=in_plane(peer), device_id_type=MESH)

    for hop in (1, 3):
        beside = lax.rem(d + hop, 4)
        pl.semaphore_signal(barrier, inc=1, device_id=along(beside), device_id_type=MESH)

    for layer in range(layers):
        for unit in range(UNITS):
            if unit < 3:
                source = w_qkv.at[layer, :, pl.ds(unit * D, D)]
            elif unit == 3:
                source = w_out.at[layer]
            elif unit < 8:
                source = w_up.at[layer, :, pl.ds((unit - 4) * D, D)]
            else:
                source = w_down.at[layer, pl.ds((unit - 8) * SHARD, SHARD)]
            pltpu.make_async_copy(
                source,
                wb.at[pl.ds(unit_row(layer, unit, f), SHARD)],
                own_sem.at[layer * UNITS + unit],
            ).start()
    vsg[f] = vec_shard[...]
    pl.semaphore_wait(barrier, 9)

    def gather_tick(t):
        @pl.when(t < count)
        def _():
            layer, unit = forward_unit(t)
            row = unit_row(layer, unit, f)
            wait_rows(own_sem.at[t], SHARD)
            first = wb.at[pl.ds(row, HALF)]
            second = wb.at[pl.ds(aligned(row + HALF, 16), HALF)]
            whole = wb.at[pl.ds(row, SHARD)]
            send(first, first, ag_send.at[t], ag_sem.at[t, 0], in_plane(fy))
            send(second, second, ag_send.at[t], ag_sem.at[t, 1], in_plane(fx))
            send(first, first, ag_send.at[t], ag_sem.at[t, 2], in_plane(fx))
            send(second, second, ag_send.at[t], ag_sem.at[t, 2], in_plane(fy))
            send(whole, whole, ag_send.at[t], ag_sem.at[t, 3], in_plane(fc))

        @pl.when(both(t >= 2, t < count + 2))
        def _():
            i = t - 2
            layer, unit = forward_unit(i)
            wait_rows(ag_sem.at[i, 0], HALF)
            wait_rows(ag_sem.at[i, 1], HALF)
            first = wb.at[pl.ds(unit_row(layer, unit, block(1 - y, x, c)), HALF)]
            other = unit_row(layer, unit, block(y, 1 - x, c))
            second = wb.at[pl.ds(aligned(other + HALF, 16), HALF)]
            send(first, first, ag_send.at[i], ag_sem.at[i, 2], in_plane(fx))
            send(second, second, ag_send.at[i], ag_sem.at[i, 2], in_plane(fy))

        @pl.when(both(t >= 4, t < count + 4))
        def _():
            i = t - 4
            layer, unit = forward_unit(i)
            wait_rows(ag_sem.at[i, 2], 4 * HALF)
            for yy, xx in ((1 - y, x), (y, 1 - x), (1 - y, 1 - x)):
                piece = wb.at[pl.ds(unit_row(layer, unit, block(yy, xx, c)), SHARD)]
                send(piece, piece, ag_send.at[i], ag_sem.at[i, 3], in_plane(fc))

        @pl.when(both(t >= 5, t < count + 5))
        def _():
            wait_rows(ag_sem.at[t - 5, 3], 4 * SHARD)

    for hop, peer in enumerate(peers):
        send(vec_shard, vsg.at[f], vec_send.at[hop], vec_recv.at[hop], in_plane(peer))

    @pl.loop(0, 5)
    def _(t):
        gather_tick(t)

    def crop_of(shape, dim, start):
        at = lax.broadcasted_iota(jnp.int32, shape, dim) + start
        which = jnp.zeros(shape, jnp.int32)
        for edge in range(L_DEV + 1):
            which = which + (at >= GLEN + edge * LLEN).astype(jnp.int32)
        return which

    for mask, rows, row_at, key_at in (
        (mask_top, TOP_ROWS, 0, 0),
        (mask_low, LOW_ROWS, TOP_ROWS, LOW_KEY),
    ):
        same = crop_of((rows, KEYS), 0, row_at) == crop_of((rows, KEYS), 1, key_at)
        mask[...] = jnp.where(same, 0.0, -1e30).astype(F32)

    xs[0, PAD - 8 :, :] = jnp.zeros((8, D), F32)
    xs[0, 0:ROWS, :] = tokens[...].astype(F32)

    for hop in range(7):
        pltpu.make_async_copy(vec_shard, vec_shard, vec_recv.at[hop]).wait()
    spread = jnp.zeros((8 * layers, D), F32)
    for owner in range(8):
        at_row = lax.broadcasted_iota(jnp.int32, (128, D), 0)
        at_col = lax.broadcasted_iota(jnp.int32, (128, D), 1)
        hit = jnp.logical_and(at_col == at_row + owner * SHARD, at_row < SHARD)
        spread = spread + nn(vsg[owner, :, 0:128], jnp.where(hit, 1.0, 0.0).astype(BF16))
        ubs[:, owner * 384 : (owner + 1) * 384] = vsg[owner, :, 128:512].astype(F32)
    vec[...] = spread

    def vector(layer, which):
        return vec[pl.ds(layer * 8 + which, 1), :]

    lane = lax.broadcasted_iota(jnp.int32, (1, 128), 1)
    left_lane = lane < HEAD_DIM
    score_scale = HEAD_DIM ** (-0.5)
    head_scaled = [
        jnp.where(left_lane, score_scale, 0.0).astype(BF16),
        jnp.where(left_lane, 0.0, score_scale).astype(BF16),
    ]
    head_plain = [
        jnp.where(left_lane, 1.0, 0.0).astype(BF16),
        jnp.where(left_lane, 0.0, 1.0).astype(BF16),
    ]
    groups = (
        (0, TOP_ROWS, 0, mask_top),
        (TOP_ROWS, LOW_ROWS, LOW_KEY, mask_low),
    )

    def weight(layer, unit):
        return pl.ds(aligned(layer * LAYER_ROWS + unit * D, 16), D)

    @pl.loop(0, layers)
    def _(layer):
        base = layer * UNITS + 5

        @pl.loop(0, PAD // STEP)
        def _(step):
            rows = step_rows(step)
            normed, _unused = stats(xs[layer, rows, :])
            nr[layer, rows, :] = (normed * vector(layer, V_G1) + vector(layer, V_B1)).astype(BF16)

        @pl.loop(0, 3)
        def _(part):
            gather_tick(base + part)
            is_q, is_v = lax.div(2 - part, 2), lax.div(part, 2)
            bias = is_q.astype(F32) * vector(layer, V_QB) + is_v.astype(F32) * vector(layer, V_VB)
            acc[...] = nn(nr[layer], wb[weight(layer, part), :])

            @pl.loop(0, PAD // STEP)
            def _(step):
                rows = step_rows(step)
                pj[layer, part, rows, :] = (acc[rows, :] + bias).astype(BF16)

        @pl.loop(0, HEADS // 2)
        def _(pair):
            @pl.when(pair == 3)
            def _():
                gather_tick(base + 3)

            lanes = pl.ds(aligned(pair * 128, 128), 128)
            for row_at, rows, key_at, mask in groups:
                here = pl.ds(row_at, rows)
                keys = pj[layer, 1, pl.ds(key_at, KEYS), lanes]
                values = pj[layer, 2, pl.ds(key_at, KEYS), lanes]
                queries = pj[layer, 0, here, lanes]
                results = []
                for side in range(2):
                    scores = nt(queries * head_scaled[side], keys) + mask[...]
                    peak = jnp.max(scores, axis=-1, keepdims=True)
                    raised = jnp.exp(scores - peak)
                    exp_total = jnp.sum(raised, axis=-1, keepdims=True)
                    probs = (raised * (1.0 / exp_total)).astype(BF16)
                    results.append(nn(probs, values))
                    log_total = peak + jnp.log(exp_total)
                    lse[layer, here, :] = jnp.where(
                        lane == pair * 2 + side, log_total, lse[layer, here, :]
                    )
                mx[layer, here, lanes] = jnp.where(left_lane, results[0], results[1]).astype(BF16)

        acc[...] = nn(mx[layer], wb[weight(layer, 3), :])

        @pl.loop(0, PAD // STEP)
        def _(step):
            rows = step_rows(step)
            now = xs[layer, rows, :] + acc[rows, :] + vector(layer, V_OB)
            x1[layer, rows, :] = now
            normed, _unused = stats(now)
            n2[layer, rows, :] = (normed * vector(layer, V_G2) + vector(layer, V_B2)).astype(BF16)

        @pl.loop(0, 4)
        def _(part):
            gather_tick(base + 4 + part)
            bias = ubs[pl.ds(layer * 8, 1), pl.ds(aligned(part * D, 128), D)]
            acc[...] = nn(n2[layer], wb[weight(layer, 4 + part), :])

            @pl.loop(0, PAD // STEP)
            def _(step):
                rows = step_rows(step)
                pre = acc[rows, :] + bias
                cdf = 0.5 + 0.5 * lax.erf(pre * (0.5**0.5))
                bell = jnp.exp(-0.5 * pre * pre) * 0.3989422804014327
                hd[layer, part, rows, :] = (pre * cdf).astype(BF16)
                gp[layer, part, rows, :] = (cdf + pre * bell).astype(BF16)

        @pl.loop(0, 4)
        def _(part):
            gather_tick(base + 8 + part)

        acc[...] = x1[layer] + vector(layer, V_DB)

        @pl.loop(0, 4)
        def _(part):
            acc[...] += nn(hd[layer, part], wb[weight(layer, 8 + part), :])

        xs[layer + 1] = acc[...]

    encoded[...] = xs[layers, 0:ROWS, :].astype(BF16)

    @pl.loop(0, count)
    def _(i):
        wait_rows(ag_send.at[i], 7 * SHARD)

    for hop in range(7):
        pltpu.make_async_copy(vec_shard, vec_shard, vec_send.at[hop]).wait()

    def here_row(i, owner):
        layer, unit = backward_unit(layers, i)
        return unit_row(layer, unit, owner)

    def half_rows(row, half):
        return pl.ds(aligned(row + half * HALF, 16), HALF)

    def credit_wait(i, which):
        @pl.when(i >= SLOTS)
        def _():
            pl.semaphore_wait(credit.at[which], 1)

    def credit_give(i, which, who):
        @pl.when(i + SLOTS < count)
        def _():
            pl.semaphore_signal(credit.at[which], inc=1, device_id=who, device_id_type=MESH)

    def reduce_tick(t):
        @pl.when(t < count)
        def _():
            slot = lax.rem(t, SLOTS)
            credit_wait(t, 0)
            for place in range(4):
                source = wb.at[pl.ds(here_row(t, 2 * place + 1 - c), SHARD)]
                send(
                    source,
                    rc.at[slot, pl.ds(place * SHARD, SHARD)],
                    s0_send.at[t],
                    core_sem.at[t],
                    in_plane(fc),
                )

        @pl.when(both(t >= 11, t < count + 11))
        def _():
            i = t - 11
            layer, unit = backward_unit(layers, i)

            @pl.when(outer)
            def _():
                wait_rows(z_sem.at[i, 2], SHARD)

            done = wb.at[pl.ds(unit_row(layer, unit, fc), SHARD)]

            @pl.when(unit < 3)
            def _():
                target = g_qkv.at[layer, :, pl.ds(aligned(unit * D, 128), D)]
                pltpu.make_async_copy(done, target, out_sem.at[i]).start()

            @pl.when(unit == 3)
            def _():
                pltpu.make_async_copy(done, g_out.at[layer], out_sem.at[i]).start()

            @pl.when(both(unit >= 4, unit < 8))
            def _():
                target = g_up.at[layer, :, pl.ds(aligned((unit - 4) * D, 128), D)]
                pltpu.make_async_copy(done, target, out_sem.at[i]).start()

            @pl.when(unit >= 8)
            def _():
                target = g_down.at[layer, pl.ds(aligned((unit - 8) * SHARD, 16), SHARD)]
                pltpu.make_async_copy(done, target, out_sem.at[i]).start()

        @pl.when(both(inner, both(t >= 9, t < count + 9)))
        def _():
            i = t - 9
            slot = lax.rem(i, SLOTS)
            wait_rows(z_sem.at[i, 1], SHARD)
            own = here_row(i, f)
            done = pl.ds(here_row(i, fc), SHARD)
            wb[done, :] = wb[pl.ds(own, SHARD), :] + rz[slot, 1]
            credit_give(i, 4, along(z_pair))
            send(wb.at[done], wb.at[done], rs_send.at[i], z_sem.at[i, 2], along(z_out))

        @pl.when(both(inner, both(t >= 7, t < count + 7)))
        def _():
            i = t - 7
            slot = lax.rem(i, SLOTS)
            wait_rows(z_sem.at[i, 0], SHARD)
            own = pl.ds(here_row(i, f), SHARD)
            wb[own, :] = wb[own, :] + rz[slot, 0]
            credit_give(i, 3, along(z_out))
            credit_wait(i, 4)
            send(wb.at[own], rz.at[slot, 1], rs_send.at[i], z_sem.at[i, 1], along(z_pair))

        @pl.when(both(t >= 5, t < count + 5))
        def _():
            i = t - 5
            slot = lax.rem(i, SLOTS)
            wait_rows(last_sem.at[i], SHARD)
            own = pl.ds(here_row(i, f), SHARD)
            spare = pl.ds(here_row(i, fc), SHARD)
            wb[own, :] = wb[own, :] + wb[spare, :]

            @pl.when(outer)
            def _():
                credit_wait(i, 3)
                send(wb.at[own], rz.at[slot, 0], rs_send.at[i], z_sem.at[i, 0], along(z_in))

        @pl.when(both(t >= 3, t < count + 3))
        def _():
            i = t - 3
            slot = lax.rem(i, SLOTS)
            wait_rows(xy_sem.at[i], 4 * HALF)
            for other in range(2):
                span = half_rows(here_row(i, block(other, x, c)), 0)
                wb[span, :] = wb[span, :] + r2[slot, pl.ds(other * HALF, HALF), :]
                span = half_rows(here_row(i, block(y, other, c)), 1)
                wb[span, :] = wb[span, :] + r2[slot, pl.ds((2 + other) * HALF, HALF), :]
            credit_give(i, 1, in_plane(fx))
            credit_give(i, 2, in_plane(fy))
            first = wb.at[half_rows(here_row(i, block(1 - y, x, c)), 0)]
            second = wb.at[half_rows(here_row(i, block(y, 1 - x, c)), 1)]
            spare_y = here_row(i, block(1 - y, x, 1 - c))
            spare_x = here_row(i, block(y, 1 - x, 1 - c))
            send(first, wb.at[half_rows(spare_y, 0)], rs_send.at[i], last_sem.at[i], in_plane(fy))
            send(second, wb.at[half_rows(spare_x, 1)], rs_send.at[i], last_sem.at[i], in_plane(fx))

        @pl.when(both(t >= 1, t < count + 1))
        def _():
            i = t - 1
            slot = lax.rem(i, SLOTS)
            wait_rows(core_sem.at[i], 4 * SHARD)
            wait_rows(s0_send.at[i], 4 * SHARD)
            for place in range(4):
                span = pl.ds(here_row(i, 2 * place + c), SHARD)
                wb[span, :] = wb[span, :] + rc[slot, pl.ds(place * SHARD, SHARD), :]
            credit_give(i, 0, in_plane(fc))
            credit_wait(i, 1)
            credit_wait(i, 2)
            for other in range(2):
                send(
                    wb.at[half_rows(here_row(i, block(other, 1 - x, c)), 0)],
                    r2.at[slot, pl.ds(other * HALF, HALF)],
                    rs_send.at[i],
                    xy_sem.at[i],
                    in_plane(fx),
                )
                send(
                    wb.at[half_rows(here_row(i, block(1 - y, other, c)), 1)],
                    r2.at[slot, pl.ds((2 + other) * HALF, HALF)],
                    rs_send.at[i],
                    xy_sem.at[i],
                    in_plane(fy),
                )

    def vector_step(layer, step):
        mine = g_vec.at[layer]

        def arrive(at):
            pltpu.make_async_copy(mine, mine, gv_recv.at[layer, at]).wait()

        def leave(at):
            pltpu.make_async_copy(mine, mine, gv_send.at[layer, at]).wait()

        def go(at, target, landed, who):
            send(mine, target, gv_send.at[layer, at], gv_recv.at[layer, landed], who)

        def add(at):
            g_vec[layer] = g_vec[layer] + vr[layer, at]

        for at, who in enumerate((fc, fx, fy)):

            @pl.when(step == at)
            def _(at=at, who=who):
                if at:
                    leave(at - 1)
                    arrive(at - 1)
                    add(at - 1)
                go(at, vr.at[layer, at], at, in_plane(who))

        @pl.when(step == 3)
        def _():
            leave(2)
            arrive(2)
            add(2)

            @pl.when(outer)
            def _():
                go(3, vr.at[layer, 3], 3, along(z_in))

        @pl.when(both(inner, step == 4))
        def _():
            arrive(3)
            add(3)
            go(4, vr.at[layer, 4], 4, along(z_pair))

        @pl.when(both(inner, step == 5))
        def _():
            leave(4)
            arrive(4)
            add(4)
            go(3, vr.at[layer, 3], 3, along(z_out))

        @pl.when(step == 6)
        def _():
            leave(3)

            @pl.when(outer)
            def _():
                arrive(3)
                g_vec[layer] = vr[layer, 3]

    up = xs.at[layers]
    up[PAD - 8 :, :] = jnp.zeros((8, D), F32)
    up[0:ROWS, :] = cotangent[...].astype(F32)
    none = jnp.zeros((8, D), F32)

    def put_vector(layer, which, value):
        g_vec[layer, pl.ds(which, 1), :] = total(value)

    def weight_grad(rows_at, left, right):
        @pl.loop(0, 3)
        def _(third):
            lanes = pl.ds(aligned(third * KEYS, 128), KEYS)
            target = pl.ds(aligned(rows_at + third * KEYS, 16), KEYS)
            wb[target, :] = tn(left[:, lanes], right[...]).astype(BF16)

    @pl.loop(0, layers)
    def _(turn):
        layer = layers - 1 - turn
        base = turn * UNITS
        for row in range(12, 16):
            g_vec[layer, row : row + 1, :] = jnp.zeros((1, D), F32)

        def branch_two(step, carry):
            rows = step_rows(step)
            rounded = up[rows, :].astype(BF16)
            br[rows, :] = rounded
            return carry + fold(rounded.astype(F32))

        put_vector(layer, V_DB, lax.fori_loop(0, PAD // STEP, branch_two, none))

        @pl.loop(0, 4)
        def _(part):
            @pl.when(turn > 0)
            def _():
                vector_step(layer + 1, part)

            acc[...] = nt(br[...], wb[weight(layer, 8 + part), :])

            def through_gelu(step, carry):
                rows = step_rows(step)
                value = (acc[rows, :] * gp[layer, part, rows, :].astype(F32)).astype(BF16)
                gb[part, rows, :] = value
                return carry + fold(value.astype(F32))

            put_vector(layer, V_UB + part, lax.fori_loop(0, PAD // STEP, through_gelu, none))
            weight_grad(layer * LAYER_ROWS + DOWN_AT + part * D, hd.at[layer, part], br)

        acc[...] = jnp.zeros((PAD, D), F32)

        @pl.loop(0, 4)
        def _(part):
            @pl.when(both(turn > 0, part < 3))
            def _():
                vector_step(layer + 1, part + 4)

            acc[...] += nt(gb[part], wb[weight(layer, 4 + part), :])
            weight_grad(layer * LAYER_ROWS + (4 + part) * D, n2.at[layer], gb.at[part])
            reduce_tick(base + part)

        def norm_back(source, gain_at, shift_at):
            def body(step, carry):
                gain_sum, shift_sum = carry
                rows = step_rows(step)
                normed, scale = stats(source[layer, rows, :])
                grad = acc[rows, :]
                t = grad * vector(layer, gain_at)
                inner_mean = jnp.mean(t * normed, axis=-1, keepdims=True)
                back = scale * (t - jnp.mean(t, axis=-1, keepdims=True) - normed * inner_mean)
                up[rows, :] = up[rows, :] + back
                return gain_sum + fold(grad * normed), shift_sum + fold(grad)

            gain_sum, shift_sum = lax.fori_loop(0, PAD // STEP, body, (none, none))
            put_vector(layer, gain_at, gain_sum)
            put_vector(layer, shift_at, shift_sum)

        norm_back(x1, V_G2, V_B2)

        put_vector(layer, V_OB, lax.fori_loop(0, PAD // STEP, branch_two, none))
        gm[...] = nt(br[...], wb[weight(layer, 3), :]).astype(BF16)
        weight_grad(layer * LAYER_ROWS + 3 * D, mx.at[layer], br)

        @pl.loop(0, HEADS // 2)
        def _(pair):
            @pl.when(lax.rem(pair, 2) == 0)
            def _():
                reduce_tick(base + 4 + lax.div(pair, 2))

            lanes = pl.ds(aligned(pair * 128, 128), 128)
            kacc[...] = jnp.zeros((PAD, 128), F32)
            vacc[...] = jnp.zeros((PAD, 128), F32)
            for row_at, rows, key_at, mask in groups:
                here = pl.ds(row_at, rows)
                there = pl.ds(key_at, KEYS)
                keys = pj[layer, 1, there, lanes]
                values = pj[layer, 2, there, lanes]
                queries = pj[layer, 0, here, lanes]
                grads = gm[here, lanes]
                q_parts, k_parts, v_parts = [], [], []
                for side in range(2):
                    log_total = jnp.sum(
                        jnp.where(lane == pair * 2 + side, lse[layer, here, :], 0.0),
                        axis=-1,
                        keepdims=True,
                    )
                    scaled = queries * head_scaled[side]
                    probs = jnp.exp(nt(scaled, keys) + mask[...] - log_total)
                    grad_probs = nt(grads * head_plain[side], values)
                    row_inner = jnp.sum(grad_probs * probs, axis=-1, keepdims=True)
                    grad_scores = (probs * (grad_probs - row_inner)).astype(BF16)
                    v_parts.append(tn(probs.astype(BF16), grads))
                    k_parts.append(tn(grad_scores, queries))
                    q_parts.append(nn(grad_scores, keys))
                grad_queries = jnp.where(left_lane, q_parts[0], q_parts[1]) * score_scale
                gb[0, here, lanes] = grad_queries.astype(BF16)
                kacc[there, :] += jnp.where(left_lane, k_parts[0], k_parts[1]) * score_scale
                vacc[there, :] += jnp.where(left_lane, v_parts[0], v_parts[1])
            gb[1, :, lanes] = kacc[...].astype(BF16)
            gb[2, :, lanes] = vacc[...].astype(BF16)

        for which, part in ((V_QB, 0), (V_VB, 2)):

            def column_sum(step, carry, part=part):
                return carry + fold(gb[part, step_rows(step), :].astype(F32))

            put_vector(layer, which, lax.fori_loop(0, PAD // STEP, column_sum, none))

        acc[...] = jnp.zeros((PAD, D), F32)

        @pl.loop(0, 3)
        def _(part):
            acc[...] += nt(gb[part], wb[weight(layer, part), :])
            weight_grad(layer * LAYER_ROWS + part * D, nr.at[layer], gb.at[part])
            reduce_tick(base + 7 + part)

        norm_back(xs, V_G1, V_B1)

        @pl.loop(0, 2)
        def _(part):
            reduce_tick(base + 10 + part)

    tokens_grad[...] = up[0:ROWS, :]

    @pl.loop(count, count + 11)
    def _(t):
        @pl.when(t < count + 7)
        def _():
            vector_step(0, t - count)

        reduce_tick(t)

    @pl.loop(0, count)
    def _(i):
        wait_rows(out_sem.at[i], SHARD)

        @pl.when(outer)
        def _():
            wait_rows(rs_send.at[i], 4 * SHARD)

        @pl.when(inner)
        def _():
            wait_rows(rs_send.at[i], 5 * SHARD)


def kernel_local(
    tokens,
    cotangent,
    norm1_gain,
    norm1_bias,
    qkv_weight,
    query_bias,
    value_bias,
    out_weight,
    out_bias,
    norm2_gain,
    norm2_bias,
    up_weight,
    up_bias,
    down_weight,
    down_bias,
):
    layers = qkv_weight.shape[0]
    small = jnp.stack(
        [
            norm1_gain,
            norm1_bias,
            query_bias,
            value_bias,
            out_bias,
            norm2_gain,
            norm2_bias,
            down_bias,
        ],
        axis=1,
    ).reshape(8 * layers, SHARD)
    small = jnp.pad(small, ((0, 0), (0, 128 - SHARD)))
    wide = jnp.pad(up_bias[:, None, :], ((0, 0), (0, 7), (0, 0))).reshape(8 * layers, 4 * SHARD)
    vec_shard = jnp.concatenate([small, wide], axis=1)

    count = layers * UNITS
    vmem = pl.BlockSpec(memory_space=pltpu.VMEM)
    hbm = pl.BlockSpec(memory_space=pl.ANY)
    dma = pltpu.SemaphoreType.DMA
    results = pl.pallas_call(
        functools.partial(encoder_kernel, layers),
        out_shape=(
            jax.ShapeDtypeStruct((ROWS, D), BF16),
            jax.ShapeDtypeStruct((ROWS, D), F32),
            jax.ShapeDtypeStruct((layers, 16, D), F32),
            jax.ShapeDtypeStruct((layers, SHARD, 3 * D), BF16),
            jax.ShapeDtypeStruct((layers, SHARD, D), BF16),
            jax.ShapeDtypeStruct((layers, SHARD, FF), BF16),
            jax.ShapeDtypeStruct((layers, 4 * SHARD, D), BF16),
        ),
        in_specs=[vmem] * 3 + [hbm] * 4,
        out_specs=(vmem, vmem, vmem, hbm, hbm, hbm, hbm),
        scratch_shapes=[
            pltpu.VMEM((layers * LAYER_ROWS, D), BF16),
            pltpu.VMEM((layers + 1, PAD, D), F32),
            pltpu.VMEM((layers, PAD, D), F32),
            pltpu.VMEM((layers, PAD, D), BF16),
            pltpu.VMEM((layers, 3, PAD, D), BF16),
            pltpu.VMEM((layers, PAD, D), BF16),
            pltpu.VMEM((layers, PAD, D), BF16),
            pltpu.VMEM((layers, 4, PAD, D), BF16),
            pltpu.VMEM((layers, 4, PAD, D), BF16),
            pltpu.VMEM((layers, PAD, 128), F32),
            pltpu.VMEM((4, PAD, D), BF16),
            pltpu.VMEM((PAD, D), BF16),
            pltpu.VMEM((PAD, D), BF16),
            pltpu.VMEM((PAD, D), F32),
            pltpu.VMEM((PAD, 128), F32),
            pltpu.VMEM((PAD, 128), F32),
            pltpu.VMEM((TOP_ROWS, KEYS), F32),
            pltpu.VMEM((LOW_ROWS, KEYS), F32),
            pltpu.VMEM((8, 8 * layers, 512), BF16),
            pltpu.VMEM((8 * layers, D), F32),
            pltpu.VMEM((8 * layers, FF), F32),
            pltpu.VMEM((layers, 5, 16, D), F32),
            pltpu.VMEM((SLOTS, 4 * SHARD, D), BF16),
            pltpu.VMEM((SLOTS, 4 * HALF, D), BF16),
            pltpu.VMEM((SLOTS, 2, SHARD, D), BF16),
            dma((count, 4)),
            dma((count,)),
            dma((count,)),
            dma((count,)),
            dma((count,)),
            dma((count,)),
            dma((count, 3)),
            dma((count,)),
            dma((count,)),
            dma((count,)),
            dma((7,)),
            dma((7,)),
            dma((layers, 5)),
            dma((layers, 5)),
            pltpu.SemaphoreType.REGULAR((5,)),
        ],
        compiler_params=pltpu.CompilerParams(
            collective_id=0, has_side_effects=True, vmem_limit_bytes=VMEM_BYTES
        ),
    )(tokens, cotangent, vec_shard, qkv_weight, out_weight, up_weight, down_weight)
    encoded, tokens_grad, g_vec, g_qkv, g_out, g_up, g_down = results
    f = lax.axis_index("fsdp")
    vectors = lax.dynamic_slice_in_dim(g_vec[:, :8], f * SHARD, SHARD, axis=2)
    up_vector = lax.dynamic_slice_in_dim(
        g_vec[:, 8:12].reshape(layers, FF), f * 4 * SHARD, 4 * SHARD, axis=1
    )
    return (
        encoded,
        tokens_grad,
        vectors[:, V_G1],
        vectors[:, V_B1],
        g_qkv.astype(F32),
        vectors[:, V_QB],
        vectors[:, V_VB],
        g_out.astype(F32),
        vectors[:, V_OB],
        vectors[:, V_G2],
        vectors[:, V_B2],
        g_up.astype(F32),
        up_vector,
        g_down.astype(F32),
        vectors[:, V_DB],
    )


def solution(mesh):
    in_specs = (
        P(("dp", "fsdp"), None),
        P(("dp", "fsdp"), None),
        P(None, "fsdp"),
        P(None, "fsdp"),
        P(None, "fsdp", None),
        P(None, "fsdp"),
        P(None, "fsdp"),
        P(None, "fsdp", None),
        P(None, "fsdp"),
        P(None, "fsdp"),
        P(None, "fsdp"),
        P(None, "fsdp", None),
        P(None, "fsdp"),
        P(None, "fsdp", None),
        P(None, "fsdp"),
    )
    out_specs = (
        P(("dp", "fsdp"), None),
        P(("dp", "fsdp"), None),
        P(None, "fsdp"),
        P(None, "fsdp"),
        P(None, "fsdp", None),
        P(None, "fsdp"),
        P(None, "fsdp"),
        P(None, "fsdp", None),
        P(None, "fsdp"),
        P(None, "fsdp"),
        P(None, "fsdp"),
        P(None, "fsdp", None),
        P(None, "fsdp"),
        P(None, "fsdp", None),
        P(None, "fsdp"),
    )
    fits = mesh.shape["dp"] == 4 and mesh.shape["fsdp"] == 8
    body = kernel_local if fits else local
    return jax.shard_map(body, mesh=mesh, in_specs=in_specs, out_specs=out_specs, check_vma=False)
```

```python
import functools

import jax
import jax.numpy as jnp
from jax import lax
from jax.experimental import pallas as pl
from jax.experimental.pallas import tpu as pltpu
from jax.sharding import PartitionSpec as P

D = 768
HEADS = 12
HEAD_DIM = 64
GLEN = 197
LLEN = 37
G_DEV = 1
L_DEV = 4


epsilon = 1e-06


def norm_rows(values_in, gain, shift):
    row_mean = jnp.mean(values_in, axis=-1, keepdims=True)
    centred = values_in - row_mean
    spread = jnp.mean(centred * centred, axis=-1, keepdims=True)
    return centred * lax.rsqrt(spread + epsilon) * gain + shift


def contract_rows(left, right):
    return lax.dot_general(
        left, right, (((0,), (0,)), ((), ())), preferred_element_type=jnp.float32
    )


def contract_cols(left, right):
    return lax.dot_general(
        left, right, (((1,), (1,)), ((), ())), preferred_element_type=jnp.float32
    )


def gather_forward(pieces):
    return (
        lax.all_gather(pieces[0], "fsdp", axis=0, tiled=True),
        lax.all_gather(pieces[1], "fsdp", axis=0, tiled=True),
        lax.all_gather(pieces[2], "fsdp", axis=0, tiled=True),
        lax.all_gather(pieces[3], "fsdp", axis=0, tiled=True),
        lax.all_gather(pieces[4], "fsdp", axis=0, tiled=True),
        lax.all_gather(pieces[5], "fsdp", axis=0, tiled=True),
        lax.all_gather(pieces[6], "fsdp", axis=0, tiled=True),
        lax.all_gather(pieces[7], "fsdp", axis=0, tiled=True),
        lax.all_gather(pieces[8], "fsdp", axis=0, tiled=True),
        lax.all_gather(pieces[9], "fsdp", axis=0, tiled=True),
        lax.all_gather(pieces[10], "fsdp", axis=0, tiled=True),
        lax.all_gather(pieces[11], "fsdp", axis=0, tiled=True),
        lax.all_gather(pieces[12], "fsdp", axis=0, tiled=True),
    )


def reduce_grads(grads):
    shares = (
        lax.psum_scatter(grads[0], "fsdp", scatter_dimension=0, tiled=True),
        lax.psum_scatter(grads[1], "fsdp", scatter_dimension=0, tiled=True),
        lax.psum_scatter(grads[2].astype(jnp.bfloat16), "fsdp", scatter_dimension=0, tiled=True),
        lax.psum_scatter(grads[3], "fsdp", scatter_dimension=0, tiled=True),
        lax.psum_scatter(grads[4], "fsdp", scatter_dimension=0, tiled=True),
        lax.psum_scatter(grads[5].astype(jnp.bfloat16), "fsdp", scatter_dimension=0, tiled=True),
        lax.psum_scatter(grads[6], "fsdp", scatter_dimension=0, tiled=True),
        lax.psum_scatter(grads[7], "fsdp", scatter_dimension=0, tiled=True),
        lax.psum_scatter(grads[8], "fsdp", scatter_dimension=0, tiled=True),
        lax.psum_scatter(grads[9].astype(jnp.bfloat16), "fsdp", scatter_dimension=0, tiled=True),
        lax.psum_scatter(grads[10], "fsdp", scatter_dimension=0, tiled=True),
        lax.psum_scatter(grads[11].astype(jnp.bfloat16), "fsdp", scatter_dimension=0, tiled=True),
        lax.psum_scatter(grads[12], "fsdp", scatter_dimension=0, tiled=True),
    )
    column_parts = (
        lax.psum_scatter(
            shares[2], "dp", scatter_dimension=1, tiled=True
        ).astype(jnp.float32),
        lax.psum_scatter(
            shares[5], "dp", scatter_dimension=1, tiled=True
        ).astype(jnp.float32),
        lax.psum_scatter(
            shares[9], "dp", scatter_dimension=1, tiled=True
        ).astype(jnp.float32),
        lax.psum_scatter(
            shares[11], "dp", scatter_dimension=1, tiled=True
        ).astype(jnp.float32),
    )
    matrices = (
        lax.all_gather(column_parts[0].astype(jnp.bfloat16), "dp", axis=1, tiled=True).astype(
            jnp.float32
        ),
        lax.all_gather(column_parts[1].astype(jnp.bfloat16), "dp", axis=1, tiled=True).astype(
            jnp.float32
        ),
        lax.all_gather(column_parts[2].astype(jnp.bfloat16), "dp", axis=1, tiled=True).astype(
            jnp.float32
        ),
        lax.all_gather(column_parts[3].astype(jnp.bfloat16), "dp", axis=1, tiled=True).astype(
            jnp.float32
        ),
    )
    vectors = lax.psum(
        (
            shares[0],
            shares[1],
            shares[3],
            shares[4],
            shares[6],
            shares[7],
            shares[8],
            shares[10],
            shares[12],
        ),
        "dp",
    )
    return (
        vectors[0],
        vectors[1],
        matrices[0],
        vectors[2],
        vectors[3],
        matrices[1],
        vectors[4],
        vectors[5],
        vectors[6],
        matrices[2],
        vectors[7],
        matrices[3],
        vectors[8],
    )


def attend_crops(queries, keys_in, values_in, crop_count, crop_length):
    shape_four = (crop_count, crop_length, HEADS, HEAD_DIM)
    scores = jnp.einsum(
        "clhe,cmhe->chlm",
        queries.reshape(shape_four),
        keys_in.reshape(shape_four),
        preferred_element_type=jnp.float32,
    ) * HEAD_DIM ** (-0.5)
    peak_score = jnp.max(scores, axis=-1, keepdims=True)
    raised = jnp.exp(scores - peak_score)
    exp_total = jnp.sum(raised, axis=-1, keepdims=True)
    attn_probs = (raised / exp_total).astype(jnp.bfloat16)
    log_total = peak_score + jnp.log(exp_total)
    result = jnp.einsum(
        "chlm,cmhe->clhe",
        attn_probs,
        values_in.reshape(shape_four),
        preferred_element_type=jnp.float32,
    )
    return (result.reshape(crop_count * crop_length, D), log_total)


def attend_back(queries, keys_in, values_in, log_total, grad_mixed, crop_count, crop_length):
    shape_four = (crop_count, crop_length, HEADS, HEAD_DIM)
    score_scale = HEAD_DIM ** (-0.5)
    query_four = queries.reshape(shape_four)
    key_four = keys_in.reshape(shape_four)
    value_four = values_in.reshape(shape_four)
    grad_four = grad_mixed.reshape(shape_four)
    scores = (
        jnp.einsum("clhe,cmhe->chlm", query_four, key_four, preferred_element_type=jnp.float32)
        * score_scale
    )
    attn_probs = jnp.exp(scores - log_total)
    grad_probs = jnp.einsum(
        "clhe,cmhe->chlm", grad_four, value_four, preferred_element_type=jnp.float32
    )
    grad_values = jnp.einsum(
        "chlm,clhe->cmhe",
        attn_probs.astype(jnp.bfloat16),
        grad_four,
        preferred_element_type=jnp.float32,
    )
    row_inner = jnp.sum(grad_probs * attn_probs, axis=-1, keepdims=True)
    grad_scores = (attn_probs * (grad_probs - row_inner)).astype(jnp.bfloat16)
    grad_queries = (
        jnp.einsum("chlm,cmhe->clhe", grad_scores, key_four, preferred_element_type=jnp.float32)
        * score_scale
    )
    grad_keys = (
        jnp.einsum("chlm,clhe->cmhe", grad_scores, query_four, preferred_element_type=jnp.float32)
        * score_scale
    )
    rows_here = crop_count * crop_length
    return jnp.concatenate(
        [
            grad_queries.reshape(rows_here, D),
            grad_keys.reshape(rows_here, D),
            grad_values.reshape(rows_here, D),
        ],
        axis=1,
    )


def forward_layer(stream, weights):
    (
        gain_one,
        shift_one,
        w_qkv,
        bias_query,
        bias_value,
        w_out,
        bias_out,
        gain_two,
        shift_two,
        w_up,
        bias_up,
        w_down,
        bias_down,
    ) = weights
    normed = norm_rows(stream, gain_one.astype(jnp.float32), shift_one.astype(jnp.float32)).astype(
        jnp.bfloat16
    )
    bias_all = jnp.concatenate([bias_query, jnp.zeros_like(bias_query), bias_value]).astype(
        jnp.float32
    )
    projected = (jnp.dot(normed, w_qkv, preferred_element_type=jnp.float32) + bias_all).astype(
        jnp.bfloat16
    )
    global_rows = G_DEV * GLEN
    global_part, global_total = attend_crops(
        projected[:global_rows, :D],
        projected[:global_rows, D : 2 * D],
        projected[:global_rows, 2 * D :],
        G_DEV,
        GLEN,
    )
    local_part, local_total = attend_crops(
        projected[global_rows:, :D],
        projected[global_rows:, D : 2 * D],
        projected[global_rows:, 2 * D :],
        L_DEV,
        LLEN,
    )
    mixed = jnp.concatenate([global_part, local_part], axis=0).astype(jnp.bfloat16)
    stream_one = (
        stream
        + jnp.dot(mixed, w_out, preferred_element_type=jnp.float32)
        + bias_out.astype(jnp.float32)
    )
    normed_two = norm_rows(
        stream_one, gain_two.astype(jnp.float32), shift_two.astype(jnp.float32)
    ).astype(jnp.bfloat16)
    pre_act = jnp.dot(normed_two, w_up, preferred_element_type=jnp.float32) + bias_up.astype(
        jnp.float32
    )
    hidden = jax.nn.gelu(pre_act, approximate=False).astype(jnp.bfloat16)
    result = (
        stream_one
        + jnp.dot(hidden, w_down, preferred_element_type=jnp.float32)
        + bias_down.astype(jnp.float32)
    )
    saved_state = (
        stream,
        normed,
        projected,
        global_total,
        local_total,
        mixed,
        stream_one,
        normed_two,
        pre_act,
        hidden,
    )
    return (result, saved_state)


def backward_layer(upstream, weights, saved_state):
    (
        gain_one,
        shift_one,
        w_qkv,
        bias_query,
        bias_value,
        w_out,
        bias_out,
        gain_two,
        shift_two,
        w_up,
        bias_up,
        w_down,
        bias_down,
    ) = weights
    (
        stream,
        normed,
        projected,
        global_total,
        local_total,
        mixed,
        stream_one,
        normed_two,
        pre_act,
        hidden,
    ) = saved_state
    branch_two = upstream.astype(jnp.bfloat16)
    grad_bias_down = jnp.sum(branch_two.astype(jnp.float32), axis=0)
    grad_w_down = contract_rows(hidden, branch_two)
    grad_hidden = contract_cols(branch_two, w_down)
    unused, gelu_pull = jax.vjp(lambda value: jax.nn.gelu(value, approximate=False), pre_act)
    grad_pre = gelu_pull(grad_hidden)[0].astype(jnp.bfloat16)
    grad_bias_up = jnp.sum(grad_pre.astype(jnp.float32), axis=0)
    grad_w_up = contract_rows(normed_two, grad_pre)
    grad_normed_two = contract_cols(grad_pre, w_up)
    unused_two, norm_pull_two = jax.vjp(
        norm_rows, stream_one, gain_two.astype(jnp.float32), shift_two.astype(jnp.float32)
    )
    grad_stream_part, grad_gain_two, grad_shift_two = norm_pull_two(grad_normed_two)
    grad_stream_one = upstream + grad_stream_part
    branch_one = grad_stream_one.astype(jnp.bfloat16)
    grad_bias_out = jnp.sum(branch_one.astype(jnp.float32), axis=0)
    grad_w_out = contract_rows(mixed, branch_one)
    grad_mixed = contract_cols(branch_one, w_out).astype(jnp.bfloat16)
    global_rows = G_DEV * GLEN
    grad_global = attend_back(
        projected[:global_rows, :D],
        projected[:global_rows, D : 2 * D],
        projected[:global_rows, 2 * D :],
        global_total,
        grad_mixed[:global_rows],
        G_DEV,
        GLEN,
    )
    grad_local = attend_back(
        projected[global_rows:, :D],
        projected[global_rows:, D : 2 * D],
        projected[global_rows:, 2 * D :],
        local_total,
        grad_mixed[global_rows:],
        L_DEV,
        LLEN,
    )
    grad_projected = jnp.concatenate([grad_global, grad_local], axis=0).astype(jnp.bfloat16)
    column_sums = jnp.sum(grad_projected.astype(jnp.float32), axis=0)
    grad_bias_query = column_sums[:D]
    grad_bias_value = column_sums[2 * D :]
    grad_w_qkv = contract_rows(normed, grad_projected)
    grad_normed = contract_cols(grad_projected, w_qkv)
    unused_one, norm_pull_one = jax.vjp(
        norm_rows, stream, gain_one.astype(jnp.float32), shift_one.astype(jnp.float32)
    )
    grad_input_part, grad_gain_one, grad_shift_one = norm_pull_one(grad_normed)
    grad_stream = grad_stream_one + grad_input_part
    grads = (
        grad_gain_one,
        grad_shift_one,
        grad_w_qkv,
        grad_bias_query,
        grad_bias_value,
        grad_w_out,
        grad_bias_out,
        grad_gain_two,
        grad_shift_two,
        grad_w_up,
        grad_bias_up,
        grad_w_down,
        grad_bias_down,
    )
    return (grad_stream, grads)


def local(
    tokens,
    cotangent,
    norm1_gain,
    norm1_bias,
    qkv_weight,
    query_bias,
    value_bias,
    out_weight,
    out_bias,
    norm2_gain,
    norm2_bias,
    up_weight,
    up_bias,
    down_weight,
    down_bias,
):
    shards = (
        norm1_gain,
        norm1_bias,
        qkv_weight,
        query_bias,
        value_bias,
        out_weight,
        out_bias,
        norm2_gain,
        norm2_bias,
        up_weight,
        up_bias,
        down_weight,
        down_bias,
    )
    layer_total = qkv_weight.shape[0]
    stream = tokens.astype(jnp.float32)
    saved_layers = []
    kept_weights = []
    for layer_index in range(layer_total):
        weights = gather_forward(tuple((w[layer_index] for w in shards)))
        stream, saved_state = forward_layer(stream, weights)
        saved_layers.append(saved_state)
        kept_weights.append(weights)
    encoded = stream.astype(jnp.bfloat16)
    upstream = cotangent.astype(jnp.float32)
    reduced_layers = [None] * layer_total
    for layer_index in reversed(range(layer_total)):
        upstream, grads = backward_layer(
            upstream, kept_weights[layer_index], saved_layers[layer_index]
        )
        reduced_layers[layer_index] = reduce_grads(grads)
    stacked = tuple(
        (
            jnp.stack(
                [reduced_layers[layer_index][member] for layer_index in range(layer_total)], axis=0
            )
            for member in range(13)
        )
    )
    return (
        encoded,
        upstream,
        stacked[0],
        stacked[1],
        stacked[2],
        stacked[3],
        stacked[4],
        stacked[5],
        stacked[6],
        stacked[7],
        stacked[8],
        stacked[9],
        stacked[10],
        stacked[11],
        stacked[12],
    )


VMEM_BYTES = 63 * 1024 * 1024

MESH = pl.DeviceIdType.MESH
F32 = jnp.float32
BF16 = jnp.bfloat16

FF = 3072
ROWS = 345
PAD = 352
STEP = 32
UNROLL = True
SHARD = 96
HALF = 48
UNITS = 12
LAYER_ROWS = UNITS * D
DOWN_AT = 8 * D
SLOTS = 6
PARTS = 2
WIDE = D // PARTS
LAG_XY, LAG_LAST, LAG_Z1, LAG_Z2, LAG_OUT = 3, 5, 7, 9, 11
LAG_PASS, LAG_WHOLE = 8, 9
HELD = 4
EARLY = 3
TOP_ROWS = 208
KEYS = 256
LOW_KEY = PAD - KEYS
LOW_ROWS = PAD - TOP_ROWS
V_G1, V_B1, V_QB, V_VB, V_OB, V_G2, V_B2, V_DB, V_UB = range(9)


def nt(left, right):
    return lax.dot_general(left, right, (((1,), (1,)), ((), ())), preferred_element_type=F32)


def tn(left, right):
    return lax.dot_general(left, right, (((0,), (0,)), ((), ())), preferred_element_type=F32)


def nn(left, right):
    return lax.dot_general(left, right, (((1,), (0,)), ((), ())), preferred_element_type=F32)


def aligned(value, by):
    return value if isinstance(value, int) else pl.multiple_of(value, by)


def unit_row(layer, unit, owner):
    is_down = unit // 8 if isinstance(unit, int) else lax.div(unit, 8)
    plain = unit * D + owner * SHARD
    down = DOWN_AT + owner * (4 * SHARD) + (unit - 8) * SHARD
    return aligned(layer * LAYER_ROWS + (1 - is_down) * plain + is_down * down, 16)


def forward_unit(index):
    return lax.div(index, UNITS), lax.rem(index, UNITS)


def backward_unit(layers, index):
    whole, half = lax.div(index, PARTS), lax.rem(index, PARTS)
    turn, place = lax.div(whole, UNITS), lax.rem(whole, UNITS)
    part = lax.div(place, 4)
    is_down, is_late = lax.div(2 - part, 2), lax.div(part, 2)
    unit = (
        is_down * (8 + place)
        + (1 - is_down - is_late) * place
        + is_late * lax.rem(place + 3, 4)
    )
    return layers - 1 - turn, unit, half


def stats(x):
    mean = jnp.mean(x, axis=-1, keepdims=True)
    centred = x - mean
    scale = lax.rsqrt(jnp.mean(centred * centred, axis=-1, keepdims=True) + epsilon)
    return centred * scale, scale


def fold(x):
    return jnp.sum(x.reshape(x.shape[0] // 8, 8, x.shape[1]), axis=0)


def total(x):
    return jnp.sum(x, axis=0, keepdims=True)


def step_rows(step):
    return pl.ds(aligned(step * STEP, STEP), STEP)


def encoder_kernel(
    layers,
    tokens,
    cotangent,
    n_g1,
    n_b1,
    n_qb,
    n_vb,
    n_ob,
    n_g2,
    n_b2,
    n_db,
    n_ub,
    w_qkv,
    w_out,
    w_up,
    w_down,
    encoded,
    tokens_grad,
    g_vec,
    g_qkv,
    g_out,
    g_up,
    g_down,
    wb,
    xs,
    x1,
    nr,
    pj,
    mx,
    n2,
    hd,
    gp,
    lse,
    gb,
    gm,
    br,
    acc,
    kacc,
    vacc,
    mask_top,
    mask_low,
    vsg,
    vec,
    ubs,
    vr,
    rc,
    r2,
    rz,
    ag_sem,
    ag_send,
    own_sem,
    core_sem,
    xy_sem,
    last_sem,
    z_sem,
    s0_send,
    rs_send,
    out_sem,
    vec_send,
    vec_recv,
    gv_send,
    gv_recv,
    credit,
):
    count = layers * UNITS
    pieces = count * PARTS
    d = lax.axis_index("dp")
    f = lax.axis_index("fsdp")
    c = lax.rem(f, 2)
    x = lax.rem(lax.div(f, 2), 2)
    y = lax.div(f, 4)
    fc = f + 1 - 2 * c
    fx = f + 2 - 4 * x
    fy = f + 4 - 8 * y
    outer = d * (3 - d) == 0
    inner = d * (3 - d) != 0
    z_in = 1 + lax.div(d, 3)
    z_out = 3 * lax.div(d, 2)
    z_pair = 3 - d
    parity = lax.rem(d, 2)
    z_near = d + 1 - 2 * parity
    in_plane = lambda who: {"fsdp": who}
    along = lambda who: {"dp": who}
    both = lambda a, b: jnp.logical_and(a, b)

    def block(yy, xx, cc):
        return yy * 4 + xx * 2 + cc

    def send(source, target, sent, landed, who):
        pltpu.make_async_remote_copy(
            src_ref=source,
            dst_ref=target,
            send_sem=sent,
            recv_sem=landed,
            device_id=who,
            device_id_type=MESH,
        ).start()

    def wait_rows(sem, rows):
        span = wb.at[pl.ds(0, rows)]
        pltpu.make_async_copy(span, span, sem).wait()

    barrier = pltpu.get_barrier_semaphore()
    peers = [lax.rem(f + hop, 8) for hop in range(1, 8)]
    for peer in peers:
        pl.semaphore_signal(barrier, inc=1, device_id=in_plane(peer), device_id_type=MESH)

    for hop in (1, 3):
        beside = lax.rem(d + hop, 4)
        pl.semaphore_signal(barrier, inc=1, device_id=along(beside), device_id_type=MESH)

    for layer in range(layers):
        for unit in range(UNITS):
            if unit < 3:
                source = w_qkv.at[layer, :, pl.ds(unit * D, D)]
            elif unit == 3:
                source = w_out.at[layer]
            elif unit < 8:
                source = w_up.at[layer, :, pl.ds((unit - 4) * D, D)]
            else:
                source = w_down.at[layer, pl.ds((unit - 8) * SHARD, SHARD)]
            pltpu.make_async_copy(
                source,
                wb.at[pl.ds(unit_row(layer, unit, f), SHARD)],
                own_sem.at[layer * UNITS + unit],
            ).start()
    vec[...] = jnp.zeros((8 * layers, D), F32)
    for at, source in enumerate((n_g1, n_b1, n_qb, n_vb, n_ob, n_g2, n_b2, n_db)):
        shard = source[...].astype(F32)
        for layer in range(layers):
            vec[8 * layer + at : 8 * layer + at + 1, 0:SHARD] = shard[layer : layer + 1]
    shard = n_ub[...].astype(F32)
    for layer in range(layers):
        vec[8 * layer : 8 * layer + 1, 128:512] = shard[layer : layer + 1]
    vsg[f] = vec[:, 0:512].astype(BF16)
    pl.semaphore_wait(barrier, 9)

    def role(i):
        return lax.rem(i, 3) * lax.div(2 * count - 3 - i, count)

    def collects(i):
        return role(i) != 2 - parity

    def gather_tick(t):
        @pl.when(t < count)
        def _():
            layer, unit = forward_unit(t)
            row = unit_row(layer, unit, f)
            wait_rows(own_sem.at[t], SHARD)
            whole = wb.at[pl.ds(row, SHARD)]

            @pl.when(collects(t))
            def _():
                first = wb.at[pl.ds(row, HALF)]
                second = wb.at[pl.ds(aligned(row + HALF, 16), HALF)]
                send(first, first, ag_send.at[t], ag_sem.at[t, 0], in_plane(fy))
                send(second, second, ag_send.at[t], ag_sem.at[t, 1], in_plane(fx))
                send(first, first, ag_send.at[t], ag_sem.at[t, 2], in_plane(fx))
                send(second, second, ag_send.at[t], ag_sem.at[t, 2], in_plane(fy))

            send(whole, whole, ag_send.at[t], ag_sem.at[t, 3], in_plane(fc))

        @pl.when(both(both(t >= 2, t < count + 2), collects(t - 2)))
        def _():
            i = t - 2
            layer, unit = forward_unit(i)
            wait_rows(ag_sem.at[i, 0], HALF)
            wait_rows(ag_sem.at[i, 1], HALF)
            first = wb.at[pl.ds(unit_row(layer, unit, block(1 - y, x, c)), HALF)]
            other = unit_row(layer, unit, block(y, 1 - x, c))
            second = wb.at[pl.ds(aligned(other + HALF, 16), HALF)]
            send(first, first, ag_send.at[i], ag_sem.at[i, 2], in_plane(fx))
            send(second, second, ag_send.at[i], ag_sem.at[i, 2], in_plane(fy))

        @pl.when(both(both(t >= 4, t < count + 4), collects(t - 4)))
        def _():
            i = t - 4
            layer, unit = forward_unit(i)
            wait_rows(ag_sem.at[i, 2], 4 * HALF)
            for yy, xx in ((1 - y, x), (y, 1 - x), (1 - y, 1 - x)):
                piece = wb.at[pl.ds(unit_row(layer, unit, block(yy, xx, c)), SHARD)]

                @pl.when(role(i) > 0)
                def _(piece=piece):
                    send(piece, piece, ag_send.at[i], ag_sem.at[i, 0], along(z_near))

                send(piece, piece, ag_send.at[i], ag_sem.at[i, 3], in_plane(fc))

        @pl.when(both(both(t >= LAG_PASS, t < count + LAG_PASS), role(t - LAG_PASS) == 2 - parity))
        def _():
            i = t - LAG_PASS
            layer, unit = forward_unit(i)
            wait_rows(ag_sem.at[i, 0], 3 * SHARD)
            for yy, xx in ((1 - y, x), (y, 1 - x), (1 - y, 1 - x)):
                piece = wb.at[pl.ds(unit_row(layer, unit, block(yy, xx, c)), SHARD)]
                send(piece, piece, ag_send.at[i], ag_sem.at[i, 3], in_plane(fc))

        @pl.when(both(t >= LAG_WHOLE, t < count + LAG_WHOLE))
        def _():
            wait_rows(ag_sem.at[t - LAG_WHOLE, 3], 4 * SHARD)

    for hop, peer in enumerate(peers):
        send(vsg.at[f], vsg.at[f], vec_send.at[hop], vec_recv.at[hop], in_plane(peer))

    @pl.loop(0, EARLY)
    def _(t):
        gather_tick(t)

    def crop_of(shape, dim, start):
        at = lax.broadcasted_iota(jnp.int32, shape, dim) + start
        which = jnp.zeros(shape, jnp.int32)
        for edge in range(L_DEV + 1):
            which = which + (at >= GLEN + edge * LLEN).astype(jnp.int32)
        return which

    for mask, rows, row_at, key_at in (
        (mask_top, TOP_ROWS, 0, 0),
        (mask_low, LOW_ROWS, TOP_ROWS, LOW_KEY),
    ):
        same = crop_of((rows, KEYS), 0, row_at) == crop_of((rows, KEYS), 1, key_at)
        mask[...] = jnp.where(same, 0.0, -1e30).astype(F32)

    xs[0, PAD - 8 :, :] = jnp.zeros((8, D), F32)
    xs[0, 0:ROWS, :] = tokens[...].astype(F32)

    for hop in range(7):
        pltpu.make_async_copy(vsg.at[0], vsg.at[0], vec_recv.at[hop]).wait()
    spread = jnp.zeros((8 * layers, D), F32)
    for owner in range(8):
        at_row = lax.broadcasted_iota(jnp.int32, (128, D), 0)
        at_col = lax.broadcasted_iota(jnp.int32, (128, D), 1)
        hit = jnp.logical_and(at_col == at_row + owner * SHARD, at_row < SHARD)
        spread = spread + nn(vsg[owner, :, 0:128], jnp.where(hit, 1.0, 0.0).astype(BF16))
        ubs[:, owner * 384 : (owner + 1) * 384] = vsg[owner, :, 128:512].astype(F32)
    vec[...] = spread

    @pl.loop(EARLY, LAG_WHOLE)
    def _(t):
        gather_tick(t)

    def vector(layer, which):
        return vec[pl.ds(layer * 8 + which, 1), :]

    lane = lax.broadcasted_iota(jnp.int32, (1, 128), 1)
    left_lane = lane < HEAD_DIM
    score_scale = HEAD_DIM ** (-0.5)
    head_scaled = [
        jnp.where(left_lane, score_scale, 0.0).astype(BF16),
        jnp.where(left_lane, 0.0, score_scale).astype(BF16),
    ]
    head_plain = [
        jnp.where(left_lane, 1.0, 0.0).astype(BF16),
        jnp.where(left_lane, 0.0, 1.0).astype(BF16),
    ]
    groups = (
        (0, TOP_ROWS, 0, mask_top),
        (TOP_ROWS, LOW_ROWS, LOW_KEY, mask_low),
    )

    def weight(layer, unit):
        return pl.ds(aligned(layer * LAYER_ROWS + unit * D, 16), D)

    @pl.loop(0, layers)
    def _(layer):
        base = layer * UNITS + LAG_WHOLE

        @pl.loop(0, PAD // STEP, unroll=UNROLL)
        def _(step):
            rows = step_rows(step)
            normed, _unused = stats(xs[layer, rows, :])
            nr[layer, rows, :] = (normed * vector(layer, V_G1) + vector(layer, V_B1)).astype(BF16)

        @pl.loop(0, 3)
        def _(part):
            gather_tick(base + part)
            is_q, is_v = lax.div(2 - part, 2), lax.div(part, 2)
            bias = is_q.astype(F32) * vector(layer, V_QB) + is_v.astype(F32) * vector(layer, V_VB)
            acc[...] = nn(nr[layer], wb[weight(layer, part), :])

            @pl.loop(0, PAD // STEP, unroll=UNROLL)
            def _(step):
                rows = step_rows(step)
                pj[layer, part, rows, :] = (acc[rows, :] + bias).astype(BF16)

        @pl.loop(0, HEADS // 2)
        def _(pair):
            @pl.when(pair == 3)
            def _():
                gather_tick(base + 3)

            lanes = pl.ds(aligned(pair * 128, 128), 128)
            for row_at, rows, key_at, mask in groups:
                here = pl.ds(row_at, rows)
                keys = pj[layer, 1, pl.ds(key_at, KEYS), lanes]
                values = pj[layer, 2, pl.ds(key_at, KEYS), lanes]
                queries = pj[layer, 0, here, lanes]
                results = []
                for side in range(2):
                    scores = nt(queries * head_scaled[side], keys) + mask[...]
                    peak = jnp.max(scores, axis=-1, keepdims=True)
                    raised = jnp.exp(scores - peak)
                    exp_total = jnp.sum(raised, axis=-1, keepdims=True)
                    probs = (raised * (1.0 / exp_total)).astype(BF16)
                    results.append(nn(probs, values))
                    log_total = peak + jnp.log(exp_total)
                    lse[layer, here, :] = jnp.where(
                        lane == pair * 2 + side, log_total, lse[layer, here, :]
                    )
                mx[layer, here, lanes] = jnp.where(left_lane, results[0], results[1]).astype(BF16)

        acc[...] = nn(mx[layer], wb[weight(layer, 3), :])

        @pl.loop(0, PAD // STEP, unroll=UNROLL)
        def _(step):
            rows = step_rows(step)
            now = xs[layer, rows, :] + acc[rows, :] + vector(layer, V_OB)
            x1[layer, rows, :] = now
            normed, _unused = stats(now)
            n2[layer, rows, :] = (normed * vector(layer, V_G2) + vector(layer, V_B2)).astype(BF16)

        @pl.loop(0, 4)
        def _(part):
            gather_tick(base + 4 + part)
            bias = ubs[pl.ds(layer * 8, 1), pl.ds(aligned(part * D, 128), D)]
            acc[...] = nn(n2[layer], wb[weight(layer, 4 + part), :])

            @pl.loop(0, PAD // STEP, unroll=UNROLL)
            def _(step):
                rows = step_rows(step)
                pre = acc[rows, :] + bias
                cdf = 0.5 + 0.5 * lax.erf(pre * (0.5**0.5))
                bell = jnp.exp(-0.5 * pre * pre) * 0.3989422804014327
                hd[layer, part, rows, :] = (pre * cdf).astype(BF16)
                gp[layer, part, rows, :] = (cdf + pre * bell).astype(BF16)

        @pl.loop(0, 4)
        def _(part):
            gather_tick(base + 8 + part)

        acc[...] = x1[layer] + vector(layer, V_DB)

        @pl.loop(0, 4)
        def _(part):
            acc[...] += nn(hd[layer, part], wb[weight(layer, 8 + part), :])

        xs[layer + 1] = acc[...]

    encoded[...] = xs[layers, 0:ROWS, :].astype(BF16)

    @pl.loop(0, count)
    def _(i):
        @pl.when(role(i) == 0)
        def _():
            wait_rows(ag_send.at[i], 7 * SHARD)

        @pl.when(role(i) == 1 + parity)
        def _():
            wait_rows(ag_send.at[i], 10 * SHARD)

        @pl.when(role(i) == 2 - parity)
        def _():
            wait_rows(ag_send.at[i], 4 * SHARD)

    for hop in range(7):
        pltpu.make_async_copy(vsg.at[0], vsg.at[0], vec_send.at[hop]).wait()

    def here_row(i, owner):
        layer, unit, _half = backward_unit(layers, i)
        return unit_row(layer, unit, owner)

    def columns(i):
        return pl.ds(aligned(lax.rem(i, PARTS) * WIDE, 128), WIDE)

    def shard_at(i, owner):
        return wb.at[pl.ds(here_row(i, owner), SHARD), columns(i)]

    def half_at(i, owner, half):
        row = here_row(i, owner) + half * HALF
        return wb.at[pl.ds(aligned(row, 16), HALF), columns(i)]

    def wait_piece(sem, rows):
        span = wb.at[pl.ds(0, rows), pl.ds(0, WIDE)]
        pltpu.make_async_copy(span, span, sem).wait()

    def during(t, lag):
        return both(t >= lag, t < pieces + lag)

    def credit_wait(i, which):
        @pl.when(i >= SLOTS)
        def _():
            pl.semaphore_wait(credit.at[which], 1)

    def credit_give(i, which, who):
        @pl.when(i + SLOTS < pieces)
        def _():
            pl.semaphore_signal(credit.at[which], inc=1, device_id=who, device_id_type=MESH)

    def reduce_tick(t):
        @pl.when(t < pieces)
        def _():
            slot = lax.rem(t, SLOTS)
            credit_wait(t, 0)
            for place in range(4):
                send(
                    shard_at(t, 2 * place + 1 - c),
                    rc.at[slot, pl.ds(place * SHARD, SHARD)],
                    s0_send.at[t],
                    core_sem.at[t],
                    in_plane(fc),
                )

        @pl.when(during(t, LAG_XY))
        def _():
            i = t - LAG_XY
            slot = lax.rem(i, SLOTS)
            wait_piece(xy_sem.at[i], 4 * HALF)
            for other in range(2):
                span = half_at(i, block(other, x, c), 0)
                span[...] = span[...] + r2[slot, pl.ds(other * HALF, HALF), :]
                span = half_at(i, block(y, other, c), 1)
                span[...] = span[...] + r2[slot, pl.ds((2 + other) * HALF, HALF), :]
            credit_give(i, 1, in_plane(fx))
            credit_give(i, 2, in_plane(fy))
            send(
                half_at(i, block(1 - y, x, c), 0),
                half_at(i, block(1 - y, x, 1 - c), 0),
                rs_send.at[i],
                last_sem.at[i],
                in_plane(fy),
            )
            send(
                half_at(i, block(y, 1 - x, c), 1),
                half_at(i, block(y, 1 - x, 1 - c), 1),
                rs_send.at[i],
                last_sem.at[i],
                in_plane(fx),
            )

        @pl.when(during(t, 1))
        def _():
            i = t - 1
            slot = lax.rem(i, SLOTS)
            wait_piece(core_sem.at[i], 4 * SHARD)
            wait_piece(s0_send.at[i], 4 * SHARD)
            for place in range(4):
                span = shard_at(i, 2 * place + c)
                span[...] = span[...] + rc[slot, pl.ds(place * SHARD, SHARD), :]
            credit_give(i, 0, in_plane(fc))
            credit_wait(i, 1)
            credit_wait(i, 2)
            for other in range(2):
                send(
                    half_at(i, block(other, 1 - x, c), 0),
                    r2.at[slot, pl.ds(other * HALF, HALF)],
                    rs_send.at[i],
                    xy_sem.at[i],
                    in_plane(fx),
                )
                send(
                    half_at(i, block(1 - y, other, c), 1),
                    r2.at[slot, pl.ds((2 + other) * HALF, HALF)],
                    rs_send.at[i],
                    xy_sem.at[i],
                    in_plane(fy),
                )

        @pl.when(during(t, LAG_LAST))
        def _():
            i = t - LAG_LAST
            slot = lax.rem(i, SLOTS)
            wait_piece(last_sem.at[i], SHARD)
            own = shard_at(i, f)
            own[...] = own[...] + shard_at(i, fc)[...]

            @pl.when(outer)
            def _():
                credit_wait(i, 3)
                send(own, rz.at[slot, 0], rs_send.at[i], z_sem.at[i, 0], along(z_in))

        @pl.when(both(inner, during(t, LAG_Z1)))
        def _():
            i = t - LAG_Z1
            slot = lax.rem(i, SLOTS)
            wait_piece(z_sem.at[i, 0], SHARD)
            own = shard_at(i, f)
            own[...] = own[...] + rz[slot, 0]
            credit_give(i, 3, along(z_out))
            credit_wait(i, 4)
            send(own, rz.at[slot, 1], rs_send.at[i], z_sem.at[i, 1], along(z_pair))

        @pl.when(both(inner, during(t, LAG_Z2)))
        def _():
            i = t - LAG_Z2
            slot = lax.rem(i, SLOTS)
            wait_piece(z_sem.at[i, 1], SHARD)
            done = shard_at(i, fc)
            done[...] = shard_at(i, f)[...] + rz[slot, 1]
            credit_give(i, 4, along(z_pair))
            send(done, done, rs_send.at[i], z_sem.at[i, 2], along(z_out))

        @pl.when(during(t, LAG_OUT))
        def _():
            i = t - LAG_OUT
            layer, unit, half = backward_unit(layers, i)

            @pl.when(outer)
            def _():
                wait_piece(z_sem.at[i, 2], SHARD)

            done = shard_at(i, fc)

            def emit(target):
                pltpu.make_async_copy(done, target, out_sem.at[i]).start()

            def wide_at(first):
                return pl.ds(aligned((unit - first) * D + half * WIDE, 128), WIDE)

            @pl.when(unit < 3)
            def _():
                emit(g_qkv.at[layer, :, wide_at(0)])

            @pl.when(unit == 3)
            def _():
                emit(g_out.at[layer, :, columns(i)])

            @pl.when(both(unit >= 4, unit < 8))
            def _():
                emit(g_up.at[layer, :, wide_at(4)])

            @pl.when(unit >= 8)
            def _():
                rows = pl.ds(aligned((unit - 8) * SHARD, 16), SHARD)
                emit(g_down.at[layer, rows, columns(i)])

    def vector_step(layer, step):
        mine = g_vec.at[layer]

        def arrive(at):
            pltpu.make_async_copy(mine, mine, gv_recv.at[layer, at]).wait()

        def leave(at):
            pltpu.make_async_copy(mine, mine, gv_send.at[layer, at]).wait()

        def go(at, target, landed, who):
            send(mine, target, gv_send.at[layer, at], gv_recv.at[layer, landed], who)

        def add(at):
            g_vec[layer] = g_vec[layer] + vr[layer, at]

        for at, who in enumerate((fc, fx, fy)):

            @pl.when(step == at)
            def _(at=at, who=who):
                if at:
                    leave(at - 1)
                    arrive(at - 1)
                    add(at - 1)
                go(at, vr.at[layer, at], at, in_plane(who))

        @pl.when(step == 3)
        def _():
            leave(2)
            arrive(2)
            add(2)

            @pl.when(outer)
            def _():
                go(3, vr.at[layer, 3], 3, along(z_in))

        @pl.when(both(inner, step == 4))
        def _():
            arrive(3)
            add(3)
            go(4, vr.at[layer, 4], 4, along(z_pair))

        @pl.when(both(inner, step == 5))
        def _():
            leave(4)
            arrive(4)
            add(4)
            go(3, vr.at[layer, 3], 3, along(z_out))

        @pl.when(step == 6)
        def _():
            leave(3)

            @pl.when(outer)
            def _():
                arrive(3)
                g_vec[layer] = vr[layer, 3]

    up = xs.at[layers]
    up[PAD - 8 :, :] = jnp.zeros((8, D), F32)
    up[0:ROWS, :] = cotangent[...].astype(F32)
    none = jnp.zeros((8, D), F32)

    def put_vector(layer, which, value):
        g_vec[layer, pl.ds(which, 1), :] = total(value)

    def weight_grad(rows_at, left, right):
        @pl.loop(0, 3)
        def _(third):
            lanes = pl.ds(aligned(third * KEYS, 128), KEYS)
            target = pl.ds(aligned(rows_at + third * KEYS, 16), KEYS)
            wb[target, :] = tn(left[:, lanes], right[...]).astype(BF16)

    @pl.loop(0, layers)
    def _(turn):
        layer = layers - 1 - turn
        base = turn * UNITS * PARTS
        for row in range(12, 16):
            g_vec[layer, row : row + 1, :] = jnp.zeros((1, D), F32)

        def branch_two(step, carry):
            rows = step_rows(step)
            rounded = up[rows, :].astype(BF16)
            br[rows, :] = rounded
            return carry + fold(rounded.astype(F32))

        put_vector(layer, V_DB, lax.fori_loop(0, PAD // STEP, branch_two, none, unroll=UNROLL))

        @pl.loop(0, 4)
        def _(part):
            @pl.when(turn > 0)
            def _():
                reduce_tick(base - HELD + part)

            acc[...] = nt(br[...], wb[weight(layer, 8 + part), :])

            def through_gelu(step, carry):
                rows = step_rows(step)
                value = (acc[rows, :] * gp[layer, part, rows, :].astype(F32)).astype(BF16)
                gb[part, rows, :] = value
                return carry + fold(value.astype(F32))

            put_vector(layer, V_UB + part, lax.fori_loop(0, PAD // STEP, through_gelu, none, unroll=UNROLL))
            weight_grad(layer * LAYER_ROWS + DOWN_AT + part * D, hd.at[layer, part], br)

        acc[...] = jnp.zeros((PAD, D), F32)

        @pl.loop(0, 4)
        def _(part):
            @pl.when(turn > 0)
            def _():
                vector_step(layer + 1, part)

            acc[...] += nt(gb[part], wb[weight(layer, 4 + part), :])
            weight_grad(layer * LAYER_ROWS + (4 + part) * D, n2.at[layer], gb.at[part])

            @pl.loop(0, 2)
            def _(again):
                reduce_tick(base + 2 * part + again)

        def norm_back(source, gain_at, shift_at):
            def body(step, carry):
                gain_sum, shift_sum = carry
                rows = step_rows(step)
                normed, scale = stats(source[layer, rows, :])
                grad = acc[rows, :]
                t = grad * vector(layer, gain_at)
                inner_mean = jnp.mean(t * normed, axis=-1, keepdims=True)
                back = scale * (t - jnp.mean(t, axis=-1, keepdims=True) - normed * inner_mean)
                up[rows, :] = up[rows, :] + back
                return gain_sum + fold(grad * normed), shift_sum + fold(grad)

            gain_sum, shift_sum = lax.fori_loop(0, PAD // STEP, body, (none, none), unroll=UNROLL)
            put_vector(layer, gain_at, gain_sum)
            put_vector(layer, shift_at, shift_sum)

        norm_back(x1, V_G2, V_B2)

        put_vector(layer, V_OB, lax.fori_loop(0, PAD // STEP, branch_two, none, unroll=UNROLL))
        gm[...] = nt(br[...], wb[weight(layer, 3), :]).astype(BF16)
        weight_grad(layer * LAYER_ROWS + 3 * D, mx.at[layer], br)

        @pl.loop(0, 2)
        def _(again):
            reduce_tick(base + 8 + again)

        @pl.loop(0, HEADS // 2)
        def _(pair):
            reduce_tick(base + 10 + pair)

            @pl.when(both(turn > 0, pair < 3))
            def _():
                vector_step(layer + 1, pair + 4)

            lanes = pl.ds(aligned(pair * 128, 128), 128)
            kacc[...] = jnp.zeros((PAD, 128), F32)
            vacc[...] = jnp.zeros((PAD, 128), F32)
            for row_at, rows, key_at, mask in groups:
                here = pl.ds(row_at, rows)
                there = pl.ds(key_at, KEYS)
                keys = pj[layer, 1, there, lanes]
                values = pj[layer, 2, there, lanes]
                queries = pj[layer, 0, here, lanes]
                grads = gm[here, lanes]
                q_parts, k_parts, v_parts = [], [], []
                for side in range(2):
                    log_total = jnp.sum(
                        jnp.where(lane == pair * 2 + side, lse[layer, here, :], 0.0),
                        axis=-1,
                        keepdims=True,
                    )
                    scaled = queries * head_scaled[side]
                    probs = jnp.exp(nt(scaled, keys) + mask[...] - log_total)
                    grad_probs = nt(grads * head_plain[side], values)
                    row_inner = jnp.sum(grad_probs * probs, axis=-1, keepdims=True)
                    grad_scores = (probs * (grad_probs - row_inner)).astype(BF16)
                    v_parts.append(tn(probs.astype(BF16), grads))
                    k_parts.append(tn(grad_scores, queries))
                    q_parts.append(nn(grad_scores, keys))
                grad_queries = jnp.where(left_lane, q_parts[0], q_parts[1]) * score_scale
                gb[0, here, lanes] = grad_queries.astype(BF16)
                kacc[there, :] += jnp.where(left_lane, k_parts[0], k_parts[1]) * score_scale
                vacc[there, :] += jnp.where(left_lane, v_parts[0], v_parts[1])
            gb[1, :, lanes] = kacc[...].astype(BF16)
            gb[2, :, lanes] = vacc[...].astype(BF16)

        for which, part in ((V_QB, 0), (V_VB, 2)):

            def column_sum(step, carry, part=part):
                return carry + fold(gb[part, step_rows(step), :].astype(F32))

            put_vector(layer, which, lax.fori_loop(0, PAD // STEP, column_sum, none, unroll=UNROLL))

        acc[...] = jnp.zeros((PAD, D), F32)

        @pl.loop(0, 3)
        def _(part):
            acc[...] += nt(gb[part], wb[weight(layer, part), :])
            weight_grad(layer * LAYER_ROWS + part * D, nr.at[layer], gb.at[part])

            @pl.when(part == 0)
            def _():
                reduce_tick(base + 16)

            reduce_tick(base + 17 + part)

        norm_back(xs, V_G1, V_B1)

    tokens_grad[...] = up[0:ROWS, :]

    @pl.loop(pieces - HELD, pieces + LAG_OUT)
    def _(t):
        step = t - (pieces - HELD)

        @pl.when(both(lax.rem(step, 2) == 0, step < 14))
        def _():
            vector_step(0, lax.div(step, 2))

        reduce_tick(t)

    @pl.loop(0, pieces)
    def _(i):
        wait_piece(out_sem.at[i], SHARD)

        @pl.when(outer)
        def _():
            wait_piece(rs_send.at[i], 4 * SHARD)

        @pl.when(inner)
        def _():
            wait_piece(rs_send.at[i], 5 * SHARD)


def closing_kernel(layers, *refs):
    encoded_in, tokens_in, vec_in = refs[:3]
    grads_in = refs[3:7]
    encoded_out, tokens_out = refs[7:9]
    small_out = refs[9:18]
    grads_out = refs[18:22]
    vec = refs[22]
    narrow = refs[23:27]
    wide = refs[27:31]
    held_encoded, held_tokens, few_sem, in_sem, out_sem = refs[31:]
    f = lax.axis_index("fsdp")
    copies = [
        pltpu.make_async_copy(vec_in, vec, few_sem.at[0]),
        pltpu.make_async_copy(encoded_in, held_encoded, few_sem.at[1]),
        pltpu.make_async_copy(tokens_in, held_tokens, few_sem.at[2]),
    ]
    reads, writes = [], []
    for layer in range(layers):
        for at in range(4):
            reads.append(
                pltpu.make_async_copy(
                    grads_in[at].at[layer], narrow[at].at[layer], in_sem.at[at, layer]
                )
            )
            writes.append(
                pltpu.make_async_copy(
                    wide[at].at[layer], grads_out[at].at[layer], out_sem.at[at, layer]
                )
            )
    for copy in reads + copies:
        copy.start()
    for layer in range(layers):
        for at in range(4):
            reads[4 * layer + at].wait()
            wide[at][layer] = narrow[at][layer].astype(F32)
            writes[4 * layer + at].start()
    for copy in copies:
        copy.wait()
    writes.append(pltpu.make_async_copy(held_encoded, encoded_out, few_sem.at[1]))
    writes.append(pltpu.make_async_copy(held_tokens, tokens_out, few_sem.at[2]))
    writes[-2].start()
    writes[-1].start()
    for layer in range(layers):
        mine = vec[layer]
        shard = jnp.zeros((8, SHARD), F32)
        ups = jnp.zeros((1, 4 * SHARD), F32)
        for owner in range(8):
            here = f == owner
            shard = jnp.where(here, mine[0:8, owner * SHARD : (owner + 1) * SHARD], shard)
            row, lane = 8 + owner // 2, (owner % 2) * 4 * SHARD
            ups = jnp.where(here, mine[row : row + 1, lane : lane + 4 * SHARD], ups)
        for which in range(8):
            small_out[which][layer : layer + 1, :] = shard[which : which + 1]
        small_out[8][layer : layer + 1, :] = ups
    for copy in writes:
        copy.wait()


def kernel_local(
    tokens,
    cotangent,
    norm1_gain,
    norm1_bias,
    qkv_weight,
    query_bias,
    value_bias,
    out_weight,
    out_bias,
    norm2_gain,
    norm2_bias,
    up_weight,
    up_bias,
    down_weight,
    down_bias,
):
    layers = qkv_weight.shape[0]
    count = layers * UNITS
    pieces = count * PARTS
    vmem = pl.BlockSpec(memory_space=pltpu.VMEM)
    hbm = pl.BlockSpec(memory_space=pltpu.MemorySpace.HBM)
    plain = pl.BlockSpec()
    dma = pltpu.SemaphoreType.DMA
    results = pl.pallas_call(
        functools.partial(encoder_kernel, layers),
        out_shape=(
            jax.ShapeDtypeStruct((ROWS, D), BF16),
            jax.ShapeDtypeStruct((ROWS, D), F32),
            jax.ShapeDtypeStruct((layers, 16, D), F32),
            jax.ShapeDtypeStruct((layers, SHARD, 3 * D), BF16),
            jax.ShapeDtypeStruct((layers, SHARD, D), BF16),
            jax.ShapeDtypeStruct((layers, SHARD, FF), BF16),
            jax.ShapeDtypeStruct((layers, 4 * SHARD, D), BF16),
        ),
        in_specs=[vmem] * 2 + [plain] * 9 + [hbm] * 4,
        out_specs=(vmem, vmem, vmem, hbm, hbm, hbm, hbm),
        scratch_shapes=[
            pltpu.VMEM((layers * LAYER_ROWS, D), BF16),
            pltpu.VMEM((layers + 1, PAD, D), F32),
            pltpu.VMEM((layers, PAD, D), F32),
            pltpu.VMEM((layers, PAD, D), BF16),
            pltpu.VMEM((layers, 3, PAD, D), BF16),
            pltpu.VMEM((layers, PAD, D), BF16),
            pltpu.VMEM((layers, PAD, D), BF16),
            pltpu.VMEM((layers, 4, PAD, D), BF16),
            pltpu.VMEM((layers, 4, PAD, D), BF16),
            pltpu.VMEM((layers, PAD, 128), F32),
            pltpu.VMEM((4, PAD, D), BF16),
            pltpu.VMEM((PAD, D), BF16),
            pltpu.VMEM((PAD, D), BF16),
            pltpu.VMEM((PAD, D), F32),
            pltpu.VMEM((PAD, 128), F32),
            pltpu.VMEM((PAD, 128), F32),
            pltpu.VMEM((TOP_ROWS, KEYS), F32),
            pltpu.VMEM((LOW_ROWS, KEYS), F32),
            pltpu.VMEM((8, 8 * layers, 512), BF16),
            pltpu.VMEM((8 * layers, D), F32),
            pltpu.VMEM((8 * layers, FF), F32),
            pltpu.VMEM((layers, 5, 16, D), F32),
            pltpu.VMEM((SLOTS, 4 * SHARD, WIDE), BF16),
            pltpu.VMEM((SLOTS, 4 * HALF, WIDE), BF16),
            pltpu.VMEM((SLOTS, 2, SHARD, WIDE), BF16),
            dma((count, 4)),
            dma((count,)),
            dma((count,)),
            dma((pieces,)),
            dma((pieces,)),
            dma((pieces,)),
            dma((pieces, 3)),
            dma((pieces,)),
            dma((pieces,)),
            dma((pieces,)),
            dma((7,)),
            dma((7,)),
            dma((layers, 5)),
            dma((layers, 5)),
            pltpu.SemaphoreType.REGULAR((5,)),
        ],
        compiler_params=pltpu.CompilerParams(
            collective_id=0, has_side_effects=True, vmem_limit_bytes=VMEM_BYTES
        ),
    )(
        tokens,
        cotangent,
        norm1_gain,
        norm1_bias,
        query_bias,
        value_bias,
        out_bias,
        norm2_gain,
        norm2_bias,
        down_bias,
        up_bias,
        qkv_weight,
        out_weight,
        up_weight,
        down_weight,
    )
    shapes = [(layers, SHARD)] * 8 + [(layers, 4 * SHARD)]
    shapes += [(layers, SHARD, 3 * D), (layers, SHARD, D), (layers, SHARD, FF)]
    shapes += [(layers, 4 * SHARD, D)]
    closing = pl.pallas_call(
        functools.partial(closing_kernel, layers),
        out_shape=[jax.ShapeDtypeStruct((ROWS, D), BF16), jax.ShapeDtypeStruct((ROWS, D), F32)]
        + [jax.ShapeDtypeStruct(shape, F32) for shape in shapes],
        in_specs=[hbm] * 7,
        out_specs=[hbm] * 2 + [plain] * 9 + [hbm] * 4,
        scratch_shapes=[pltpu.VMEM((layers, 16, D), F32)]
        + [pltpu.VMEM(shape, BF16) for shape in shapes[9:]]
        + [pltpu.VMEM(shape, F32) for shape in shapes[9:]]
        + [pltpu.VMEM((ROWS, D), BF16), pltpu.VMEM((ROWS, D), F32)]
        + [dma((3,)), dma((4, layers)), dma((4, layers))],
        compiler_params=pltpu.CompilerParams(vmem_limit_bytes=VMEM_BYTES),
    )(*results)
    by = dict(zip(("encoded", "tokens_grad"), closing[:2]))
    small = closing[2:11]
    g_qkv, g_out, g_up, g_down = closing[11:]
    return (
        by["encoded"],
        by["tokens_grad"],
        small[V_G1],
        small[V_B1],
        g_qkv,
        small[V_QB],
        small[V_VB],
        g_out,
        small[V_OB],
        small[V_G2],
        small[V_B2],
        g_up,
        small[V_UB],
        g_down,
        small[V_DB],
    )


def solution(mesh):
    in_specs = (
        P(("dp", "fsdp"), None),
        P(("dp", "fsdp"), None),
        P(None, "fsdp"),
        P(None, "fsdp"),
        P(None, "fsdp", None),
        P(None, "fsdp"),
        P(None, "fsdp"),
        P(None, "fsdp", None),
        P(None, "fsdp"),
        P(None, "fsdp"),
        P(None, "fsdp"),
        P(None, "fsdp", None),
        P(None, "fsdp"),
        P(None, "fsdp", None),
        P(None, "fsdp"),
    )
    out_specs = (
        P(("dp", "fsdp"), None),
        P(("dp", "fsdp"), None),
        P(None, "fsdp"),
        P(None, "fsdp"),
        P(None, "fsdp", None),
        P(None, "fsdp"),
        P(None, "fsdp"),
        P(None, "fsdp", None),
        P(None, "fsdp"),
        P(None, "fsdp"),
        P(None, "fsdp"),
        P(None, "fsdp", None),
        P(None, "fsdp"),
        P(None, "fsdp", None),
        P(None, "fsdp"),
    )
    fits = mesh.shape["dp"] == 4 and mesh.shape["fsdp"] == 8
    body = kernel_local if fits else local
    return jax.shard_map(body, mesh=mesh, in_specs=in_specs, out_specs=out_specs, check_vma=False)
```

```python
import functools

import jax
import jax.numpy as jnp
from jax import lax
from jax.experimental import pallas as pl
from jax.experimental.pallas import tpu as pltpu
from jax.sharding import PartitionSpec as P

D = 768
HEADS = 12
HEAD_DIM = 64
GLEN = 197
LLEN = 37
G_DEV = 1
L_DEV = 4


epsilon = 1e-06


def norm_rows(values_in, gain, shift):
    row_mean = jnp.mean(values_in, axis=-1, keepdims=True)
    centred = values_in - row_mean
    spread = jnp.mean(centred * centred, axis=-1, keepdims=True)
    return centred * lax.rsqrt(spread + epsilon) * gain + shift


def contract_rows(left, right):
    return lax.dot_general(
        left, right, (((0,), (0,)), ((), ())), preferred_element_type=jnp.float32
    )


def contract_cols(left, right):
    return lax.dot_general(
        left, right, (((1,), (1,)), ((), ())), preferred_element_type=jnp.float32
    )


def gather_forward(pieces):
    return (
        lax.all_gather(pieces[0], "fsdp", axis=0, tiled=True),
        lax.all_gather(pieces[1], "fsdp", axis=0, tiled=True),
        lax.all_gather(pieces[2], "fsdp", axis=0, tiled=True),
        lax.all_gather(pieces[3], "fsdp", axis=0, tiled=True),
        lax.all_gather(pieces[4], "fsdp", axis=0, tiled=True),
        lax.all_gather(pieces[5], "fsdp", axis=0, tiled=True),
        lax.all_gather(pieces[6], "fsdp", axis=0, tiled=True),
        lax.all_gather(pieces[7], "fsdp", axis=0, tiled=True),
        lax.all_gather(pieces[8], "fsdp", axis=0, tiled=True),
        lax.all_gather(pieces[9], "fsdp", axis=0, tiled=True),
        lax.all_gather(pieces[10], "fsdp", axis=0, tiled=True),
        lax.all_gather(pieces[11], "fsdp", axis=0, tiled=True),
        lax.all_gather(pieces[12], "fsdp", axis=0, tiled=True),
    )


def reduce_grads(grads):
    shares = (
        lax.psum_scatter(grads[0], "fsdp", scatter_dimension=0, tiled=True),
        lax.psum_scatter(grads[1], "fsdp", scatter_dimension=0, tiled=True),
        lax.psum_scatter(grads[2].astype(jnp.bfloat16), "fsdp", scatter_dimension=0, tiled=True),
        lax.psum_scatter(grads[3], "fsdp", scatter_dimension=0, tiled=True),
        lax.psum_scatter(grads[4], "fsdp", scatter_dimension=0, tiled=True),
        lax.psum_scatter(grads[5].astype(jnp.bfloat16), "fsdp", scatter_dimension=0, tiled=True),
        lax.psum_scatter(grads[6], "fsdp", scatter_dimension=0, tiled=True),
        lax.psum_scatter(grads[7], "fsdp", scatter_dimension=0, tiled=True),
        lax.psum_scatter(grads[8], "fsdp", scatter_dimension=0, tiled=True),
        lax.psum_scatter(grads[9].astype(jnp.bfloat16), "fsdp", scatter_dimension=0, tiled=True),
        lax.psum_scatter(grads[10], "fsdp", scatter_dimension=0, tiled=True),
        lax.psum_scatter(grads[11].astype(jnp.bfloat16), "fsdp", scatter_dimension=0, tiled=True),
        lax.psum_scatter(grads[12], "fsdp", scatter_dimension=0, tiled=True),
    )
    column_parts = (
        lax.psum_scatter(
            shares[2], "dp", scatter_dimension=1, tiled=True
        ).astype(jnp.float32),
        lax.psum_scatter(
            shares[5], "dp", scatter_dimension=1, tiled=True
        ).astype(jnp.float32),
        lax.psum_scatter(
            shares[9], "dp", scatter_dimension=1, tiled=True
        ).astype(jnp.float32),
        lax.psum_scatter(
            shares[11], "dp", scatter_dimension=1, tiled=True
        ).astype(jnp.float32),
    )
    matrices = (
        lax.all_gather(column_parts[0].astype(jnp.bfloat16), "dp", axis=1, tiled=True).astype(
            jnp.float32
        ),
        lax.all_gather(column_parts[1].astype(jnp.bfloat16), "dp", axis=1, tiled=True).astype(
            jnp.float32
        ),
        lax.all_gather(column_parts[2].astype(jnp.bfloat16), "dp", axis=1, tiled=True).astype(
            jnp.float32
        ),
        lax.all_gather(column_parts[3].astype(jnp.bfloat16), "dp", axis=1, tiled=True).astype(
            jnp.float32
        ),
    )
    vectors = lax.psum(
        (
            shares[0],
            shares[1],
            shares[3],
            shares[4],
            shares[6],
            shares[7],
            shares[8],
            shares[10],
            shares[12],
        ),
        "dp",
    )
    return (
        vectors[0],
        vectors[1],
        matrices[0],
        vectors[2],
        vectors[3],
        matrices[1],
        vectors[4],
        vectors[5],
        vectors[6],
        matrices[2],
        vectors[7],
        matrices[3],
        vectors[8],
    )


def attend_crops(queries, keys_in, values_in, crop_count, crop_length):
    shape_four = (crop_count, crop_length, HEADS, HEAD_DIM)
    scores = jnp.einsum(
        "clhe,cmhe->chlm",
        queries.reshape(shape_four),
        keys_in.reshape(shape_four),
        preferred_element_type=jnp.float32,
    ) * HEAD_DIM ** (-0.5)
    peak_score = jnp.max(scores, axis=-1, keepdims=True)
    raised = jnp.exp(scores - peak_score)
    exp_total = jnp.sum(raised, axis=-1, keepdims=True)
    attn_probs = (raised / exp_total).astype(jnp.bfloat16)
    log_total = peak_score + jnp.log(exp_total)
    result = jnp.einsum(
        "chlm,cmhe->clhe",
        attn_probs,
        values_in.reshape(shape_four),
        preferred_element_type=jnp.float32,
    )
    return (result.reshape(crop_count * crop_length, D), log_total)


def attend_back(queries, keys_in, values_in, log_total, grad_mixed, crop_count, crop_length):
    shape_four = (crop_count, crop_length, HEADS, HEAD_DIM)
    score_scale = HEAD_DIM ** (-0.5)
    query_four = queries.reshape(shape_four)
    key_four = keys_in.reshape(shape_four)
    value_four = values_in.reshape(shape_four)
    grad_four = grad_mixed.reshape(shape_four)
    scores = (
        jnp.einsum("clhe,cmhe->chlm", query_four, key_four, preferred_element_type=jnp.float32)
        * score_scale
    )
    attn_probs = jnp.exp(scores - log_total)
    grad_probs = jnp.einsum(
        "clhe,cmhe->chlm", grad_four, value_four, preferred_element_type=jnp.float32
    )
    grad_values = jnp.einsum(
        "chlm,clhe->cmhe",
        attn_probs.astype(jnp.bfloat16),
        grad_four,
        preferred_element_type=jnp.float32,
    )
    row_inner = jnp.sum(grad_probs * attn_probs, axis=-1, keepdims=True)
    grad_scores = (attn_probs * (grad_probs - row_inner)).astype(jnp.bfloat16)
    grad_queries = (
        jnp.einsum("chlm,cmhe->clhe", grad_scores, key_four, preferred_element_type=jnp.float32)
        * score_scale
    )
    grad_keys = (
        jnp.einsum("chlm,clhe->cmhe", grad_scores, query_four, preferred_element_type=jnp.float32)
        * score_scale
    )
    rows_here = crop_count * crop_length
    return jnp.concatenate(
        [
            grad_queries.reshape(rows_here, D),
            grad_keys.reshape(rows_here, D),
            grad_values.reshape(rows_here, D),
        ],
        axis=1,
    )


def forward_layer(stream, weights):
    (
        gain_one,
        shift_one,
        w_qkv,
        bias_query,
        bias_value,
        w_out,
        bias_out,
        gain_two,
        shift_two,
        w_up,
        bias_up,
        w_down,
        bias_down,
    ) = weights
    normed = norm_rows(stream, gain_one.astype(jnp.float32), shift_one.astype(jnp.float32)).astype(
        jnp.bfloat16
    )
    bias_all = jnp.concatenate([bias_query, jnp.zeros_like(bias_query), bias_value]).astype(
        jnp.float32
    )
    projected = (jnp.dot(normed, w_qkv, preferred_element_type=jnp.float32) + bias_all).astype(
        jnp.bfloat16
    )
    global_rows = G_DEV * GLEN
    global_part, global_total = attend_crops(
        projected[:global_rows, :D],
        projected[:global_rows, D : 2 * D],
        projected[:global_rows, 2 * D :],
        G_DEV,
        GLEN,
    )
    local_part, local_total = attend_crops(
        projected[global_rows:, :D],
        projected[global_rows:, D : 2 * D],
        projected[global_rows:, 2 * D :],
        L_DEV,
        LLEN,
    )
    mixed = jnp.concatenate([global_part, local_part], axis=0).astype(jnp.bfloat16)
    stream_one = (
        stream
        + jnp.dot(mixed, w_out, preferred_element_type=jnp.float32)
        + bias_out.astype(jnp.float32)
    )
    normed_two = norm_rows(
        stream_one, gain_two.astype(jnp.float32), shift_two.astype(jnp.float32)
    ).astype(jnp.bfloat16)
    pre_act = jnp.dot(normed_two, w_up, preferred_element_type=jnp.float32) + bias_up.astype(
        jnp.float32
    )
    hidden = jax.nn.gelu(pre_act, approximate=False).astype(jnp.bfloat16)
    result = (
        stream_one
        + jnp.dot(hidden, w_down, preferred_element_type=jnp.float32)
        + bias_down.astype(jnp.float32)
    )
    saved_state = (
        stream,
        normed,
        projected,
        global_total,
        local_total,
        mixed,
        stream_one,
        normed_two,
        pre_act,
        hidden,
    )
    return (result, saved_state)


def backward_layer(upstream, weights, saved_state):
    (
        gain_one,
        shift_one,
        w_qkv,
        bias_query,
        bias_value,
        w_out,
        bias_out,
        gain_two,
        shift_two,
        w_up,
        bias_up,
        w_down,
        bias_down,
    ) = weights
    (
        stream,
        normed,
        projected,
        global_total,
        local_total,
        mixed,
        stream_one,
        normed_two,
        pre_act,
        hidden,
    ) = saved_state
    branch_two = upstream.astype(jnp.bfloat16)
    grad_bias_down = jnp.sum(branch_two.astype(jnp.float32), axis=0)
    grad_w_down = contract_rows(hidden, branch_two)
    grad_hidden = contract_cols(branch_two, w_down)
    unused, gelu_pull = jax.vjp(lambda value: jax.nn.gelu(value, approximate=False), pre_act)
    grad_pre = gelu_pull(grad_hidden)[0].astype(jnp.bfloat16)
    grad_bias_up = jnp.sum(grad_pre.astype(jnp.float32), axis=0)
    grad_w_up = contract_rows(normed_two, grad_pre)
    grad_normed_two = contract_cols(grad_pre, w_up)
    unused_two, norm_pull_two = jax.vjp(
        norm_rows, stream_one, gain_two.astype(jnp.float32), shift_two.astype(jnp.float32)
    )
    grad_stream_part, grad_gain_two, grad_shift_two = norm_pull_two(grad_normed_two)
    grad_stream_one = upstream + grad_stream_part
    branch_one = grad_stream_one.astype(jnp.bfloat16)
    grad_bias_out = jnp.sum(branch_one.astype(jnp.float32), axis=0)
    grad_w_out = contract_rows(mixed, branch_one)
    grad_mixed = contract_cols(branch_one, w_out).astype(jnp.bfloat16)
    global_rows = G_DEV * GLEN
    grad_global = attend_back(
        projected[:global_rows, :D],
        projected[:global_rows, D : 2 * D],
        projected[:global_rows, 2 * D :],
        global_total,
        grad_mixed[:global_rows],
        G_DEV,
        GLEN,
    )
    grad_local = attend_back(
        projected[global_rows:, :D],
        projected[global_rows:, D : 2 * D],
        projected[global_rows:, 2 * D :],
        local_total,
        grad_mixed[global_rows:],
        L_DEV,
        LLEN,
    )
    grad_projected = jnp.concatenate([grad_global, grad_local], axis=0).astype(jnp.bfloat16)
    column_sums = jnp.sum(grad_projected.astype(jnp.float32), axis=0)
    grad_bias_query = column_sums[:D]
    grad_bias_value = column_sums[2 * D :]
    grad_w_qkv = contract_rows(normed, grad_projected)
    grad_normed = contract_cols(grad_projected, w_qkv)
    unused_one, norm_pull_one = jax.vjp(
        norm_rows, stream, gain_one.astype(jnp.float32), shift_one.astype(jnp.float32)
    )
    grad_input_part, grad_gain_one, grad_shift_one = norm_pull_one(grad_normed)
    grad_stream = grad_stream_one + grad_input_part
    grads = (
        grad_gain_one,
        grad_shift_one,
        grad_w_qkv,
        grad_bias_query,
        grad_bias_value,
        grad_w_out,
        grad_bias_out,
        grad_gain_two,
        grad_shift_two,
        grad_w_up,
        grad_bias_up,
        grad_w_down,
        grad_bias_down,
    )
    return (grad_stream, grads)


def local(
    tokens,
    cotangent,
    norm1_gain,
    norm1_bias,
    qkv_weight,
    query_bias,
    value_bias,
    out_weight,
    out_bias,
    norm2_gain,
    norm2_bias,
    up_weight,
    up_bias,
    down_weight,
    down_bias,
):
    shards = (
        norm1_gain,
        norm1_bias,
        qkv_weight,
        query_bias,
        value_bias,
        out_weight,
        out_bias,
        norm2_gain,
        norm2_bias,
        up_weight,
        up_bias,
        down_weight,
        down_bias,
    )
    layer_total = qkv_weight.shape[0]
    stream = tokens.astype(jnp.float32)
    saved_layers = []
    kept_weights = []
    for layer_index in range(layer_total):
        weights = gather_forward(tuple((w[layer_index] for w in shards)))
        stream, saved_state = forward_layer(stream, weights)
        saved_layers.append(saved_state)
        kept_weights.append(weights)
    encoded = stream.astype(jnp.bfloat16)
    upstream = cotangent.astype(jnp.float32)
    reduced_layers = [None] * layer_total
    for layer_index in reversed(range(layer_total)):
        upstream, grads = backward_layer(
            upstream, kept_weights[layer_index], saved_layers[layer_index]
        )
        reduced_layers[layer_index] = reduce_grads(grads)
    stacked = tuple(
        (
            jnp.stack(
                [reduced_layers[layer_index][member] for layer_index in range(layer_total)], axis=0
            )
            for member in range(13)
        )
    )
    return (
        encoded,
        upstream,
        stacked[0],
        stacked[1],
        stacked[2],
        stacked[3],
        stacked[4],
        stacked[5],
        stacked[6],
        stacked[7],
        stacked[8],
        stacked[9],
        stacked[10],
        stacked[11],
        stacked[12],
    )


VMEM_BYTES = 65408 * 1024

MESH = pl.DeviceIdType.MESH
F32 = jnp.float32
BF16 = jnp.bfloat16

FF = 3072
ROWS = 345
PAD = 352
STEP = 32
UNROLL = True
SHARD = 96
HALF = 48
UNITS = 12
SLOTS = 6
CORE_SLOTS = 4
RING = 8
PARTS = 2
WIDE = D // PARTS
LAG_XY, LAG_LAST, LAG_Z1, LAG_Z2, LAG_OUT = 4, 6, 8, 10, 12
LAG_PASS, LAG_WHOLE = 8, 9
EARLY_UNITS = 2
EARLY = 3
VEC_EVERY = 5
TOP_ROWS = 208
KEYS = 256
LOW_KEY = PAD - KEYS
LOW_ROWS = PAD - TOP_ROWS
V_G1, V_B1, V_QB, V_VB, V_OB, V_G2, V_B2, V_DB, V_UB = range(9)


def nt(left, right):
    return lax.dot_general(left, right, (((1,), (1,)), ((), ())), preferred_element_type=F32)


def tn(left, right):
    return lax.dot_general(left, right, (((0,), (0,)), ((), ())), preferred_element_type=F32)


def nn(left, right):
    return lax.dot_general(left, right, (((1,), (0,)), ((), ())), preferred_element_type=F32)


def aligned(value, by):
    return value if isinstance(value, int) else pl.multiple_of(value, by)


def twelfth(index):
    return lax.div(index * 43, 512)


def backward_unit(layers, index):
    whole = lax.div(index, PARTS)
    half = index - PARTS * whole
    turn = twelfth(whole)
    place = whole - UNITS * turn
    part = lax.div(place, 4)
    within = place - 4 * part
    is_down, is_late = lax.div(2 - part, 2), lax.div(part, 2)
    late = within + 3 - 4 * lax.div(within + 3, 4)
    unit = is_down * 8 + (1 - is_late) * place + is_late * late
    return layers - 1 - turn, unit, half


def stats(x):
    mean = jnp.mean(x, axis=-1, keepdims=True)
    centred = x - mean
    scale = lax.rsqrt(jnp.mean(centred * centred, axis=-1, keepdims=True) + epsilon)
    return centred * scale, scale


def fold(x):
    return jnp.sum(x.reshape(x.shape[0] // 8, 8, x.shape[1]), axis=0)


def total(x):
    return jnp.sum(x, axis=0, keepdims=True)


def step_rows(step):
    return pl.ds(aligned(step * STEP, STEP), STEP)


def encoder_kernel(
    layers,
    tokens,
    cotangent,
    n_g1,
    n_b1,
    n_qb,
    n_vb,
    n_ob,
    n_g2,
    n_b2,
    n_db,
    n_ub,
    w_qkv,
    w_out,
    w_up,
    w_down,
    encoded,
    tokens_grad,
    g_vec,
    g_qkv,
    g_out,
    g_up,
    g_down,
    wb,
    xs,
    x1,
    nr,
    pj,
    mx,
    n2,
    hd,
    gp,
    lse,
    gb,
    gm,
    br,
    acc,
    kacc,
    vacc,
    mask_top,
    mask_low,
    vsg,
    vec,
    ubs,
    gv,
    gvs,
    vr,
    vz,
    held,
    held_cot,
    held_grad,
    rc,
    r2,
    rz,
    ag_sem,
    ag_send,
    own_sem,
    core_sem,
    xy_sem,
    last_sem,
    z_sem,
    s0_send,
    rs_send,
    out_sem,
    vec_sem,
    gv_sem,
    io_sem,
):
    count = layers * UNITS
    pieces = count * PARTS
    d = lax.axis_index("dp")
    f = lax.axis_index("fsdp")
    c = lax.rem(f, 2)
    x = lax.rem(lax.div(f, 2), 2)
    y = lax.div(f, 4)
    fc = f + 1 - 2 * c
    fx = f + 2 - 4 * x
    fy = f + 4 - 8 * y
    outer = d * (3 - d) == 0
    inner = d * (3 - d) != 0
    z_in = 1 + lax.div(d, 3)
    z_out = 3 * lax.div(d, 2)
    z_pair = 3 - d
    parity = lax.rem(d, 2)
    z_near = d + 1 - 2 * parity
    in_plane = lambda who: {"fsdp": who}
    along = lambda who: {"dp": who}
    both = lambda a, b: jnp.logical_and(a, b)

    first_rows = pl.ds(0, HALF)
    second_rows = pl.ds(HALF, HALF)

    def send(source, target, sent, landed, who):
        pltpu.make_async_remote_copy(
            src_ref=source,
            dst_ref=target,
            send_sem=sent,
            recv_sem=landed,
            device_id=who,
            device_id_type=MESH,
        ).start()

    def wait_blocks(sem, blocks):
        span = wb.at[pl.ds(0, blocks), 0, 0, 0]
        pltpu.make_async_copy(span, span, sem).wait()

    def wait_half(sem):
        span = wb.at[0, 0, 0, 0, pl.ds(0, HALF)]
        pltpu.make_async_copy(span, span, sem).wait()

    def wait_piece(sem, blocks):
        span = wb.at[pl.ds(0, blocks), 0, 0, 0, :, pl.ds(0, WIDE)]
        pltpu.make_async_copy(span, span, sem).wait()

    barrier = pltpu.get_barrier_semaphore()
    peers = [lax.rem(f + hop, 8) for hop in range(1, 8)]
    for peer in peers:
        pl.semaphore_signal(barrier, inc=1, device_id=in_plane(peer), device_id_type=MESH)
    for hop in range(1, 4):
        beside = lax.rem(d + hop, 4)
        pl.semaphore_signal(barrier, inc=1, device_id=along(beside), device_id_type=MESH)

    for layer in range(layers):
        for unit in range(UNITS):
            if unit < 3:
                source = w_qkv.at[layer, :, pl.ds(unit * D, D)]
            elif unit == 3:
                source = w_out.at[layer]
            elif unit < 8:
                source = w_up.at[layer, :, pl.ds((unit - 4) * D, D)]
            else:
                source = w_down.at[layer, pl.ds((unit - 8) * SHARD, SHARD)]
            pltpu.make_async_copy(
                source,
                wb.at[layer * UNITS + unit, y, x, c],
                own_sem.at[layer * UNITS + unit],
            ).start()
    vec[...] = jnp.zeros((8 * layers, D), F32)
    for at, source in enumerate((n_g1, n_b1, n_qb, n_vb, n_ob, n_g2, n_b2, n_db)):
        shard = source[...].astype(F32)
        for layer in range(layers):
            vec[8 * layer + at : 8 * layer + at + 1, 0:SHARD] = shard[layer : layer + 1]
    shard = n_ub[...].astype(F32)
    for layer in range(layers):
        vec[8 * layer : 8 * layer + 1, 128:512] = shard[layer : layer + 1]
    vsg[f] = vec[:, 0:512].astype(BF16)
    tokens_in = pltpu.make_async_copy(tokens, held, io_sem.at[0])
    cotangent_in = pltpu.make_async_copy(cotangent, held_cot, io_sem.at[1])
    encoded_out = pltpu.make_async_copy(held, encoded, io_sem.at[2])
    tokens_out = pltpu.make_async_copy(held_grad, tokens_grad, io_sem.at[3])
    tokens_in.start()
    cotangent_in.start()
    gvs[...] = jnp.zeros((8, 8, 512), F32)
    pl.semaphore_wait(barrier, 10)

    def role(i):
        return lax.rem(i, 3) * lax.div(2 * count - 3 - i, count)

    def collects(i):
        return role(i) != 2 - parity

    def gather_tick(t):
        @pl.when(t < count)
        def _():
            own = wb.at[t, y, x, c]
            wait_blocks(own_sem.at[t], 1)

            @pl.when(collects(t))
            def _():
                first = wb.at[t, y, x, c, first_rows]
                second = wb.at[t, y, x, c, second_rows]
                send(first, first, ag_send.at[t], ag_sem.at[t, 0], in_plane(fy))
                send(second, second, ag_send.at[t], ag_sem.at[t, 1], in_plane(fx))
                send(first, first, ag_send.at[t], ag_sem.at[t, 2], in_plane(fx))
                send(second, second, ag_send.at[t], ag_sem.at[t, 2], in_plane(fy))

            send(own, own, ag_send.at[t], ag_sem.at[t, 3], in_plane(fc))

        @pl.when(both(both(t >= 2, t < count + 2), collects(t - 2)))
        def _():
            i = t - 2
            wait_half(ag_sem.at[i, 0])
            wait_half(ag_sem.at[i, 1])
            first = wb.at[i, 1 - y, x, c, first_rows]
            second = wb.at[i, y, 1 - x, c, second_rows]
            send(first, first, ag_send.at[i], ag_sem.at[i, 2], in_plane(fx))
            send(second, second, ag_send.at[i], ag_sem.at[i, 2], in_plane(fy))

        @pl.when(both(both(t >= 4, t < count + 4), collects(t - 4)))
        def _():
            i = t - 4
            wait_blocks(ag_sem.at[i, 2], 2)
            for piece in (wb.at[i, 1 - y, :, c], wb.at[i, y, 1 - x, c]):

                @pl.when(role(i) > 0)
                def _(piece=piece):
                    send(piece, piece, ag_send.at[i], ag_sem.at[i, 0], along(z_near))

                send(piece, piece, ag_send.at[i], ag_sem.at[i, 3], in_plane(fc))

        @pl.when(both(both(t >= LAG_PASS, t < count + LAG_PASS), role(t - LAG_PASS) == 2 - parity))
        def _():
            i = t - LAG_PASS
            wait_blocks(ag_sem.at[i, 0], 3)
            for piece in (wb.at[i, 1 - y, :, c], wb.at[i, y, 1 - x, c]):
                send(piece, piece, ag_send.at[i], ag_sem.at[i, 3], in_plane(fc))

        @pl.when(both(t >= LAG_WHOLE, t < count + LAG_WHOLE))
        def _():
            wait_blocks(ag_sem.at[t - LAG_WHOLE, 3], 4)

    for peer in peers:
        send(vsg.at[f], vsg.at[f], vec_sem.at[0], vec_sem.at[1], in_plane(peer))

    @pl.loop(0, EARLY)
    def _(t):
        gather_tick(t)

    def crop_of(shape, dim, start):
        at = lax.broadcasted_iota(jnp.int32, shape, dim) + start
        which = jnp.zeros(shape, jnp.int32)
        for edge in range(L_DEV + 1):
            which = which + (at >= GLEN + edge * LLEN).astype(jnp.int32)
        return which

    for mask, rows, row_at, key_at in (
        (mask_top, TOP_ROWS, 0, 0),
        (mask_low, LOW_ROWS, TOP_ROWS, LOW_KEY),
    ):
        same = crop_of((rows, KEYS), 0, row_at) == crop_of((rows, KEYS), 1, key_at)
        mask[...] = jnp.where(same, 0.0, -1e30).astype(F32)

    xs[0, PAD - 8 :, :] = jnp.zeros((8, D), F32)
    tokens_in.wait()
    xs[0, 0:ROWS, :] = held[...].astype(F32)

    seven = vsg.at[pl.ds(0, 7)]
    pltpu.make_async_copy(seven, seven, vec_sem.at[1]).wait()
    spread = jnp.zeros((8 * layers, D), F32)
    for owner in range(8):
        at_row = lax.broadcasted_iota(jnp.int32, (128, D), 0)
        at_col = lax.broadcasted_iota(jnp.int32, (128, D), 1)
        hit = jnp.logical_and(at_col == at_row + owner * SHARD, at_row < SHARD)
        spread = spread + nn(vsg[owner, :, 0:128], jnp.where(hit, 1.0, 0.0).astype(BF16))
        wide = vsg[owner, :, 128:512].astype(F32)
        for layer in range(layers):
            row, lane = 8 * layer, owner * 4 * SHARD
            ubs[layer : layer + 1, lane : lane + 4 * SHARD] = wide[row : row + 1]
    vec[...] = spread

    @pl.loop(EARLY, LAG_WHOLE)
    def _(t):
        gather_tick(t)

    def vector(layer, which):
        return vec[pl.ds(layer * 8 + which, 1), :]

    lane = lax.broadcasted_iota(jnp.int32, (1, 128), 1)
    left_lane = lane < HEAD_DIM
    score_scale = HEAD_DIM ** (-0.5)
    head_scaled = [
        jnp.where(left_lane, score_scale, 0.0).astype(BF16),
        jnp.where(left_lane, 0.0, score_scale).astype(BF16),
    ]
    head_plain = [
        jnp.where(left_lane, 1.0, 0.0).astype(BF16),
        jnp.where(left_lane, 0.0, 1.0).astype(BF16),
    ]
    groups = (
        (0, TOP_ROWS, 0, mask_top),
        (TOP_ROWS, LOW_ROWS, LOW_KEY, mask_low),
    )

    def weight(layer, unit):
        return wb[layer * UNITS + unit].reshape(D, D)

    def down_places(part):
        return [(unit, lax.div(part, 2), lax.rem(part, 2), core) for core in range(2) for unit in range(4)]

    def down_weight(layer, part):
        blocks = [wb[layer * UNITS + 8 + u, yy, xx, cc] for u, yy, xx, cc in down_places(part)]
        return jnp.concatenate(blocks, axis=0)

    def put_down(first, units, part, grad):
        for at, (u, yy, xx, cc) in enumerate(down_places(part)):
            if u < units:
                wb[first + u, yy, xx, cc] = grad[at * SHARD : (at + 1) * SHARD]

    def piece_at(i):
        layer, unit, half = backward_unit(layers, i)
        early = lax.div(pieces + EARLY_UNITS * PARTS - 1 - i, pieces)
        ahead = layers * UNITS + lax.div(i, PARTS)
        at = early * ahead + (1 - early) * (layer * UNITS + unit)
        return at, pl.ds(aligned(half * WIDE, 128), WIDE)

    def during(t, lag):
        return both(t >= lag, t < pieces + lag)

    def ring(i):
        return lax.rem(i, RING)

    def long_ring(i):
        return lax.rem(i, 2 * RING)

    def reduce_tick(t):
        @pl.when(t < pieces)
        def _():
            n, cols = piece_at(t)
            send(
                wb.at[n, :, :, 1 - c, :, cols],
                rc.at[lax.rem(t, CORE_SLOTS)],
                s0_send.at[ring(t)],
                core_sem.at[ring(t)],
                in_plane(fc),
            )

        @pl.when(during(t, LAG_XY))
        def _():
            i = t - LAG_XY
            n, cols = piece_at(i)
            slot = lax.rem(i, SLOTS)
            wait_piece(xy_sem.at[ring(i)], 2)
            along_x = wb.at[n, :, x, c, first_rows, cols]
            along_y = wb.at[n, y, :, c, second_rows, cols]
            along_x[...] = along_x[...] + r2[slot, 0]
            along_y[...] = along_y[...] + r2[slot, 1]
            send(
                wb.at[n, 1 - y, x, c, first_rows, cols],
                wb.at[n, 1 - y, x, 1 - c, first_rows, cols],
                rs_send.at[long_ring(i)],
                last_sem.at[ring(i)],
                in_plane(fy),
            )
            send(
                wb.at[n, y, 1 - x, c, second_rows, cols],
                wb.at[n, y, 1 - x, 1 - c, second_rows, cols],
                rs_send.at[long_ring(i)],
                last_sem.at[ring(i)],
                in_plane(fx),
            )

        @pl.when(during(t, 1))
        def _():
            i = t - 1
            n, cols = piece_at(i)
            slot = lax.rem(i, SLOTS)
            wait_piece(core_sem.at[ring(i)], 4)
            wait_piece(s0_send.at[ring(i)], 4)
            mine = wb.at[n, :, :, c, :, cols]
            mine[...] = mine[...] + rc[lax.rem(i, CORE_SLOTS)]
            send(
                wb.at[n, :, 1 - x, c, first_rows, cols],
                r2.at[slot, 0],
                rs_send.at[long_ring(i)],
                xy_sem.at[ring(i)],
                in_plane(fx),
            )
            send(
                wb.at[n, 1 - y, :, c, second_rows, cols],
                r2.at[slot, 1],
                rs_send.at[long_ring(i)],
                xy_sem.at[ring(i)],
                in_plane(fy),
            )

        @pl.when(during(t, LAG_OUT))
        def _():
            i = t - LAG_OUT
            n, cols = piece_at(i)
            layer, unit, half = backward_unit(layers, i)

            @pl.when(outer)
            def _():
                wait_piece(z_sem.at[ring(i), 2], 1)

            done = wb.at[n, y, x, 1 - c, :, cols]

            @pl.when(outer)
            def _():
                wait_piece(rs_send.at[long_ring(i)], 4)

            @pl.when(inner)
            def _():
                wait_piece(rs_send.at[long_ring(i)], 5)

            @pl.when(i >= RING)
            def _():
                wait_piece(out_sem.at[ring(i)], 1)

            def emit(target):
                pltpu.make_async_copy(done, target, out_sem.at[ring(i)]).start()

            def wide_at(first):
                return pl.ds(aligned((unit - first) * D + half * WIDE, 128), WIDE)

            @pl.when(unit < 3)
            def _():
                emit(g_qkv.at[layer, :, wide_at(0)])

            @pl.when(unit == 3)
            def _():
                emit(g_out.at[layer, :, cols])

            @pl.when(both(unit >= 4, unit < 8))
            def _():
                emit(g_up.at[layer, :, wide_at(4)])

            @pl.when(unit >= 8)
            def _():
                rows = pl.ds(aligned((unit - 8) * SHARD, 16), SHARD)
                emit(g_down.at[layer, rows, cols])

        @pl.when(during(t, LAG_LAST))
        def _():
            i = t - LAG_LAST
            n, cols = piece_at(i)
            wait_piece(last_sem.at[ring(i)], 1)
            own = wb.at[n, y, x, c, :, cols]
            own[...] = own[...] + wb[n, y, x, 1 - c, :, cols]

            @pl.when(outer)
            def _():
                to = rz.at[lax.rem(i, SLOTS), 0]
                send(own, to, rs_send.at[long_ring(i)], z_sem.at[ring(i), 0], along(z_in))

        @pl.when(both(inner, during(t, LAG_Z1)))
        def _():
            i = t - LAG_Z1
            n, cols = piece_at(i)
            slot = lax.rem(i, SLOTS)
            wait_piece(z_sem.at[ring(i), 0], 1)
            own = wb.at[n, y, x, c, :, cols]
            own[...] = own[...] + rz[slot, 0]
            send(own, rz.at[slot, 1], rs_send.at[long_ring(i)], z_sem.at[ring(i), 1], along(z_pair))

        @pl.when(both(inner, during(t, LAG_Z2)))
        def _():
            i = t - LAG_Z2
            n, cols = piece_at(i)
            wait_piece(z_sem.at[ring(i), 1], 1)
            done = wb.at[n, y, x, 1 - c, :, cols]
            done[...] = wb[n, y, x, c, :, cols] + rz[lax.rem(i, SLOTS), 1]
            send(done, done, rs_send.at[long_ring(i)], z_sem.at[ring(i), 2], along(z_out))

    @pl.loop(0, layers)
    def _(layer):
        base = layer * UNITS + LAG_WHOLE

        @pl.loop(0, PAD // STEP, unroll=UNROLL)
        def _(step):
            rows = step_rows(step)
            normed, _unused = stats(xs[layer, rows, :])
            nr[layer, rows, :] = (normed * vector(layer, V_G1) + vector(layer, V_B1)).astype(BF16)

        @pl.loop(0, 3)
        def _(part):
            gather_tick(base + part)
            is_q, is_v = lax.div(2 - part, 2), lax.div(part, 2)
            bias = is_q.astype(F32) * vector(layer, V_QB) + is_v.astype(F32) * vector(layer, V_VB)
            acc[...] = nn(nr[layer], weight(layer, part))

            @pl.loop(0, PAD // STEP, unroll=UNROLL)
            def _(step):
                rows = step_rows(step)
                pj[layer, part, rows, :] = (acc[rows, :] + bias).astype(BF16)

        @pl.loop(0, HEADS // 2)
        def _(pair):
            @pl.when(pair == 3)
            def _():
                gather_tick(base + 3)

            lanes = pl.ds(aligned(pair * 128, 128), 128)
            for row_at, rows, key_at, mask in groups:
                here = pl.ds(row_at, rows)
                keys = pj[layer, 1, pl.ds(key_at, KEYS), lanes]
                values = pj[layer, 2, pl.ds(key_at, KEYS), lanes]
                queries = pj[layer, 0, here, lanes]
                results = []
                for side in range(2):
                    scores = nt(queries * head_scaled[side], keys) + mask[...]
                    peak = jnp.max(scores, axis=-1, keepdims=True)
                    raised = jnp.exp(scores - peak)
                    exp_total = jnp.sum(raised, axis=-1, keepdims=True)
                    probs = (raised * (1.0 / exp_total)).astype(BF16)
                    results.append(nn(probs, values))
                    log_total = peak + jnp.log(exp_total)
                    lse[layer, here, :] = jnp.where(
                        lane == pair * 2 + side, log_total, lse[layer, here, :]
                    )
                mx[layer, here, lanes] = jnp.where(left_lane, results[0], results[1]).astype(BF16)

        acc[...] = nn(mx[layer], weight(layer, 3))

        @pl.loop(0, PAD // STEP, unroll=UNROLL)
        def _(step):
            rows = step_rows(step)
            now = xs[layer, rows, :] + acc[rows, :] + vector(layer, V_OB)
            x1[layer, rows, :] = now
            normed, _unused = stats(now)
            n2[layer, rows, :] = (normed * vector(layer, V_G2) + vector(layer, V_B2)).astype(BF16)

        @pl.loop(0, 4)
        def _(part):
            gather_tick(base + 4 + part)
            bias = ubs[pl.ds(layer, 1), pl.ds(aligned(part * D, 128), D)]
            acc[...] = nn(n2[layer], weight(layer, 4 + part))

            @pl.loop(0, PAD // STEP, unroll=UNROLL)
            def _(step):
                rows = step_rows(step)
                pre = acc[rows, :] + bias
                cdf = 0.5 + 0.5 * lax.erf(pre * (0.5**0.5))
                bell = jnp.exp(-0.5 * pre * pre) * 0.3989422804014327
                hd[layer, part, rows, :] = (pre * cdf).astype(BF16)
                gp[layer, part, rows, :] = (cdf + pre * bell).astype(BF16)

        @pl.when(layer == layers - 1)
        def _():
            acc[PAD - 8 :, :] = jnp.zeros((8, D), F32)
            cotangent_in.wait()
            acc[0:ROWS, :] = held_cot[...].astype(F32)
            br[...] = acc[...].astype(BF16)

            @pl.loop(0, 4)
            def _(part):
                grad = tn(hd[layer, part], br[...]).astype(BF16)
                put_down(layers * UNITS, EARLY_UNITS, part, grad)

        @pl.loop(0, 4)
        def _(part):
            gather_tick(base + 8 + part)

        @pl.when(layer == layers - 1)
        def _():
            @pl.loop(0, 2)
            def _(t):
                reduce_tick(t)

        acc[...] = x1[layer] + vector(layer, V_DB)

        @pl.loop(0, 4)
        def _(part):
            acc[...] += nn(hd[layer, part], down_weight(layer, part))

        xs[layer + 1] = acc[...]

    reduce_tick(2)
    held[...] = xs[layers, 0:ROWS, :].astype(BF16)
    encoded_out.start()

    @pl.loop(0, count)
    def _(i):
        @pl.when(role(i) == 0)
        def _():
            wait_blocks(ag_send.at[i], 7)

        @pl.when(role(i) == 1 + parity)
        def _():
            wait_blocks(ag_send.at[i], 10)

        @pl.when(role(i) == 2 - parity)
        def _():
            wait_blocks(ag_send.at[i], 4)

    pltpu.make_async_copy(seven, seven, vec_sem.at[0]).wait()

    def vector_step(layer, step):
        def wait_vec(at, copies):
            span = gvs.at[pl.ds(0, copies)]
            pltpu.make_async_copy(span, span, gv_sem.at[layer, at]).wait()

        @pl.when(step == 0)
        def _():
            for owner in range(8):
                gvs[owner, :, 0:SHARD] = gv[layer, 0:8, owner * SHARD : (owner + 1) * SHARD]
                row, lane = 8 + owner // 2, (owner % 2) * 4 * SHARD
                gvs[owner, 0:1, 128:512] = gv[layer, row : row + 1, lane : lane + 4 * SHARD]
            vr[layer, f] = gvs[f]
            for peer in peers:
                send(
                    gvs.at[peer],
                    vr.at[layer, f],
                    gv_sem.at[layer, 0],
                    gv_sem.at[layer, 1],
                    in_plane(peer),
                )

        @pl.when(step == 1)
        def _():
            wait_vec(0, 7)
            wait_vec(1, 7)
            in_sum = vr[layer, 0]
            for source in range(1, 8):
                in_sum = in_sum + vr[layer, source]
            vz[layer, d] = in_sum
            for hop in range(3):
                send(
                    vz.at[layer, d],
                    vz.at[layer, d],
                    gv_sem.at[layer, 2],
                    gv_sem.at[layer, 3],
                    along(lax.rem(d + 1 + hop, 4)),
                )

        @pl.when(step == 2)
        def _():
            wait_vec(2, 3)
            wait_vec(3, 3)
            g_vec[layer] = (vz[layer, 0] + vz[layer, 1]) + (vz[layer, 2] + vz[layer, 3])

    up = xs.at[layers]
    up[PAD - 8 :, :] = jnp.zeros((8, D), F32)
    up[0:ROWS, :] = held_cot[...].astype(F32)
    none = jnp.zeros((8, D), F32)

    def put_vector(layer, which, value):
        gv[layer, pl.ds(which, 1), :] = total(value)

    def weight_grad(unit, left, right):
        grad = tn(left[...], right[...]).astype(BF16)
        wb[unit] = grad.reshape(2, 2, 2, SHARD, D)

    @pl.loop(0, layers)
    def _(turn):
        layer = layers - 1 - turn
        base = 4 + turn * (UNITS * PARTS - 4)

        def branch_two(step, carry):
            rows = step_rows(step)
            rounded = up[rows, :].astype(BF16)
            br[rows, :] = rounded
            return carry + fold(rounded.astype(F32))

        put_vector(layer, V_DB, lax.fori_loop(0, PAD // STEP, branch_two, none, unroll=UNROLL))

        @pl.loop(0, 4)
        def _(part):
            @pl.when(both(part < 3, 2 * turn + part >= 2))
            def _():
                reduce_tick(base - 3 + part)

            acc[...] = nt(br[...], down_weight(layer, part))

            def through_gelu(step, carry):
                rows = step_rows(step)
                value = (acc[rows, :] * gp[layer, part, rows, :].astype(F32)).astype(BF16)
                gb[part, rows, :] = value
                return carry + fold(value.astype(F32))

            put_vector(layer, V_UB + part, lax.fori_loop(0, PAD // STEP, through_gelu, none, unroll=UNROLL))
            grad = tn(hd[layer, part], br[...]).astype(BF16)
            put_down(layer * UNITS + 8, 4, part, grad)

        acc[...] = jnp.zeros((PAD, D), F32)

        @pl.loop(0, 4)
        def _(part):
            @pl.when(both(turn > 0, part == 0))
            def _():
                vector_step(layer + 1, 0)

            acc[...] += nt(gb[part], weight(layer, 4 + part))
            weight_grad(layer * UNITS + 4 + part, n2.at[layer], gb.at[part])

            @pl.loop(0, 2)
            def _(again):
                reduce_tick(base + 2 * part + again)

        def norm_back(source, gain_at, shift_at):
            def body(step, carry):
                gain_sum, shift_sum = carry
                rows = step_rows(step)
                normed, scale = stats(source[layer, rows, :])
                grad = acc[rows, :]
                t = grad * vector(layer, gain_at)
                inner_mean = jnp.mean(t * normed, axis=-1, keepdims=True)
                back = scale * (t - jnp.mean(t, axis=-1, keepdims=True) - normed * inner_mean)
                up[rows, :] = up[rows, :] + back
                return gain_sum + fold(grad * normed), shift_sum + fold(grad)

            gain_sum, shift_sum = lax.fori_loop(0, PAD // STEP, body, (none, none), unroll=UNROLL)
            put_vector(layer, gain_at, gain_sum)
            put_vector(layer, shift_at, shift_sum)

        norm_back(x1, V_G2, V_B2)

        put_vector(layer, V_OB, lax.fori_loop(0, PAD // STEP, branch_two, none, unroll=UNROLL))
        gm[...] = nt(br[...], weight(layer, 3)).astype(BF16)
        weight_grad(layer * UNITS + 3, mx.at[layer], br)

        @pl.loop(0, 2)
        def _(again):
            reduce_tick(base + 8 + again)

        @pl.loop(0, HEADS // 2)
        def _(pair):
            @pl.when(lax.rem(pair, 3) < 2)
            def _():
                reduce_tick(base + 10 + pair - lax.div(pair, 3))

            @pl.when(both(turn > 0, lax.rem(pair, 5) == 0))
            def _():
                vector_step(layer + 1, 1 + lax.div(pair, 5))

            lanes = pl.ds(aligned(pair * 128, 128), 128)
            kacc[...] = jnp.zeros((PAD, 128), F32)
            vacc[...] = jnp.zeros((PAD, 128), F32)
            for row_at, rows, key_at, mask in groups:
                here = pl.ds(row_at, rows)
                there = pl.ds(key_at, KEYS)
                keys = pj[layer, 1, there, lanes]
                values = pj[layer, 2, there, lanes]
                queries = pj[layer, 0, here, lanes]
                grads = gm[here, lanes]
                q_parts, k_parts, v_parts = [], [], []
                for side in range(2):
                    log_total = jnp.sum(
                        jnp.where(lane == pair * 2 + side, lse[layer, here, :], 0.0),
                        axis=-1,
                        keepdims=True,
                    )
                    scaled = queries * head_scaled[side]
                    probs = jnp.exp(nt(scaled, keys) + mask[...] - log_total)
                    grad_probs = nt(grads * head_plain[side], values)
                    row_inner = jnp.sum(grad_probs * probs, axis=-1, keepdims=True)
                    grad_scores = (probs * (grad_probs - row_inner)).astype(BF16)
                    v_parts.append(tn(probs.astype(BF16), grads))
                    k_parts.append(tn(grad_scores, queries))
                    q_parts.append(nn(grad_scores, keys))
                grad_queries = jnp.where(left_lane, q_parts[0], q_parts[1]) * score_scale
                gb[0, here, lanes] = grad_queries.astype(BF16)
                kacc[there, :] += jnp.where(left_lane, k_parts[0], k_parts[1]) * score_scale
                vacc[there, :] += jnp.where(left_lane, v_parts[0], v_parts[1])
            gb[1, :, lanes] = kacc[...].astype(BF16)
            gb[2, :, lanes] = vacc[...].astype(BF16)

        for which, part in ((V_QB, 0), (V_VB, 2)):

            def column_sum(step, carry, part=part):
                return carry + fold(gb[part, step_rows(step), :].astype(F32))

            put_vector(layer, which, lax.fori_loop(0, PAD // STEP, column_sum, none, unroll=UNROLL))

        acc[...] = jnp.zeros((PAD, D), F32)

        @pl.loop(0, 3)
        def _(part):
            acc[...] += nt(gb[part], weight(layer, part))
            weight_grad(layer * UNITS + part, nr.at[layer], gb.at[part])

            reduce_tick(base + 14 + part)

        norm_back(xs, V_G1, V_B1)

    held_grad[...] = up[0:ROWS, :]
    tokens_out.start()
    encoded_out.wait()

    @pl.loop(pieces - 7, pieces + LAG_OUT)
    def _(t):
        step = t - (pieces - 7)

        @pl.when(both(lax.rem(step, VEC_EVERY) == 0, step < 3 * VEC_EVERY))
        def _():
            vector_step(0, lax.div(step, VEC_EVERY))

        reduce_tick(t)

    for at in range(RING):
        wait_piece(out_sem.at[at], 1)

    tokens_out.wait()


def closing_kernel(layers, *refs):
    encoded_in, tokens_in, vec_in = refs[:3]
    grads_in = refs[3:7]
    encoded_out, tokens_out = refs[7:9]
    small_out = refs[9:18]
    grads_out = refs[18:22]
    vec = refs[22]
    narrow = refs[23:27]
    wide = refs[27:31]
    held_encoded, held_tokens, few_sem, in_sem, out_sem = refs[31:]
    copies = [
        pltpu.make_async_copy(vec_in, vec, few_sem.at[0]),
        pltpu.make_async_copy(encoded_in, held_encoded, few_sem.at[1]),
        pltpu.make_async_copy(tokens_in, held_tokens, few_sem.at[2]),
    ]
    reads, writes = [], []
    for layer in range(layers):
        for at in range(4):
            reads.append(
                pltpu.make_async_copy(
                    grads_in[at].at[layer], narrow[at].at[layer], in_sem.at[at, layer]
                )
            )
            writes.append(
                pltpu.make_async_copy(
                    wide[at].at[layer], grads_out[at].at[layer], out_sem.at[at, layer]
                )
            )
    for copy in reads + copies:
        copy.start()
    for layer in range(layers):
        for at in range(4):
            reads[4 * layer + at].wait()
            wide[at][layer] = narrow[at][layer].astype(F32)
            writes[4 * layer + at].start()
    for copy in copies:
        copy.wait()
    writes.append(pltpu.make_async_copy(held_encoded, encoded_out, few_sem.at[1]))
    writes.append(pltpu.make_async_copy(held_tokens, tokens_out, few_sem.at[2]))
    writes[-2].start()
    writes[-1].start()
    for layer in range(layers):
        mine = vec[layer]
        for which in range(8):
            small_out[which][layer : layer + 1, :] = mine[which : which + 1, 0:SHARD]
        small_out[8][layer : layer + 1, :] = mine[0:1, 128:512]
    for copy in writes:
        copy.wait()


def kernel_local(
    tokens,
    cotangent,
    norm1_gain,
    norm1_bias,
    qkv_weight,
    query_bias,
    value_bias,
    out_weight,
    out_bias,
    norm2_gain,
    norm2_bias,
    up_weight,
    up_bias,
    down_weight,
    down_bias,
):
    layers = qkv_weight.shape[0]
    count = layers * UNITS
    pieces = count * PARTS
    hbm = pl.BlockSpec(memory_space=pltpu.MemorySpace.HBM)
    plain = pl.BlockSpec()
    dma = pltpu.SemaphoreType.DMA
    results = pl.pallas_call(
        functools.partial(encoder_kernel, layers),
        out_shape=(
            jax.ShapeDtypeStruct((ROWS, D), BF16),
            jax.ShapeDtypeStruct((ROWS, D), F32),
            jax.ShapeDtypeStruct((layers, 8, 512), F32),
            jax.ShapeDtypeStruct((layers, SHARD, 3 * D), BF16),
            jax.ShapeDtypeStruct((layers, SHARD, D), BF16),
            jax.ShapeDtypeStruct((layers, SHARD, FF), BF16),
            jax.ShapeDtypeStruct((layers, 4 * SHARD, D), BF16),
        ),
        in_specs=[hbm] * 2 + [plain] * 9 + [hbm] * 4,
        out_specs=(hbm, hbm, plain, hbm, hbm, hbm, hbm),
        scratch_shapes=[
            pltpu.VMEM((count + EARLY_UNITS, 2, 2, 2, SHARD, D), BF16),
            pltpu.VMEM((layers + 1, PAD, D), F32),
            pltpu.VMEM((layers, PAD, D), F32),
            pltpu.VMEM((layers, PAD, D), BF16),
            pltpu.VMEM((layers, 3, PAD, D), BF16),
            pltpu.VMEM((layers, PAD, D), BF16),
            pltpu.VMEM((layers, PAD, D), BF16),
            pltpu.VMEM((layers, 4, PAD, D), BF16),
            pltpu.VMEM((layers, 4, PAD, D), BF16),
            pltpu.VMEM((layers, PAD, 128), F32),
            pltpu.VMEM((4, PAD, D), BF16),
            pltpu.VMEM((PAD, D), BF16),
            pltpu.VMEM((PAD, D), BF16),
            pltpu.VMEM((PAD, D), F32),
            pltpu.VMEM((PAD, 128), F32),
            pltpu.VMEM((PAD, 128), F32),
            pltpu.VMEM((TOP_ROWS, KEYS), F32),
            pltpu.VMEM((LOW_ROWS, KEYS), F32),
            pltpu.VMEM((8, 8 * layers, 512), BF16),
            pltpu.VMEM((8 * layers, D), F32),
            pltpu.VMEM((layers, FF), F32),
            pltpu.VMEM((layers, 16, D), F32),
            pltpu.VMEM((8, 8, 512), F32),
            pltpu.VMEM((layers, 8, 8, 512), F32),
            pltpu.VMEM((layers, 4, 8, 512), F32),
            pltpu.VMEM((ROWS, D), BF16),
            pltpu.VMEM((ROWS, D), BF16),
            pltpu.VMEM((ROWS, D), F32),
            pltpu.VMEM((CORE_SLOTS, 2, 2, SHARD, WIDE), BF16),
            pltpu.VMEM((SLOTS, 2, 2, HALF, WIDE), BF16),
            pltpu.VMEM((SLOTS, 2, SHARD, WIDE), BF16),
            dma((count, 4)),
            dma((count,)),
            dma((count,)),
            dma((RING,)),
            dma((RING,)),
            dma((RING,)),
            dma((RING, 3)),
            dma((RING,)),
            dma((2 * RING,)),
            dma((RING,)),
            dma((2,)),
            dma((layers, 4)),
            dma((4,)),
        ],
        compiler_params=pltpu.CompilerParams(
            collective_id=0, has_side_effects=True, vmem_limit_bytes=VMEM_BYTES
        ),
    )(
        tokens,
        cotangent,
        norm1_gain,
        norm1_bias,
        query_bias,
        value_bias,
        out_bias,
        norm2_gain,
        norm2_bias,
        down_bias,
        up_bias,
        qkv_weight,
        out_weight,
        up_weight,
        down_weight,
    )
    shapes = [(layers, SHARD)] * 8 + [(layers, 4 * SHARD)]
    shapes += [(layers, SHARD, 3 * D), (layers, SHARD, D), (layers, SHARD, FF)]
    shapes += [(layers, 4 * SHARD, D)]
    closing = pl.pallas_call(
        functools.partial(closing_kernel, layers),
        out_shape=[jax.ShapeDtypeStruct((ROWS, D), BF16), jax.ShapeDtypeStruct((ROWS, D), F32)]
        + [jax.ShapeDtypeStruct(shape, F32) for shape in shapes],
        in_specs=[hbm] * 7,
        out_specs=[hbm] * 2 + [plain] * 9 + [hbm] * 4,
        scratch_shapes=[pltpu.VMEM((layers, 8, 512), F32)]
        + [pltpu.VMEM(shape, BF16) for shape in shapes[9:]]
        + [pltpu.VMEM(shape, F32) for shape in shapes[9:]]
        + [pltpu.VMEM((ROWS, D), BF16), pltpu.VMEM((ROWS, D), F32)]
        + [dma((3,)), dma((4, layers)), dma((4, layers))],
        compiler_params=pltpu.CompilerParams(vmem_limit_bytes=VMEM_BYTES),
    )(*results)
    by = dict(zip(("encoded", "tokens_grad"), closing[:2]))
    small = closing[2:11]
    g_qkv, g_out, g_up, g_down = closing[11:]
    return (
        by["encoded"],
        by["tokens_grad"],
        small[V_G1],
        small[V_B1],
        g_qkv,
        small[V_QB],
        small[V_VB],
        g_out,
        small[V_OB],
        small[V_G2],
        small[V_B2],
        g_up,
        small[V_UB],
        g_down,
        small[V_DB],
    )


def solution(mesh):
    in_specs = (
        P(("dp", "fsdp"), None),
        P(("dp", "fsdp"), None),
        P(None, "fsdp"),
        P(None, "fsdp"),
        P(None, "fsdp", None),
        P(None, "fsdp"),
        P(None, "fsdp"),
        P(None, "fsdp", None),
        P(None, "fsdp"),
        P(None, "fsdp"),
        P(None, "fsdp"),
        P(None, "fsdp", None),
        P(None, "fsdp"),
        P(None, "fsdp", None),
        P(None, "fsdp"),
    )
    out_specs = (
        P(("dp", "fsdp"), None),
        P(("dp", "fsdp"), None),
        P(None, "fsdp"),
        P(None, "fsdp"),
        P(None, "fsdp", None),
        P(None, "fsdp"),
        P(None, "fsdp"),
        P(None, "fsdp", None),
        P(None, "fsdp"),
        P(None, "fsdp"),
        P(None, "fsdp"),
        P(None, "fsdp", None),
        P(None, "fsdp"),
        P(None, "fsdp", None),
        P(None, "fsdp"),
    )
    fits = mesh.shape["dp"] == 4 and mesh.shape["fsdp"] == 8
    body = kernel_local if fits else local
    return jax.shard_map(body, mesh=mesh, in_specs=in_specs, out_specs=out_specs, check_vma=False)
```

```python
import functools

import jax
import jax.numpy as jnp
from jax import lax
from jax.experimental import pallas as pl
from jax.experimental.pallas import tpu as pltpu
from jax.sharding import PartitionSpec as P

D = 768
HEADS = 12
HEAD_DIM = 64
GLEN = 197
LLEN = 37
G_DEV = 1
L_DEV = 4


epsilon = 1e-06


def norm_rows(values_in, gain, shift):
    row_mean = jnp.mean(values_in, axis=-1, keepdims=True)
    centred = values_in - row_mean
    spread = jnp.mean(centred * centred, axis=-1, keepdims=True)
    return centred * lax.rsqrt(spread + epsilon) * gain + shift


def contract_rows(left, right):
    return lax.dot_general(
        left, right, (((0,), (0,)), ((), ())), preferred_element_type=jnp.float32
    )


def contract_cols(left, right):
    return lax.dot_general(
        left, right, (((1,), (1,)), ((), ())), preferred_element_type=jnp.float32
    )


def gather_forward(pieces):
    return (
        lax.all_gather(pieces[0], "fsdp", axis=0, tiled=True),
        lax.all_gather(pieces[1], "fsdp", axis=0, tiled=True),
        lax.all_gather(pieces[2], "fsdp", axis=0, tiled=True),
        lax.all_gather(pieces[3], "fsdp", axis=0, tiled=True),
        lax.all_gather(pieces[4], "fsdp", axis=0, tiled=True),
        lax.all_gather(pieces[5], "fsdp", axis=0, tiled=True),
        lax.all_gather(pieces[6], "fsdp", axis=0, tiled=True),
        lax.all_gather(pieces[7], "fsdp", axis=0, tiled=True),
        lax.all_gather(pieces[8], "fsdp", axis=0, tiled=True),
        lax.all_gather(pieces[9], "fsdp", axis=0, tiled=True),
        lax.all_gather(pieces[10], "fsdp", axis=0, tiled=True),
        lax.all_gather(pieces[11], "fsdp", axis=0, tiled=True),
        lax.all_gather(pieces[12], "fsdp", axis=0, tiled=True),
    )


def reduce_grads(grads):
    shares = (
        lax.psum_scatter(grads[0], "fsdp", scatter_dimension=0, tiled=True),
        lax.psum_scatter(grads[1], "fsdp", scatter_dimension=0, tiled=True),
        lax.psum_scatter(grads[2].astype(jnp.bfloat16), "fsdp", scatter_dimension=0, tiled=True),
        lax.psum_scatter(grads[3], "fsdp", scatter_dimension=0, tiled=True),
        lax.psum_scatter(grads[4], "fsdp", scatter_dimension=0, tiled=True),
        lax.psum_scatter(grads[5].astype(jnp.bfloat16), "fsdp", scatter_dimension=0, tiled=True),
        lax.psum_scatter(grads[6], "fsdp", scatter_dimension=0, tiled=True),
        lax.psum_scatter(grads[7], "fsdp", scatter_dimension=0, tiled=True),
        lax.psum_scatter(grads[8], "fsdp", scatter_dimension=0, tiled=True),
        lax.psum_scatter(grads[9].astype(jnp.bfloat16), "fsdp", scatter_dimension=0, tiled=True),
        lax.psum_scatter(grads[10], "fsdp", scatter_dimension=0, tiled=True),
        lax.psum_scatter(grads[11].astype(jnp.bfloat16), "fsdp", scatter_dimension=0, tiled=True),
        lax.psum_scatter(grads[12], "fsdp", scatter_dimension=0, tiled=True),
    )
    column_parts = (
        lax.psum_scatter(
            shares[2], "dp", scatter_dimension=1, tiled=True
        ).astype(jnp.float32),
        lax.psum_scatter(
            shares[5], "dp", scatter_dimension=1, tiled=True
        ).astype(jnp.float32),
        lax.psum_scatter(
            shares[9], "dp", scatter_dimension=1, tiled=True
        ).astype(jnp.float32),
        lax.psum_scatter(
            shares[11], "dp", scatter_dimension=1, tiled=True
        ).astype(jnp.float32),
    )
    matrices = (
        lax.all_gather(column_parts[0].astype(jnp.bfloat16), "dp", axis=1, tiled=True).astype(
            jnp.float32
        ),
        lax.all_gather(column_parts[1].astype(jnp.bfloat16), "dp", axis=1, tiled=True).astype(
            jnp.float32
        ),
        lax.all_gather(column_parts[2].astype(jnp.bfloat16), "dp", axis=1, tiled=True).astype(
            jnp.float32
        ),
        lax.all_gather(column_parts[3].astype(jnp.bfloat16), "dp", axis=1, tiled=True).astype(
            jnp.float32
        ),
    )
    vectors = lax.psum(
        (
            shares[0],
            shares[1],
            shares[3],
            shares[4],
            shares[6],
            shares[7],
            shares[8],
            shares[10],
            shares[12],
        ),
        "dp",
    )
    return (
        vectors[0],
        vectors[1],
        matrices[0],
        vectors[2],
        vectors[3],
        matrices[1],
        vectors[4],
        vectors[5],
        vectors[6],
        matrices[2],
        vectors[7],
        matrices[3],
        vectors[8],
    )


def attend_crops(queries, keys_in, values_in, crop_count, crop_length):
    shape_four = (crop_count, crop_length, HEADS, HEAD_DIM)
    scores = jnp.einsum(
        "clhe,cmhe->chlm",
        queries.reshape(shape_four),
        keys_in.reshape(shape_four),
        preferred_element_type=jnp.float32,
    ) * HEAD_DIM ** (-0.5)
    peak_score = jnp.max(scores, axis=-1, keepdims=True)
    raised = jnp.exp(scores - peak_score)
    exp_total = jnp.sum(raised, axis=-1, keepdims=True)
    attn_probs = (raised / exp_total).astype(jnp.bfloat16)
    log_total = peak_score + jnp.log(exp_total)
    result = jnp.einsum(
        "chlm,cmhe->clhe",
        attn_probs,
        values_in.reshape(shape_four),
        preferred_element_type=jnp.float32,
    )
    return (result.reshape(crop_count * crop_length, D), log_total)


def attend_back(queries, keys_in, values_in, log_total, grad_mixed, crop_count, crop_length):
    shape_four = (crop_count, crop_length, HEADS, HEAD_DIM)
    score_scale = HEAD_DIM ** (-0.5)
    query_four = queries.reshape(shape_four)
    key_four = keys_in.reshape(shape_four)
    value_four = values_in.reshape(shape_four)
    grad_four = grad_mixed.reshape(shape_four)
    scores = (
        jnp.einsum("clhe,cmhe->chlm", query_four, key_four, preferred_element_type=jnp.float32)
        * score_scale
    )
    attn_probs = jnp.exp(scores - log_total)
    grad_probs = jnp.einsum(
        "clhe,cmhe->chlm", grad_four, value_four, preferred_element_type=jnp.float32
    )
    grad_values = jnp.einsum(
        "chlm,clhe->cmhe",
        attn_probs.astype(jnp.bfloat16),
        grad_four,
        preferred_element_type=jnp.float32,
    )
    row_inner = jnp.sum(grad_probs * attn_probs, axis=-1, keepdims=True)
    grad_scores = (attn_probs * (grad_probs - row_inner)).astype(jnp.bfloat16)
    grad_queries = (
        jnp.einsum("chlm,cmhe->clhe", grad_scores, key_four, preferred_element_type=jnp.float32)
        * score_scale
    )
    grad_keys = (
        jnp.einsum("chlm,clhe->cmhe", grad_scores, query_four, preferred_element_type=jnp.float32)
        * score_scale
    )
    rows_here = crop_count * crop_length
    return jnp.concatenate(
        [
            grad_queries.reshape(rows_here, D),
            grad_keys.reshape(rows_here, D),
            grad_values.reshape(rows_here, D),
        ],
        axis=1,
    )


def forward_layer(stream, weights):
    (
        gain_one,
        shift_one,
        w_qkv,
        bias_query,
        bias_value,
        w_out,
        bias_out,
        gain_two,
        shift_two,
        w_up,
        bias_up,
        w_down,
        bias_down,
    ) = weights
    normed = norm_rows(stream, gain_one.astype(jnp.float32), shift_one.astype(jnp.float32)).astype(
        jnp.bfloat16
    )
    bias_all = jnp.concatenate([bias_query, jnp.zeros_like(bias_query), bias_value]).astype(
        jnp.float32
    )
    projected = (jnp.dot(normed, w_qkv, preferred_element_type=jnp.float32) + bias_all).astype(
        jnp.bfloat16
    )
    global_rows = G_DEV * GLEN
    global_part, global_total = attend_crops(
        projected[:global_rows, :D],
        projected[:global_rows, D : 2 * D],
        projected[:global_rows, 2 * D :],
        G_DEV,
        GLEN,
    )
    local_part, local_total = attend_crops(
        projected[global_rows:, :D],
        projected[global_rows:, D : 2 * D],
        projected[global_rows:, 2 * D :],
        L_DEV,
        LLEN,
    )
    mixed = jnp.concatenate([global_part, local_part], axis=0).astype(jnp.bfloat16)
    stream_one = (
        stream
        + jnp.dot(mixed, w_out, preferred_element_type=jnp.float32)
        + bias_out.astype(jnp.float32)
    )
    normed_two = norm_rows(
        stream_one, gain_two.astype(jnp.float32), shift_two.astype(jnp.float32)
    ).astype(jnp.bfloat16)
    pre_act = jnp.dot(normed_two, w_up, preferred_element_type=jnp.float32) + bias_up.astype(
        jnp.float32
    )
    hidden = jax.nn.gelu(pre_act, approximate=False).astype(jnp.bfloat16)
    result = (
        stream_one
        + jnp.dot(hidden, w_down, preferred_element_type=jnp.float32)
        + bias_down.astype(jnp.float32)
    )
    saved_state = (
        stream,
        normed,
        projected,
        global_total,
        local_total,
        mixed,
        stream_one,
        normed_two,
        pre_act,
        hidden,
    )
    return (result, saved_state)


def backward_layer(upstream, weights, saved_state):
    (
        gain_one,
        shift_one,
        w_qkv,
        bias_query,
        bias_value,
        w_out,
        bias_out,
        gain_two,
        shift_two,
        w_up,
        bias_up,
        w_down,
        bias_down,
    ) = weights
    (
        stream,
        normed,
        projected,
        global_total,
        local_total,
        mixed,
        stream_one,
        normed_two,
        pre_act,
        hidden,
    ) = saved_state
    branch_two = upstream.astype(jnp.bfloat16)
    grad_bias_down = jnp.sum(branch_two.astype(jnp.float32), axis=0)
    grad_w_down = contract_rows(hidden, branch_two)
    grad_hidden = contract_cols(branch_two, w_down)
    unused, gelu_pull = jax.vjp(lambda value: jax.nn.gelu(value, approximate=False), pre_act)
    grad_pre = gelu_pull(grad_hidden)[0].astype(jnp.bfloat16)
    grad_bias_up = jnp.sum(grad_pre.astype(jnp.float32), axis=0)
    grad_w_up = contract_rows(normed_two, grad_pre)
    grad_normed_two = contract_cols(grad_pre, w_up)
    unused_two, norm_pull_two = jax.vjp(
        norm_rows, stream_one, gain_two.astype(jnp.float32), shift_two.astype(jnp.float32)
    )
    grad_stream_part, grad_gain_two, grad_shift_two = norm_pull_two(grad_normed_two)
    grad_stream_one = upstream + grad_stream_part
    branch_one = grad_stream_one.astype(jnp.bfloat16)
    grad_bias_out = jnp.sum(branch_one.astype(jnp.float32), axis=0)
    grad_w_out = contract_rows(mixed, branch_one)
    grad_mixed = contract_cols(branch_one, w_out).astype(jnp.bfloat16)
    global_rows = G_DEV * GLEN
    grad_global = attend_back(
        projected[:global_rows, :D],
        projected[:global_rows, D : 2 * D],
        projected[:global_rows, 2 * D :],
        global_total,
        grad_mixed[:global_rows],
        G_DEV,
        GLEN,
    )
    grad_local = attend_back(
        projected[global_rows:, :D],
        projected[global_rows:, D : 2 * D],
        projected[global_rows:, 2 * D :],
        local_total,
        grad_mixed[global_rows:],
        L_DEV,
        LLEN,
    )
    grad_projected = jnp.concatenate([grad_global, grad_local], axis=0).astype(jnp.bfloat16)
    column_sums = jnp.sum(grad_projected.astype(jnp.float32), axis=0)
    grad_bias_query = column_sums[:D]
    grad_bias_value = column_sums[2 * D :]
    grad_w_qkv = contract_rows(normed, grad_projected)
    grad_normed = contract_cols(grad_projected, w_qkv)
    unused_one, norm_pull_one = jax.vjp(
        norm_rows, stream, gain_one.astype(jnp.float32), shift_one.astype(jnp.float32)
    )
    grad_input_part, grad_gain_one, grad_shift_one = norm_pull_one(grad_normed)
    grad_stream = grad_stream_one + grad_input_part
    grads = (
        grad_gain_one,
        grad_shift_one,
        grad_w_qkv,
        grad_bias_query,
        grad_bias_value,
        grad_w_out,
        grad_bias_out,
        grad_gain_two,
        grad_shift_two,
        grad_w_up,
        grad_bias_up,
        grad_w_down,
        grad_bias_down,
    )
    return (grad_stream, grads)


def local(
    tokens,
    cotangent,
    norm1_gain,
    norm1_bias,
    qkv_weight,
    query_bias,
    value_bias,
    out_weight,
    out_bias,
    norm2_gain,
    norm2_bias,
    up_weight,
    up_bias,
    down_weight,
    down_bias,
):
    shards = (
        norm1_gain,
        norm1_bias,
        qkv_weight,
        query_bias,
        value_bias,
        out_weight,
        out_bias,
        norm2_gain,
        norm2_bias,
        up_weight,
        up_bias,
        down_weight,
        down_bias,
    )
    layer_total = qkv_weight.shape[0]
    stream = tokens.astype(jnp.float32)
    saved_layers = []
    kept_weights = []
    for layer_index in range(layer_total):
        weights = gather_forward(tuple((w[layer_index] for w in shards)))
        stream, saved_state = forward_layer(stream, weights)
        saved_layers.append(saved_state)
        kept_weights.append(weights)
    encoded = stream.astype(jnp.bfloat16)
    upstream = cotangent.astype(jnp.float32)
    reduced_layers = [None] * layer_total
    for layer_index in reversed(range(layer_total)):
        upstream, grads = backward_layer(
            upstream, kept_weights[layer_index], saved_layers[layer_index]
        )
        reduced_layers[layer_index] = reduce_grads(grads)
    stacked = tuple(
        (
            jnp.stack(
                [reduced_layers[layer_index][member] for layer_index in range(layer_total)], axis=0
            )
            for member in range(13)
        )
    )
    return (
        encoded,
        upstream,
        stacked[0],
        stacked[1],
        stacked[2],
        stacked[3],
        stacked[4],
        stacked[5],
        stacked[6],
        stacked[7],
        stacked[8],
        stacked[9],
        stacked[10],
        stacked[11],
        stacked[12],
    )


VMEM_BYTES = 65408 * 1024

MESH = pl.DeviceIdType.MESH
F32 = jnp.float32
BF16 = jnp.bfloat16

FF = 3072
ROWS = 345
PAD = 352
STEP = 32
UNROLL = True
SHARD = 96
HALF = 48
UNITS = 12
SLOTS = 6
CORE_SLOTS = 4
RING = 8
PARTS = 2
WIDE = D // PARTS
LAG_XY, LAG_LAST, LAG_Z1, LAG_Z2, LAG_OUT = 4, 6, 8, 10, 12
LAG_PASS, LAG_WHOLE = 8, 9
EARLY_UNITS = 2
EARLY = 3
VEC_EVERY = 5
TOP_ROWS = 208
KEYS = 256
LOW_KEY = PAD - KEYS
LOW_ROWS = PAD - TOP_ROWS
V_G1, V_B1, V_QB, V_VB, V_OB, V_G2, V_B2, V_DB, V_UB = range(9)


def nt(left, right):
    return lax.dot_general(left, right, (((1,), (1,)), ((), ())), preferred_element_type=F32)


def tn(left, right):
    return lax.dot_general(left, right, (((0,), (0,)), ((), ())), preferred_element_type=F32)


def nn(left, right):
    return lax.dot_general(left, right, (((1,), (0,)), ((), ())), preferred_element_type=F32)


def aligned(value, by):
    return value if isinstance(value, int) else pl.multiple_of(value, by)


def twelfth(index):
    return lax.div(index * 43, 512)


def backward_unit(layers, index):
    whole = lax.div(index, PARTS)
    half = index - PARTS * whole
    turn = twelfth(whole)
    place = whole - UNITS * turn
    part = lax.div(place, 4)
    within = place - 4 * part
    is_down, is_late = lax.div(2 - part, 2), lax.div(part, 2)
    late = within + 3 - 4 * lax.div(within + 3, 4)
    unit = is_down * 8 + (1 - is_late) * place + is_late * late
    return layers - 1 - turn, unit, half


def stats(x):
    mean = jnp.mean(x, axis=-1, keepdims=True)
    centred = x - mean
    scale = lax.rsqrt(jnp.mean(centred * centred, axis=-1, keepdims=True) + epsilon)
    return centred * scale, scale


def fold(x):
    return jnp.sum(x.reshape(x.shape[0] // 8, 8, x.shape[1]), axis=0)


def total(x):
    return jnp.sum(x, axis=0, keepdims=True)


def step_rows(step):
    return pl.ds(aligned(step * STEP, STEP), STEP)


def encoder_kernel(
    layers,
    tokens,
    cotangent,
    n_g1,
    n_b1,
    n_qb,
    n_vb,
    n_ob,
    n_g2,
    n_b2,
    n_db,
    n_ub,
    w_qkv,
    w_out,
    w_up,
    w_down,
    encoded,
    tokens_grad,
    g_vec,
    g_qkv,
    g_out,
    g_up,
    g_down,
    wb,
    xs,
    x1,
    nr,
    pj,
    mx,
    n2,
    hd,
    gp,
    lse,
    gb,
    gm,
    br,
    acc,
    kacc,
    vacc,
    mask_top,
    mask_low,
    vsg,
    vec,
    ubs,
    gv,
    gvs,
    vr,
    vz,
    held,
    held_cot,
    held_grad,
    rc,
    r2,
    rz,
    ag_sem,
    ag_send,
    own_sem,
    core_sem,
    xy_sem,
    last_sem,
    z_sem,
    s0_send,
    rs_send,
    out_sem,
    vec_sem,
    gv_sem,
    io_sem,
):
    count = layers * UNITS
    pieces = count * PARTS
    d = lax.axis_index("dp")
    f = lax.axis_index("fsdp")
    c = lax.rem(f, 2)
    x = lax.rem(lax.div(f, 2), 2)
    y = lax.div(f, 4)
    fc = f + 1 - 2 * c
    fx = f + 2 - 4 * x
    fy = f + 4 - 8 * y
    outer = d * (3 - d) == 0
    inner = d * (3 - d) != 0
    z_in = 1 + lax.div(d, 3)
    z_out = 3 * lax.div(d, 2)
    z_pair = 3 - d
    parity = lax.rem(d, 2)
    z_near = d + 1 - 2 * parity
    in_plane = lambda who: {"fsdp": who}
    along = lambda who: {"dp": who}
    both = lambda a, b: jnp.logical_and(a, b)

    first_rows = pl.ds(0, HALF)
    second_rows = pl.ds(HALF, HALF)

    def send(source, target, sent, landed, who):
        pltpu.make_async_remote_copy(
            src_ref=source,
            dst_ref=target,
            send_sem=sent,
            recv_sem=landed,
            device_id=who,
            device_id_type=MESH,
        ).start()

    def wait_blocks(sem, blocks):
        span = wb.at[pl.ds(0, blocks), 0, 0, 0]
        pltpu.make_async_copy(span, span, sem).wait()

    def wait_half(sem):
        span = wb.at[0, 0, 0, 0, pl.ds(0, HALF)]
        pltpu.make_async_copy(span, span, sem).wait()

    def wait_piece(sem, blocks):
        span = wb.at[pl.ds(0, blocks), 0, 0, 0, :, pl.ds(0, WIDE)]
        pltpu.make_async_copy(span, span, sem).wait()

    barrier = pltpu.get_barrier_semaphore()
    peers = [lax.rem(f + hop, 8) for hop in range(1, 8)]
    for peer in peers:
        pl.semaphore_signal(barrier, inc=1, device_id=in_plane(peer), device_id_type=MESH)
    for hop in range(1, 4):
        beside = lax.rem(d + hop, 4)
        pl.semaphore_signal(barrier, inc=1, device_id=along(beside), device_id_type=MESH)

    for layer in range(layers):
        for unit in range(UNITS):
            if unit < 3:
                source = w_qkv.at[layer, :, pl.ds(unit * D, D)]
            elif unit == 3:
                source = w_out.at[layer]
            elif unit < 8:
                source = w_up.at[layer, :, pl.ds((unit - 4) * D, D)]
            else:
                source = w_down.at[layer, pl.ds((unit - 8) * SHARD, SHARD)]
            pltpu.make_async_copy(
                source,
                wb.at[layer * UNITS + unit, y, x, c],
                own_sem.at[layer * UNITS + unit],
            ).start()
    small = acc.at[0 : 16 * layers, 0:128]
    small[...] = jnp.zeros((16 * layers, 128), F32)
    for at, source in enumerate((n_g1, n_b1, n_qb, n_vb, n_ob, n_g2, n_b2, n_db)):
        shard = source[...].astype(F32)
        for layer in range(layers):
            row = 8 * layer + at
            acc[row : row + 1, 0:SHARD] = shard[layer : layer + 1]
    shard = n_ub[...].astype(F32)
    for layer in range(layers):
        for third in range(3):
            row = 8 * layers + 3 * layer + third
            acc[row : row + 1, 0:128] = shard[layer : layer + 1, third * 128 : third * 128 + 128]
    vsg[f] = small[...].astype(BF16)
    tokens_in = pltpu.make_async_copy(tokens, held, io_sem.at[0])
    cotangent_in = pltpu.make_async_copy(cotangent, held_cot, io_sem.at[1])
    encoded_out = pltpu.make_async_copy(held, encoded, io_sem.at[2])
    tokens_out = pltpu.make_async_copy(held_grad, tokens_grad, io_sem.at[3])
    tokens_in.start()
    cotangent_in.start()
    gvs[...] = jnp.zeros((8, 16, 128), F32)
    pl.semaphore_wait(barrier, 10)

    def role(i):
        return lax.rem(i, 3) * lax.div(2 * count - 3 - i, count)

    def collects(i):
        return role(i) != 2 - parity

    def gather_tick(t):
        @pl.when(t < count)
        def _():
            own = wb.at[t, y, x, c]
            wait_blocks(own_sem.at[t], 1)

            @pl.when(collects(t))
            def _():
                first = wb.at[t, y, x, c, first_rows]
                second = wb.at[t, y, x, c, second_rows]
                send(first, first, ag_send.at[t], ag_sem.at[t, 0], in_plane(fy))
                send(second, second, ag_send.at[t], ag_sem.at[t, 1], in_plane(fx))
                send(first, first, ag_send.at[t], ag_sem.at[t, 2], in_plane(fx))
                send(second, second, ag_send.at[t], ag_sem.at[t, 2], in_plane(fy))

            send(own, own, ag_send.at[t], ag_sem.at[t, 3], in_plane(fc))

        @pl.when(both(both(t >= 2, t < count + 2), collects(t - 2)))
        def _():
            i = t - 2
            wait_half(ag_sem.at[i, 0])
            wait_half(ag_sem.at[i, 1])
            first = wb.at[i, 1 - y, x, c, first_rows]
            second = wb.at[i, y, 1 - x, c, second_rows]
            send(first, first, ag_send.at[i], ag_sem.at[i, 2], in_plane(fx))
            send(second, second, ag_send.at[i], ag_sem.at[i, 2], in_plane(fy))

        @pl.when(both(both(t >= 4, t < count + 4), collects(t - 4)))
        def _():
            i = t - 4
            wait_blocks(ag_sem.at[i, 2], 2)
            for piece in (wb.at[i, 1 - y, :, c], wb.at[i, y, 1 - x, c]):

                @pl.when(role(i) > 0)
                def _(piece=piece):
                    send(piece, piece, ag_send.at[i], ag_sem.at[i, 0], along(z_near))

                send(piece, piece, ag_send.at[i], ag_sem.at[i, 3], in_plane(fc))

        @pl.when(both(both(t >= LAG_PASS, t < count + LAG_PASS), role(t - LAG_PASS) == 2 - parity))
        def _():
            i = t - LAG_PASS
            wait_blocks(ag_sem.at[i, 0], 3)
            for piece in (wb.at[i, 1 - y, :, c], wb.at[i, y, 1 - x, c]):
                send(piece, piece, ag_send.at[i], ag_sem.at[i, 3], in_plane(fc))

        @pl.when(both(t >= LAG_WHOLE, t < count + LAG_WHOLE))
        def _():
            wait_blocks(ag_sem.at[t - LAG_WHOLE, 3], 4)

    for peer in peers:
        send(vsg.at[f], vsg.at[f], vec_sem.at[0], vec_sem.at[1], in_plane(peer))

    @pl.loop(0, EARLY)
    def _(t):
        gather_tick(t)

    def crop_of(shape, dim, start):
        at = lax.broadcasted_iota(jnp.int32, shape, dim) + start
        which = jnp.zeros(shape, jnp.int32)
        for edge in range(L_DEV + 1):
            which = which + (at >= GLEN + edge * LLEN).astype(jnp.int32)
        return which

    for mask, rows, row_at, key_at in (
        (mask_top, TOP_ROWS, 0, 0),
        (mask_low, LOW_ROWS, TOP_ROWS, LOW_KEY),
    ):
        same = crop_of((rows, KEYS), 0, row_at) == crop_of((rows, KEYS), 1, key_at)
        mask[...] = jnp.where(same, 0.0, -1e30).astype(F32)

    xs[0, PAD - 8 :, :] = jnp.zeros((8, D), F32)
    tokens_in.wait()
    xs[0, 0:ROWS, :] = held[...].astype(F32)

    seven = vsg.at[pl.ds(0, 7)]
    pltpu.make_async_copy(seven, seven, vec_sem.at[1]).wait()
    spread = jnp.zeros((8 * layers, D), F32)
    for owner in range(8):
        at_row = lax.broadcasted_iota(jnp.int32, (128, D), 0)
        at_col = lax.broadcasted_iota(jnp.int32, (128, D), 1)
        hit = jnp.logical_and(at_col == at_row + owner * SHARD, at_row < SHARD)
        spread = spread + nn(vsg[owner, 0 : 8 * layers, :], jnp.where(hit, 1.0, 0.0).astype(BF16))
        wide = vsg[owner, 8 * layers :, :].astype(F32)
        for layer in range(layers):
            for third in range(3):
                row, lane = 3 * layer + third, owner * 4 * SHARD + third * 128
                ubs[layer : layer + 1, lane : lane + 128] = wide[row : row + 1]
    vec[...] = spread

    @pl.loop(EARLY, LAG_WHOLE)
    def _(t):
        gather_tick(t)

    def vector(layer, which):
        return vec[pl.ds(layer * 8 + which, 1), :]

    lane = lax.broadcasted_iota(jnp.int32, (1, 128), 1)
    left_lane = lane < HEAD_DIM
    score_scale = HEAD_DIM ** (-0.5)
    head_scaled = [
        jnp.where(left_lane, score_scale, 0.0).astype(BF16),
        jnp.where(left_lane, 0.0, score_scale).astype(BF16),
    ]
    head_plain = [
        jnp.where(left_lane, 1.0, 0.0).astype(BF16),
        jnp.where(left_lane, 0.0, 1.0).astype(BF16),
    ]
    groups = (
        (0, TOP_ROWS, 0, mask_top),
        (TOP_ROWS, LOW_ROWS, LOW_KEY, mask_low),
    )

    def weight(layer, unit):
        return wb[layer * UNITS + unit].reshape(D, D)

    def down_places(part):
        return [(unit, lax.div(part, 2), lax.rem(part, 2), core) for core in range(2) for unit in range(4)]

    def down_weight(layer, part):
        blocks = [wb[layer * UNITS + 8 + u, yy, xx, cc] for u, yy, xx, cc in down_places(part)]
        return jnp.concatenate(blocks, axis=0)

    def put_down(first, units, part, grad):
        for at, (u, yy, xx, cc) in enumerate(down_places(part)):
            if u < units:
                wb[first + u, yy, xx, cc] = grad[at * SHARD : (at + 1) * SHARD]

    def piece_at(i):
        layer, unit, half = backward_unit(layers, i)
        early = lax.div(pieces + EARLY_UNITS * PARTS - 1 - i, pieces)
        ahead = layers * UNITS + lax.div(i, PARTS)
        at = early * ahead + (1 - early) * (layer * UNITS + unit)
        return at, pl.ds(aligned(half * WIDE, 128), WIDE)

    def during(t, lag):
        return both(t >= lag, t < pieces + lag)

    def ring(i):
        return lax.rem(i, RING)

    def long_ring(i):
        return lax.rem(i, 2 * RING)

    def reduce_tick(t):
        @pl.when(t < pieces)
        def _():
            n, cols = piece_at(t)
            send(
                wb.at[n, :, :, 1 - c, :, cols],
                rc.at[lax.rem(t, CORE_SLOTS)],
                s0_send.at[ring(t)],
                core_sem.at[ring(t)],
                in_plane(fc),
            )

        @pl.when(during(t, LAG_XY))
        def _():
            i = t - LAG_XY
            n, cols = piece_at(i)
            slot = lax.rem(i, SLOTS)
            wait_piece(xy_sem.at[ring(i)], 2)
            along_x = wb.at[n, :, x, c, first_rows, cols]
            along_y = wb.at[n, y, :, c, second_rows, cols]
            along_x[...] = along_x[...] + r2[slot, 0]
            along_y[...] = along_y[...] + r2[slot, 1]
            send(
                wb.at[n, 1 - y, x, c, first_rows, cols],
                wb.at[n, 1 - y, x, 1 - c, first_rows, cols],
                rs_send.at[long_ring(i)],
                last_sem.at[ring(i)],
                in_plane(fy),
            )
            send(
                wb.at[n, y, 1 - x, c, second_rows, cols],
                wb.at[n, y, 1 - x, 1 - c, second_rows, cols],
                rs_send.at[long_ring(i)],
                last_sem.at[ring(i)],
                in_plane(fx),
            )

        @pl.when(during(t, 1))
        def _():
            i = t - 1
            n, cols = piece_at(i)
            slot = lax.rem(i, SLOTS)
            wait_piece(core_sem.at[ring(i)], 4)
            wait_piece(s0_send.at[ring(i)], 4)
            mine = wb.at[n, :, :, c, :, cols]
            mine[...] = mine[...] + rc[lax.rem(i, CORE_SLOTS)]
            send(
                wb.at[n, :, 1 - x, c, first_rows, cols],
                r2.at[slot, 0],
                rs_send.at[long_ring(i)],
                xy_sem.at[ring(i)],
                in_plane(fx),
            )
            send(
                wb.at[n, 1 - y, :, c, second_rows, cols],
                r2.at[slot, 1],
                rs_send.at[long_ring(i)],
                xy_sem.at[ring(i)],
                in_plane(fy),
            )

        @pl.when(during(t, LAG_OUT))
        def _():
            i = t - LAG_OUT
            n, cols = piece_at(i)
            layer, unit, half = backward_unit(layers, i)

            @pl.when(outer)
            def _():
                wait_piece(z_sem.at[ring(i), 2], 1)

            done = wb.at[n, y, x, 1 - c, :, cols]

            @pl.when(outer)
            def _():
                wait_piece(rs_send.at[long_ring(i)], 4)

            @pl.when(inner)
            def _():
                wait_piece(rs_send.at[long_ring(i)], 5)

            @pl.when(i >= RING)
            def _():
                wait_piece(out_sem.at[ring(i)], 1)

            def emit(target):
                pltpu.make_async_copy(done, target, out_sem.at[ring(i)]).start()

            def wide_at(first):
                return pl.ds(aligned((unit - first) * D + half * WIDE, 128), WIDE)

            @pl.when(unit < 3)
            def _():
                emit(g_qkv.at[layer, :, wide_at(0)])

            @pl.when(unit == 3)
            def _():
                emit(g_out.at[layer, :, cols])

            @pl.when(both(unit >= 4, unit < 8))
            def _():
                emit(g_up.at[layer, :, wide_at(4)])

            @pl.when(unit >= 8)
            def _():
                rows = pl.ds(aligned((unit - 8) * SHARD, 16), SHARD)
                emit(g_down.at[layer, rows, cols])

        @pl.when(during(t, LAG_LAST))
        def _():
            i = t - LAG_LAST
            n, cols = piece_at(i)
            wait_piece(last_sem.at[ring(i)], 1)
            own = wb.at[n, y, x, c, :, cols]
            own[...] = own[...] + wb[n, y, x, 1 - c, :, cols]

            @pl.when(outer)
            def _():
                to = rz.at[lax.rem(i, SLOTS), 0]
                send(own, to, rs_send.at[long_ring(i)], z_sem.at[ring(i), 0], along(z_in))

        @pl.when(both(inner, during(t, LAG_Z1)))
        def _():
            i = t - LAG_Z1
            n, cols = piece_at(i)
            slot = lax.rem(i, SLOTS)
            wait_piece(z_sem.at[ring(i), 0], 1)
            own = wb.at[n, y, x, c, :, cols]
            own[...] = own[...] + rz[slot, 0]
            send(own, rz.at[slot, 1], rs_send.at[long_ring(i)], z_sem.at[ring(i), 1], along(z_pair))

        @pl.when(both(inner, during(t, LAG_Z2)))
        def _():
            i = t - LAG_Z2
            n, cols = piece_at(i)
            wait_piece(z_sem.at[ring(i), 1], 1)
            done = wb.at[n, y, x, 1 - c, :, cols]
            done[...] = wb[n, y, x, c, :, cols] + rz[lax.rem(i, SLOTS), 1]
            send(done, done, rs_send.at[long_ring(i)], z_sem.at[ring(i), 2], along(z_out))

    @pl.loop(0, layers)
    def _(layer):
        base = layer * UNITS + LAG_WHOLE

        @pl.loop(0, PAD // STEP, unroll=UNROLL)
        def _(step):
            rows = step_rows(step)
            normed, _unused = stats(xs[layer, rows, :])
            nr[layer, rows, :] = (normed * vector(layer, V_G1) + vector(layer, V_B1)).astype(BF16)

        @pl.loop(0, 3)
        def _(part):
            gather_tick(base + part)
            is_q, is_v = lax.div(2 - part, 2), lax.div(part, 2)
            bias = is_q.astype(F32) * vector(layer, V_QB) + is_v.astype(F32) * vector(layer, V_VB)
            acc[...] = nn(nr[layer], weight(layer, part))

            @pl.loop(0, PAD // STEP, unroll=UNROLL)
            def _(step):
                rows = step_rows(step)
                pj[layer, part, rows, :] = (acc[rows, :] + bias).astype(BF16)

        @pl.loop(0, HEADS // 2)
        def _(pair):
            @pl.when(pair == 3)
            def _():
                gather_tick(base + 3)

            lanes = pl.ds(aligned(pair * 128, 128), 128)
            for row_at, rows, key_at, mask in groups:
                here = pl.ds(row_at, rows)
                keys = pj[layer, 1, pl.ds(key_at, KEYS), lanes]
                values = pj[layer, 2, pl.ds(key_at, KEYS), lanes]
                queries = pj[layer, 0, here, lanes]
                results = []
                for side in range(2):
                    scores = nt(queries * head_scaled[side], keys) + mask[...]
                    peak = jnp.max(scores, axis=-1, keepdims=True)
                    raised = jnp.exp(scores - peak)
                    exp_total = jnp.sum(raised, axis=-1, keepdims=True)
                    probs = (raised * (1.0 / exp_total)).astype(BF16)
                    results.append(nn(probs, values))
                    log_total = peak + jnp.log(exp_total)
                    lse[layer, here, :] = jnp.where(
                        lane == pair * 2 + side, log_total, lse[layer, here, :]
                    )
                mx[layer, here, lanes] = jnp.where(left_lane, results[0], results[1]).astype(BF16)

        acc[...] = nn(mx[layer], weight(layer, 3))

        @pl.loop(0, PAD // STEP, unroll=UNROLL)
        def _(step):
            rows = step_rows(step)
            now = xs[layer, rows, :] + acc[rows, :] + vector(layer, V_OB)
            x1[layer, rows, :] = now
            normed, _unused = stats(now)
            n2[layer, rows, :] = (normed * vector(layer, V_G2) + vector(layer, V_B2)).astype(BF16)

        @pl.when(layer == layers - 1)
        def _():
            acc[PAD - 8 :, :] = jnp.zeros((8, D), F32)
            cotangent_in.wait()
            acc[0:ROWS, :] = held_cot[...].astype(F32)
            br[...] = acc[...].astype(BF16)

        @pl.loop(0, 4)
        def _(part):
            gather_tick(base + 4 + part)
            bias = ubs[pl.ds(layer, 1), pl.ds(aligned(part * D, 128), D)]
            acc[...] = nn(n2[layer], weight(layer, 4 + part))

            @pl.loop(0, PAD // STEP, unroll=UNROLL)
            def _(step):
                rows = step_rows(step)
                pre = acc[rows, :] + bias
                cdf = 0.5 + 0.5 * lax.erf(pre * (0.5**0.5))
                bell = jnp.exp(-0.5 * pre * pre) * 0.3989422804014327
                hd[layer, part, rows, :] = (pre * cdf).astype(BF16)
                gp[layer, part, rows, :] = (cdf + pre * bell).astype(BF16)

            @pl.when(layer == layers - 1)
            def _():
                grad = tn(hd[layer, part], br[...]).astype(BF16)
                put_down(layers * UNITS, EARLY_UNITS, part, grad)

        @pl.loop(0, 4)
        def _(part):
            gather_tick(base + 8 + part)

        @pl.when(layer == layers - 1)
        def _():
            @pl.loop(0, 2)
            def _(t):
                reduce_tick(t)

        acc[...] = x1[layer] + vector(layer, V_DB)

        @pl.loop(0, 4)
        def _(part):
            acc[...] += nn(hd[layer, part], down_weight(layer, part))

        xs[layer + 1] = acc[...]

    reduce_tick(2)
    held[...] = xs[layers, 0:ROWS, :].astype(BF16)
    encoded_out.start()

    @pl.loop(0, count)
    def _(i):
        @pl.when(role(i) == 0)
        def _():
            wait_blocks(ag_send.at[i], 7)

        @pl.when(role(i) == 1 + parity)
        def _():
            wait_blocks(ag_send.at[i], 10)

        @pl.when(role(i) == 2 - parity)
        def _():
            wait_blocks(ag_send.at[i], 4)

    pltpu.make_async_copy(seven, seven, vec_sem.at[0]).wait()

    def vector_step(layer, step):
        def wait_vec(at, copies):
            span = gvs.at[pl.ds(0, copies)]
            pltpu.make_async_copy(span, span, gv_sem.at[layer, at]).wait()

        @pl.when(step == 0)
        def _():
            for owner in range(8):
                gvs[owner, 0:8, 0:SHARD] = gv[layer, 0:8, owner * SHARD : (owner + 1) * SHARD]
                row = 8 + owner // 2
                for third in range(3):
                    lane = (owner % 2) * 4 * SHARD + third * 128
                    wide = gv[layer, row : row + 1, lane : lane + 128]
                    gvs[owner, 8 + third : 9 + third, :] = wide
            vr[layer, f] = gvs[f]
            for peer in peers:
                send(
                    gvs.at[peer],
                    vr.at[layer, f],
                    gv_sem.at[layer, 0],
                    gv_sem.at[layer, 1],
                    in_plane(peer),
                )

        @pl.when(step == 1)
        def _():
            wait_vec(0, 7)
            wait_vec(1, 7)
            in_sum = vr[layer, 0]
            for source in range(1, 8):
                in_sum = in_sum + vr[layer, source]
            vz[layer, d] = in_sum
            for hop in range(3):
                send(
                    vz.at[layer, d],
                    vz.at[layer, d],
                    gv_sem.at[layer, 2],
                    gv_sem.at[layer, 3],
                    along(lax.rem(d + 1 + hop, 4)),
                )

        @pl.when(step == 2)
        def _():
            wait_vec(2, 3)
            wait_vec(3, 3)
            g_vec[layer] = (vz[layer, 0] + vz[layer, 1]) + (vz[layer, 2] + vz[layer, 3])

    up = xs.at[layers]
    up[PAD - 8 :, :] = jnp.zeros((8, D), F32)
    up[0:ROWS, :] = held_cot[...].astype(F32)
    none = jnp.zeros((8, D), F32)

    def put_vector(layer, which, value):
        gv[layer, pl.ds(which, 1), :] = total(value)

    def weight_grad(unit, left, right):
        grad = tn(left[...], right[...]).astype(BF16)
        wb[unit] = grad.reshape(2, 2, 2, SHARD, D)

    @pl.loop(0, layers)
    def _(turn):
        layer = layers - 1 - turn
        base = 4 + turn * (UNITS * PARTS - 4)

        def branch_two(step, carry):
            rows = step_rows(step)
            rounded = up[rows, :].astype(BF16)
            br[rows, :] = rounded
            return carry + fold(rounded.astype(F32))

        put_vector(layer, V_DB, lax.fori_loop(0, PAD // STEP, branch_two, none, unroll=UNROLL))

        @pl.loop(0, 4)
        def _(part):
            @pl.when(4 * turn + part >= 3)
            def _():
                reduce_tick(base - 4 + part)

            acc[...] = nt(br[...], down_weight(layer, part))

            def through_gelu(step, carry):
                rows = step_rows(step)
                value = (acc[rows, :] * gp[layer, part, rows, :].astype(F32)).astype(BF16)
                gb[part, rows, :] = value
                return carry + fold(value.astype(F32))

            put_vector(layer, V_UB + part, lax.fori_loop(0, PAD // STEP, through_gelu, none, unroll=UNROLL))
            grad = tn(hd[layer, part], br[...]).astype(BF16)
            put_down(layer * UNITS + 8, 4, part, grad)

        acc[...] = jnp.zeros((PAD, D), F32)

        @pl.loop(0, 4)
        def _(part):
            @pl.when(both(turn > 0, part == 0))
            def _():
                vector_step(layer + 1, 0)

            acc[...] += nt(gb[part], weight(layer, 4 + part))
            weight_grad(layer * UNITS + 4 + part, n2.at[layer], gb.at[part])
            reduce_tick(base + part)

        def norm_back(source, gain_at, shift_at):
            def body(step, carry):
                gain_sum, shift_sum = carry
                rows = step_rows(step)
                normed, scale = stats(source[layer, rows, :])
                grad = acc[rows, :]
                t = grad * vector(layer, gain_at)
                inner_mean = jnp.mean(t * normed, axis=-1, keepdims=True)
                back = scale * (t - jnp.mean(t, axis=-1, keepdims=True) - normed * inner_mean)
                up[rows, :] = up[rows, :] + back
                return gain_sum + fold(grad * normed), shift_sum + fold(grad)

            gain_sum, shift_sum = lax.fori_loop(0, PAD // STEP, body, (none, none), unroll=UNROLL)
            put_vector(layer, gain_at, gain_sum)
            put_vector(layer, shift_at, shift_sum)

        norm_back(x1, V_G2, V_B2)

        put_vector(layer, V_OB, lax.fori_loop(0, PAD // STEP, branch_two, none, unroll=UNROLL))
        gm[...] = nt(br[...], weight(layer, 3)).astype(BF16)
        weight_grad(layer * UNITS + 3, mx.at[layer], br)

        @pl.loop(0, 2)
        def _(again):
            reduce_tick(base + 4 + again)

        @pl.loop(0, HEADS // 2)
        def _(pair):
            reduce_tick(base + 6 + pair)

            @pl.when(both(turn > 0, lax.rem(pair, 5) == 0))
            def _():
                vector_step(layer + 1, 1 + lax.div(pair, 5))

            lanes = pl.ds(aligned(pair * 128, 128), 128)
            kacc[...] = jnp.zeros((PAD, 128), F32)
            vacc[...] = jnp.zeros((PAD, 128), F32)
            for row_at, rows, key_at, mask in groups:
                here = pl.ds(row_at, rows)
                there = pl.ds(key_at, KEYS)
                keys = pj[layer, 1, there, lanes]
                values = pj[layer, 2, there, lanes]
                queries = pj[layer, 0, here, lanes]
                grads = gm[here, lanes]
                q_parts, k_parts, v_parts = [], [], []
                for side in range(2):
                    log_total = jnp.sum(
                        jnp.where(lane == pair * 2 + side, lse[layer, here, :], 0.0),
                        axis=-1,
                        keepdims=True,
                    )
                    scaled = queries * head_scaled[side]
                    probs = jnp.exp(nt(scaled, keys) + mask[...] - log_total)
                    grad_probs = nt(grads * head_plain[side], values)
                    row_inner = jnp.sum(grad_probs * probs, axis=-1, keepdims=True)
                    grad_scores = (probs * (grad_probs - row_inner)).astype(BF16)
                    v_parts.append(tn(probs.astype(BF16), grads))
                    k_parts.append(tn(grad_scores, queries))
                    q_parts.append(nn(grad_scores, keys))
                grad_queries = jnp.where(left_lane, q_parts[0], q_parts[1]) * score_scale
                gb[0, here, lanes] = grad_queries.astype(BF16)
                kacc[there, :] += jnp.where(left_lane, k_parts[0], k_parts[1]) * score_scale
                vacc[there, :] += jnp.where(left_lane, v_parts[0], v_parts[1])
            gb[1, :, lanes] = kacc[...].astype(BF16)
            gb[2, :, lanes] = vacc[...].astype(BF16)

        for which, part in ((V_QB, 0), (V_VB, 2)):

            def column_sum(step, carry, part=part):
                return carry + fold(gb[part, step_rows(step), :].astype(F32))

            put_vector(layer, which, lax.fori_loop(0, PAD // STEP, column_sum, none, unroll=UNROLL))

        acc[...] = jnp.zeros((PAD, D), F32)

        @pl.loop(0, 3)
        def _(part):
            acc[...] += nt(gb[part], weight(layer, part))
            weight_grad(layer * UNITS + part, nr.at[layer], gb.at[part])

            reduce_tick(base + 12 + part)

        norm_back(xs, V_G1, V_B1)
        reduce_tick(base + 15)

    held_grad[...] = up[0:ROWS, :]
    tokens_out.start()
    encoded_out.wait()

    @pl.loop(pieces - 8, pieces + LAG_OUT)
    def _(t):
        step = t - (pieces - 8)

        @pl.when(both(lax.rem(step, VEC_EVERY) == 0, step < 3 * VEC_EVERY))
        def _():
            vector_step(0, lax.div(step, VEC_EVERY))

        reduce_tick(t)

    for at in range(RING):
        wait_piece(out_sem.at[at], 1)

    tokens_out.wait()


def closing_kernel(layers, *refs):
    encoded_in, tokens_in, vec_in = refs[:3]
    grads_in = refs[3:7]
    encoded_out, tokens_out = refs[7:9]
    small_out = refs[9:18]
    grads_out = refs[18:22]
    vec = refs[22]
    narrow = refs[23:27]
    wide = refs[27:31]
    held_encoded, held_tokens, few_sem, in_sem, out_sem = refs[31:]
    copies = [
        pltpu.make_async_copy(vec_in, vec, few_sem.at[0]),
        pltpu.make_async_copy(encoded_in, held_encoded, few_sem.at[1]),
        pltpu.make_async_copy(tokens_in, held_tokens, few_sem.at[2]),
    ]
    reads, writes = [], []
    for layer in range(layers):
        for at in range(4):
            reads.append(
                pltpu.make_async_copy(
                    grads_in[at].at[layer], narrow[at].at[layer], in_sem.at[at, layer]
                )
            )
            writes.append(
                pltpu.make_async_copy(
                    wide[at].at[layer], grads_out[at].at[layer], out_sem.at[at, layer]
                )
            )
    for copy in reads + copies:
        copy.start()
    for layer in range(layers):
        for at in range(4):
            reads[4 * layer + at].wait()
            wide[at][layer] = narrow[at][layer].astype(F32)
            writes[4 * layer + at].start()
    for copy in copies:
        copy.wait()
    writes.append(pltpu.make_async_copy(held_encoded, encoded_out, few_sem.at[1]))
    writes.append(pltpu.make_async_copy(held_tokens, tokens_out, few_sem.at[2]))
    writes[-2].start()
    writes[-1].start()
    for layer in range(layers):
        mine = vec[layer]
        for which in range(8):
            small_out[which][layer : layer + 1, :] = mine[which : which + 1, 0:SHARD]
        for third in range(3):
            lanes = slice(third * 128, third * 128 + 128)
            small_out[8][layer : layer + 1, lanes] = mine[8 + third : 9 + third]
    for copy in writes:
        copy.wait()


def kernel_local(
    tokens,
    cotangent,
    norm1_gain,
    norm1_bias,
    qkv_weight,
    query_bias,
    value_bias,
    out_weight,
    out_bias,
    norm2_gain,
    norm2_bias,
    up_weight,
    up_bias,
    down_weight,
    down_bias,
):
    layers = qkv_weight.shape[0]
    count = layers * UNITS
    pieces = count * PARTS
    hbm = pl.BlockSpec(memory_space=pltpu.MemorySpace.HBM)
    plain = pl.BlockSpec()
    dma = pltpu.SemaphoreType.DMA
    results = pl.pallas_call(
        functools.partial(encoder_kernel, layers),
        out_shape=(
            jax.ShapeDtypeStruct((ROWS, D), BF16),
            jax.ShapeDtypeStruct((ROWS, D), F32),
            jax.ShapeDtypeStruct((layers, 16, 128), F32),
            jax.ShapeDtypeStruct((layers, SHARD, 3 * D), BF16),
            jax.ShapeDtypeStruct((layers, SHARD, D), BF16),
            jax.ShapeDtypeStruct((layers, SHARD, FF), BF16),
            jax.ShapeDtypeStruct((layers, 4 * SHARD, D), BF16),
        ),
        in_specs=[hbm] * 2 + [plain] * 9 + [hbm] * 4,
        out_specs=(hbm, hbm, plain, hbm, hbm, hbm, hbm),
        scratch_shapes=[
            pltpu.VMEM((count + EARLY_UNITS, 2, 2, 2, SHARD, D), BF16),
            pltpu.VMEM((layers + 1, PAD, D), F32),
            pltpu.VMEM((layers, PAD, D), F32),
            pltpu.VMEM((layers, PAD, D), BF16),
            pltpu.VMEM((layers, 3, PAD, D), BF16),
            pltpu.VMEM((layers, PAD, D), BF16),
            pltpu.VMEM((layers, PAD, D), BF16),
            pltpu.VMEM((layers, 4, PAD, D), BF16),
            pltpu.VMEM((layers, 4, PAD, D), BF16),
            pltpu.VMEM((layers, PAD, 128), F32),
            pltpu.VMEM((4, PAD, D), BF16),
            pltpu.VMEM((PAD, D), BF16),
            pltpu.VMEM((PAD, D), BF16),
            pltpu.VMEM((PAD, D), F32),
            pltpu.VMEM((PAD, 128), F32),
            pltpu.VMEM((PAD, 128), F32),
            pltpu.VMEM((TOP_ROWS, KEYS), F32),
            pltpu.VMEM((LOW_ROWS, KEYS), F32),
            pltpu.VMEM((8, 16 * layers, 128), BF16),
            pltpu.VMEM((8 * layers, D), F32),
            pltpu.VMEM((layers, FF), F32),
            pltpu.VMEM((layers, 16, D), F32),
            pltpu.VMEM((8, 16, 128), F32),
            pltpu.VMEM((layers, 8, 16, 128), F32),
            pltpu.VMEM((layers, 4, 16, 128), F32),
            pltpu.VMEM((ROWS, D), BF16),
            pltpu.VMEM((ROWS, D), BF16),
            pltpu.VMEM((ROWS, D), F32),
            pltpu.VMEM((CORE_SLOTS, 2, 2, SHARD, WIDE), BF16),
            pltpu.VMEM((SLOTS, 2, 2, HALF, WIDE), BF16),
            pltpu.VMEM((SLOTS, 2, SHARD, WIDE), BF16),
            dma((count, 4)),
            dma((count,)),
            dma((count,)),
            dma((RING,)),
            dma((RING,)),
            dma((RING,)),
            dma((RING, 3)),
            dma((RING,)),
            dma((2 * RING,)),
            dma((RING,)),
            dma((2,)),
            dma((layers, 4)),
            dma((4,)),
        ],
        compiler_params=pltpu.CompilerParams(
            collective_id=0, has_side_effects=True, vmem_limit_bytes=VMEM_BYTES
        ),
    )(
        tokens,
        cotangent,
        norm1_gain,
        norm1_bias,
        query_bias,
        value_bias,
        out_bias,
        norm2_gain,
        norm2_bias,
        down_bias,
        up_bias,
        qkv_weight,
        out_weight,
        up_weight,
        down_weight,
    )
    shapes = [(layers, SHARD)] * 8 + [(layers, 4 * SHARD)]
    shapes += [(layers, SHARD, 3 * D), (layers, SHARD, D), (layers, SHARD, FF)]
    shapes += [(layers, 4 * SHARD, D)]
    closing = pl.pallas_call(
        functools.partial(closing_kernel, layers),
        out_shape=[jax.ShapeDtypeStruct((ROWS, D), BF16), jax.ShapeDtypeStruct((ROWS, D), F32)]
        + [jax.ShapeDtypeStruct(shape, F32) for shape in shapes],
        in_specs=[hbm] * 7,
        out_specs=[hbm] * 2 + [plain] * 9 + [hbm] * 4,
        scratch_shapes=[pltpu.VMEM((layers, 16, 128), F32)]
        + [pltpu.VMEM(shape, BF16) for shape in shapes[9:]]
        + [pltpu.VMEM(shape, F32) for shape in shapes[9:]]
        + [pltpu.VMEM((ROWS, D), BF16), pltpu.VMEM((ROWS, D), F32)]
        + [dma((3,)), dma((4, layers)), dma((4, layers))],
        compiler_params=pltpu.CompilerParams(vmem_limit_bytes=VMEM_BYTES),
    )(*results)
    by = dict(zip(("encoded", "tokens_grad"), closing[:2]))
    small = closing[2:11]
    g_qkv, g_out, g_up, g_down = closing[11:]
    return (
        by["encoded"],
        by["tokens_grad"],
        small[V_G1],
        small[V_B1],
        g_qkv,
        small[V_QB],
        small[V_VB],
        g_out,
        small[V_OB],
        small[V_G2],
        small[V_B2],
        g_up,
        small[V_UB],
        g_down,
        small[V_DB],
    )


def solution(mesh):
    in_specs = (
        P(("dp", "fsdp"), None),
        P(("dp", "fsdp"), None),
        P(None, "fsdp"),
        P(None, "fsdp"),
        P(None, "fsdp", None),
        P(None, "fsdp"),
        P(None, "fsdp"),
        P(None, "fsdp", None),
        P(None, "fsdp"),
        P(None, "fsdp"),
        P(None, "fsdp"),
        P(None, "fsdp", None),
        P(None, "fsdp"),
        P(None, "fsdp", None),
        P(None, "fsdp"),
    )
    out_specs = (
        P(("dp", "fsdp"), None),
        P(("dp", "fsdp"), None),
        P(None, "fsdp"),
        P(None, "fsdp"),
        P(None, "fsdp", None),
        P(None, "fsdp"),
        P(None, "fsdp"),
        P(None, "fsdp", None),
        P(None, "fsdp"),
        P(None, "fsdp"),
        P(None, "fsdp"),
        P(None, "fsdp", None),
        P(None, "fsdp"),
        P(None, "fsdp", None),
        P(None, "fsdp"),
    )
    fits = mesh.shape["dp"] == 4 and mesh.shape["fsdp"] == 8
    body = kernel_local if fits else local
    return jax.shard_map(body, mesh=mesh, in_specs=in_specs, out_specs=out_specs, check_vma=False)
```

```python
import functools

import jax
import jax.numpy as jnp
from jax import lax
from jax.experimental import pallas as pl
from jax.experimental.pallas import tpu as pltpu
from jax.sharding import PartitionSpec as P

D = 768
HEADS = 12
HEAD_DIM = 64
GLEN = 197
LLEN = 37
G_DEV = 1
L_DEV = 4


epsilon = 1e-06


def norm_rows(values_in, gain, shift):
    row_mean = jnp.mean(values_in, axis=-1, keepdims=True)
    centred = values_in - row_mean
    spread = jnp.mean(centred * centred, axis=-1, keepdims=True)
    return centred * lax.rsqrt(spread + epsilon) * gain + shift


def contract_rows(left, right):
    return lax.dot_general(
        left, right, (((0,), (0,)), ((), ())), preferred_element_type=jnp.float32
    )


def contract_cols(left, right):
    return lax.dot_general(
        left, right, (((1,), (1,)), ((), ())), preferred_element_type=jnp.float32
    )


def gather_forward(pieces):
    return (
        lax.all_gather(pieces[0], "fsdp", axis=0, tiled=True),
        lax.all_gather(pieces[1], "fsdp", axis=0, tiled=True),
        lax.all_gather(pieces[2], "fsdp", axis=0, tiled=True),
        lax.all_gather(pieces[3], "fsdp", axis=0, tiled=True),
        lax.all_gather(pieces[4], "fsdp", axis=0, tiled=True),
        lax.all_gather(pieces[5], "fsdp", axis=0, tiled=True),
        lax.all_gather(pieces[6], "fsdp", axis=0, tiled=True),
        lax.all_gather(pieces[7], "fsdp", axis=0, tiled=True),
        lax.all_gather(pieces[8], "fsdp", axis=0, tiled=True),
        lax.all_gather(pieces[9], "fsdp", axis=0, tiled=True),
        lax.all_gather(pieces[10], "fsdp", axis=0, tiled=True),
        lax.all_gather(pieces[11], "fsdp", axis=0, tiled=True),
        lax.all_gather(pieces[12], "fsdp", axis=0, tiled=True),
    )


def reduce_grads(grads):
    shares = (
        lax.psum_scatter(grads[0], "fsdp", scatter_dimension=0, tiled=True),
        lax.psum_scatter(grads[1], "fsdp", scatter_dimension=0, tiled=True),
        lax.psum_scatter(grads[2].astype(jnp.bfloat16), "fsdp", scatter_dimension=0, tiled=True),
        lax.psum_scatter(grads[3], "fsdp", scatter_dimension=0, tiled=True),
        lax.psum_scatter(grads[4], "fsdp", scatter_dimension=0, tiled=True),
        lax.psum_scatter(grads[5].astype(jnp.bfloat16), "fsdp", scatter_dimension=0, tiled=True),
        lax.psum_scatter(grads[6], "fsdp", scatter_dimension=0, tiled=True),
        lax.psum_scatter(grads[7], "fsdp", scatter_dimension=0, tiled=True),
        lax.psum_scatter(grads[8], "fsdp", scatter_dimension=0, tiled=True),
        lax.psum_scatter(grads[9].astype(jnp.bfloat16), "fsdp", scatter_dimension=0, tiled=True),
        lax.psum_scatter(grads[10], "fsdp", scatter_dimension=0, tiled=True),
        lax.psum_scatter(grads[11].astype(jnp.bfloat16), "fsdp", scatter_dimension=0, tiled=True),
        lax.psum_scatter(grads[12], "fsdp", scatter_dimension=0, tiled=True),
    )
    column_parts = (
        lax.psum_scatter(
            shares[2], "dp", scatter_dimension=1, tiled=True
        ).astype(jnp.float32),
        lax.psum_scatter(
            shares[5], "dp", scatter_dimension=1, tiled=True
        ).astype(jnp.float32),
        lax.psum_scatter(
            shares[9], "dp", scatter_dimension=1, tiled=True
        ).astype(jnp.float32),
        lax.psum_scatter(
            shares[11], "dp", scatter_dimension=1, tiled=True
        ).astype(jnp.float32),
    )
    matrices = (
        lax.all_gather(column_parts[0].astype(jnp.bfloat16), "dp", axis=1, tiled=True).astype(
            jnp.float32
        ),
        lax.all_gather(column_parts[1].astype(jnp.bfloat16), "dp", axis=1, tiled=True).astype(
            jnp.float32
        ),
        lax.all_gather(column_parts[2].astype(jnp.bfloat16), "dp", axis=1, tiled=True).astype(
            jnp.float32
        ),
        lax.all_gather(column_parts[3].astype(jnp.bfloat16), "dp", axis=1, tiled=True).astype(
            jnp.float32
        ),
    )
    vectors = lax.psum(
        (
            shares[0],
            shares[1],
            shares[3],
            shares[4],
            shares[6],
            shares[7],
            shares[8],
            shares[10],
            shares[12],
        ),
        "dp",
    )
    return (
        vectors[0],
        vectors[1],
        matrices[0],
        vectors[2],
        vectors[3],
        matrices[1],
        vectors[4],
        vectors[5],
        vectors[6],
        matrices[2],
        vectors[7],
        matrices[3],
        vectors[8],
    )


def attend_crops(queries, keys_in, values_in, crop_count, crop_length):
    shape_four = (crop_count, crop_length, HEADS, HEAD_DIM)
    scores = jnp.einsum(
        "clhe,cmhe->chlm",
        queries.reshape(shape_four),
        keys_in.reshape(shape_four),
        preferred_element_type=jnp.float32,
    ) * HEAD_DIM ** (-0.5)
    peak_score = jnp.max(scores, axis=-1, keepdims=True)
    raised = jnp.exp(scores - peak_score)
    exp_total = jnp.sum(raised, axis=-1, keepdims=True)
    attn_probs = (raised / exp_total).astype(jnp.bfloat16)
    log_total = peak_score + jnp.log(exp_total)
    result = jnp.einsum(
        "chlm,cmhe->clhe",
        attn_probs,
        values_in.reshape(shape_four),
        preferred_element_type=jnp.float32,
    )
    return (result.reshape(crop_count * crop_length, D), log_total)


def attend_back(queries, keys_in, values_in, log_total, grad_mixed, crop_count, crop_length):
    shape_four = (crop_count, crop_length, HEADS, HEAD_DIM)
    score_scale = HEAD_DIM ** (-0.5)
    query_four = queries.reshape(shape_four)
    key_four = keys_in.reshape(shape_four)
    value_four = values_in.reshape(shape_four)
    grad_four = grad_mixed.reshape(shape_four)
    scores = (
        jnp.einsum("clhe,cmhe->chlm", query_four, key_four, preferred_element_type=jnp.float32)
        * score_scale
    )
    attn_probs = jnp.exp(scores - log_total)
    grad_probs = jnp.einsum(
        "clhe,cmhe->chlm", grad_four, value_four, preferred_element_type=jnp.float32
    )
    grad_values = jnp.einsum(
        "chlm,clhe->cmhe",
        attn_probs.astype(jnp.bfloat16),
        grad_four,
        preferred_element_type=jnp.float32,
    )
    row_inner = jnp.sum(grad_probs * attn_probs, axis=-1, keepdims=True)
    grad_scores = (attn_probs * (grad_probs - row_inner)).astype(jnp.bfloat16)
    grad_queries = (
        jnp.einsum("chlm,cmhe->clhe", grad_scores, key_four, preferred_element_type=jnp.float32)
        * score_scale
    )
    grad_keys = (
        jnp.einsum("chlm,clhe->cmhe", grad_scores, query_four, preferred_element_type=jnp.float32)
        * score_scale
    )
    rows_here = crop_count * crop_length
    return jnp.concatenate(
        [
            grad_queries.reshape(rows_here, D),
            grad_keys.reshape(rows_here, D),
            grad_values.reshape(rows_here, D),
        ],
        axis=1,
    )


def forward_layer(stream, weights):
    (
        gain_one,
        shift_one,
        w_qkv,
        bias_query,
        bias_value,
        w_out,
        bias_out,
        gain_two,
        shift_two,
        w_up,
        bias_up,
        w_down,
        bias_down,
    ) = weights
    normed = norm_rows(stream, gain_one.astype(jnp.float32), shift_one.astype(jnp.float32)).astype(
        jnp.bfloat16
    )
    bias_all = jnp.concatenate([bias_query, jnp.zeros_like(bias_query), bias_value]).astype(
        jnp.float32
    )
    projected = (jnp.dot(normed, w_qkv, preferred_element_type=jnp.float32) + bias_all).astype(
        jnp.bfloat16
    )
    global_rows = G_DEV * GLEN
    global_part, global_total = attend_crops(
        projected[:global_rows, :D],
        projected[:global_rows, D : 2 * D],
        projected[:global_rows, 2 * D :],
        G_DEV,
        GLEN,
    )
    local_part, local_total = attend_crops(
        projected[global_rows:, :D],
        projected[global_rows:, D : 2 * D],
        projected[global_rows:, 2 * D :],
        L_DEV,
        LLEN,
    )
    mixed = jnp.concatenate([global_part, local_part], axis=0).astype(jnp.bfloat16)
    stream_one = (
        stream
        + jnp.dot(mixed, w_out, preferred_element_type=jnp.float32)
        + bias_out.astype(jnp.float32)
    )
    normed_two = norm_rows(
        stream_one, gain_two.astype(jnp.float32), shift_two.astype(jnp.float32)
    ).astype(jnp.bfloat16)
    pre_act = jnp.dot(normed_two, w_up, preferred_element_type=jnp.float32) + bias_up.astype(
        jnp.float32
    )
    hidden = jax.nn.gelu(pre_act, approximate=False).astype(jnp.bfloat16)
    result = (
        stream_one
        + jnp.dot(hidden, w_down, preferred_element_type=jnp.float32)
        + bias_down.astype(jnp.float32)
    )
    saved_state = (
        stream,
        normed,
        projected,
        global_total,
        local_total,
        mixed,
        stream_one,
        normed_two,
        pre_act,
        hidden,
    )
    return (result, saved_state)


def backward_layer(upstream, weights, saved_state):
    (
        gain_one,
        shift_one,
        w_qkv,
        bias_query,
        bias_value,
        w_out,
        bias_out,
        gain_two,
        shift_two,
        w_up,
        bias_up,
        w_down,
        bias_down,
    ) = weights
    (
        stream,
        normed,
        projected,
        global_total,
        local_total,
        mixed,
        stream_one,
        normed_two,
        pre_act,
        hidden,
    ) = saved_state
    branch_two = upstream.astype(jnp.bfloat16)
    grad_bias_down = jnp.sum(branch_two.astype(jnp.float32), axis=0)
    grad_w_down = contract_rows(hidden, branch_two)
    grad_hidden = contract_cols(branch_two, w_down)
    unused, gelu_pull = jax.vjp(lambda value: jax.nn.gelu(value, approximate=False), pre_act)
    grad_pre = gelu_pull(grad_hidden)[0].astype(jnp.bfloat16)
    grad_bias_up = jnp.sum(grad_pre.astype(jnp.float32), axis=0)
    grad_w_up = contract_rows(normed_two, grad_pre)
    grad_normed_two = contract_cols(grad_pre, w_up)
    unused_two, norm_pull_two = jax.vjp(
        norm_rows, stream_one, gain_two.astype(jnp.float32), shift_two.astype(jnp.float32)
    )
    grad_stream_part, grad_gain_two, grad_shift_two = norm_pull_two(grad_normed_two)
    grad_stream_one = upstream + grad_stream_part
    branch_one = grad_stream_one.astype(jnp.bfloat16)
    grad_bias_out = jnp.sum(branch_one.astype(jnp.float32), axis=0)
    grad_w_out = contract_rows(mixed, branch_one)
    grad_mixed = contract_cols(branch_one, w_out).astype(jnp.bfloat16)
    global_rows = G_DEV * GLEN
    grad_global = attend_back(
        projected[:global_rows, :D],
        projected[:global_rows, D : 2 * D],
        projected[:global_rows, 2 * D :],
        global_total,
        grad_mixed[:global_rows],
        G_DEV,
        GLEN,
    )
    grad_local = attend_back(
        projected[global_rows:, :D],
        projected[global_rows:, D : 2 * D],
        projected[global_rows:, 2 * D :],
        local_total,
        grad_mixed[global_rows:],
        L_DEV,
        LLEN,
    )
    grad_projected = jnp.concatenate([grad_global, grad_local], axis=0).astype(jnp.bfloat16)
    column_sums = jnp.sum(grad_projected.astype(jnp.float32), axis=0)
    grad_bias_query = column_sums[:D]
    grad_bias_value = column_sums[2 * D :]
    grad_w_qkv = contract_rows(normed, grad_projected)
    grad_normed = contract_cols(grad_projected, w_qkv)
    unused_one, norm_pull_one = jax.vjp(
        norm_rows, stream, gain_one.astype(jnp.float32), shift_one.astype(jnp.float32)
    )
    grad_input_part, grad_gain_one, grad_shift_one = norm_pull_one(grad_normed)
    grad_stream = grad_stream_one + grad_input_part
    grads = (
        grad_gain_one,
        grad_shift_one,
        grad_w_qkv,
        grad_bias_query,
        grad_bias_value,
        grad_w_out,
        grad_bias_out,
        grad_gain_two,
        grad_shift_two,
        grad_w_up,
        grad_bias_up,
        grad_w_down,
        grad_bias_down,
    )
    return (grad_stream, grads)


def local(
    tokens,
    cotangent,
    norm1_gain,
    norm1_bias,
    qkv_weight,
    query_bias,
    value_bias,
    out_weight,
    out_bias,
    norm2_gain,
    norm2_bias,
    up_weight,
    up_bias,
    down_weight,
    down_bias,
):
    shards = (
        norm1_gain,
        norm1_bias,
        qkv_weight,
        query_bias,
        value_bias,
        out_weight,
        out_bias,
        norm2_gain,
        norm2_bias,
        up_weight,
        up_bias,
        down_weight,
        down_bias,
    )
    layer_total = qkv_weight.shape[0]
    stream = tokens.astype(jnp.float32)
    saved_layers = []
    kept_weights = []
    for layer_index in range(layer_total):
        weights = gather_forward(tuple((w[layer_index] for w in shards)))
        stream, saved_state = forward_layer(stream, weights)
        saved_layers.append(saved_state)
        kept_weights.append(weights)
    encoded = stream.astype(jnp.bfloat16)
    upstream = cotangent.astype(jnp.float32)
    reduced_layers = [None] * layer_total
    for layer_index in reversed(range(layer_total)):
        upstream, grads = backward_layer(
            upstream, kept_weights[layer_index], saved_layers[layer_index]
        )
        reduced_layers[layer_index] = reduce_grads(grads)
    stacked = tuple(
        (
            jnp.stack(
                [reduced_layers[layer_index][member] for layer_index in range(layer_total)], axis=0
            )
            for member in range(13)
        )
    )
    return (
        encoded,
        upstream,
        stacked[0],
        stacked[1],
        stacked[2],
        stacked[3],
        stacked[4],
        stacked[5],
        stacked[6],
        stacked[7],
        stacked[8],
        stacked[9],
        stacked[10],
        stacked[11],
        stacked[12],
    )


VMEM_BYTES = 65408 * 1024

MESH = pl.DeviceIdType.MESH
F32 = jnp.float32
BF16 = jnp.bfloat16

FF = 3072
ROWS = 345
PAD = 352
STEP = 32
UNROLL = True
SHARD = 96
HALF = 48
UNITS = 12
SLOTS = 6
CORE_SLOTS = 4
RING = 8
PARTS = 2
WIDE = D // PARTS
LAG_XY, LAG_LAST, LAG_Z1, LAG_Z2, LAG_OUT = 4, 6, 8, 10, 12
LAG_NEXT, LAG_PLANE, LAG_PASS, LAG_WHOLE = 2, 4, 8, 9
EARLY_UNITS = 2
EARLY_PIECES = EARLY_UNITS * PARTS
GAP = 3
EARLY = 3
VEC_EVERY = 4
TOP_ROWS = 208
KEYS = 256
LOW_KEY = PAD - KEYS
LOW_ROWS = PAD - TOP_ROWS
V_G1, V_B1, V_QB, V_VB, V_OB, V_G2, V_B2, V_DB, V_UB = range(9)


def nt(left, right):
    return lax.dot_general(left, right, (((1,), (1,)), ((), ())), preferred_element_type=F32)


def tn(left, right):
    return lax.dot_general(left, right, (((0,), (0,)), ((), ())), preferred_element_type=F32)


def nn(left, right):
    return lax.dot_general(left, right, (((1,), (0,)), ((), ())), preferred_element_type=F32)


def aligned(value, by):
    return value if isinstance(value, int) else pl.multiple_of(value, by)


def twelfth(index):
    return lax.div(index * 43, 512)


def backward_unit(layers, index):
    whole = lax.div(index, PARTS)
    half = index - PARTS * whole
    turn = twelfth(whole)
    place = whole - UNITS * turn
    part = lax.div(place, 4)
    within = place - 4 * part
    is_down, is_late = lax.div(2 - part, 2), lax.div(part, 2)
    late = within + 3 - 4 * lax.div(within + 3, 4)
    unit = is_down * 8 + (1 - is_late) * place + is_late * late
    return layers - 1 - turn, unit, half


def stats(x):
    mean = jnp.mean(x, axis=-1, keepdims=True)
    centred = x - mean
    scale = lax.rsqrt(jnp.mean(centred * centred, axis=-1, keepdims=True) + epsilon)
    return centred * scale, scale


def fold(x):
    return jnp.sum(x.reshape(x.shape[0] // 8, 8, x.shape[1]), axis=0)


def total(x):
    return jnp.sum(x, axis=0, keepdims=True)


def step_rows(step):
    return pl.ds(aligned(step * STEP, STEP), STEP)


def encoder_kernel(
    layers,
    tokens,
    cotangent,
    n_g1,
    n_b1,
    n_qb,
    n_vb,
    n_ob,
    n_g2,
    n_b2,
    n_db,
    n_ub,
    w_qkv,
    w_out,
    w_up,
    w_down,
    encoded,
    tokens_grad,
    g_vec,
    g_qkv,
    g_out,
    g_up,
    g_down,
    wb,
    xs,
    x1,
    nr,
    pj,
    mx,
    n2,
    hd,
    gp,
    lse,
    gb,
    gm,
    br,
    acc,
    kacc,
    vacc,
    mask_top,
    mask_low,
    vsg,
    vec,
    ubs,
    gv,
    gvs,
    vr,
    vz,
    held,
    held_cot,
    held_grad,
    rc,
    r2,
    rz,
    ag_sem,
    ag_send,
    own_sem,
    core_sem,
    xy_sem,
    last_sem,
    z_sem,
    s0_send,
    rs_send,
    out_sem,
    vec_sem,
    gv_sem,
    io_sem,
):
    count = layers * UNITS
    pieces = count * PARTS
    d = lax.axis_index("dp")
    f = lax.axis_index("fsdp")
    c = lax.rem(f, 2)
    x = lax.rem(lax.div(f, 2), 2)
    y = lax.div(f, 4)
    fc = f + 1 - 2 * c
    fx = f + 2 - 4 * x
    fy = f + 4 - 8 * y
    outer = d * (3 - d) == 0
    inner = d * (3 - d) != 0
    z_in = 1 + lax.div(d, 3)
    z_out = 3 * lax.div(d, 2)
    z_pair = 3 - d
    parity = lax.rem(d, 2)
    z_near = d + 1 - 2 * parity
    in_plane = lambda who: {"fsdp": who}
    along = lambda who: {"dp": who}
    both = lambda a, b: jnp.logical_and(a, b)

    first_rows = pl.ds(0, HALF)
    second_rows = pl.ds(HALF, HALF)

    def send(source, target, sent, landed, who):
        pltpu.make_async_remote_copy(
            src_ref=source,
            dst_ref=target,
            send_sem=sent,
            recv_sem=landed,
            device_id=who,
            device_id_type=MESH,
        ).start()

    def wait_blocks(sem, blocks):
        span = wb.at[pl.ds(0, blocks), 0, 0, 0]
        pltpu.make_async_copy(span, span, sem).wait()

    def wait_half(sem):
        span = wb.at[0, 0, 0, 0, pl.ds(0, HALF)]
        pltpu.make_async_copy(span, span, sem).wait()

    def wait_piece(sem, blocks):
        span = wb.at[pl.ds(0, blocks), 0, 0, 0, :, pl.ds(0, WIDE)]
        pltpu.make_async_copy(span, span, sem).wait()

    barrier = pltpu.get_barrier_semaphore()
    peers = [lax.rem(f + hop, 8) for hop in range(1, 8)]
    for peer in peers:
        pl.semaphore_signal(barrier, inc=1, device_id=in_plane(peer), device_id_type=MESH)

    @pl.when(outer)
    def _():
        pl.semaphore_signal(barrier, inc=1, device_id=along(z_in), device_id_type=MESH)

    @pl.when(inner)
    def _():
        pl.semaphore_signal(barrier, inc=1, device_id=along(z_out), device_id_type=MESH)
        pl.semaphore_signal(barrier, inc=1, device_id=along(z_pair), device_id_type=MESH)

    for layer in range(layers):
        for unit in range(UNITS):
            if unit < 3:
                source = w_qkv.at[layer, :, pl.ds(unit * D, D)]
            elif unit == 3:
                source = w_out.at[layer]
            elif unit < 8:
                source = w_up.at[layer, :, pl.ds((unit - 4) * D, D)]
            else:
                source = w_down.at[layer, pl.ds((unit - 8) * SHARD, SHARD)]
            pltpu.make_async_copy(
                source,
                wb.at[layer * UNITS + unit, y, x, c],
                own_sem.at[layer],
            ).start()
    small = acc.at[0 : 16 * layers, 0:128]
    small[...] = jnp.zeros((16 * layers, 128), F32)
    for at, source in enumerate((n_g1, n_b1, n_qb, n_vb, n_ob, n_g2, n_b2, n_db)):
        shard = source[...].astype(F32)
        for layer in range(layers):
            row = 8 * layer + at
            acc[row : row + 1, 0:SHARD] = shard[layer : layer + 1]
    shard = n_ub[...].astype(F32)
    for layer in range(layers):
        for third in range(3):
            row = 8 * layers + 3 * layer + third
            acc[row : row + 1, 0:128] = shard[layer : layer + 1, third * 128 : third * 128 + 128]
    vsg[f] = small[...].astype(BF16)
    tokens_in = pltpu.make_async_copy(tokens, held, io_sem.at[0])
    cotangent_in = pltpu.make_async_copy(cotangent, held_cot, io_sem.at[1])
    encoded_out = pltpu.make_async_copy(held, encoded, io_sem.at[2])
    tokens_out = pltpu.make_async_copy(held_grad, tokens_grad, io_sem.at[3])
    tokens_in.start()
    cotangent_in.start()
    gvs[...] = jnp.zeros((8, 16, 128), F32)
    pl.semaphore_wait(barrier, 8 + lax.div(d * (3 - d), 2))

    def role(i):
        return lax.rem(i, 3) * lax.div(2 * count - 3 - i, count)

    def collects(i):
        return role(i) != 2 - parity

    def gather_tick(t):
        @pl.when(t < count)
        def _():
            own = wb.at[t, y, x, c]

            @pl.when(lax.rem(t, UNITS) == 0)
            def _():
                wait_blocks(own_sem.at[lax.div(t, UNITS)], UNITS)

            @pl.when(collects(t))
            def _():
                first = wb.at[t, y, x, c, first_rows]
                second = wb.at[t, y, x, c, second_rows]
                send(first, first, ag_send.at[0], ag_sem.at[t, 0], in_plane(fy))
                send(second, second, ag_send.at[0], ag_sem.at[t, 1], in_plane(fx))
                send(first, first, ag_send.at[0], ag_sem.at[t, 2], in_plane(fx))
                send(second, second, ag_send.at[0], ag_sem.at[t, 2], in_plane(fy))

            send(own, own, ag_send.at[0], ag_sem.at[t, 3], in_plane(fc))

        @pl.when(both(both(t >= LAG_NEXT, t < count + LAG_NEXT), collects(t - LAG_NEXT)))
        def _():
            i = t - LAG_NEXT
            wait_half(ag_sem.at[i, 0])
            wait_half(ag_sem.at[i, 1])
            first = wb.at[i, 1 - y, x, c, first_rows]
            second = wb.at[i, y, 1 - x, c, second_rows]
            send(first, first, ag_send.at[0], ag_sem.at[i, 2], in_plane(fx))
            send(second, second, ag_send.at[0], ag_sem.at[i, 2], in_plane(fy))

        @pl.when(both(both(t >= LAG_PLANE, t < count + LAG_PLANE), collects(t - LAG_PLANE)))
        def _():
            i = t - LAG_PLANE
            wait_blocks(ag_sem.at[i, 2], 2)
            for piece in (wb.at[i, 1 - y, :, c], wb.at[i, y, 1 - x, c]):

                @pl.when(role(i) > 0)
                def _(piece=piece):
                    send(piece, piece, ag_send.at[0], ag_sem.at[i, 0], along(z_near))

                send(piece, piece, ag_send.at[0], ag_sem.at[i, 3], in_plane(fc))

        @pl.when(both(both(t >= LAG_PASS, t < count + LAG_PASS), role(t - LAG_PASS) == 2 - parity))
        def _():
            i = t - LAG_PASS
            wait_blocks(ag_sem.at[i, 0], 3)
            for piece in (wb.at[i, 1 - y, :, c], wb.at[i, y, 1 - x, c]):
                send(piece, piece, ag_send.at[0], ag_sem.at[i, 3], in_plane(fc))

        @pl.when(both(t >= LAG_WHOLE, t < count + LAG_WHOLE))
        def _():
            wait_blocks(ag_sem.at[t - LAG_WHOLE, 3], 4)

    for peer in peers:
        send(vsg.at[f], vsg.at[f], vec_sem.at[0], vec_sem.at[1], in_plane(peer))

    @pl.loop(0, EARLY)
    def _(t):
        gather_tick(t)

    def crop_of(shape, dim, start):
        at = lax.broadcasted_iota(jnp.int32, shape, dim) + start
        which = jnp.zeros(shape, jnp.int32)
        for edge in range(L_DEV + 1):
            which = which + (at >= GLEN + edge * LLEN).astype(jnp.int32)
        return which

    for mask, rows, row_at, key_at in (
        (mask_top, TOP_ROWS, 0, 0),
        (mask_low, LOW_ROWS, TOP_ROWS, LOW_KEY),
    ):
        same = crop_of((rows, KEYS), 0, row_at) == crop_of((rows, KEYS), 1, key_at)
        mask[...] = jnp.where(same, 0.0, -1e30).astype(F32)

    xs[0, PAD - 8 :, :] = jnp.zeros((8, D), F32)
    tokens_in.wait()
    xs[0, 0:ROWS, :] = held[...].astype(F32)

    seven = vsg.at[pl.ds(0, 7)]
    pltpu.make_async_copy(seven, seven, vec_sem.at[1]).wait()
    spread = jnp.zeros((8 * layers, D), F32)
    for owner in range(8):
        at_row = lax.broadcasted_iota(jnp.int32, (128, D), 0)
        at_col = lax.broadcasted_iota(jnp.int32, (128, D), 1)
        hit = jnp.logical_and(at_col == at_row + owner * SHARD, at_row < SHARD)
        spread = spread + nn(vsg[owner, 0 : 8 * layers, :], jnp.where(hit, 1.0, 0.0).astype(BF16))
        wide = vsg[owner, 8 * layers :, :].astype(F32)
        for layer in range(layers):
            for third in range(3):
                row, lane = 3 * layer + third, owner * 4 * SHARD + third * 128
                ubs[layer : layer + 1, lane : lane + 128] = wide[row : row + 1]
    vec[...] = spread

    @pl.loop(EARLY, LAG_WHOLE)
    def _(t):
        gather_tick(t)

    def vector(layer, which):
        return vec[pl.ds(layer * 8 + which, 1), :]

    lane = lax.broadcasted_iota(jnp.int32, (1, 128), 1)
    left_lane = lane < HEAD_DIM
    score_scale = HEAD_DIM ** (-0.5)
    head_scaled = [
        jnp.where(left_lane, score_scale, 0.0).astype(BF16),
        jnp.where(left_lane, 0.0, score_scale).astype(BF16),
    ]
    head_plain = [
        jnp.where(left_lane, 1.0, 0.0).astype(BF16),
        jnp.where(left_lane, 0.0, 1.0).astype(BF16),
    ]
    groups = (
        (0, TOP_ROWS, 0, mask_top),
        (TOP_ROWS, LOW_ROWS, LOW_KEY, mask_low),
    )

    def weight(layer, unit):
        return wb[layer * UNITS + unit].reshape(D, D)

    def down_places(part):
        return [(unit, lax.div(part, 2), lax.rem(part, 2), core) for core in range(2) for unit in range(4)]

    def down_weight(layer, part):
        blocks = [wb[layer * UNITS + 8 + u, yy, xx, cc] for u, yy, xx, cc in down_places(part)]
        return jnp.concatenate(blocks, axis=0)

    def put_down(first, units, part, grad):
        for at, (u, yy, xx, cc) in enumerate(down_places(part)):
            if u < units:
                wb[first + u, yy, xx, cc] = grad[at * SHARD : (at + 1) * SHARD]

    def piece_at(i):
        layer, unit, half = backward_unit(layers, i)
        early = lax.div(pieces + EARLY_UNITS * PARTS - 1 - i, pieces)
        ahead = layers * UNITS + lax.div(i, PARTS)
        at = early * ahead + (1 - early) * (layer * UNITS + unit)
        return at, pl.ds(aligned(half * WIDE, 128), WIDE)

    def during(t, lag):
        at = t - lag
        begun = jnp.logical_or(at < EARLY_PIECES, at >= EARLY_PIECES + GAP)
        return both(begun, both(at >= 0, at < pieces + GAP))

    def piece_of(t, lag):
        at = t - lag
        span = 4 * pieces
        return at - GAP * lax.div(at + span - (EARLY_PIECES + GAP), span)

    def ring(i):
        return lax.rem(i, RING)

    def long_ring(i):
        return lax.rem(i, 2 * RING)

    def reduce_tick(t):
        @pl.when(during(t, 0))
        def _():
            i = piece_of(t, 0)
            n, cols = piece_at(i)
            send(
                wb.at[n, :, :, 1 - c, :, cols],
                rc.at[lax.rem(i, CORE_SLOTS)],
                s0_send.at[ring(i)],
                core_sem.at[ring(i)],
                in_plane(fc),
            )

        @pl.when(during(t, LAG_XY))
        def _():
            i = piece_of(t, LAG_XY)
            n, cols = piece_at(i)
            slot = lax.rem(i, SLOTS)
            wait_piece(xy_sem.at[ring(i)], 2)
            along_x = wb.at[n, :, x, c, first_rows, cols]
            along_y = wb.at[n, y, :, c, second_rows, cols]
            along_x[...] = along_x[...] + r2[slot, 0]
            along_y[...] = along_y[...] + r2[slot, 1]
            send(
                wb.at[n, 1 - y, x, c, first_rows, cols],
                wb.at[n, 1 - y, x, 1 - c, first_rows, cols],
                rs_send.at[long_ring(i)],
                last_sem.at[ring(i)],
                in_plane(fy),
            )
            send(
                wb.at[n, y, 1 - x, c, second_rows, cols],
                wb.at[n, y, 1 - x, 1 - c, second_rows, cols],
                rs_send.at[long_ring(i)],
                last_sem.at[ring(i)],
                in_plane(fx),
            )

        @pl.when(during(t, 1))
        def _():
            i = piece_of(t, 1)
            n, cols = piece_at(i)
            slot = lax.rem(i, SLOTS)
            wait_piece(core_sem.at[ring(i)], 4)
            wait_piece(s0_send.at[ring(i)], 4)
            mine = wb.at[n, :, :, c, :, cols]
            mine[...] = mine[...] + rc[lax.rem(i, CORE_SLOTS)]
            send(
                wb.at[n, :, 1 - x, c, first_rows, cols],
                r2.at[slot, 0],
                rs_send.at[long_ring(i)],
                xy_sem.at[ring(i)],
                in_plane(fx),
            )
            send(
                wb.at[n, 1 - y, :, c, second_rows, cols],
                r2.at[slot, 1],
                rs_send.at[long_ring(i)],
                xy_sem.at[ring(i)],
                in_plane(fy),
            )

        @pl.when(during(t, LAG_OUT))
        def _():
            i = piece_of(t, LAG_OUT)
            n, cols = piece_at(i)
            layer, unit, half = backward_unit(layers, i)

            @pl.when(outer)
            def _():
                wait_piece(z_sem.at[ring(i), 2], 1)

            done = wb.at[n, y, x, 1 - c, :, cols]

            @pl.when(outer)
            def _():
                wait_piece(rs_send.at[long_ring(i)], 4)

            @pl.when(inner)
            def _():
                wait_piece(rs_send.at[long_ring(i)], 5)

            @pl.when(i >= RING)
            def _():
                wait_piece(out_sem.at[ring(i)], 1)

            def emit(target):
                pltpu.make_async_copy(done, target, out_sem.at[ring(i)]).start()

            def wide_at(first):
                return pl.ds(aligned((unit - first) * D + half * WIDE, 128), WIDE)

            @pl.when(unit < 3)
            def _():
                emit(g_qkv.at[layer, :, wide_at(0)])

            @pl.when(unit == 3)
            def _():
                emit(g_out.at[layer, :, cols])

            @pl.when(both(unit >= 4, unit < 8))
            def _():
                emit(g_up.at[layer, :, wide_at(4)])

            @pl.when(unit >= 8)
            def _():
                rows = pl.ds(aligned((unit - 8) * SHARD, 16), SHARD)
                emit(g_down.at[layer, rows, cols])

        @pl.when(during(t, LAG_LAST))
        def _():
            i = piece_of(t, LAG_LAST)
            n, cols = piece_at(i)
            wait_piece(last_sem.at[ring(i)], 1)
            own = wb.at[n, y, x, c, :, cols]
            own[...] = own[...] + wb[n, y, x, 1 - c, :, cols]

            @pl.when(outer)
            def _():
                to = rz.at[lax.rem(i, SLOTS), 0]
                send(own, to, rs_send.at[long_ring(i)], z_sem.at[ring(i), 0], along(z_in))

        @pl.when(both(inner, during(t, LAG_Z1)))
        def _():
            i = piece_of(t, LAG_Z1)
            n, cols = piece_at(i)
            slot = lax.rem(i, SLOTS)
            wait_piece(z_sem.at[ring(i), 0], 1)
            own = wb.at[n, y, x, c, :, cols]
            own[...] = own[...] + rz[slot, 0]
            send(own, rz.at[slot, 1], rs_send.at[long_ring(i)], z_sem.at[ring(i), 1], along(z_pair))

        @pl.when(both(inner, during(t, LAG_Z2)))
        def _():
            i = piece_of(t, LAG_Z2)
            n, cols = piece_at(i)
            wait_piece(z_sem.at[ring(i), 1], 1)
            done = wb.at[n, y, x, 1 - c, :, cols]
            done[...] = wb[n, y, x, c, :, cols] + rz[lax.rem(i, SLOTS), 1]
            send(done, done, rs_send.at[long_ring(i)], z_sem.at[ring(i), 2], along(z_out))

    @pl.loop(0, layers)
    def _(layer):
        base = layer * UNITS + LAG_WHOLE

        @pl.loop(0, PAD // STEP, unroll=UNROLL)
        def _(step):
            rows = step_rows(step)
            normed, _unused = stats(xs[layer, rows, :])
            nr[layer, rows, :] = (normed * vector(layer, V_G1) + vector(layer, V_B1)).astype(BF16)

        @pl.loop(0, 3)
        def _(part):
            gather_tick(base + part)
            is_q, is_v = lax.div(2 - part, 2), lax.div(part, 2)
            bias = is_q.astype(F32) * vector(layer, V_QB) + is_v.astype(F32) * vector(layer, V_VB)
            acc[...] = nn(nr[layer], weight(layer, part))

            @pl.loop(0, PAD // STEP, unroll=UNROLL)
            def _(step):
                rows = step_rows(step)
                pj[layer, part, rows, :] = (acc[rows, :] + bias).astype(BF16)

        @pl.loop(0, HEADS // 2)
        def _(pair):
            @pl.when(pair == 3)
            def _():
                gather_tick(base + 3)

            lanes = pl.ds(aligned(pair * 128, 128), 128)
            for row_at, rows, key_at, mask in groups:
                here = pl.ds(row_at, rows)
                keys = pj[layer, 1, pl.ds(key_at, KEYS), lanes]
                values = pj[layer, 2, pl.ds(key_at, KEYS), lanes]
                queries = pj[layer, 0, here, lanes]
                results = []
                for side in range(2):
                    scores = nt(queries * head_scaled[side], keys) + mask[...]
                    peak = jnp.max(scores, axis=-1, keepdims=True)
                    raised = jnp.exp(scores - peak)
                    exp_total = jnp.sum(raised, axis=-1, keepdims=True)
                    probs = (raised * (1.0 / exp_total)).astype(BF16)
                    results.append(nn(probs, values))
                    log_total = peak + jnp.log(exp_total)
                    lse[layer, here, :] = jnp.where(
                        lane == pair * 2 + side, log_total, lse[layer, here, :]
                    )
                mx[layer, here, lanes] = jnp.where(left_lane, results[0], results[1]).astype(BF16)

        acc[...] = nn(mx[layer], weight(layer, 3))

        @pl.loop(0, PAD // STEP, unroll=UNROLL)
        def _(step):
            rows = step_rows(step)
            now = xs[layer, rows, :] + acc[rows, :] + vector(layer, V_OB)
            x1[layer, rows, :] = now
            normed, _unused = stats(now)
            n2[layer, rows, :] = (normed * vector(layer, V_G2) + vector(layer, V_B2)).astype(BF16)

        @pl.when(layer == layers - 1)
        def _():
            acc[PAD - 8 :, :] = jnp.zeros((8, D), F32)
            cotangent_in.wait()
            acc[0:ROWS, :] = held_cot[...].astype(F32)
            br[...] = acc[...].astype(BF16)

        @pl.loop(0, 4)
        def _(part):
            gather_tick(base + 4 + part)
            bias = ubs[pl.ds(layer, 1), pl.ds(aligned(part * D, 128), D)]
            acc[...] = nn(n2[layer], weight(layer, 4 + part))

            @pl.loop(0, PAD // STEP, unroll=UNROLL)
            def _(step):
                rows = step_rows(step)
                pre = acc[rows, :] + bias
                cdf = 0.5 + 0.5 * lax.erf(pre * (0.5**0.5))
                bell = jnp.exp(-0.5 * pre * pre) * 0.3989422804014327
                hd[layer, part, rows, :] = (pre * cdf).astype(BF16)
                gp[layer, part, rows, :] = (cdf + pre * bell).astype(BF16)

            @pl.when(layer == layers - 1)
            def _():
                grad = tn(hd[layer, part], br[...]).astype(BF16)
                put_down(layers * UNITS, EARLY_UNITS, part, grad)

        @pl.loop(0, 4)
        def _(part):
            gather_tick(base + 8 + part)

        @pl.when(layer == layers - 1)
        def _():
            @pl.loop(0, 2)
            def _(t):
                reduce_tick(t)

        acc[...] = x1[layer] + vector(layer, V_DB)

        @pl.loop(0, 4)
        def _(part):
            acc[...] += nn(hd[layer, part], down_weight(layer, part))

        xs[layer + 1] = acc[...]

    reduce_tick(2)
    held[...] = xs[layers, 0:ROWS, :].astype(BF16)
    encoded_out.start()

    span = wb.at[pl.ds(0, 7 * count // 8)]
    pltpu.make_async_copy(span, span, ag_send.at[0]).wait()
    pltpu.make_async_copy(seven, seven, vec_sem.at[0]).wait()

    def vector_step(layer, step):
        def wait_vec(at, copies):
            span = gvs.at[pl.ds(0, copies)]
            pltpu.make_async_copy(span, span, gv_sem.at[layer, at]).wait()

        def z_go(source, target, at, who):
            send(
                vz.at[layer, source],
                vz.at[layer, target],
                gv_sem.at[layer, at],
                gv_sem.at[layer, at + 1],
                along(who),
            )

        @pl.when(step == 0)
        def _():
            for owner in range(8):
                gvs[owner, 0:8, 0:SHARD] = gv[layer, 0:8, owner * SHARD : (owner + 1) * SHARD]
                row = 8 + owner // 2
                for third in range(3):
                    lane = (owner % 2) * 4 * SHARD + third * 128
                    wide = gv[layer, row : row + 1, lane : lane + 128]
                    gvs[owner, 8 + third : 9 + third, :] = wide
            vr[layer, f] = gvs[f]
            for peer in peers:
                send(
                    gvs.at[peer],
                    vr.at[layer, f],
                    gv_sem.at[layer, 0],
                    gv_sem.at[layer, 1],
                    in_plane(peer),
                )

        @pl.when(step == 1)
        def _():
            wait_vec(0, 7)
            wait_vec(1, 7)
            in_sum = vr[layer, 0]
            for source in range(1, 8):
                in_sum = in_sum + vr[layer, source]
            vz[layer, 0] = in_sum

            @pl.when(outer)
            def _():
                z_go(0, 1, 2, z_in)

        @pl.when(both(inner, step == 2))
        def _():
            wait_vec(3, 1)
            vz[layer, 0] = vz[layer, 0] + vz[layer, 1]
            z_go(0, 2, 4, z_pair)

        @pl.when(both(inner, step == 3))
        def _():
            wait_vec(4, 1)
            wait_vec(5, 1)
            vz[layer, 3] = vz[layer, 0] + vz[layer, 2]
            z_go(3, 3, 6, z_out)

        @pl.when(step == 4)
        def _():
            @pl.when(outer)
            def _():
                wait_vec(2, 1)
                wait_vec(7, 1)

            @pl.when(inner)
            def _():
                wait_vec(6, 1)

            g_vec[layer] = vz[layer, 3]

    up = xs.at[layers]
    up[PAD - 8 :, :] = jnp.zeros((8, D), F32)
    up[0:ROWS, :] = held_cot[...].astype(F32)
    none = jnp.zeros((8, D), F32)

    def put_vector(layer, which, value):
        gv[layer, pl.ds(which, 1), :] = total(value)

    def weight_grad(unit, left, right):
        grad = tn(left[...], right[...]).astype(BF16)
        wb[unit] = grad.reshape(2, 2, 2, SHARD, D)

    @pl.loop(0, layers)
    def _(turn):
        layer = layers - 1 - turn
        base = EARLY_PIECES + GAP + turn * (UNITS * PARTS - 4)

        def branch_two(step, carry):
            rows = step_rows(step)
            rounded = up[rows, :].astype(BF16)
            br[rows, :] = rounded
            return carry + fold(rounded.astype(F32))

        put_vector(layer, V_DB, lax.fori_loop(0, PAD // STEP, branch_two, none, unroll=UNROLL))

        @pl.loop(0, 4)
        def _(part):
            reduce_tick(base - 4 + part)

            acc[...] = nt(br[...], down_weight(layer, part))

            def through_gelu(step, carry):
                rows = step_rows(step)
                value = (acc[rows, :] * gp[layer, part, rows, :].astype(F32)).astype(BF16)
                gb[part, rows, :] = value
                return carry + fold(value.astype(F32))

            put_vector(layer, V_UB + part, lax.fori_loop(0, PAD // STEP, through_gelu, none, unroll=UNROLL))
            grad = tn(hd[layer, part], br[...]).astype(BF16)
            put_down(layer * UNITS + 8, 4, part, grad)

        acc[...] = jnp.zeros((PAD, D), F32)

        @pl.loop(0, 4)
        def _(part):
            @pl.when(both(turn > 0, part == 0))
            def _():
                vector_step(layer + 1, 0)

            acc[...] += nt(gb[part], weight(layer, 4 + part))
            weight_grad(layer * UNITS + 4 + part, n2.at[layer], gb.at[part])
            reduce_tick(base + part)

        def norm_back(source, gain_at, shift_at):
            def body(step, carry):
                gain_sum, shift_sum = carry
                rows = step_rows(step)
                normed, scale = stats(source[layer, rows, :])
                grad = acc[rows, :]
                t = grad * vector(layer, gain_at)
                inner_mean = jnp.mean(t * normed, axis=-1, keepdims=True)
                back = scale * (t - jnp.mean(t, axis=-1, keepdims=True) - normed * inner_mean)
                up[rows, :] = up[rows, :] + back
                return gain_sum + fold(grad * normed), shift_sum + fold(grad)

            gain_sum, shift_sum = lax.fori_loop(0, PAD // STEP, body, (none, none), unroll=UNROLL)
            put_vector(layer, gain_at, gain_sum)
            put_vector(layer, shift_at, shift_sum)

        norm_back(x1, V_G2, V_B2)

        put_vector(layer, V_OB, lax.fori_loop(0, PAD // STEP, branch_two, none, unroll=UNROLL))
        gm[...] = nt(br[...], weight(layer, 3)).astype(BF16)
        weight_grad(layer * UNITS + 3, mx.at[layer], br)

        @pl.loop(0, 2)
        def _(again):
            reduce_tick(base + 4 + again)

        @pl.loop(0, HEADS // 2)
        def _(pair):
            reduce_tick(base + 6 + pair)

            @pl.when(both(turn > 0, lax.rem(pair, 2) == 0))
            def _():
                vector_step(layer + 1, 1 + lax.div(pair, 2))

            lanes = pl.ds(aligned(pair * 128, 128), 128)
            kacc[...] = jnp.zeros((PAD, 128), F32)
            vacc[...] = jnp.zeros((PAD, 128), F32)
            for row_at, rows, key_at, mask in groups:
                here = pl.ds(row_at, rows)
                there = pl.ds(key_at, KEYS)
                keys = pj[layer, 1, there, lanes]
                values = pj[layer, 2, there, lanes]
                queries = pj[layer, 0, here, lanes]
                grads = gm[here, lanes]
                q_parts, k_parts, v_parts = [], [], []
                for side in range(2):
                    log_total = jnp.sum(
                        jnp.where(lane == pair * 2 + side, lse[layer, here, :], 0.0),
                        axis=-1,
                        keepdims=True,
                    )
                    scaled = queries * head_scaled[side]
                    probs = jnp.exp(nt(scaled, keys) + mask[...] - log_total)
                    grad_probs = nt(grads * head_plain[side], values)
                    row_inner = jnp.sum(grad_probs * probs, axis=-1, keepdims=True)
                    grad_scores = (probs * (grad_probs - row_inner)).astype(BF16)
                    v_parts.append(tn(probs.astype(BF16), grads))
                    k_parts.append(tn(grad_scores, queries))
                    q_parts.append(nn(grad_scores, keys))
                grad_queries = jnp.where(left_lane, q_parts[0], q_parts[1]) * score_scale
                gb[0, here, lanes] = grad_queries.astype(BF16)
                kacc[there, :] += jnp.where(left_lane, k_parts[0], k_parts[1]) * score_scale
                vacc[there, :] += jnp.where(left_lane, v_parts[0], v_parts[1])
            gb[1, :, lanes] = kacc[...].astype(BF16)
            gb[2, :, lanes] = vacc[...].astype(BF16)

        for which, part in ((V_QB, 0), (V_VB, 2)):

            def column_sum(step, carry, part=part):
                return carry + fold(gb[part, step_rows(step), :].astype(F32))

            put_vector(layer, which, lax.fori_loop(0, PAD // STEP, column_sum, none, unroll=UNROLL))

        acc[...] = jnp.zeros((PAD, D), F32)

        @pl.loop(0, 3)
        def _(part):
            acc[...] += nt(gb[part], weight(layer, part))
            weight_grad(layer * UNITS + part, nr.at[layer], gb.at[part])

            reduce_tick(base + 12 + part)

            @pl.when(both(turn > 0, part == 1))
            def _():
                vector_step(layer + 1, 4)

        norm_back(xs, V_G1, V_B1)
        reduce_tick(base + 15)

    held_grad[...] = up[0:ROWS, :]
    tokens_out.start()
    encoded_out.wait()

    @pl.loop(pieces + GAP - 8, pieces + GAP + LAG_OUT)
    def _(t):
        step = t - (pieces + GAP - 8)

        @pl.when(both(lax.rem(step, VEC_EVERY) == 0, step < 5 * VEC_EVERY))
        def _():
            vector_step(0, lax.div(step, VEC_EVERY))

        reduce_tick(t)

    for at in range(RING):
        wait_piece(out_sem.at[at], 1)

    tokens_out.wait()


def closing_kernel(layers, *refs):
    encoded_in, tokens_in, vec_in = refs[:3]
    grads_in = refs[3:7]
    encoded_out, tokens_out = refs[7:9]
    small_out = refs[9:18]
    grads_out = refs[18:22]
    vec = refs[22]
    narrow = refs[23:27]
    wide = refs[27:31]
    held_encoded, held_tokens, few_sem, in_sem, out_sem = refs[31:]
    copies = [
        pltpu.make_async_copy(vec_in, vec, few_sem.at[0]),
        pltpu.make_async_copy(encoded_in, held_encoded, few_sem.at[1]),
        pltpu.make_async_copy(tokens_in, held_tokens, few_sem.at[2]),
    ]
    reads, writes = [], []
    for layer in range(layers):
        for at in range(4):
            reads.append(
                pltpu.make_async_copy(
                    grads_in[at].at[layer], narrow[at].at[layer], in_sem.at[at, layer]
                )
            )
            writes.append(
                pltpu.make_async_copy(
                    wide[at].at[layer], grads_out[at].at[layer], out_sem.at[at, layer]
                )
            )
    for copy in reads + copies:
        copy.start()
    for layer in range(layers):
        for at in range(4):
            reads[4 * layer + at].wait()
            wide[at][layer] = narrow[at][layer].astype(F32)
            writes[4 * layer + at].start()
    for copy in copies:
        copy.wait()
    writes.append(pltpu.make_async_copy(held_encoded, encoded_out, few_sem.at[1]))
    writes.append(pltpu.make_async_copy(held_tokens, tokens_out, few_sem.at[2]))
    writes[-2].start()
    writes[-1].start()
    for layer in range(layers):
        mine = vec[layer]
        for which in range(8):
            small_out[which][layer : layer + 1, :] = mine[which : which + 1, 0:SHARD]
        for third in range(3):
            lanes = slice(third * 128, third * 128 + 128)
            small_out[8][layer : layer + 1, lanes] = mine[8 + third : 9 + third]
    for copy in writes:
        copy.wait()


def kernel_local(
    tokens,
    cotangent,
    norm1_gain,
    norm1_bias,
    qkv_weight,
    query_bias,
    value_bias,
    out_weight,
    out_bias,
    norm2_gain,
    norm2_bias,
    up_weight,
    up_bias,
    down_weight,
    down_bias,
):
    layers = qkv_weight.shape[0]
    count = layers * UNITS
    pieces = count * PARTS
    hbm = pl.BlockSpec(memory_space=pltpu.MemorySpace.HBM)
    plain = pl.BlockSpec()
    dma = pltpu.SemaphoreType.DMA
    results = pl.pallas_call(
        functools.partial(encoder_kernel, layers),
        out_shape=(
            jax.ShapeDtypeStruct((ROWS, D), BF16),
            jax.ShapeDtypeStruct((ROWS, D), F32),
            jax.ShapeDtypeStruct((layers, 16, 128), F32),
            jax.ShapeDtypeStruct((layers, SHARD, 3 * D), BF16),
            jax.ShapeDtypeStruct((layers, SHARD, D), BF16),
            jax.ShapeDtypeStruct((layers, SHARD, FF), BF16),
            jax.ShapeDtypeStruct((layers, 4 * SHARD, D), BF16),
        ),
        in_specs=[hbm] * 2 + [plain] * 9 + [hbm] * 4,
        out_specs=(hbm, hbm, plain, hbm, hbm, hbm, hbm),
        scratch_shapes=[
            pltpu.VMEM((count + EARLY_UNITS, 2, 2, 2, SHARD, D), BF16),
            pltpu.VMEM((layers + 1, PAD, D), F32),
            pltpu.VMEM((layers, PAD, D), F32),
            pltpu.VMEM((layers, PAD, D), BF16),
            pltpu.VMEM((layers, 3, PAD, D), BF16),
            pltpu.VMEM((layers, PAD, D), BF16),
            pltpu.VMEM((layers, PAD, D), BF16),
            pltpu.VMEM((layers, 4, PAD, D), BF16),
            pltpu.VMEM((layers, 4, PAD, D), BF16),
            pltpu.VMEM((layers, PAD, 128), F32),
            pltpu.VMEM((4, PAD, D), BF16),
            pltpu.VMEM((PAD, D), BF16),
            pltpu.VMEM((PAD, D), BF16),
            pltpu.VMEM((PAD, D), F32),
            pltpu.VMEM((PAD, 128), F32),
            pltpu.VMEM((PAD, 128), F32),
            pltpu.VMEM((TOP_ROWS, KEYS), F32),
            pltpu.VMEM((LOW_ROWS, KEYS), F32),
            pltpu.VMEM((8, 16 * layers, 128), BF16),
            pltpu.VMEM((8 * layers, D), F32),
            pltpu.VMEM((layers, FF), F32),
            pltpu.VMEM((layers, 16, D), F32),
            pltpu.VMEM((8, 16, 128), F32),
            pltpu.VMEM((layers, 8, 16, 128), F32),
            pltpu.VMEM((layers, 4, 16, 128), F32),
            pltpu.VMEM((ROWS, D), BF16),
            pltpu.VMEM((ROWS, D), BF16),
            pltpu.VMEM((ROWS, D), F32),
            pltpu.VMEM((CORE_SLOTS, 2, 2, SHARD, WIDE), BF16),
            pltpu.VMEM((SLOTS, 2, 2, HALF, WIDE), BF16),
            pltpu.VMEM((SLOTS, 2, SHARD, WIDE), BF16),
            dma((count, 4)),
            dma((1,)),
            dma((layers,)),
            dma((RING,)),
            dma((RING,)),
            dma((RING,)),
            dma((RING, 3)),
            dma((RING,)),
            dma((2 * RING,)),
            dma((RING,)),
            dma((2,)),
            dma((layers, 8)),
            dma((4,)),
        ],
        compiler_params=pltpu.CompilerParams(
            collective_id=0, has_side_effects=True, vmem_limit_bytes=VMEM_BYTES
        ),
    )(
        tokens,
        cotangent,
        norm1_gain,
        norm1_bias,
        query_bias,
        value_bias,
        out_bias,
        norm2_gain,
        norm2_bias,
        down_bias,
        up_bias,
        qkv_weight,
        out_weight,
        up_weight,
        down_weight,
    )
    shapes = [(layers, SHARD)] * 8 + [(layers, 4 * SHARD)]
    shapes += [(layers, SHARD, 3 * D), (layers, SHARD, D), (layers, SHARD, FF)]
    shapes += [(layers, 4 * SHARD, D)]
    closing = pl.pallas_call(
        functools.partial(closing_kernel, layers),
        out_shape=[jax.ShapeDtypeStruct((ROWS, D), BF16), jax.ShapeDtypeStruct((ROWS, D), F32)]
        + [jax.ShapeDtypeStruct(shape, F32) for shape in shapes],
        in_specs=[hbm] * 7,
        out_specs=[hbm] * 2 + [plain] * 9 + [hbm] * 4,
        scratch_shapes=[pltpu.VMEM((layers, 16, 128), F32)]
        + [pltpu.VMEM(shape, BF16) for shape in shapes[9:]]
        + [pltpu.VMEM(shape, F32) for shape in shapes[9:]]
        + [pltpu.VMEM((ROWS, D), BF16), pltpu.VMEM((ROWS, D), F32)]
        + [dma((3,)), dma((4, layers)), dma((4, layers))],
        compiler_params=pltpu.CompilerParams(vmem_limit_bytes=VMEM_BYTES),
    )(*results)
    by = dict(zip(("encoded", "tokens_grad"), closing[:2]))
    small = closing[2:11]
    g_qkv, g_out, g_up, g_down = closing[11:]
    return (
        by["encoded"],
        by["tokens_grad"],
        small[V_G1],
        small[V_B1],
        g_qkv,
        small[V_QB],
        small[V_VB],
        g_out,
        small[V_OB],
        small[V_G2],
        small[V_B2],
        g_up,
        small[V_UB],
        g_down,
        small[V_DB],
    )


def solution(mesh):
    in_specs = (
        P(("dp", "fsdp"), None),
        P(("dp", "fsdp"), None),
        P(None, "fsdp"),
        P(None, "fsdp"),
        P(None, "fsdp", None),
        P(None, "fsdp"),
        P(None, "fsdp"),
        P(None, "fsdp", None),
        P(None, "fsdp"),
        P(None, "fsdp"),
        P(None, "fsdp"),
        P(None, "fsdp", None),
        P(None, "fsdp"),
        P(None, "fsdp", None),
        P(None, "fsdp"),
    )
    out_specs = (
        P(("dp", "fsdp"), None),
        P(("dp", "fsdp"), None),
        P(None, "fsdp"),
        P(None, "fsdp"),
        P(None, "fsdp", None),
        P(None, "fsdp"),
        P(None, "fsdp"),
        P(None, "fsdp", None),
        P(None, "fsdp"),
        P(None, "fsdp"),
        P(None, "fsdp"),
        P(None, "fsdp", None),
        P(None, "fsdp"),
        P(None, "fsdp", None),
        P(None, "fsdp"),
    )
    fits = mesh.shape["dp"] == 4 and mesh.shape["fsdp"] == 8
    body = kernel_local if fits else local
    return jax.shard_map(body, mesh=mesh, in_specs=in_specs, out_specs=out_specs, check_vma=False)
```

```python
import functools

import jax
import jax.numpy as jnp
from jax import lax
from jax.experimental import pallas as pl
from jax.experimental.pallas import tpu as pltpu
from jax.sharding import PartitionSpec as P

D = 768
HEADS = 12
HEAD_DIM = 64
GLEN = 197
LLEN = 37
G_DEV = 1
L_DEV = 4


epsilon = 1e-06


def norm_rows(values_in, gain, shift):
    row_mean = jnp.mean(values_in, axis=-1, keepdims=True)
    centred = values_in - row_mean
    spread = jnp.mean(centred * centred, axis=-1, keepdims=True)
    return centred * lax.rsqrt(spread + epsilon) * gain + shift


def contract_rows(left, right):
    return lax.dot_general(
        left, right, (((0,), (0,)), ((), ())), preferred_element_type=jnp.float32
    )


def contract_cols(left, right):
    return lax.dot_general(
        left, right, (((1,), (1,)), ((), ())), preferred_element_type=jnp.float32
    )


def gather_forward(pieces):
    return (
        lax.all_gather(pieces[0], "fsdp", axis=0, tiled=True),
        lax.all_gather(pieces[1], "fsdp", axis=0, tiled=True),
        lax.all_gather(pieces[2], "fsdp", axis=0, tiled=True),
        lax.all_gather(pieces[3], "fsdp", axis=0, tiled=True),
        lax.all_gather(pieces[4], "fsdp", axis=0, tiled=True),
        lax.all_gather(pieces[5], "fsdp", axis=0, tiled=True),
        lax.all_gather(pieces[6], "fsdp", axis=0, tiled=True),
        lax.all_gather(pieces[7], "fsdp", axis=0, tiled=True),
        lax.all_gather(pieces[8], "fsdp", axis=0, tiled=True),
        lax.all_gather(pieces[9], "fsdp", axis=0, tiled=True),
        lax.all_gather(pieces[10], "fsdp", axis=0, tiled=True),
        lax.all_gather(pieces[11], "fsdp", axis=0, tiled=True),
        lax.all_gather(pieces[12], "fsdp", axis=0, tiled=True),
    )


def reduce_grads(grads):
    shares = (
        lax.psum_scatter(grads[0], "fsdp", scatter_dimension=0, tiled=True),
        lax.psum_scatter(grads[1], "fsdp", scatter_dimension=0, tiled=True),
        lax.psum_scatter(grads[2].astype(jnp.bfloat16), "fsdp", scatter_dimension=0, tiled=True),
        lax.psum_scatter(grads[3], "fsdp", scatter_dimension=0, tiled=True),
        lax.psum_scatter(grads[4], "fsdp", scatter_dimension=0, tiled=True),
        lax.psum_scatter(grads[5].astype(jnp.bfloat16), "fsdp", scatter_dimension=0, tiled=True),
        lax.psum_scatter(grads[6], "fsdp", scatter_dimension=0, tiled=True),
        lax.psum_scatter(grads[7], "fsdp", scatter_dimension=0, tiled=True),
        lax.psum_scatter(grads[8], "fsdp", scatter_dimension=0, tiled=True),
        lax.psum_scatter(grads[9].astype(jnp.bfloat16), "fsdp", scatter_dimension=0, tiled=True),
        lax.psum_scatter(grads[10], "fsdp", scatter_dimension=0, tiled=True),
        lax.psum_scatter(grads[11].astype(jnp.bfloat16), "fsdp", scatter_dimension=0, tiled=True),
        lax.psum_scatter(grads[12], "fsdp", scatter_dimension=0, tiled=True),
    )
    column_parts = (
        lax.psum_scatter(
            shares[2], "dp", scatter_dimension=1, tiled=True
        ).astype(jnp.float32),
        lax.psum_scatter(
            shares[5], "dp", scatter_dimension=1, tiled=True
        ).astype(jnp.float32),
        lax.psum_scatter(
            shares[9], "dp", scatter_dimension=1, tiled=True
        ).astype(jnp.float32),
        lax.psum_scatter(
            shares[11], "dp", scatter_dimension=1, tiled=True
        ).astype(jnp.float32),
    )
    matrices = (
        lax.all_gather(column_parts[0].astype(jnp.bfloat16), "dp", axis=1, tiled=True).astype(
            jnp.float32
        ),
        lax.all_gather(column_parts[1].astype(jnp.bfloat16), "dp", axis=1, tiled=True).astype(
            jnp.float32
        ),
        lax.all_gather(column_parts[2].astype(jnp.bfloat16), "dp", axis=1, tiled=True).astype(
            jnp.float32
        ),
        lax.all_gather(column_parts[3].astype(jnp.bfloat16), "dp", axis=1, tiled=True).astype(
            jnp.float32
        ),
    )
    vectors = lax.psum(
        (
            shares[0],
            shares[1],
            shares[3],
            shares[4],
            shares[6],
            shares[7],
            shares[8],
            shares[10],
            shares[12],
        ),
        "dp",
    )
    return (
        vectors[0],
        vectors[1],
        matrices[0],
        vectors[2],
        vectors[3],
        matrices[1],
        vectors[4],
        vectors[5],
        vectors[6],
        matrices[2],
        vectors[7],
        matrices[3],
        vectors[8],
    )


def attend_crops(queries, keys_in, values_in, crop_count, crop_length):
    shape_four = (crop_count, crop_length, HEADS, HEAD_DIM)
    scores = jnp.einsum(
        "clhe,cmhe->chlm",
        queries.reshape(shape_four),
        keys_in.reshape(shape_four),
        preferred_element_type=jnp.float32,
    ) * HEAD_DIM ** (-0.5)
    peak_score = jnp.max(scores, axis=-1, keepdims=True)
    raised = jnp.exp(scores - peak_score)
    exp_total = jnp.sum(raised, axis=-1, keepdims=True)
    attn_probs = (raised / exp_total).astype(jnp.bfloat16)
    log_total = peak_score + jnp.log(exp_total)
    result = jnp.einsum(
        "chlm,cmhe->clhe",
        attn_probs,
        values_in.reshape(shape_four),
        preferred_element_type=jnp.float32,
    )
    return (result.reshape(crop_count * crop_length, D), log_total)


def attend_back(queries, keys_in, values_in, log_total, grad_mixed, crop_count, crop_length):
    shape_four = (crop_count, crop_length, HEADS, HEAD_DIM)
    score_scale = HEAD_DIM ** (-0.5)
    query_four = queries.reshape(shape_four)
    key_four = keys_in.reshape(shape_four)
    value_four = values_in.reshape(shape_four)
    grad_four = grad_mixed.reshape(shape_four)
    scores = (
        jnp.einsum("clhe,cmhe->chlm", query_four, key_four, preferred_element_type=jnp.float32)
        * score_scale
    )
    attn_probs = jnp.exp(scores - log_total)
    grad_probs = jnp.einsum(
        "clhe,cmhe->chlm", grad_four, value_four, preferred_element_type=jnp.float32
    )
    grad_values = jnp.einsum(
        "chlm,clhe->cmhe",
        attn_probs.astype(jnp.bfloat16),
        grad_four,
        preferred_element_type=jnp.float32,
    )
    row_inner = jnp.sum(grad_probs * attn_probs, axis=-1, keepdims=True)
    grad_scores = (attn_probs * (grad_probs - row_inner)).astype(jnp.bfloat16)
    grad_queries = (
        jnp.einsum("chlm,cmhe->clhe", grad_scores, key_four, preferred_element_type=jnp.float32)
        * score_scale
    )
    grad_keys = (
        jnp.einsum("chlm,clhe->cmhe", grad_scores, query_four, preferred_element_type=jnp.float32)
        * score_scale
    )
    rows_here = crop_count * crop_length
    return jnp.concatenate(
        [
            grad_queries.reshape(rows_here, D),
            grad_keys.reshape(rows_here, D),
            grad_values.reshape(rows_here, D),
        ],
        axis=1,
    )


def forward_layer(stream, weights):
    (
        gain_one,
        shift_one,
        w_qkv,
        bias_query,
        bias_value,
        w_out,
        bias_out,
        gain_two,
        shift_two,
        w_up,
        bias_up,
        w_down,
        bias_down,
    ) = weights
    normed = norm_rows(stream, gain_one.astype(jnp.float32), shift_one.astype(jnp.float32)).astype(
        jnp.bfloat16
    )
    bias_all = jnp.concatenate([bias_query, jnp.zeros_like(bias_query), bias_value]).astype(
        jnp.float32
    )
    projected = (jnp.dot(normed, w_qkv, preferred_element_type=jnp.float32) + bias_all).astype(
        jnp.bfloat16
    )
    global_rows = G_DEV * GLEN
    global_part, global_total = attend_crops(
        projected[:global_rows, :D],
        projected[:global_rows, D : 2 * D],
        projected[:global_rows, 2 * D :],
        G_DEV,
        GLEN,
    )
    local_part, local_total = attend_crops(
        projected[global_rows:, :D],
        projected[global_rows:, D : 2 * D],
        projected[global_rows:, 2 * D :],
        L_DEV,
        LLEN,
    )
    mixed = jnp.concatenate([global_part, local_part], axis=0).astype(jnp.bfloat16)
    stream_one = (
        stream
        + jnp.dot(mixed, w_out, preferred_element_type=jnp.float32)
        + bias_out.astype(jnp.float32)
    )
    normed_two = norm_rows(
        stream_one, gain_two.astype(jnp.float32), shift_two.astype(jnp.float32)
    ).astype(jnp.bfloat16)
    pre_act = jnp.dot(normed_two, w_up, preferred_element_type=jnp.float32) + bias_up.astype(
        jnp.float32
    )
    hidden = jax.nn.gelu(pre_act, approximate=False).astype(jnp.bfloat16)
    result = (
        stream_one
        + jnp.dot(hidden, w_down, preferred_element_type=jnp.float32)
        + bias_down.astype(jnp.float32)
    )
    saved_state = (
        stream,
        normed,
        projected,
        global_total,
        local_total,
        mixed,
        stream_one,
        normed_two,
        pre_act,
        hidden,
    )
    return (result, saved_state)


def backward_layer(upstream, weights, saved_state):
    (
        gain_one,
        shift_one,
        w_qkv,
        bias_query,
        bias_value,
        w_out,
        bias_out,
        gain_two,
        shift_two,
        w_up,
        bias_up,
        w_down,
        bias_down,
    ) = weights
    (
        stream,
        normed,
        projected,
        global_total,
        local_total,
        mixed,
        stream_one,
        normed_two,
        pre_act,
        hidden,
    ) = saved_state
    branch_two = upstream.astype(jnp.bfloat16)
    grad_bias_down = jnp.sum(branch_two.astype(jnp.float32), axis=0)
    grad_w_down = contract_rows(hidden, branch_two)
    grad_hidden = contract_cols(branch_two, w_down)
    unused, gelu_pull = jax.vjp(lambda value: jax.nn.gelu(value, approximate=False), pre_act)
    grad_pre = gelu_pull(grad_hidden)[0].astype(jnp.bfloat16)
    grad_bias_up = jnp.sum(grad_pre.astype(jnp.float32), axis=0)
    grad_w_up = contract_rows(normed_two, grad_pre)
    grad_normed_two = contract_cols(grad_pre, w_up)
    unused_two, norm_pull_two = jax.vjp(
        norm_rows, stream_one, gain_two.astype(jnp.float32), shift_two.astype(jnp.float32)
    )
    grad_stream_part, grad_gain_two, grad_shift_two = norm_pull_two(grad_normed_two)
    grad_stream_one = upstream + grad_stream_part
    branch_one = grad_stream_one.astype(jnp.bfloat16)
    grad_bias_out = jnp.sum(branch_one.astype(jnp.float32), axis=0)
    grad_w_out = contract_rows(mixed, branch_one)
    grad_mixed = contract_cols(branch_one, w_out).astype(jnp.bfloat16)
    global_rows = G_DEV * GLEN
    grad_global = attend_back(
        projected[:global_rows, :D],
        projected[:global_rows, D : 2 * D],
        projected[:global_rows, 2 * D :],
        global_total,
        grad_mixed[:global_rows],
        G_DEV,
        GLEN,
    )
    grad_local = attend_back(
        projected[global_rows:, :D],
        projected[global_rows:, D : 2 * D],
        projected[global_rows:, 2 * D :],
        local_total,
        grad_mixed[global_rows:],
        L_DEV,
        LLEN,
    )
    grad_projected = jnp.concatenate([grad_global, grad_local], axis=0).astype(jnp.bfloat16)
    column_sums = jnp.sum(grad_projected.astype(jnp.float32), axis=0)
    grad_bias_query = column_sums[:D]
    grad_bias_value = column_sums[2 * D :]
    grad_w_qkv = contract_rows(normed, grad_projected)
    grad_normed = contract_cols(grad_projected, w_qkv)
    unused_one, norm_pull_one = jax.vjp(
        norm_rows, stream, gain_one.astype(jnp.float32), shift_one.astype(jnp.float32)
    )
    grad_input_part, grad_gain_one, grad_shift_one = norm_pull_one(grad_normed)
    grad_stream = grad_stream_one + grad_input_part
    grads = (
        grad_gain_one,
        grad_shift_one,
        grad_w_qkv,
        grad_bias_query,
        grad_bias_value,
        grad_w_out,
        grad_bias_out,
        grad_gain_two,
        grad_shift_two,
        grad_w_up,
        grad_bias_up,
        grad_w_down,
        grad_bias_down,
    )
    return (grad_stream, grads)


def local(
    tokens,
    cotangent,
    norm1_gain,
    norm1_bias,
    qkv_weight,
    query_bias,
    value_bias,
    out_weight,
    out_bias,
    norm2_gain,
    norm2_bias,
    up_weight,
    up_bias,
    down_weight,
    down_bias,
):
    shards = (
        norm1_gain,
        norm1_bias,
        qkv_weight,
        query_bias,
        value_bias,
        out_weight,
        out_bias,
        norm2_gain,
        norm2_bias,
        up_weight,
        up_bias,
        down_weight,
        down_bias,
    )
    layer_total = qkv_weight.shape[0]
    stream = tokens.astype(jnp.float32)
    saved_layers = []
    kept_weights = []
    for layer_index in range(layer_total):
        weights = gather_forward(tuple((w[layer_index] for w in shards)))
        stream, saved_state = forward_layer(stream, weights)
        saved_layers.append(saved_state)
        kept_weights.append(weights)
    encoded = stream.astype(jnp.bfloat16)
    upstream = cotangent.astype(jnp.float32)
    reduced_layers = [None] * layer_total
    for layer_index in reversed(range(layer_total)):
        upstream, grads = backward_layer(
            upstream, kept_weights[layer_index], saved_layers[layer_index]
        )
        reduced_layers[layer_index] = reduce_grads(grads)
    stacked = tuple(
        (
            jnp.stack(
                [reduced_layers[layer_index][member] for layer_index in range(layer_total)], axis=0
            )
            for member in range(13)
        )
    )
    return (
        encoded,
        upstream,
        stacked[0],
        stacked[1],
        stacked[2],
        stacked[3],
        stacked[4],
        stacked[5],
        stacked[6],
        stacked[7],
        stacked[8],
        stacked[9],
        stacked[10],
        stacked[11],
        stacked[12],
    )


VMEM_BYTES = 65408 * 1024

MESH = pl.DeviceIdType.MESH
F32 = jnp.float32
BF16 = jnp.bfloat16

FF = 3072
ROWS = 345
PAD = 352
STEP = 32
UNROLL = True
SHARD = 96
HALF = 48
UNITS = 12
SLOTS = 6
CORE_SLOTS = 4
RING = 8
PARTS = 2
WIDE = D // PARTS
LAG_XY, LAG_LAST, LAG_Z1, LAG_Z2, LAG_OUT = 4, 6, 8, 10, 12
LAG_NEXT, LAG_PLANE, LAG_PASS, LAG_WHOLE = 2, 4, 8, 9
EARLY_UNITS = 2
EARLY_PIECES = EARLY_UNITS * PARTS
GAP = 3
EARLY = 3
VEC_EVERY = 4
TOP_ROWS = 208
KEYS = 256
LOW_KEY = PAD - KEYS
LOW_ROWS = PAD - TOP_ROWS
V_G1, V_B1, V_QB, V_VB, V_OB, V_G2, V_B2, V_DB, V_UB = range(9)


def nt(left, right):
    return lax.dot_general(left, right, (((1,), (1,)), ((), ())), preferred_element_type=F32)


def tn(left, right):
    return lax.dot_general(left, right, (((0,), (0,)), ((), ())), preferred_element_type=F32)


def nn(left, right):
    return lax.dot_general(left, right, (((1,), (0,)), ((), ())), preferred_element_type=F32)


def aligned(value, by):
    return value if isinstance(value, int) else pl.multiple_of(value, by)


def shift(value, by):
    return lax.shift_right_arithmetic(value, jnp.int32(by))


def low_bits(value, by):
    return value - shift(value, by) * (1 << by)


def power_above(value):
    return (value - 1).bit_length()


def backward_unit(layers, index):
    whole = shift(index, 1)
    half = index - PARTS * whole
    turn = shift(whole * 43, 9)
    place = whole - UNITS * turn
    part = shift(place, 2)
    within = place - 4 * part
    is_down, is_late = shift(2 - part, 1), shift(part, 1)
    late = low_bits(within + 3, 2)
    unit = is_down * 8 + (1 - is_late) * place + is_late * late
    return layers - 1 - turn, unit, half


def stats(x):
    mean = jnp.mean(x, axis=-1, keepdims=True)
    centred = x - mean
    scale = lax.rsqrt(jnp.mean(centred * centred, axis=-1, keepdims=True) + epsilon)
    return centred * scale, scale


def fold(x):
    return jnp.sum(x.reshape(x.shape[0] // 8, 8, x.shape[1]), axis=0)


def total(x):
    return jnp.sum(x, axis=0, keepdims=True)


def step_rows(step):
    return pl.ds(aligned(step * STEP, STEP), STEP)


def encoder_kernel(
    layers,
    tokens,
    cotangent,
    n_g1,
    n_b1,
    n_qb,
    n_vb,
    n_ob,
    n_g2,
    n_b2,
    n_db,
    n_ub,
    w_qkv,
    w_out,
    w_up,
    w_down,
    encoded,
    tokens_grad,
    g_vec,
    g_qkv,
    g_out,
    g_up,
    g_down,
    wb,
    xs,
    x1,
    nr,
    pj,
    mx,
    n2,
    hd,
    gp,
    lse,
    gb,
    gm,
    br,
    acc,
    kacc,
    vacc,
    mask_top,
    mask_low,
    vsg,
    vec,
    ubs,
    gv,
    gvs,
    vr,
    vz,
    held,
    held_cot,
    held_grad,
    rc,
    r2,
    rz,
    ag_sem,
    ag_send,
    own_sem,
    core_sem,
    xy_sem,
    last_sem,
    z_sem,
    s0_send,
    rs_send,
    out_sem,
    vec_sem,
    gv_sem,
    io_sem,
):
    count = layers * UNITS
    pieces = count * PARTS
    d = lax.axis_index("dp")
    f = lax.axis_index("fsdp")
    c = lax.rem(f, 2)
    x = lax.rem(lax.div(f, 2), 2)
    y = lax.div(f, 4)
    fc = f + 1 - 2 * c
    fx = f + 2 - 4 * x
    fy = f + 4 - 8 * y
    outer = d * (3 - d) == 0
    inner = d * (3 - d) != 0
    z_in = 1 + lax.div(d, 3)
    z_out = 3 * lax.div(d, 2)
    z_pair = 3 - d
    parity = lax.rem(d, 2)
    z_near = d + 1 - 2 * parity
    in_plane = lambda who: {"fsdp": who}
    along = lambda who: {"dp": who}
    both = lambda a, b: jnp.logical_and(a, b)

    first_rows = pl.ds(0, HALF)
    second_rows = pl.ds(HALF, HALF)

    def send(source, target, sent, landed, who):
        pltpu.make_async_remote_copy(
            src_ref=source,
            dst_ref=target,
            send_sem=sent,
            recv_sem=landed,
            device_id=who,
            device_id_type=MESH,
        ).start()

    def wait_blocks(sem, blocks):
        span = wb.at[pl.ds(0, blocks), 0, 0, 0]
        pltpu.make_async_copy(span, span, sem).wait()

    def wait_half(sem):
        span = wb.at[0, 0, 0, 0, pl.ds(0, HALF)]
        pltpu.make_async_copy(span, span, sem).wait()

    def wait_piece(sem, blocks):
        span = wb.at[pl.ds(0, blocks), 0, 0, 0, :, pl.ds(0, WIDE)]
        pltpu.make_async_copy(span, span, sem).wait()

    barrier = pltpu.get_barrier_semaphore()
    peers = [lax.rem(f + hop, 8) for hop in range(1, 8)]
    for peer in peers:
        pl.semaphore_signal(barrier, inc=1, device_id=in_plane(peer), device_id_type=MESH)

    @pl.when(outer)
    def _():
        pl.semaphore_signal(barrier, inc=1, device_id=along(z_in), device_id_type=MESH)

    @pl.when(inner)
    def _():
        pl.semaphore_signal(barrier, inc=1, device_id=along(z_out), device_id_type=MESH)
        pl.semaphore_signal(barrier, inc=1, device_id=along(z_pair), device_id_type=MESH)

    for layer in range(layers):
        for unit in range(UNITS):
            if unit < 3:
                source = w_qkv.at[layer, :, pl.ds(unit * D, D)]
            elif unit == 3:
                source = w_out.at[layer]
            elif unit < 8:
                source = w_up.at[layer, :, pl.ds((unit - 4) * D, D)]
            else:
                source = w_down.at[layer, pl.ds((unit - 8) * SHARD, SHARD)]
            pltpu.make_async_copy(
                source,
                wb.at[layer * UNITS + unit, y, x, c],
                own_sem.at[layer],
            ).start()
    small = acc.at[0 : 16 * layers, 0:128]
    small[...] = jnp.zeros((16 * layers, 128), F32)
    for at, source in enumerate((n_g1, n_b1, n_qb, n_vb, n_ob, n_g2, n_b2, n_db)):
        shard = source[...].astype(F32)
        for layer in range(layers):
            row = 8 * layer + at
            acc[row : row + 1, 0:SHARD] = shard[layer : layer + 1]
    shard = n_ub[...].astype(F32)
    for layer in range(layers):
        for third in range(3):
            row = 8 * layers + 3 * layer + third
            acc[row : row + 1, 0:128] = shard[layer : layer + 1, third * 128 : third * 128 + 128]
    vsg[f] = small[...].astype(BF16)
    tokens_in = pltpu.make_async_copy(tokens, held, io_sem.at[0])
    cotangent_in = pltpu.make_async_copy(cotangent, held_cot, io_sem.at[1])
    encoded_out = pltpu.make_async_copy(held, encoded, io_sem.at[2])
    tokens_out = pltpu.make_async_copy(held_grad, tokens_grad, io_sem.at[3])
    tokens_in.start()
    cotangent_in.start()
    gvs[...] = jnp.zeros((8, 16, 128), F32)
    pl.semaphore_wait(barrier, 8 + lax.div(d * (3 - d), 2))

    def role(i):
        bits = power_above(count)
        of_three = i - 3 * shift(i * 43, 7)
        return of_three * shift((1 << bits) + count - 3 - i, bits)

    def collects(i):
        return role(i) != 2 - parity

    def gather_tick(t):
        @pl.when(t < count)
        def _():
            own = wb.at[t, y, x, c]

            @pl.when(lax.rem(t, UNITS) == 0)
            def _():
                wait_blocks(own_sem.at[lax.div(t, UNITS)], UNITS)

            @pl.when(collects(t))
            def _():
                first = wb.at[t, y, x, c, first_rows]
                second = wb.at[t, y, x, c, second_rows]
                send(first, first, ag_send.at[0], ag_sem.at[t, 0], in_plane(fy))
                send(second, second, ag_send.at[0], ag_sem.at[t, 1], in_plane(fx))
                send(first, first, ag_send.at[0], ag_sem.at[t, 2], in_plane(fx))
                send(second, second, ag_send.at[0], ag_sem.at[t, 2], in_plane(fy))

            send(own, own, ag_send.at[0], ag_sem.at[t, 3], in_plane(fc))

        @pl.when(both(both(t >= LAG_NEXT, t < count + LAG_NEXT), collects(t - LAG_NEXT)))
        def _():
            i = t - LAG_NEXT
            wait_half(ag_sem.at[i, 0])
            wait_half(ag_sem.at[i, 1])
            first = wb.at[i, 1 - y, x, c, first_rows]
            second = wb.at[i, y, 1 - x, c, second_rows]
            send(first, first, ag_send.at[0], ag_sem.at[i, 2], in_plane(fx))
            send(second, second, ag_send.at[0], ag_sem.at[i, 2], in_plane(fy))

        @pl.when(both(both(t >= LAG_PLANE, t < count + LAG_PLANE), collects(t - LAG_PLANE)))
        def _():
            i = t - LAG_PLANE
            wait_blocks(ag_sem.at[i, 2], 2)
            for piece in (wb.at[i, 1 - y, :, c], wb.at[i, y, 1 - x, c]):

                @pl.when(role(i) > 0)
                def _(piece=piece):
                    send(piece, piece, ag_send.at[0], ag_sem.at[i, 0], along(z_near))

                send(piece, piece, ag_send.at[0], ag_sem.at[i, 3], in_plane(fc))

        @pl.when(both(both(t >= LAG_PASS, t < count + LAG_PASS), role(t - LAG_PASS) == 2 - parity))
        def _():
            i = t - LAG_PASS
            wait_blocks(ag_sem.at[i, 0], 3)
            for piece in (wb.at[i, 1 - y, :, c], wb.at[i, y, 1 - x, c]):
                send(piece, piece, ag_send.at[0], ag_sem.at[i, 3], in_plane(fc))

        @pl.when(both(t >= LAG_WHOLE, t < count + LAG_WHOLE))
        def _():
            wait_blocks(ag_sem.at[t - LAG_WHOLE, 3], 4)

    for peer in peers:
        send(vsg.at[f], vsg.at[f], vec_sem.at[0], vec_sem.at[1], in_plane(peer))

    @pl.loop(0, EARLY)
    def _(t):
        gather_tick(t)

    def crop_of(shape, dim, start):
        at = lax.broadcasted_iota(jnp.int32, shape, dim) + start
        which = jnp.zeros(shape, jnp.int32)
        for edge in range(L_DEV + 1):
            which = which + (at >= GLEN + edge * LLEN).astype(jnp.int32)
        return which

    for mask, rows, row_at, key_at in (
        (mask_top, TOP_ROWS, 0, 0),
        (mask_low, LOW_ROWS, TOP_ROWS, LOW_KEY),
    ):
        same = crop_of((rows, KEYS), 0, row_at) == crop_of((rows, KEYS), 1, key_at)
        mask[...] = jnp.where(same, 0.0, -1e30).astype(F32)

    xs[0, PAD - 8 :, :] = jnp.zeros((8, D), F32)
    tokens_in.wait()
    xs[0, 0:ROWS, :] = held[...].astype(F32)

    seven = vsg.at[pl.ds(0, 7)]
    pltpu.make_async_copy(seven, seven, vec_sem.at[1]).wait()
    spread = jnp.zeros((8 * layers, D), F32)
    for owner in range(8):
        at_row = lax.broadcasted_iota(jnp.int32, (128, D), 0)
        at_col = lax.broadcasted_iota(jnp.int32, (128, D), 1)
        hit = jnp.logical_and(at_col == at_row + owner * SHARD, at_row < SHARD)
        spread = spread + nn(vsg[owner, 0 : 8 * layers, :], jnp.where(hit, 1.0, 0.0).astype(BF16))
        wide = vsg[owner, 8 * layers :, :].astype(F32)
        for layer in range(layers):
            for third in range(3):
                row, lane = 3 * layer + third, owner * 4 * SHARD + third * 128
                ubs[layer : layer + 1, lane : lane + 128] = wide[row : row + 1]
    vec[...] = spread

    @pl.loop(EARLY, LAG_WHOLE)
    def _(t):
        gather_tick(t)

    def vector(layer, which):
        return vec[pl.ds(layer * 8 + which, 1), :]

    lane = lax.broadcasted_iota(jnp.int32, (1, 128), 1)
    left_lane = lane < HEAD_DIM
    score_scale = HEAD_DIM ** (-0.5)
    head_scaled = [
        jnp.where(left_lane, score_scale, 0.0).astype(BF16),
        jnp.where(left_lane, 0.0, score_scale).astype(BF16),
    ]
    head_plain = [
        jnp.where(left_lane, 1.0, 0.0).astype(BF16),
        jnp.where(left_lane, 0.0, 1.0).astype(BF16),
    ]
    groups = (
        (0, TOP_ROWS, 0, mask_top),
        (TOP_ROWS, LOW_ROWS, LOW_KEY, mask_low),
    )

    def weight(layer, unit):
        return wb[layer * UNITS + unit].reshape(D, D)

    def down_places(part):
        return [(unit, lax.div(part, 2), lax.rem(part, 2), core) for core in range(2) for unit in range(4)]

    def down_weight(layer, part):
        blocks = [wb[layer * UNITS + 8 + u, yy, xx, cc] for u, yy, xx, cc in down_places(part)]
        return jnp.concatenate(blocks, axis=0)

    def put_down(first, units, part, grad):
        for at, (u, yy, xx, cc) in enumerate(down_places(part)):
            if u < units:
                wb[first + u, yy, xx, cc] = grad[at * SHARD : (at + 1) * SHARD]

    def piece_at(i):
        layer, unit, half = backward_unit(layers, i)
        bits = power_above(pieces)
        early = shift((1 << bits) + EARLY_PIECES - 1 - i, bits)
        ahead = layers * UNITS + shift(i, 1)
        at = early * ahead + (1 - early) * (layer * UNITS + unit)
        return at, pl.ds(aligned(half * WIDE, 128), WIDE)

    def during(t, lag):
        at = t - lag
        begun = jnp.logical_or(at < EARLY_PIECES, at >= EARLY_PIECES + GAP)
        return both(begun, both(at >= 0, at < pieces + GAP))

    def piece_of(t, lag):
        at = t - lag
        bits = power_above(2 * pieces)
        return at - GAP * shift(at + (1 << bits) - (EARLY_PIECES + GAP), bits)

    def ring(i):
        return low_bits(i, 3)

    def long_ring(i):
        return low_bits(i, 4)

    def slot_of(i):
        return i - SLOTS * shift(i * 43, 8)

    def reduce_tick(t):
        @pl.when(during(t, 0))
        def _():
            i = piece_of(t, 0)
            n, cols = piece_at(i)
            send(
                wb.at[n, :, :, 1 - c, :, cols],
                rc.at[low_bits(i, 2)],
                s0_send.at[ring(i)],
                core_sem.at[ring(i)],
                in_plane(fc),
            )

        @pl.when(during(t, LAG_XY))
        def _():
            i = piece_of(t, LAG_XY)
            n, cols = piece_at(i)
            slot = slot_of(i)
            wait_piece(xy_sem.at[ring(i)], 2)
            along_x = wb.at[n, :, x, c, first_rows, cols]
            along_y = wb.at[n, y, :, c, second_rows, cols]
            along_x[...] = along_x[...] + r2[slot, 0]
            along_y[...] = along_y[...] + r2[slot, 1]
            send(
                wb.at[n, 1 - y, x, c, first_rows, cols],
                wb.at[n, 1 - y, x, 1 - c, first_rows, cols],
                rs_send.at[long_ring(i)],
                last_sem.at[ring(i)],
                in_plane(fy),
            )
            send(
                wb.at[n, y, 1 - x, c, second_rows, cols],
                wb.at[n, y, 1 - x, 1 - c, second_rows, cols],
                rs_send.at[long_ring(i)],
                last_sem.at[ring(i)],
                in_plane(fx),
            )

        @pl.when(during(t, 1))
        def _():
            i = piece_of(t, 1)
            n, cols = piece_at(i)
            slot = slot_of(i)
            wait_piece(core_sem.at[ring(i)], 4)
            wait_piece(s0_send.at[ring(i)], 4)
            mine = wb.at[n, :, :, c, :, cols]
            mine[...] = mine[...] + rc[low_bits(i, 2)]
            send(
                wb.at[n, :, 1 - x, c, first_rows, cols],
                r2.at[slot, 0],
                rs_send.at[long_ring(i)],
                xy_sem.at[ring(i)],
                in_plane(fx),
            )
            send(
                wb.at[n, 1 - y, :, c, second_rows, cols],
                r2.at[slot, 1],
                rs_send.at[long_ring(i)],
                xy_sem.at[ring(i)],
                in_plane(fy),
            )

        @pl.when(during(t, LAG_OUT))
        def _():
            i = piece_of(t, LAG_OUT)
            n, cols = piece_at(i)
            layer, unit, half = backward_unit(layers, i)

            @pl.when(outer)
            def _():
                wait_piece(z_sem.at[ring(i), 2], 1)

            done = wb.at[n, y, x, 1 - c, :, cols]

            @pl.when(outer)
            def _():
                wait_piece(rs_send.at[long_ring(i)], 4)

            @pl.when(inner)
            def _():
                wait_piece(rs_send.at[long_ring(i)], 5)

            @pl.when(i >= RING)
            def _():
                wait_piece(out_sem.at[ring(i)], 1)

            def emit(target):
                pltpu.make_async_copy(done, target, out_sem.at[ring(i)]).start()

            def wide_at(first):
                return pl.ds(aligned((unit - first) * D + half * WIDE, 128), WIDE)

            @pl.when(unit < 3)
            def _():
                emit(g_qkv.at[layer, :, wide_at(0)])

            @pl.when(unit == 3)
            def _():
                emit(g_out.at[layer, :, cols])

            @pl.when(both(unit >= 4, unit < 8))
            def _():
                emit(g_up.at[layer, :, wide_at(4)])

            @pl.when(unit >= 8)
            def _():
                rows = pl.ds(aligned((unit - 8) * SHARD, 16), SHARD)
                emit(g_down.at[layer, rows, cols])

        @pl.when(during(t, LAG_LAST))
        def _():
            i = piece_of(t, LAG_LAST)
            n, cols = piece_at(i)
            wait_piece(last_sem.at[ring(i)], 1)
            own = wb.at[n, y, x, c, :, cols]
            own[...] = own[...] + wb[n, y, x, 1 - c, :, cols]

            @pl.when(outer)
            def _():
                to = rz.at[slot_of(i), 0]
                send(own, to, rs_send.at[long_ring(i)], z_sem.at[ring(i), 0], along(z_in))

        @pl.when(both(inner, during(t, LAG_Z1)))
        def _():
            i = piece_of(t, LAG_Z1)
            n, cols = piece_at(i)
            slot = slot_of(i)
            wait_piece(z_sem.at[ring(i), 0], 1)
            own = wb.at[n, y, x, c, :, cols]
            own[...] = own[...] + rz[slot, 0]
            send(own, rz.at[slot, 1], rs_send.at[long_ring(i)], z_sem.at[ring(i), 1], along(z_pair))

        @pl.when(both(inner, during(t, LAG_Z2)))
        def _():
            i = piece_of(t, LAG_Z2)
            n, cols = piece_at(i)
            wait_piece(z_sem.at[ring(i), 1], 1)
            done = wb.at[n, y, x, 1 - c, :, cols]
            done[...] = wb[n, y, x, c, :, cols] + rz[slot_of(i), 1]
            send(done, done, rs_send.at[long_ring(i)], z_sem.at[ring(i), 2], along(z_out))

    @pl.loop(0, layers)
    def _(layer):
        base = layer * UNITS + LAG_WHOLE

        @pl.loop(0, PAD // STEP, unroll=UNROLL)
        def _(step):
            rows = step_rows(step)
            normed, _unused = stats(xs[layer, rows, :])
            nr[layer, rows, :] = (normed * vector(layer, V_G1) + vector(layer, V_B1)).astype(BF16)

        @pl.loop(0, 3)
        def _(part):
            gather_tick(base + part)
            is_q, is_v = lax.div(2 - part, 2), lax.div(part, 2)
            bias = is_q.astype(F32) * vector(layer, V_QB) + is_v.astype(F32) * vector(layer, V_VB)
            acc[...] = nn(nr[layer], weight(layer, part))

            @pl.loop(0, PAD // STEP, unroll=UNROLL)
            def _(step):
                rows = step_rows(step)
                pj[layer, part, rows, :] = (acc[rows, :] + bias).astype(BF16)

        @pl.loop(0, HEADS // 2)
        def _(pair):
            @pl.when(pair == 3)
            def _():
                gather_tick(base + 3)

            lanes = pl.ds(aligned(pair * 128, 128), 128)
            for row_at, rows, key_at, mask in groups:
                here = pl.ds(row_at, rows)
                keys = pj[layer, 1, pl.ds(key_at, KEYS), lanes]
                values = pj[layer, 2, pl.ds(key_at, KEYS), lanes]
                queries = pj[layer, 0, here, lanes]
                results = []
                for side in range(2):
                    scores = nt(queries * head_scaled[side], keys) + mask[...]
                    peak = jnp.max(scores, axis=-1, keepdims=True)
                    raised = jnp.exp(scores - peak)
                    exp_total = jnp.sum(raised, axis=-1, keepdims=True)
                    probs = (raised * (1.0 / exp_total)).astype(BF16)
                    results.append(nn(probs, values))
                    log_total = peak + jnp.log(exp_total)
                    lse[layer, here, :] = jnp.where(
                        lane == pair * 2 + side, log_total, lse[layer, here, :]
                    )
                mx[layer, here, lanes] = jnp.where(left_lane, results[0], results[1]).astype(BF16)

        acc[...] = nn(mx[layer], weight(layer, 3))

        @pl.loop(0, PAD // STEP, unroll=UNROLL)
        def _(step):
            rows = step_rows(step)
            now = xs[layer, rows, :] + acc[rows, :] + vector(layer, V_OB)
            x1[layer, rows, :] = now
            normed, _unused = stats(now)
            n2[layer, rows, :] = (normed * vector(layer, V_G2) + vector(layer, V_B2)).astype(BF16)

        @pl.when(layer == layers - 1)
        def _():
            acc[PAD - 8 :, :] = jnp.zeros((8, D), F32)
            cotangent_in.wait()
            acc[0:ROWS, :] = held_cot[...].astype(F32)
            br[...] = acc[...].astype(BF16)

        @pl.loop(0, 4)
        def _(part):
            gather_tick(base + 4 + part)
            bias = ubs[pl.ds(layer, 1), pl.ds(aligned(part * D, 128), D)]
            acc[...] = nn(n2[layer], weight(layer, 4 + part))

            @pl.loop(0, PAD // STEP, unroll=UNROLL)
            def _(step):
                rows = step_rows(step)
                pre = acc[rows, :] + bias
                cdf = 0.5 + 0.5 * lax.erf(pre * (0.5**0.5))
                bell = jnp.exp(-0.5 * pre * pre) * 0.3989422804014327
                hd[layer, part, rows, :] = (pre * cdf).astype(BF16)
                gp[layer, part, rows, :] = (cdf + pre * bell).astype(BF16)

            @pl.when(layer == layers - 1)
            def _():
                grad = tn(hd[layer, part], br[...]).astype(BF16)
                put_down(layers * UNITS, EARLY_UNITS, part, grad)

        @pl.loop(0, 4)
        def _(part):
            gather_tick(base + 8 + part)

        @pl.when(layer == layers - 1)
        def _():
            @pl.loop(0, 2)
            def _(t):
                reduce_tick(t)

        acc[...] = x1[layer] + vector(layer, V_DB)

        @pl.loop(0, 4)
        def _(part):
            acc[...] += nn(hd[layer, part], down_weight(layer, part))

        xs[layer + 1] = acc[...]

    reduce_tick(2)
    held[...] = xs[layers, 0:ROWS, :].astype(BF16)
    encoded_out.start()

    span = wb.at[pl.ds(0, 7 * count // 8)]
    pltpu.make_async_copy(span, span, ag_send.at[0]).wait()
    pltpu.make_async_copy(seven, seven, vec_sem.at[0]).wait()

    def vector_step(layer, step):
        def wait_vec(at, copies):
            span = gvs.at[pl.ds(0, copies)]
            pltpu.make_async_copy(span, span, gv_sem.at[layer, at]).wait()

        def z_go(source, target, at, who):
            send(
                vz.at[layer, source],
                vz.at[layer, target],
                gv_sem.at[layer, at],
                gv_sem.at[layer, at + 1],
                along(who),
            )

        @pl.when(step == 0)
        def _():
            for owner in range(8):
                gvs[owner, 0:8, 0:SHARD] = gv[layer, 0:8, owner * SHARD : (owner + 1) * SHARD]
                row = 8 + owner // 2
                for third in range(3):
                    lane = (owner % 2) * 4 * SHARD + third * 128
                    wide = gv[layer, row : row + 1, lane : lane + 128]
                    gvs[owner, 8 + third : 9 + third, :] = wide
            vr[layer, f] = gvs[f]
            for peer in peers:
                send(
                    gvs.at[peer],
                    vr.at[layer, f],
                    gv_sem.at[layer, 0],
                    gv_sem.at[layer, 1],
                    in_plane(peer),
                )

        @pl.when(step == 1)
        def _():
            wait_vec(0, 7)
            wait_vec(1, 7)
            in_sum = vr[layer, 0]
            for source in range(1, 8):
                in_sum = in_sum + vr[layer, source]
            vz[layer, 0] = in_sum

            @pl.when(outer)
            def _():
                z_go(0, 1, 2, z_in)

        @pl.when(both(inner, step == 2))
        def _():
            wait_vec(3, 1)
            vz[layer, 0] = vz[layer, 0] + vz[layer, 1]
            z_go(0, 2, 4, z_pair)

        @pl.when(both(inner, step == 3))
        def _():
            wait_vec(4, 1)
            wait_vec(5, 1)
            vz[layer, 3] = vz[layer, 0] + vz[layer, 2]
            z_go(3, 3, 6, z_out)

        @pl.when(step == 4)
        def _():
            @pl.when(outer)
            def _():
                wait_vec(2, 1)
                wait_vec(7, 1)

            @pl.when(inner)
            def _():
                wait_vec(6, 1)

            g_vec[layer] = vz[layer, 3]

    up = xs.at[layers]
    up[PAD - 8 :, :] = jnp.zeros((8, D), F32)
    up[0:ROWS, :] = held_cot[...].astype(F32)
    none = jnp.zeros((8, D), F32)

    def put_vector(layer, which, value):
        gv[layer, pl.ds(which, 1), :] = total(value)

    def weight_grad(unit, left, right):
        grad = tn(left[...], right[...]).astype(BF16)
        wb[unit] = grad.reshape(2, 2, 2, SHARD, D)

    @pl.loop(0, layers)
    def _(turn):
        layer = layers - 1 - turn
        base = EARLY_PIECES + GAP + turn * (UNITS * PARTS - 4)

        def branch_two(step, carry):
            rows = step_rows(step)
            rounded = up[rows, :].astype(BF16)
            br[rows, :] = rounded
            return carry + fold(rounded.astype(F32))

        put_vector(layer, V_DB, lax.fori_loop(0, PAD // STEP, branch_two, none, unroll=UNROLL))

        @pl.loop(0, 4)
        def _(part):
            reduce_tick(base - 4 + part)

            acc[...] = nt(br[...], down_weight(layer, part))

            def through_gelu(step, carry):
                rows = step_rows(step)
                value = (acc[rows, :] * gp[layer, part, rows, :].astype(F32)).astype(BF16)
                gb[part, rows, :] = value
                return carry + fold(value.astype(F32))

            put_vector(layer, V_UB + part, lax.fori_loop(0, PAD // STEP, through_gelu, none, unroll=UNROLL))
            grad = tn(hd[layer, part], br[...]).astype(BF16)
            put_down(layer * UNITS + 8, 4, part, grad)

        acc[...] = jnp.zeros((PAD, D), F32)

        @pl.loop(0, 4)
        def _(part):
            @pl.when(both(turn > 0, part == 0))
            def _():
                vector_step(layer + 1, 0)

            acc[...] += nt(gb[part], weight(layer, 4 + part))
            weight_grad(layer * UNITS + 4 + part, n2.at[layer], gb.at[part])
            reduce_tick(base + part)

        def norm_back(source, gain_at, shift_at):
            def body(step, carry):
                gain_sum, shift_sum = carry
                rows = step_rows(step)
                normed, scale = stats(source[layer, rows, :])
                grad = acc[rows, :]
                t = grad * vector(layer, gain_at)
                inner_mean = jnp.mean(t * normed, axis=-1, keepdims=True)
                back = scale * (t - jnp.mean(t, axis=-1, keepdims=True) - normed * inner_mean)
                up[rows, :] = up[rows, :] + back
                return gain_sum + fold(grad * normed), shift_sum + fold(grad)

            gain_sum, shift_sum = lax.fori_loop(0, PAD // STEP, body, (none, none), unroll=UNROLL)
            put_vector(layer, gain_at, gain_sum)
            put_vector(layer, shift_at, shift_sum)

        norm_back(x1, V_G2, V_B2)

        put_vector(layer, V_OB, lax.fori_loop(0, PAD // STEP, branch_two, none, unroll=UNROLL))
        gm[...] = nt(br[...], weight(layer, 3)).astype(BF16)
        weight_grad(layer * UNITS + 3, mx.at[layer], br)

        @pl.loop(0, 2)
        def _(again):
            reduce_tick(base + 4 + again)

        @pl.loop(0, HEADS // 2)
        def _(pair):
            reduce_tick(base + 6 + pair)

            @pl.when(both(turn > 0, lax.rem(pair, 2) == 0))
            def _():
                vector_step(layer + 1, 1 + lax.div(pair, 2))

            lanes = pl.ds(aligned(pair * 128, 128), 128)
            kacc[...] = jnp.zeros((PAD, 128), F32)
            vacc[...] = jnp.zeros((PAD, 128), F32)
            for row_at, rows, key_at, mask in groups:
                here = pl.ds(row_at, rows)
                there = pl.ds(key_at, KEYS)
                keys = pj[layer, 1, there, lanes]
                values = pj[layer, 2, there, lanes]
                queries = pj[layer, 0, here, lanes]
                grads = gm[here, lanes]
                q_parts, k_parts, v_parts = [], [], []
                for side in range(2):
                    log_total = jnp.sum(
                        jnp.where(lane == pair * 2 + side, lse[layer, here, :], 0.0),
                        axis=-1,
                        keepdims=True,
                    )
                    scaled = queries * head_scaled[side]
                    probs = jnp.exp(nt(scaled, keys) + mask[...] - log_total)
                    grad_probs = nt(grads * head_plain[side], values)
                    row_inner = jnp.sum(grad_probs * probs, axis=-1, keepdims=True)
                    grad_scores = (probs * (grad_probs - row_inner)).astype(BF16)
                    v_parts.append(tn(probs.astype(BF16), grads))
                    k_parts.append(tn(grad_scores, queries))
                    q_parts.append(nn(grad_scores, keys))
                grad_queries = jnp.where(left_lane, q_parts[0], q_parts[1]) * score_scale
                gb[0, here, lanes] = grad_queries.astype(BF16)
                kacc[there, :] += jnp.where(left_lane, k_parts[0], k_parts[1]) * score_scale
                vacc[there, :] += jnp.where(left_lane, v_parts[0], v_parts[1])
            gb[1, :, lanes] = kacc[...].astype(BF16)
            gb[2, :, lanes] = vacc[...].astype(BF16)

        for which, part in ((V_QB, 0), (V_VB, 2)):

            def column_sum(step, carry, part=part):
                return carry + fold(gb[part, step_rows(step), :].astype(F32))

            put_vector(layer, which, lax.fori_loop(0, PAD // STEP, column_sum, none, unroll=UNROLL))

        acc[...] = jnp.zeros((PAD, D), F32)

        @pl.loop(0, 3)
        def _(part):
            acc[...] += nt(gb[part], weight(layer, part))
            weight_grad(layer * UNITS + part, nr.at[layer], gb.at[part])

            reduce_tick(base + 12 + part)

            @pl.when(both(turn > 0, part == 1))
            def _():
                vector_step(layer + 1, 4)

        norm_back(xs, V_G1, V_B1)
        reduce_tick(base + 15)

    held_grad[...] = up[0:ROWS, :]
    tokens_out.start()
    encoded_out.wait()

    @pl.loop(pieces + GAP - 8, pieces + GAP + LAG_OUT)
    def _(t):
        step = t - (pieces + GAP - 8)

        @pl.when(both(lax.rem(step, VEC_EVERY) == 0, step < 5 * VEC_EVERY))
        def _():
            vector_step(0, lax.div(step, VEC_EVERY))

        reduce_tick(t)

    for at in range(RING):
        wait_piece(out_sem.at[at], 1)

    tokens_out.wait()


def closing_kernel(layers, *refs):
    encoded_in, tokens_in, vec_in = refs[:3]
    grads_in = refs[3:7]
    encoded_out, tokens_out = refs[7:9]
    small_out = refs[9:18]
    grads_out = refs[18:22]
    vec = refs[22]
    narrow = refs[23:27]
    wide = refs[27:31]
    held_encoded, held_tokens, few_sem, in_sem, out_sem = refs[31:]
    copies = [
        pltpu.make_async_copy(vec_in, vec, few_sem.at[0]),
        pltpu.make_async_copy(encoded_in, held_encoded, few_sem.at[1]),
        pltpu.make_async_copy(tokens_in, held_tokens, few_sem.at[2]),
    ]
    reads, writes = [], []
    for layer in range(layers):
        for at in range(4):
            reads.append(
                pltpu.make_async_copy(
                    grads_in[at].at[layer], narrow[at].at[layer], in_sem.at[at, layer]
                )
            )
            writes.append(
                pltpu.make_async_copy(
                    wide[at].at[layer], grads_out[at].at[layer], out_sem.at[at, layer]
                )
            )
    for copy in reads + copies:
        copy.start()
    for layer in range(layers):
        for at in range(4):
            reads[4 * layer + at].wait()
            wide[at][layer] = narrow[at][layer].astype(F32)
            writes[4 * layer + at].start()
    for copy in copies:
        copy.wait()
    writes.append(pltpu.make_async_copy(held_encoded, encoded_out, few_sem.at[1]))
    writes.append(pltpu.make_async_copy(held_tokens, tokens_out, few_sem.at[2]))
    writes[-2].start()
    writes[-1].start()
    for layer in range(layers):
        mine = vec[layer]
        for which in range(8):
            small_out[which][layer : layer + 1, :] = mine[which : which + 1, 0:SHARD]
        for third in range(3):
            lanes = slice(third * 128, third * 128 + 128)
            small_out[8][layer : layer + 1, lanes] = mine[8 + third : 9 + third]
    for copy in writes:
        copy.wait()


def kernel_local(
    tokens,
    cotangent,
    norm1_gain,
    norm1_bias,
    qkv_weight,
    query_bias,
    value_bias,
    out_weight,
    out_bias,
    norm2_gain,
    norm2_bias,
    up_weight,
    up_bias,
    down_weight,
    down_bias,
):
    layers = qkv_weight.shape[0]
    count = layers * UNITS
    pieces = count * PARTS
    hbm = pl.BlockSpec(memory_space=pltpu.MemorySpace.HBM)
    plain = pl.BlockSpec()
    dma = pltpu.SemaphoreType.DMA
    results = pl.pallas_call(
        functools.partial(encoder_kernel, layers),
        out_shape=(
            jax.ShapeDtypeStruct((ROWS, D), BF16),
            jax.ShapeDtypeStruct((ROWS, D), F32),
            jax.ShapeDtypeStruct((layers, 16, 128), F32),
            jax.ShapeDtypeStruct((layers, SHARD, 3 * D), BF16),
            jax.ShapeDtypeStruct((layers, SHARD, D), BF16),
            jax.ShapeDtypeStruct((layers, SHARD, FF), BF16),
            jax.ShapeDtypeStruct((layers, 4 * SHARD, D), BF16),
        ),
        in_specs=[hbm] * 2 + [plain] * 9 + [hbm] * 4,
        out_specs=(hbm, hbm, plain, hbm, hbm, hbm, hbm),
        scratch_shapes=[
            pltpu.VMEM((count + EARLY_UNITS, 2, 2, 2, SHARD, D), BF16),
            pltpu.VMEM((layers + 1, PAD, D), F32),
            pltpu.VMEM((layers, PAD, D), F32),
            pltpu.VMEM((layers, PAD, D), BF16),
            pltpu.VMEM((layers, 3, PAD, D), BF16),
            pltpu.VMEM((layers, PAD, D), BF16),
            pltpu.VMEM((layers, PAD, D), BF16),
            pltpu.VMEM((layers, 4, PAD, D), BF16),
            pltpu.VMEM((layers, 4, PAD, D), BF16),
            pltpu.VMEM((layers, PAD, 128), F32),
            pltpu.VMEM((4, PAD, D), BF16),
            pltpu.VMEM((PAD, D), BF16),
            pltpu.VMEM((PAD, D), BF16),
            pltpu.VMEM((PAD, D), F32),
            pltpu.VMEM((PAD, 128), F32),
            pltpu.VMEM((PAD, 128), F32),
            pltpu.VMEM((TOP_ROWS, KEYS), F32),
            pltpu.VMEM((LOW_ROWS, KEYS), F32),
            pltpu.VMEM((8, 16 * layers, 128), BF16),
            pltpu.VMEM((8 * layers, D), F32),
            pltpu.VMEM((layers, FF), F32),
            pltpu.VMEM((layers, 16, D), F32),
            pltpu.VMEM((8, 16, 128), F32),
            pltpu.VMEM((layers, 8, 16, 128), F32),
            pltpu.VMEM((layers, 4, 16, 128), F32),
            pltpu.VMEM((ROWS, D), BF16),
            pltpu.VMEM((ROWS, D), BF16),
            pltpu.VMEM((ROWS, D), F32),
            pltpu.VMEM((CORE_SLOTS, 2, 2, SHARD, WIDE), BF16),
            pltpu.VMEM((SLOTS, 2, 2, HALF, WIDE), BF16),
            pltpu.VMEM((SLOTS, 2, SHARD, WIDE), BF16),
            dma((count, 4)),
            dma((1,)),
            dma((layers,)),
            dma((RING,)),
            dma((RING,)),
            dma((RING,)),
            dma((RING, 3)),
            dma((RING,)),
            dma((2 * RING,)),
            dma((RING,)),
            dma((2,)),
            dma((layers, 8)),
            dma((4,)),
        ],
        compiler_params=pltpu.CompilerParams(
            collective_id=0, has_side_effects=True, vmem_limit_bytes=VMEM_BYTES
        ),
    )(
        tokens,
        cotangent,
        norm1_gain,
        norm1_bias,
        query_bias,
        value_bias,
        out_bias,
        norm2_gain,
        norm2_bias,
        down_bias,
        up_bias,
        qkv_weight,
        out_weight,
        up_weight,
        down_weight,
    )
    shapes = [(layers, SHARD)] * 8 + [(layers, 4 * SHARD)]
    shapes += [(layers, SHARD, 3 * D), (layers, SHARD, D), (layers, SHARD, FF)]
    shapes += [(layers, 4 * SHARD, D)]
    closing = pl.pallas_call(
        functools.partial(closing_kernel, layers),
        out_shape=[jax.ShapeDtypeStruct((ROWS, D), BF16), jax.ShapeDtypeStruct((ROWS, D), F32)]
        + [jax.ShapeDtypeStruct(shape, F32) for shape in shapes],
        in_specs=[hbm] * 7,
        out_specs=[hbm] * 2 + [plain] * 9 + [hbm] * 4,
        scratch_shapes=[pltpu.VMEM((layers, 16, 128), F32)]
        + [pltpu.VMEM(shape, BF16) for shape in shapes[9:]]
        + [pltpu.VMEM(shape, F32) for shape in shapes[9:]]
        + [pltpu.VMEM((ROWS, D), BF16), pltpu.VMEM((ROWS, D), F32)]
        + [dma((3,)), dma((4, layers)), dma((4, layers))],
        compiler_params=pltpu.CompilerParams(vmem_limit_bytes=VMEM_BYTES),
    )(*results)
    by = dict(zip(("encoded", "tokens_grad"), closing[:2]))
    small = closing[2:11]
    g_qkv, g_out, g_up, g_down = closing[11:]
    return (
        by["encoded"],
        by["tokens_grad"],
        small[V_G1],
        small[V_B1],
        g_qkv,
        small[V_QB],
        small[V_VB],
        g_out,
        small[V_OB],
        small[V_G2],
        small[V_B2],
        g_up,
        small[V_UB],
        g_down,
        small[V_DB],
    )


def solution(mesh):
    in_specs = (
        P(("dp", "fsdp"), None),
        P(("dp", "fsdp"), None),
        P(None, "fsdp"),
        P(None, "fsdp"),
        P(None, "fsdp", None),
        P(None, "fsdp"),
        P(None, "fsdp"),
        P(None, "fsdp", None),
        P(None, "fsdp"),
        P(None, "fsdp"),
        P(None, "fsdp"),
        P(None, "fsdp", None),
        P(None, "fsdp"),
        P(None, "fsdp", None),
        P(None, "fsdp"),
    )
    out_specs = (
        P(("dp", "fsdp"), None),
        P(("dp", "fsdp"), None),
        P(None, "fsdp"),
        P(None, "fsdp"),
        P(None, "fsdp", None),
        P(None, "fsdp"),
        P(None, "fsdp"),
        P(None, "fsdp", None),
        P(None, "fsdp"),
        P(None, "fsdp"),
        P(None, "fsdp"),
        P(None, "fsdp", None),
        P(None, "fsdp"),
        P(None, "fsdp", None),
        P(None, "fsdp"),
    )
    fits = mesh.shape["dp"] == 4 and mesh.shape["fsdp"] == 8
    body = kernel_local if fits else local
    return jax.shard_map(body, mesh=mesh, in_specs=in_specs, out_specs=out_specs, check_vma=False)
```

```python
import functools

import jax
import jax.numpy as jnp
from jax import lax
from jax.experimental import pallas as pl
from jax.experimental.pallas import tpu as pltpu
from jax.sharding import PartitionSpec as P

D = 768
HEADS = 12
HEAD_DIM = 64
GLEN = 197
LLEN = 37
G_DEV = 1
L_DEV = 4


epsilon = 1e-06


def norm_rows(values_in, gain, shift):
    row_mean = jnp.mean(values_in, axis=-1, keepdims=True)
    centred = values_in - row_mean
    spread = jnp.mean(centred * centred, axis=-1, keepdims=True)
    return centred * lax.rsqrt(spread + epsilon) * gain + shift


def contract_rows(left, right):
    return lax.dot_general(
        left, right, (((0,), (0,)), ((), ())), preferred_element_type=jnp.float32
    )


def contract_cols(left, right):
    return lax.dot_general(
        left, right, (((1,), (1,)), ((), ())), preferred_element_type=jnp.float32
    )


def gather_forward(pieces):
    return (
        lax.all_gather(pieces[0], "fsdp", axis=0, tiled=True),
        lax.all_gather(pieces[1], "fsdp", axis=0, tiled=True),
        lax.all_gather(pieces[2], "fsdp", axis=0, tiled=True),
        lax.all_gather(pieces[3], "fsdp", axis=0, tiled=True),
        lax.all_gather(pieces[4], "fsdp", axis=0, tiled=True),
        lax.all_gather(pieces[5], "fsdp", axis=0, tiled=True),
        lax.all_gather(pieces[6], "fsdp", axis=0, tiled=True),
        lax.all_gather(pieces[7], "fsdp", axis=0, tiled=True),
        lax.all_gather(pieces[8], "fsdp", axis=0, tiled=True),
        lax.all_gather(pieces[9], "fsdp", axis=0, tiled=True),
        lax.all_gather(pieces[10], "fsdp", axis=0, tiled=True),
        lax.all_gather(pieces[11], "fsdp", axis=0, tiled=True),
        lax.all_gather(pieces[12], "fsdp", axis=0, tiled=True),
    )


def reduce_grads(grads):
    shares = (
        lax.psum_scatter(grads[0], "fsdp", scatter_dimension=0, tiled=True),
        lax.psum_scatter(grads[1], "fsdp", scatter_dimension=0, tiled=True),
        lax.psum_scatter(grads[2].astype(jnp.bfloat16), "fsdp", scatter_dimension=0, tiled=True),
        lax.psum_scatter(grads[3], "fsdp", scatter_dimension=0, tiled=True),
        lax.psum_scatter(grads[4], "fsdp", scatter_dimension=0, tiled=True),
        lax.psum_scatter(grads[5].astype(jnp.bfloat16), "fsdp", scatter_dimension=0, tiled=True),
        lax.psum_scatter(grads[6], "fsdp", scatter_dimension=0, tiled=True),
        lax.psum_scatter(grads[7], "fsdp", scatter_dimension=0, tiled=True),
        lax.psum_scatter(grads[8], "fsdp", scatter_dimension=0, tiled=True),
        lax.psum_scatter(grads[9].astype(jnp.bfloat16), "fsdp", scatter_dimension=0, tiled=True),
        lax.psum_scatter(grads[10], "fsdp", scatter_dimension=0, tiled=True),
        lax.psum_scatter(grads[11].astype(jnp.bfloat16), "fsdp", scatter_dimension=0, tiled=True),
        lax.psum_scatter(grads[12], "fsdp", scatter_dimension=0, tiled=True),
    )
    column_parts = (
        lax.psum_scatter(
            shares[2], "dp", scatter_dimension=1, tiled=True
        ).astype(jnp.float32),
        lax.psum_scatter(
            shares[5], "dp", scatter_dimension=1, tiled=True
        ).astype(jnp.float32),
        lax.psum_scatter(
            shares[9], "dp", scatter_dimension=1, tiled=True
        ).astype(jnp.float32),
        lax.psum_scatter(
            shares[11], "dp", scatter_dimension=1, tiled=True
        ).astype(jnp.float32),
    )
    matrices = (
        lax.all_gather(column_parts[0].astype(jnp.bfloat16), "dp", axis=1, tiled=True).astype(
            jnp.float32
        ),
        lax.all_gather(column_parts[1].astype(jnp.bfloat16), "dp", axis=1, tiled=True).astype(
            jnp.float32
        ),
        lax.all_gather(column_parts[2].astype(jnp.bfloat16), "dp", axis=1, tiled=True).astype(
            jnp.float32
        ),
        lax.all_gather(column_parts[3].astype(jnp.bfloat16), "dp", axis=1, tiled=True).astype(
            jnp.float32
        ),
    )
    vectors = lax.psum(
        (
            shares[0],
            shares[1],
            shares[3],
            shares[4],
            shares[6],
            shares[7],
            shares[8],
            shares[10],
            shares[12],
        ),
        "dp",
    )
    return (
        vectors[0],
        vectors[1],
        matrices[0],
        vectors[2],
        vectors[3],
        matrices[1],
        vectors[4],
        vectors[5],
        vectors[6],
        matrices[2],
        vectors[7],
        matrices[3],
        vectors[8],
    )


def attend_crops(queries, keys_in, values_in, crop_count, crop_length):
    shape_four = (crop_count, crop_length, HEADS, HEAD_DIM)
    scores = jnp.einsum(
        "clhe,cmhe->chlm",
        queries.reshape(shape_four),
        keys_in.reshape(shape_four),
        preferred_element_type=jnp.float32,
    ) * HEAD_DIM ** (-0.5)
    peak_score = jnp.max(scores, axis=-1, keepdims=True)
    raised = jnp.exp(scores - peak_score)
    exp_total = jnp.sum(raised, axis=-1, keepdims=True)
    attn_probs = (raised / exp_total).astype(jnp.bfloat16)
    log_total = peak_score + jnp.log(exp_total)
    result = jnp.einsum(
        "chlm,cmhe->clhe",
        attn_probs,
        values_in.reshape(shape_four),
        preferred_element_type=jnp.float32,
    )
    return (result.reshape(crop_count * crop_length, D), log_total)


def attend_back(queries, keys_in, values_in, log_total, grad_mixed, crop_count, crop_length):
    shape_four = (crop_count, crop_length, HEADS, HEAD_DIM)
    score_scale = HEAD_DIM ** (-0.5)
    query_four = queries.reshape(shape_four)
    key_four = keys_in.reshape(shape_four)
    value_four = values_in.reshape(shape_four)
    grad_four = grad_mixed.reshape(shape_four)
    scores = (
        jnp.einsum("clhe,cmhe->chlm", query_four, key_four, preferred_element_type=jnp.float32)
        * score_scale
    )
    attn_probs = jnp.exp(scores - log_total)
    grad_probs = jnp.einsum(
        "clhe,cmhe->chlm", grad_four, value_four, preferred_element_type=jnp.float32
    )
    grad_values = jnp.einsum(
        "chlm,clhe->cmhe",
        attn_probs.astype(jnp.bfloat16),
        grad_four,
        preferred_element_type=jnp.float32,
    )
    row_inner = jnp.sum(grad_probs * attn_probs, axis=-1, keepdims=True)
    grad_scores = (attn_probs * (grad_probs - row_inner)).astype(jnp.bfloat16)
    grad_queries = (
        jnp.einsum("chlm,cmhe->clhe", grad_scores, key_four, preferred_element_type=jnp.float32)
        * score_scale
    )
    grad_keys = (
        jnp.einsum("chlm,clhe->cmhe", grad_scores, query_four, preferred_element_type=jnp.float32)
        * score_scale
    )
    rows_here = crop_count * crop_length
    return jnp.concatenate(
        [
            grad_queries.reshape(rows_here, D),
            grad_keys.reshape(rows_here, D),
            grad_values.reshape(rows_here, D),
        ],
        axis=1,
    )


def forward_layer(stream, weights):
    (
        gain_one,
        shift_one,
        w_qkv,
        bias_query,
        bias_value,
        w_out,
        bias_out,
        gain_two,
        shift_two,
        w_up,
        bias_up,
        w_down,
        bias_down,
    ) = weights
    normed = norm_rows(stream, gain_one.astype(jnp.float32), shift_one.astype(jnp.float32)).astype(
        jnp.bfloat16
    )
    bias_all = jnp.concatenate([bias_query, jnp.zeros_like(bias_query), bias_value]).astype(
        jnp.float32
    )
    projected = (jnp.dot(normed, w_qkv, preferred_element_type=jnp.float32) + bias_all).astype(
        jnp.bfloat16
    )
    global_rows = G_DEV * GLEN
    global_part, global_total = attend_crops(
        projected[:global_rows, :D],
        projected[:global_rows, D : 2 * D],
        projected[:global_rows, 2 * D :],
        G_DEV,
        GLEN,
    )
    local_part, local_total = attend_crops(
        projected[global_rows:, :D],
        projected[global_rows:, D : 2 * D],
        projected[global_rows:, 2 * D :],
        L_DEV,
        LLEN,
    )
    mixed = jnp.concatenate([global_part, local_part], axis=0).astype(jnp.bfloat16)
    stream_one = (
        stream
        + jnp.dot(mixed, w_out, preferred_element_type=jnp.float32)
        + bias_out.astype(jnp.float32)
    )
    normed_two = norm_rows(
        stream_one, gain_two.astype(jnp.float32), shift_two.astype(jnp.float32)
    ).astype(jnp.bfloat16)
    pre_act = jnp.dot(normed_two, w_up, preferred_element_type=jnp.float32) + bias_up.astype(
        jnp.float32
    )
    hidden = jax.nn.gelu(pre_act, approximate=False).astype(jnp.bfloat16)
    result = (
        stream_one
        + jnp.dot(hidden, w_down, preferred_element_type=jnp.float32)
        + bias_down.astype(jnp.float32)
    )
    saved_state = (
        stream,
        normed,
        projected,
        global_total,
        local_total,
        mixed,
        stream_one,
        normed_two,
        pre_act,
        hidden,
    )
    return (result, saved_state)


def backward_layer(upstream, weights, saved_state):
    (
        gain_one,
        shift_one,
        w_qkv,
        bias_query,
        bias_value,
        w_out,
        bias_out,
        gain_two,
        shift_two,
        w_up,
        bias_up,
        w_down,
        bias_down,
    ) = weights
    (
        stream,
        normed,
        projected,
        global_total,
        local_total,
        mixed,
        stream_one,
        normed_two,
        pre_act,
        hidden,
    ) = saved_state
    branch_two = upstream.astype(jnp.bfloat16)
    grad_bias_down = jnp.sum(branch_two.astype(jnp.float32), axis=0)
    grad_w_down = contract_rows(hidden, branch_two)
    grad_hidden = contract_cols(branch_two, w_down)
    unused, gelu_pull = jax.vjp(lambda value: jax.nn.gelu(value, approximate=False), pre_act)
    grad_pre = gelu_pull(grad_hidden)[0].astype(jnp.bfloat16)
    grad_bias_up = jnp.sum(grad_pre.astype(jnp.float32), axis=0)
    grad_w_up = contract_rows(normed_two, grad_pre)
    grad_normed_two = contract_cols(grad_pre, w_up)
    unused_two, norm_pull_two = jax.vjp(
        norm_rows, stream_one, gain_two.astype(jnp.float32), shift_two.astype(jnp.float32)
    )
    grad_stream_part, grad_gain_two, grad_shift_two = norm_pull_two(grad_normed_two)
    grad_stream_one = upstream + grad_stream_part
    branch_one = grad_stream_one.astype(jnp.bfloat16)
    grad_bias_out = jnp.sum(branch_one.astype(jnp.float32), axis=0)
    grad_w_out = contract_rows(mixed, branch_one)
    grad_mixed = contract_cols(branch_one, w_out).astype(jnp.bfloat16)
    global_rows = G_DEV * GLEN
    grad_global = attend_back(
        projected[:global_rows, :D],
        projected[:global_rows, D : 2 * D],
        projected[:global_rows, 2 * D :],
        global_total,
        grad_mixed[:global_rows],
        G_DEV,
        GLEN,
    )
    grad_local = attend_back(
        projected[global_rows:, :D],
        projected[global_rows:, D : 2 * D],
        projected[global_rows:, 2 * D :],
        local_total,
        grad_mixed[global_rows:],
        L_DEV,
        LLEN,
    )
    grad_projected = jnp.concatenate([grad_global, grad_local], axis=0).astype(jnp.bfloat16)
    column_sums = jnp.sum(grad_projected.astype(jnp.float32), axis=0)
    grad_bias_query = column_sums[:D]
    grad_bias_value = column_sums[2 * D :]
    grad_w_qkv = contract_rows(normed, grad_projected)
    grad_normed = contract_cols(grad_projected, w_qkv)
    unused_one, norm_pull_one = jax.vjp(
        norm_rows, stream, gain_one.astype(jnp.float32), shift_one.astype(jnp.float32)
    )
    grad_input_part, grad_gain_one, grad_shift_one = norm_pull_one(grad_normed)
    grad_stream = grad_stream_one + grad_input_part
    grads = (
        grad_gain_one,
        grad_shift_one,
        grad_w_qkv,
        grad_bias_query,
        grad_bias_value,
        grad_w_out,
        grad_bias_out,
        grad_gain_two,
        grad_shift_two,
        grad_w_up,
        grad_bias_up,
        grad_w_down,
        grad_bias_down,
    )
    return (grad_stream, grads)


def local(
    tokens,
    cotangent,
    norm1_gain,
    norm1_bias,
    qkv_weight,
    query_bias,
    value_bias,
    out_weight,
    out_bias,
    norm2_gain,
    norm2_bias,
    up_weight,
    up_bias,
    down_weight,
    down_bias,
):
    shards = (
        norm1_gain,
        norm1_bias,
        qkv_weight,
        query_bias,
        value_bias,
        out_weight,
        out_bias,
        norm2_gain,
        norm2_bias,
        up_weight,
        up_bias,
        down_weight,
        down_bias,
    )
    layer_total = qkv_weight.shape[0]
    stream = tokens.astype(jnp.float32)
    saved_layers = []
    kept_weights = []
    for layer_index in range(layer_total):
        weights = gather_forward(tuple((w[layer_index] for w in shards)))
        stream, saved_state = forward_layer(stream, weights)
        saved_layers.append(saved_state)
        kept_weights.append(weights)
    encoded = stream.astype(jnp.bfloat16)
    upstream = cotangent.astype(jnp.float32)
    reduced_layers = [None] * layer_total
    for layer_index in reversed(range(layer_total)):
        upstream, grads = backward_layer(
            upstream, kept_weights[layer_index], saved_layers[layer_index]
        )
        reduced_layers[layer_index] = reduce_grads(grads)
    stacked = tuple(
        (
            jnp.stack(
                [reduced_layers[layer_index][member] for layer_index in range(layer_total)], axis=0
            )
            for member in range(13)
        )
    )
    return (
        encoded,
        upstream,
        stacked[0],
        stacked[1],
        stacked[2],
        stacked[3],
        stacked[4],
        stacked[5],
        stacked[6],
        stacked[7],
        stacked[8],
        stacked[9],
        stacked[10],
        stacked[11],
        stacked[12],
    )


VMEM_BYTES = 65408 * 1024

MESH = pl.DeviceIdType.MESH
F32 = jnp.float32
BF16 = jnp.bfloat16

FF = 3072
ROWS = 345
PAD = 352
STEP = 32
UNROLL = True
SHARD = 96
HALF = 48
UNITS = 12
SLOTS = 7
CORE_SLOTS = 4
RING = 8
PARTS = 2
WIDE = D // PARTS
LAG_XY, LAG_LAST, LAG_Z1, LAG_Z2, LAG_OUT = 4, 6, 8, 10, 13
LAG_NEXT, LAG_PLANE, LAG_PASS, LAG_WHOLE = 2, 4, 8, 9
EARLY_UNITS = 2
EARLY_PIECES = EARLY_UNITS * PARTS
GAP = 3
EARLY = 3
VEC_EVERY = 4
TOP_ROWS = 208
KEYS = 256
LOW_KEY = PAD - KEYS
LOW_ROWS = PAD - TOP_ROWS
V_G1, V_B1, V_QB, V_VB, V_OB, V_G2, V_B2, V_DB, V_UB = range(9)


def nt(left, right):
    return lax.dot_general(left, right, (((1,), (1,)), ((), ())), preferred_element_type=F32)


def tn(left, right):
    return lax.dot_general(left, right, (((0,), (0,)), ((), ())), preferred_element_type=F32)


def nn(left, right):
    return lax.dot_general(left, right, (((1,), (0,)), ((), ())), preferred_element_type=F32)


def aligned(value, by):
    return value if isinstance(value, int) else pl.multiple_of(value, by)


def shift(value, by):
    return lax.shift_right_arithmetic(value, jnp.int32(by))


def low_bits(value, by):
    return value - shift(value, by) * (1 << by)


def power_above(value):
    return (value - 1).bit_length()


def backward_unit(layers, index):
    whole = shift(index, 1)
    half = index - PARTS * whole
    turn = shift(whole * 43, 9)
    place = whole - UNITS * turn
    part = shift(place, 2)
    within = place - 4 * part
    is_down, is_late = shift(2 - part, 1), shift(part, 1)
    late = low_bits(within + 3, 2)
    unit = is_down * 8 + (1 - is_late) * place + is_late * late
    return layers - 1 - turn, unit, half


def stats(x):
    mean = jnp.mean(x, axis=-1, keepdims=True)
    centred = x - mean
    scale = lax.rsqrt(jnp.mean(centred * centred, axis=-1, keepdims=True) + epsilon)
    return centred * scale, scale


def fold(x):
    return jnp.sum(x.reshape(x.shape[0] // 8, 8, x.shape[1]), axis=0)


def total(x):
    return jnp.sum(x, axis=0, keepdims=True)


def step_rows(step):
    return pl.ds(aligned(step * STEP, STEP), STEP)


def encoder_kernel(
    layers,
    tokens,
    cotangent,
    n_g1,
    n_b1,
    n_qb,
    n_vb,
    n_ob,
    n_g2,
    n_b2,
    n_db,
    n_ub,
    w_qkv,
    w_out,
    w_up,
    w_down,
    encoded,
    tokens_grad,
    g_vec,
    g_qkv,
    g_out,
    g_up,
    g_down,
    wb,
    xs,
    x1,
    nr,
    pj,
    mx,
    n2,
    hd,
    gp,
    lse,
    gb,
    gm,
    br,
    acc,
    kacc,
    vacc,
    mask_top,
    mask_low,
    vsg,
    vec,
    ubs,
    gv,
    gvs,
    vr,
    vz,
    held,
    held_cot,
    held_grad,
    rc,
    r2,
    rz,
    ag_sem,
    ag_send,
    own_sem,
    core_sem,
    xy_sem,
    last_sem,
    z_sem,
    s0_send,
    rs_send,
    out_sem,
    vec_sem,
    gv_sem,
    io_sem,
):
    count = layers * UNITS
    pieces = count * PARTS
    d = lax.axis_index("dp")
    f = lax.axis_index("fsdp")
    c = lax.rem(f, 2)
    x = lax.rem(lax.div(f, 2), 2)
    y = lax.div(f, 4)
    fc = f + 1 - 2 * c
    fx = f + 2 - 4 * x
    fy = f + 4 - 8 * y
    outer = d * (3 - d) == 0
    inner = d * (3 - d) != 0
    z_in = 1 + lax.div(d, 3)
    z_out = 3 * lax.div(d, 2)
    z_pair = 3 - d
    parity = lax.rem(d, 2)
    z_near = d + 1 - 2 * parity
    in_plane = lambda who: {"fsdp": who}
    along = lambda who: {"dp": who}
    both = lambda a, b: jnp.logical_and(a, b)

    first_rows = pl.ds(0, HALF)
    second_rows = pl.ds(HALF, HALF)

    def send(source, target, sent, landed, who):
        pltpu.make_async_remote_copy(
            src_ref=source,
            dst_ref=target,
            send_sem=sent,
            recv_sem=landed,
            device_id=who,
            device_id_type=MESH,
        ).start()

    def wait_blocks(sem, blocks):
        span = wb.at[pl.ds(0, blocks), 0, 0, 0]
        pltpu.make_async_copy(span, span, sem).wait()

    def wait_half(sem):
        span = wb.at[0, 0, 0, 0, pl.ds(0, HALF)]
        pltpu.make_async_copy(span, span, sem).wait()

    def wait_piece(sem, blocks):
        span = wb.at[pl.ds(0, blocks), 0, 0, 0, :, pl.ds(0, WIDE)]
        pltpu.make_async_copy(span, span, sem).wait()

    barrier = pltpu.get_barrier_semaphore()
    peers = [lax.rem(f + hop, 8) for hop in range(1, 8)]
    for peer in peers:
        pl.semaphore_signal(barrier, inc=1, device_id=in_plane(peer), device_id_type=MESH)

    @pl.when(outer)
    def _():
        pl.semaphore_signal(barrier, inc=1, device_id=along(z_in), device_id_type=MESH)

    @pl.when(inner)
    def _():
        pl.semaphore_signal(barrier, inc=1, device_id=along(z_out), device_id_type=MESH)
        pl.semaphore_signal(barrier, inc=1, device_id=along(z_pair), device_id_type=MESH)

    for layer in range(layers):
        for unit in range(UNITS):
            if unit < 3:
                source = w_qkv.at[layer, :, pl.ds(unit * D, D)]
            elif unit == 3:
                source = w_out.at[layer]
            elif unit < 8:
                source = w_up.at[layer, :, pl.ds((unit - 4) * D, D)]
            else:
                source = w_down.at[layer, pl.ds((unit - 8) * SHARD, SHARD)]
            pltpu.make_async_copy(
                source,
                wb.at[layer * UNITS + unit, y, x, c],
                own_sem.at[layer],
            ).start()
    small = acc.at[0 : 16 * layers, 0:128]
    small[...] = jnp.zeros((16 * layers, 128), F32)
    for at, source in enumerate((n_g1, n_b1, n_qb, n_vb, n_ob, n_g2, n_b2, n_db)):
        shard = source[...].astype(F32)
        for layer in range(layers):
            row = 8 * layer + at
            acc[row : row + 1, 0:SHARD] = shard[layer : layer + 1]
    shard = n_ub[...].astype(F32)
    for layer in range(layers):
        for third in range(3):
            row = 8 * layers + 3 * layer + third
            acc[row : row + 1, 0:128] = shard[layer : layer + 1, third * 128 : third * 128 + 128]
    vsg[f] = small[...].astype(BF16)
    tokens_in = pltpu.make_async_copy(tokens, held, io_sem.at[0])
    cotangent_in = pltpu.make_async_copy(cotangent, held_cot, io_sem.at[1])
    encoded_out = pltpu.make_async_copy(held, encoded, io_sem.at[2])
    tokens_out = pltpu.make_async_copy(held_grad, tokens_grad, io_sem.at[3])
    tokens_in.start()
    cotangent_in.start()
    gvs[...] = jnp.zeros((8, 16, 128), F32)
    pl.semaphore_wait(barrier, 8 + lax.div(d * (3 - d), 2))

    def role(i):
        bits = power_above(count)
        of_three = i - 3 * shift(i * 43, 7)
        return of_three * shift((1 << bits) + count - 3 - i, bits)

    def collects(i):
        return role(i) != 2 - parity

    def gather_tick(t):
        @pl.when(t < count)
        def _():
            own = wb.at[t, y, x, c]

            @pl.when(lax.rem(t, UNITS) == 0)
            def _():
                wait_blocks(own_sem.at[lax.div(t, UNITS)], UNITS)

            @pl.when(collects(t))
            def _():
                first = wb.at[t, y, x, c, first_rows]
                second = wb.at[t, y, x, c, second_rows]
                send(first, first, ag_send.at[0], ag_sem.at[t, 0], in_plane(fy))
                send(second, second, ag_send.at[0], ag_sem.at[t, 1], in_plane(fx))
                send(first, first, ag_send.at[0], ag_sem.at[t, 2], in_plane(fx))
                send(second, second, ag_send.at[0], ag_sem.at[t, 2], in_plane(fy))

            send(own, own, ag_send.at[0], ag_sem.at[t, 3], in_plane(fc))

        @pl.when(both(both(t >= LAG_NEXT, t < count + LAG_NEXT), collects(t - LAG_NEXT)))
        def _():
            i = t - LAG_NEXT
            wait_half(ag_sem.at[i, 0])
            wait_half(ag_sem.at[i, 1])
            first = wb.at[i, 1 - y, x, c, first_rows]
            second = wb.at[i, y, 1 - x, c, second_rows]
            send(first, first, ag_send.at[0], ag_sem.at[i, 2], in_plane(fx))
            send(second, second, ag_send.at[0], ag_sem.at[i, 2], in_plane(fy))

        @pl.when(both(both(t >= LAG_PLANE, t < count + LAG_PLANE), collects(t - LAG_PLANE)))
        def _():
            i = t - LAG_PLANE
            wait_blocks(ag_sem.at[i, 2], 2)
            for piece in (wb.at[i, 1 - y, :, c], wb.at[i, y, 1 - x, c]):

                @pl.when(role(i) > 0)
                def _(piece=piece):
                    send(piece, piece, ag_send.at[0], ag_sem.at[i, 0], along(z_near))

                send(piece, piece, ag_send.at[0], ag_sem.at[i, 3], in_plane(fc))

        @pl.when(both(both(t >= LAG_PASS, t < count + LAG_PASS), role(t - LAG_PASS) == 2 - parity))
        def _():
            i = t - LAG_PASS
            wait_blocks(ag_sem.at[i, 0], 3)
            for piece in (wb.at[i, 1 - y, :, c], wb.at[i, y, 1 - x, c]):
                send(piece, piece, ag_send.at[0], ag_sem.at[i, 3], in_plane(fc))

        @pl.when(both(t >= LAG_WHOLE, t < count + LAG_WHOLE))
        def _():
            wait_blocks(ag_sem.at[t - LAG_WHOLE, 3], 4)

    for peer in peers:
        send(vsg.at[f], vsg.at[f], vec_sem.at[0], vec_sem.at[1], in_plane(peer))

    @pl.loop(0, EARLY)
    def _(t):
        gather_tick(t)

    def crop_of(shape, dim, start):
        at = lax.broadcasted_iota(jnp.int32, shape, dim) + start
        which = jnp.zeros(shape, jnp.int32)
        for edge in range(L_DEV + 1):
            which = which + (at >= GLEN + edge * LLEN).astype(jnp.int32)
        return which

    for mask, rows, row_at, key_at in (
        (mask_top, TOP_ROWS, 0, 0),
        (mask_low, LOW_ROWS, TOP_ROWS, LOW_KEY),
    ):
        same = crop_of((rows, KEYS), 0, row_at) == crop_of((rows, KEYS), 1, key_at)
        mask[...] = jnp.where(same, 0.0, -1e30).astype(F32)

    xs[0, PAD - 8 :, :] = jnp.zeros((8, D), F32)
    tokens_in.wait()
    xs[0, 0:ROWS, :] = held[...].astype(F32)

    seven = vsg.at[pl.ds(0, 7)]
    pltpu.make_async_copy(seven, seven, vec_sem.at[1]).wait()
    spread = jnp.zeros((8 * layers, D), F32)
    for owner in range(8):
        at_row = lax.broadcasted_iota(jnp.int32, (128, D), 0)
        at_col = lax.broadcasted_iota(jnp.int32, (128, D), 1)
        hit = jnp.logical_and(at_col == at_row + owner * SHARD, at_row < SHARD)
        spread = spread + nn(vsg[owner, 0 : 8 * layers, :], jnp.where(hit, 1.0, 0.0).astype(BF16))
        wide = vsg[owner, 8 * layers :, :].astype(F32)
        for layer in range(layers):
            for third in range(3):
                row, lane = 3 * layer + third, owner * 4 * SHARD + third * 128
                ubs[layer : layer + 1, lane : lane + 128] = wide[row : row + 1]
    vec[...] = spread

    @pl.loop(EARLY, LAG_WHOLE)
    def _(t):
        gather_tick(t)

    def vector(layer, which):
        return vec[pl.ds(layer * 8 + which, 1), :]

    lane = lax.broadcasted_iota(jnp.int32, (1, 128), 1)
    left_lane = lane < HEAD_DIM
    score_scale = HEAD_DIM ** (-0.5)
    head_scaled = [
        jnp.where(left_lane, score_scale, 0.0).astype(BF16),
        jnp.where(left_lane, 0.0, score_scale).astype(BF16),
    ]
    head_plain = [
        jnp.where(left_lane, 1.0, 0.0).astype(BF16),
        jnp.where(left_lane, 0.0, 1.0).astype(BF16),
    ]
    groups = (
        (0, TOP_ROWS, 0, mask_top),
        (TOP_ROWS, LOW_ROWS, LOW_KEY, mask_low),
    )

    def weight(layer, unit):
        return wb[layer * UNITS + unit].reshape(D, D)

    def down_places(part):
        return [(unit, lax.div(part, 2), lax.rem(part, 2), core) for core in range(2) for unit in range(4)]

    def down_weight(layer, part):
        blocks = [wb[layer * UNITS + 8 + u, yy, xx, cc] for u, yy, xx, cc in down_places(part)]
        return jnp.concatenate(blocks, axis=0)

    def put_down(first, units, part, grad):
        for at, (u, yy, xx, cc) in enumerate(down_places(part)):
            if u < units:
                wb[first + u, yy, xx, cc] = grad[at * SHARD : (at + 1) * SHARD]

    def piece_at(i):
        layer, unit, half = backward_unit(layers, i)
        bits = power_above(pieces)
        early = shift((1 << bits) + EARLY_PIECES - 1 - i, bits)
        ahead = layers * UNITS + shift(i, 1)
        at = early * ahead + (1 - early) * (layer * UNITS + unit)
        return at, pl.ds(aligned(half * WIDE, 128), WIDE)

    def during(t, lag):
        at = t - lag
        begun = jnp.logical_or(at < EARLY_PIECES, at >= EARLY_PIECES + GAP)
        return both(begun, both(at >= 0, at < pieces + GAP))

    def piece_of(t, lag):
        at = t - lag
        bits = power_above(2 * pieces)
        return at - GAP * shift(at + (1 << bits) - (EARLY_PIECES + GAP), bits)

    def ring(i):
        return low_bits(i, 3)

    def long_ring(i):
        return low_bits(i, 4)

    def slot_of(i):
        return i - SLOTS * shift(i * 37, 8)

    def reduce_tick(t):
        @pl.when(during(t, 0))
        def _():
            i = piece_of(t, 0)
            n, cols = piece_at(i)
            send(
                wb.at[n, :, :, 1 - c, :, cols],
                rc.at[low_bits(i, 2)],
                s0_send.at[ring(i)],
                core_sem.at[ring(i)],
                in_plane(fc),
            )

        @pl.when(during(t, LAG_XY))
        def _():
            i = piece_of(t, LAG_XY)
            n, cols = piece_at(i)
            slot = slot_of(i)
            wait_piece(xy_sem.at[ring(i)], 2)
            along_x = wb.at[n, :, x, c, first_rows, cols]
            along_y = wb.at[n, y, :, c, second_rows, cols]
            along_x[...] = along_x[...] + r2[slot, 0]
            along_y[...] = along_y[...] + r2[slot, 1]
            send(
                wb.at[n, 1 - y, x, c, first_rows, cols],
                wb.at[n, 1 - y, x, 1 - c, first_rows, cols],
                rs_send.at[long_ring(i)],
                last_sem.at[ring(i)],
                in_plane(fy),
            )
            send(
                wb.at[n, y, 1 - x, c, second_rows, cols],
                wb.at[n, y, 1 - x, 1 - c, second_rows, cols],
                rs_send.at[long_ring(i)],
                last_sem.at[ring(i)],
                in_plane(fx),
            )

        @pl.when(during(t, 1))
        def _():
            i = piece_of(t, 1)
            n, cols = piece_at(i)
            slot = slot_of(i)
            wait_piece(core_sem.at[ring(i)], 4)
            wait_piece(s0_send.at[ring(i)], 4)
            mine = wb.at[n, :, :, c, :, cols]
            mine[...] = mine[...] + rc[low_bits(i, 2)]
            send(
                wb.at[n, :, 1 - x, c, first_rows, cols],
                r2.at[slot, 0],
                rs_send.at[long_ring(i)],
                xy_sem.at[ring(i)],
                in_plane(fx),
            )
            send(
                wb.at[n, 1 - y, :, c, second_rows, cols],
                r2.at[slot, 1],
                rs_send.at[long_ring(i)],
                xy_sem.at[ring(i)],
                in_plane(fy),
            )

        @pl.when(during(t, LAG_OUT))
        def _():
            i = piece_of(t, LAG_OUT)
            n, cols = piece_at(i)
            layer, unit, half = backward_unit(layers, i)

            @pl.when(outer)
            def _():
                wait_piece(z_sem.at[ring(i), 2], 1)

            done = wb.at[n, y, x, 1 - c, :, cols]

            @pl.when(outer)
            def _():
                wait_piece(rs_send.at[long_ring(i)], 4)

            @pl.when(inner)
            def _():
                wait_piece(rs_send.at[long_ring(i)], 5)

            @pl.when(i >= RING)
            def _():
                wait_piece(out_sem.at[ring(i)], 1)

            def emit(target):
                pltpu.make_async_copy(done, target, out_sem.at[ring(i)]).start()

            def wide_at(first):
                return pl.ds(aligned((unit - first) * D + half * WIDE, 128), WIDE)

            @pl.when(unit < 3)
            def _():
                emit(g_qkv.at[layer, :, wide_at(0)])

            @pl.when(unit == 3)
            def _():
                emit(g_out.at[layer, :, cols])

            @pl.when(both(unit >= 4, unit < 8))
            def _():
                emit(g_up.at[layer, :, wide_at(4)])

            @pl.when(unit >= 8)
            def _():
                rows = pl.ds(aligned((unit - 8) * SHARD, 16), SHARD)
                emit(g_down.at[layer, rows, cols])

        @pl.when(during(t, LAG_LAST))
        def _():
            i = piece_of(t, LAG_LAST)
            n, cols = piece_at(i)
            wait_piece(last_sem.at[ring(i)], 1)
            own = wb.at[n, y, x, c, :, cols]
            own[...] = own[...] + wb[n, y, x, 1 - c, :, cols]

            @pl.when(outer)
            def _():
                to = rz.at[slot_of(i), 0]
                send(own, to, rs_send.at[long_ring(i)], z_sem.at[ring(i), 0], along(z_in))

        @pl.when(both(inner, during(t, LAG_Z1)))
        def _():
            i = piece_of(t, LAG_Z1)
            n, cols = piece_at(i)
            slot = slot_of(i)
            wait_piece(z_sem.at[ring(i), 0], 1)
            own = wb.at[n, y, x, c, :, cols]
            own[...] = own[...] + rz[slot, 0]
            send(own, rz.at[slot, 1], rs_send.at[long_ring(i)], z_sem.at[ring(i), 1], along(z_pair))

        @pl.when(both(inner, during(t, LAG_Z2)))
        def _():
            i = piece_of(t, LAG_Z2)
            n, cols = piece_at(i)
            wait_piece(z_sem.at[ring(i), 1], 1)
            done = wb.at[n, y, x, 1 - c, :, cols]
            done[...] = wb[n, y, x, c, :, cols] + rz[slot_of(i), 1]
            send(done, done, rs_send.at[long_ring(i)], z_sem.at[ring(i), 2], along(z_out))

    @pl.loop(0, layers)
    def _(layer):
        base = layer * UNITS + LAG_WHOLE

        @pl.loop(0, PAD // STEP, unroll=UNROLL)
        def _(step):
            rows = step_rows(step)
            normed, _unused = stats(xs[layer, rows, :])
            nr[layer, rows, :] = (normed * vector(layer, V_G1) + vector(layer, V_B1)).astype(BF16)

        @pl.loop(0, 3)
        def _(part):
            gather_tick(base + part)
            is_q, is_v = lax.div(2 - part, 2), lax.div(part, 2)
            bias = is_q.astype(F32) * vector(layer, V_QB) + is_v.astype(F32) * vector(layer, V_VB)
            acc[...] = nn(nr[layer], weight(layer, part))

            @pl.loop(0, PAD // STEP, unroll=UNROLL)
            def _(step):
                rows = step_rows(step)
                pj[layer, part, rows, :] = (acc[rows, :] + bias).astype(BF16)

        @pl.loop(0, HEADS // 2)
        def _(pair):
            @pl.when(pair == 3)
            def _():
                gather_tick(base + 3)

            lanes = pl.ds(aligned(pair * 128, 128), 128)
            for row_at, rows, key_at, mask in groups:
                here = pl.ds(row_at, rows)
                keys = pj[layer, 1, pl.ds(key_at, KEYS), lanes]
                values = pj[layer, 2, pl.ds(key_at, KEYS), lanes]
                queries = pj[layer, 0, here, lanes]
                results = []
                for side in range(2):
                    scores = nt(queries * head_scaled[side], keys) + mask[...]
                    peak = jnp.max(scores, axis=-1, keepdims=True)
                    raised = jnp.exp(scores - peak)
                    exp_total = jnp.sum(raised, axis=-1, keepdims=True)
                    probs = (raised * (1.0 / exp_total)).astype(BF16)
                    results.append(nn(probs, values))
                    log_total = peak + jnp.log(exp_total)
                    lse[layer, here, :] = jnp.where(
                        lane == pair * 2 + side, log_total, lse[layer, here, :]
                    )
                mx[layer, here, lanes] = jnp.where(left_lane, results[0], results[1]).astype(BF16)

        acc[...] = nn(mx[layer], weight(layer, 3))

        @pl.loop(0, PAD // STEP, unroll=UNROLL)
        def _(step):
            rows = step_rows(step)
            now = xs[layer, rows, :] + acc[rows, :] + vector(layer, V_OB)
            x1[layer, rows, :] = now
            normed, _unused = stats(now)
            n2[layer, rows, :] = (normed * vector(layer, V_G2) + vector(layer, V_B2)).astype(BF16)

        @pl.when(layer == layers - 1)
        def _():
            acc[PAD - 8 :, :] = jnp.zeros((8, D), F32)
            cotangent_in.wait()
            acc[0:ROWS, :] = held_cot[...].astype(F32)
            br[...] = acc[...].astype(BF16)

        @pl.loop(0, 4)
        def _(part):
            gather_tick(base + 4 + part)
            bias = ubs[pl.ds(layer, 1), pl.ds(aligned(part * D, 128), D)]
            acc[...] = nn(n2[layer], weight(layer, 4 + part))

            @pl.loop(0, PAD // STEP, unroll=UNROLL)
            def _(step):
                rows = step_rows(step)
                pre = acc[rows, :] + bias
                cdf = 0.5 + 0.5 * lax.erf(pre * (0.5**0.5))
                bell = jnp.exp(-0.5 * pre * pre) * 0.3989422804014327
                hd[layer, part, rows, :] = (pre * cdf).astype(BF16)
                gp[layer, part, rows, :] = (cdf + pre * bell).astype(BF16)

            @pl.when(layer == layers - 1)
            def _():
                grad = tn(hd[layer, part], br[...]).astype(BF16)
                put_down(layers * UNITS, EARLY_UNITS, part, grad)

        @pl.loop(0, 4)
        def _(part):
            gather_tick(base + 8 + part)

        @pl.when(layer == layers - 1)
        def _():
            @pl.loop(0, 2)
            def _(t):
                reduce_tick(t)

        acc[...] = x1[layer] + vector(layer, V_DB)

        @pl.loop(0, 4)
        def _(part):
            acc[...] += nn(hd[layer, part], down_weight(layer, part))

        xs[layer + 1] = acc[...]

    reduce_tick(2)
    held[...] = xs[layers, 0:ROWS, :].astype(BF16)
    encoded_out.start()

    span = wb.at[pl.ds(0, 7 * count // 8)]
    pltpu.make_async_copy(span, span, ag_send.at[0]).wait()
    pltpu.make_async_copy(seven, seven, vec_sem.at[0]).wait()

    def vector_step(layer, step):
        def wait_vec(at, copies):
            span = gvs.at[pl.ds(0, copies)]
            pltpu.make_async_copy(span, span, gv_sem.at[layer, at]).wait()

        def z_go(source, target, at, who):
            send(
                vz.at[layer, source],
                vz.at[layer, target],
                gv_sem.at[layer, at],
                gv_sem.at[layer, at + 1],
                along(who),
            )

        @pl.when(step == 0)
        def _():
            for owner in range(8):
                gvs[owner, 0:8, 0:SHARD] = gv[layer, 0:8, owner * SHARD : (owner + 1) * SHARD]
                row = 8 + owner // 2
                for third in range(3):
                    lane = (owner % 2) * 4 * SHARD + third * 128
                    wide = gv[layer, row : row + 1, lane : lane + 128]
                    gvs[owner, 8 + third : 9 + third, :] = wide
            vr[layer, f] = gvs[f]
            for peer in peers:
                send(
                    gvs.at[peer],
                    vr.at[layer, f],
                    gv_sem.at[layer, 0],
                    gv_sem.at[layer, 1],
                    in_plane(peer),
                )

        @pl.when(step == 1)
        def _():
            wait_vec(0, 7)
            wait_vec(1, 7)
            in_sum = vr[layer, 0]
            for source in range(1, 8):
                in_sum = in_sum + vr[layer, source]
            vz[layer, 0] = in_sum

            @pl.when(outer)
            def _():
                z_go(0, 1, 2, z_in)

        @pl.when(both(inner, step == 2))
        def _():
            wait_vec(3, 1)
            vz[layer, 0] = vz[layer, 0] + vz[layer, 1]
            z_go(0, 2, 4, z_pair)

        @pl.when(both(inner, step == 3))
        def _():
            wait_vec(4, 1)
            wait_vec(5, 1)
            vz[layer, 3] = vz[layer, 0] + vz[layer, 2]
            z_go(3, 3, 6, z_out)

        @pl.when(step == 4)
        def _():
            @pl.when(outer)
            def _():
                wait_vec(2, 1)
                wait_vec(7, 1)

            @pl.when(inner)
            def _():
                wait_vec(6, 1)

            g_vec[layer] = vz[layer, 3]

    up = xs.at[layers]
    up[PAD - 8 :, :] = jnp.zeros((8, D), F32)
    up[0:ROWS, :] = held_cot[...].astype(F32)
    none = jnp.zeros((8, D), F32)

    def put_vector(layer, which, value):
        gv[layer, pl.ds(which, 1), :] = total(value)

    def weight_grad(unit, left, right):
        grad = tn(left[...], right[...]).astype(BF16)
        wb[unit] = grad.reshape(2, 2, 2, SHARD, D)

    @pl.loop(0, layers)
    def _(turn):
        layer = layers - 1 - turn
        base = EARLY_PIECES + GAP + turn * (UNITS * PARTS - 4)

        def branch_two(step, carry):
            rows = step_rows(step)
            rounded = up[rows, :].astype(BF16)
            br[rows, :] = rounded
            return carry + fold(rounded.astype(F32))

        put_vector(layer, V_DB, lax.fori_loop(0, PAD // STEP, branch_two, none, unroll=UNROLL))

        @pl.loop(0, 4)
        def _(part):
            reduce_tick(base - 4 + part)

            acc[...] = nt(br[...], down_weight(layer, part))

            def through_gelu(step, carry):
                rows = step_rows(step)
                value = (acc[rows, :] * gp[layer, part, rows, :].astype(F32)).astype(BF16)
                gb[part, rows, :] = value
                return carry + fold(value.astype(F32))

            put_vector(layer, V_UB + part, lax.fori_loop(0, PAD // STEP, through_gelu, none, unroll=UNROLL))
            grad = tn(hd[layer, part], br[...]).astype(BF16)
            put_down(layer * UNITS + 8, 4, part, grad)

        acc[...] = jnp.zeros((PAD, D), F32)

        @pl.loop(0, 4)
        def _(part):
            @pl.when(both(turn > 0, part == 0))
            def _():
                vector_step(layer + 1, 0)

            acc[...] += nt(gb[part], weight(layer, 4 + part))
            weight_grad(layer * UNITS + 4 + part, n2.at[layer], gb.at[part])
            reduce_tick(base + part)

        def norm_back(source, gain_at, shift_at):
            def body(step, carry):
                gain_sum, shift_sum = carry
                rows = step_rows(step)
                normed, scale = stats(source[layer, rows, :])
                grad = acc[rows, :]
                t = grad * vector(layer, gain_at)
                inner_mean = jnp.mean(t * normed, axis=-1, keepdims=True)
                back = scale * (t - jnp.mean(t, axis=-1, keepdims=True) - normed * inner_mean)
                up[rows, :] = up[rows, :] + back
                return gain_sum + fold(grad * normed), shift_sum + fold(grad)

            gain_sum, shift_sum = lax.fori_loop(0, PAD // STEP, body, (none, none), unroll=UNROLL)
            put_vector(layer, gain_at, gain_sum)
            put_vector(layer, shift_at, shift_sum)

        norm_back(x1, V_G2, V_B2)

        put_vector(layer, V_OB, lax.fori_loop(0, PAD // STEP, branch_two, none, unroll=UNROLL))
        gm[...] = nt(br[...], weight(layer, 3)).astype(BF16)
        weight_grad(layer * UNITS + 3, mx.at[layer], br)

        @pl.loop(0, 2)
        def _(again):
            reduce_tick(base + 4 + again)

        @pl.loop(0, HEADS // 2)
        def _(pair):
            reduce_tick(base + 6 + pair)

            @pl.when(both(turn > 0, lax.rem(pair, 2) == 0))
            def _():
                vector_step(layer + 1, 1 + lax.div(pair, 2))

            lanes = pl.ds(aligned(pair * 128, 128), 128)
            kacc[...] = jnp.zeros((PAD, 128), F32)
            vacc[...] = jnp.zeros((PAD, 128), F32)
            for row_at, rows, key_at, mask in groups:
                here = pl.ds(row_at, rows)
                there = pl.ds(key_at, KEYS)
                keys = pj[layer, 1, there, lanes]
                values = pj[layer, 2, there, lanes]
                queries = pj[layer, 0, here, lanes]
                grads = gm[here, lanes]
                q_parts, k_parts, v_parts = [], [], []
                for side in range(2):
                    log_total = jnp.sum(
                        jnp.where(lane == pair * 2 + side, lse[layer, here, :], 0.0),
                        axis=-1,
                        keepdims=True,
                    )
                    scaled = queries * head_scaled[side]
                    probs = jnp.exp(nt(scaled, keys) + mask[...] - log_total)
                    grad_probs = nt(grads * head_plain[side], values)
                    row_inner = jnp.sum(grad_probs * probs, axis=-1, keepdims=True)
                    grad_scores = (probs * (grad_probs - row_inner)).astype(BF16)
                    v_parts.append(tn(probs.astype(BF16), grads))
                    k_parts.append(tn(grad_scores, queries))
                    q_parts.append(nn(grad_scores, keys))
                grad_queries = jnp.where(left_lane, q_parts[0], q_parts[1]) * score_scale
                gb[0, here, lanes] = grad_queries.astype(BF16)
                kacc[there, :] += jnp.where(left_lane, k_parts[0], k_parts[1]) * score_scale
                vacc[there, :] += jnp.where(left_lane, v_parts[0], v_parts[1])
            gb[1, :, lanes] = kacc[...].astype(BF16)
            gb[2, :, lanes] = vacc[...].astype(BF16)

        for which, part in ((V_QB, 0), (V_VB, 2)):

            def column_sum(step, carry, part=part):
                return carry + fold(gb[part, step_rows(step), :].astype(F32))

            put_vector(layer, which, lax.fori_loop(0, PAD // STEP, column_sum, none, unroll=UNROLL))

        acc[...] = jnp.zeros((PAD, D), F32)

        @pl.loop(0, 3)
        def _(part):
            acc[...] += nt(gb[part], weight(layer, part))
            weight_grad(layer * UNITS + part, nr.at[layer], gb.at[part])

            reduce_tick(base + 12 + part)

            @pl.when(both(turn > 0, part == 1))
            def _():
                vector_step(layer + 1, 4)

        norm_back(xs, V_G1, V_B1)
        reduce_tick(base + 15)

    held_grad[...] = up[0:ROWS, :]
    tokens_out.start()
    encoded_out.wait()

    @pl.loop(pieces + GAP - 8, pieces + GAP + LAG_OUT)
    def _(t):
        step = t - (pieces + GAP - 8)

        @pl.when(both(lax.rem(step, VEC_EVERY) == 0, step < 5 * VEC_EVERY))
        def _():
            vector_step(0, lax.div(step, VEC_EVERY))

        reduce_tick(t)

    for at in range(RING):
        wait_piece(out_sem.at[at], 1)

    tokens_out.wait()


def closing_kernel(layers, *refs):
    encoded_in, tokens_in, vec_in = refs[:3]
    grads_in = refs[3:7]
    encoded_out, tokens_out = refs[7:9]
    small_out = refs[9:18]
    grads_out = refs[18:22]
    vec = refs[22]
    narrow = refs[23:27]
    wide = refs[27:31]
    held_encoded, held_tokens, few_sem, in_sem, out_sem = refs[31:]
    copies = [
        pltpu.make_async_copy(vec_in, vec, few_sem.at[0]),
        pltpu.make_async_copy(encoded_in, held_encoded, few_sem.at[1]),
        pltpu.make_async_copy(tokens_in, held_tokens, few_sem.at[2]),
    ]
    reads, writes = [], []
    for layer in range(layers):
        for at in range(4):
            reads.append(
                pltpu.make_async_copy(
                    grads_in[at].at[layer], narrow[at].at[layer], in_sem.at[at, layer]
                )
            )
            writes.append(
                pltpu.make_async_copy(
                    wide[at].at[layer], grads_out[at].at[layer], out_sem.at[at, layer]
                )
            )
    for copy in reads + copies:
        copy.start()
    for layer in range(layers):
        for at in range(4):
            reads[4 * layer + at].wait()
            wide[at][layer] = narrow[at][layer].astype(F32)
            writes[4 * layer + at].start()
    for copy in copies:
        copy.wait()
    writes.append(pltpu.make_async_copy(held_encoded, encoded_out, few_sem.at[1]))
    writes.append(pltpu.make_async_copy(held_tokens, tokens_out, few_sem.at[2]))
    writes[-2].start()
    writes[-1].start()
    for layer in range(layers):
        mine = vec[layer]
        for which in range(8):
            small_out[which][layer : layer + 1, :] = mine[which : which + 1, 0:SHARD]
        for third in range(3):
            lanes = slice(third * 128, third * 128 + 128)
            small_out[8][layer : layer + 1, lanes] = mine[8 + third : 9 + third]
    for copy in writes:
        copy.wait()


def kernel_local(
    tokens,
    cotangent,
    norm1_gain,
    norm1_bias,
    qkv_weight,
    query_bias,
    value_bias,
    out_weight,
    out_bias,
    norm2_gain,
    norm2_bias,
    up_weight,
    up_bias,
    down_weight,
    down_bias,
):
    layers = qkv_weight.shape[0]
    count = layers * UNITS
    pieces = count * PARTS
    hbm = pl.BlockSpec(memory_space=pltpu.MemorySpace.HBM)
    plain = pl.BlockSpec()
    dma = pltpu.SemaphoreType.DMA
    results = pl.pallas_call(
        functools.partial(encoder_kernel, layers),
        out_shape=(
            jax.ShapeDtypeStruct((ROWS, D), BF16),
            jax.ShapeDtypeStruct((ROWS, D), F32),
            jax.ShapeDtypeStruct((layers, 16, 128), F32),
            jax.ShapeDtypeStruct((layers, SHARD, 3 * D), BF16),
            jax.ShapeDtypeStruct((layers, SHARD, D), BF16),
            jax.ShapeDtypeStruct((layers, SHARD, FF), BF16),
            jax.ShapeDtypeStruct((layers, 4 * SHARD, D), BF16),
        ),
        in_specs=[hbm] * 2 + [plain] * 9 + [hbm] * 4,
        out_specs=(hbm, hbm, plain, hbm, hbm, hbm, hbm),
        scratch_shapes=[
            pltpu.VMEM((count + EARLY_UNITS, 2, 2, 2, SHARD, D), BF16),
            pltpu.VMEM((layers + 1, PAD, D), F32),
            pltpu.VMEM((layers, PAD, D), F32),
            pltpu.VMEM((layers, PAD, D), BF16),
            pltpu.VMEM((layers, 3, PAD, D), BF16),
            pltpu.VMEM((layers, PAD, D), BF16),
            pltpu.VMEM((layers, PAD, D), BF16),
            pltpu.VMEM((layers, 4, PAD, D), BF16),
            pltpu.VMEM((layers, 4, PAD, D), BF16),
            pltpu.VMEM((layers, PAD, 128), F32),
            pltpu.VMEM((4, PAD, D), BF16),
            pltpu.VMEM((PAD, D), BF16),
            pltpu.VMEM((PAD, D), BF16),
            pltpu.VMEM((PAD, D), F32),
            pltpu.VMEM((PAD, 128), F32),
            pltpu.VMEM((PAD, 128), F32),
            pltpu.VMEM((TOP_ROWS, KEYS), F32),
            pltpu.VMEM((LOW_ROWS, KEYS), F32),
            pltpu.VMEM((8, 16 * layers, 128), BF16),
            pltpu.VMEM((8 * layers, D), F32),
            pltpu.VMEM((layers, FF), F32),
            pltpu.VMEM((layers, 16, D), F32),
            pltpu.VMEM((8, 16, 128), F32),
            pltpu.VMEM((layers, 8, 16, 128), F32),
            pltpu.VMEM((layers, 4, 16, 128), F32),
            pltpu.VMEM((ROWS, D), BF16),
            pltpu.VMEM((ROWS, D), BF16),
            pltpu.VMEM((ROWS, D), F32),
            pltpu.VMEM((CORE_SLOTS, 2, 2, SHARD, WIDE), BF16),
            pltpu.VMEM((SLOTS, 2, 2, HALF, WIDE), BF16),
            pltpu.VMEM((SLOTS, 2, SHARD, WIDE), BF16),
            dma((count, 4)),
            dma((1,)),
            dma((layers,)),
            dma((RING,)),
            dma((RING,)),
            dma((RING,)),
            dma((RING, 3)),
            dma((RING,)),
            dma((2 * RING,)),
            dma((RING,)),
            dma((2,)),
            dma((layers, 8)),
            dma((4,)),
        ],
        compiler_params=pltpu.CompilerParams(
            collective_id=0, has_side_effects=True, vmem_limit_bytes=VMEM_BYTES
        ),
    )(
        tokens,
        cotangent,
        norm1_gain,
        norm1_bias,
        query_bias,
        value_bias,
        out_bias,
        norm2_gain,
        norm2_bias,
        down_bias,
        up_bias,
        qkv_weight,
        out_weight,
        up_weight,
        down_weight,
    )
    shapes = [(layers, SHARD)] * 8 + [(layers, 4 * SHARD)]
    shapes += [(layers, SHARD, 3 * D), (layers, SHARD, D), (layers, SHARD, FF)]
    shapes += [(layers, 4 * SHARD, D)]
    closing = pl.pallas_call(
        functools.partial(closing_kernel, layers),
        out_shape=[jax.ShapeDtypeStruct((ROWS, D), BF16), jax.ShapeDtypeStruct((ROWS, D), F32)]
        + [jax.ShapeDtypeStruct(shape, F32) for shape in shapes],
        in_specs=[hbm] * 7,
        out_specs=[hbm] * 2 + [plain] * 9 + [hbm] * 4,
        scratch_shapes=[pltpu.VMEM((layers, 16, 128), F32)]
        + [pltpu.VMEM(shape, BF16) for shape in shapes[9:]]
        + [pltpu.VMEM(shape, F32) for shape in shapes[9:]]
        + [pltpu.VMEM((ROWS, D), BF16), pltpu.VMEM((ROWS, D), F32)]
        + [dma((3,)), dma((4, layers)), dma((4, layers))],
        compiler_params=pltpu.CompilerParams(vmem_limit_bytes=VMEM_BYTES),
    )(*results)
    by = dict(zip(("encoded", "tokens_grad"), closing[:2]))
    small = closing[2:11]
    g_qkv, g_out, g_up, g_down = closing[11:]
    return (
        by["encoded"],
        by["tokens_grad"],
        small[V_G1],
        small[V_B1],
        g_qkv,
        small[V_QB],
        small[V_VB],
        g_out,
        small[V_OB],
        small[V_G2],
        small[V_B2],
        g_up,
        small[V_UB],
        g_down,
        small[V_DB],
    )


def solution(mesh):
    in_specs = (
        P(("dp", "fsdp"), None),
        P(("dp", "fsdp"), None),
        P(None, "fsdp"),
        P(None, "fsdp"),
        P(None, "fsdp", None),
        P(None, "fsdp"),
        P(None, "fsdp"),
        P(None, "fsdp", None),
        P(None, "fsdp"),
        P(None, "fsdp"),
        P(None, "fsdp"),
        P(None, "fsdp", None),
        P(None, "fsdp"),
        P(None, "fsdp", None),
        P(None, "fsdp"),
    )
    out_specs = (
        P(("dp", "fsdp"), None),
        P(("dp", "fsdp"), None),
        P(None, "fsdp"),
        P(None, "fsdp"),
        P(None, "fsdp", None),
        P(None, "fsdp"),
        P(None, "fsdp"),
        P(None, "fsdp", None),
        P(None, "fsdp"),
        P(None, "fsdp"),
        P(None, "fsdp"),
        P(None, "fsdp", None),
        P(None, "fsdp"),
        P(None, "fsdp", None),
        P(None, "fsdp"),
    )
    fits = mesh.shape["dp"] == 4 and mesh.shape["fsdp"] == 8
    body = kernel_local if fits else local
    return jax.shard_map(body, mesh=mesh, in_specs=in_specs, out_specs=out_specs, check_vma=False)
```
